32 devices in a mesh: grp: 2 (over x), row: 8 (over z, y), col: 2 (over core).
Axes of the slice: x: 2, y: 2, z: 4, core: 2. Of those that a mesh axis runs over, the one named last changes fastest.
Arguments:
- object_field: bfloat16 [2, 4096, 1024], P(None, ('grp', 'row'), 'col'), parts along dimension 1
- probe_modes: bfloat16 [2, 256, 8, 256], P(None, None, 'grp'), parts along dimension 2, may hold values from -6 to 6
- positions: int32 [16, 2, 4, 2], P(('grp', 'row'), 'col'), parts along dimension 0, may hold values from 0 to 1792, as said below
- counts: int32 [16, 2], P(('grp', 'row'), 'col'), parts along dimension 0, may hold values from 0 to 4, as said below
- intensities: bfloat16 [16, 2, 4, 256, 256], P(('grp', 'row'), 'col'), parts along dimension 0, may hold values from 0.5 to 64
Outputs:
- new_object: float32 [2, 4096, 1024], P(None, ('grp', 'row'), 'col'), parts along dimension 1
- new_probe: float32 [2, 256, 8, 256], P(None, None, 'grp'), parts along dimension 2
The draws below stay inside these ranges and needn't reach their ends.
There are 2 independent parts, one for each index of `grp`. The reference program is written for one: setup_inputs(seed, part) draws one part's arguments, and reference() takes and returns one part's arrays. A program takes and returns all parts, laid end to end along the dimension named above; each array names one. Nothing has to cross between parts.
Inputs may be any that keep to these rules, and one draw needn't show every extreme that they name: `positions`: every window lies inside the object, and every slot's start, live or not, lies inside the tile of the device that holds the slot. `counts`: the two tiles 2 j and 2 j + 1 along row (same col) hold exactly 4 live positions together; some tile is full in every draw.
All inputs are finite; a program needn't handle non-finite values.
Results may differ from the reference program's by a relative error of at most 0.0093.
Values may be sent and summed in bfloat16 or wider, within the bound.
No kernel may reach another device: no remote copies, remote signals or barrier semaphores. Data moves between devices by JAX's collectives and lax.ppermute only.
A program may use at most 64 MiB of HBM per device.

```python
import math
import jax
import jax.numpy as jnp
import numpy as np
from jax import lax

WIN = 256
MODES = 4
TR = 256
TC = 512
SLOTS = 4
NR = 2048
NC = 1024
N_ROW = 8
N_COL = 2


def draw_object_field(key, part):
    key = jax.random.fold_in(key, 11)
    key_rows, key_cols, key_cells, key_phase = jax.random.split(key, 4)
    spread = 0.6
    ramp = 0.5 + jnp.arange(NR, dtype=jnp.float32) / NR
    row_factor = jnp.exp(jax.random.uniform(key_rows, (NR,), jnp.float32, -spread, spread))
    col_factor = jnp.exp(jax.random.uniform(key_cols, (NC,), jnp.float32, -spread, spread))
    cells = jax.random.uniform(key_cells, (NR, NC), jnp.float32, 0.7, 1.3)
    phase = jax.random.uniform(key_phase, (NR, NC), jnp.float32, -math.pi, math.pi)
    magnitude = (ramp * row_factor)[:, None] * col_factor[None, :] * cells
    return jnp.stack([magnitude * jnp.cos(phase), magnitude * jnp.sin(phase)]).astype(jnp.bfloat16)


def draw_positions(key, part):
    key = jax.random.fold_in(key, 23)
    key_rows, key_cols = jax.random.split(key, 2)
    row_ids = jnp.arange(N_ROW, dtype=jnp.int32)
    col_ids = jnp.arange(N_COL, dtype=jnp.int32)
    row_span = TR - jnp.where(row_ids == N_ROW - 1, WIN - 1, 0)
    col_span = TC - jnp.where(col_ids == N_COL - 1, WIN - 1, 0)
    row_high = jnp.broadcast_to(row_span[:, None, None], (N_ROW, N_COL, SLOTS))
    col_high = jnp.broadcast_to(col_span[None, :, None], (N_ROW, N_COL, SLOTS))
    row_off = jax.random.randint(key_rows, (N_ROW, N_COL, SLOTS), 0, row_high)
    col_off = jax.random.randint(key_cols, (N_ROW, N_COL, SLOTS), 0, col_high)
    row_off = row_off.at[N_ROW - 1, N_COL - 1, 0].set(TR - WIN)
    col_off = col_off.at[N_ROW - 1, N_COL - 1, 0].set(TC - WIN)
    row_off = row_off.at[0, 0, SLOTS - 1].set(0)
    col_off = col_off.at[0, 0, SLOTS - 1].set(0)
    start_rows = row_off + (row_ids * TR)[:, None, None]
    start_cols = col_off + (col_ids * TC)[None, :, None]
    return jnp.stack([start_rows, start_cols], axis=-1).astype(jnp.int32)


def draw_counts(key, part):
    key = jax.random.fold_in(key, 37)
    key_base, key_pair, key_col, key_side = jax.random.split(key, 4)
    lower_counts = jax.random.randint(key_base, (N_ROW // 2, N_COL), 0, SLOTS + 1)
    chosen_pair = jax.random.randint(key_pair, (), 0, N_ROW // 2)
    chosen_col = jax.random.randint(key_col, (), 0, N_COL)
    chosen_side = jax.random.randint(key_side, (), 0, 2)
    pair_ids = jnp.arange(N_ROW // 2, dtype=jnp.int32)[:, None]
    col_ids = jnp.arange(N_COL, dtype=jnp.int32)[None, :]
    forced = (pair_ids == chosen_pair) & (col_ids == chosen_col)
    lower_counts = jnp.where(forced, chosen_side * SLOTS, lower_counts)
    upper_counts = SLOTS - lower_counts
    return jnp.stack([lower_counts, upper_counts], axis=1).reshape(N_ROW, N_COL).astype(jnp.int32)


def levels(key, dims, cuts, smallest, top_value):
    loudness, own = 1.0, jax.random.fold_in(key, 6)
    for axis_at, blocks in cuts:
        heights = jnp.exp(jax.random.uniform(jax.random.fold_in(own, axis_at), (blocks,), jnp.float32, smallest / len(cuts), top_value / len(cuts)))
        loudness = loudness * jnp.repeat(heights, dims[axis_at] // blocks).reshape([-1 if axis == axis_at else 1 for axis in range(len(dims))])
    return loudness


def gaussian(key, dims, scale, most, held_as=jnp.bfloat16):
    return jnp.clip(scale * jax.random.normal(key, dims, jnp.float32), -most, most).astype(held_as)


def setup_inputs(seed: int = 0, part: int = 0) -> dict:
    keys = jax.random.split(jax.random.key(seed), 6)
    own_keys = jax.random.split(jax.random.fold_in(keys[5], part), 6)
    object_field = draw_object_field(jax.random.fold_in(jax.random.fold_in(keys[5], part), 71), part)
    probe_modes = gaussian(own_keys[1], (2, WIN, MODES, WIN), 1.0, 6.0)
    positions = draw_positions(jax.random.fold_in(jax.random.fold_in(keys[5], part), 71), part)
    counts = draw_counts(jax.random.fold_in(jax.random.fold_in(keys[5], part), 71), part)
    intensities = jnp.clip(jnp.exp(math.log(64.0) - 4.8520303 * jax.random.uniform(own_keys[4], (N_ROW, N_COL, SLOTS, WIN, WIN), jnp.float32) ** levels(own_keys[4], (N_ROW, N_COL, SLOTS, WIN, WIN), ((0, 8), (1, 2)), -0.2, 0.2)), 0.5, 64.0).astype(jnp.bfloat16)
    return dict(object_field=object_field, probe_modes=probe_modes, positions=positions, counts=counts, intensities=intensities)


def dft_tables(win_size):
    grid = np.arange(win_size)
    angle = 2.0 * np.pi * (grid[:, None] * grid[None, :] % win_size) / win_size
    factor = 1.0 / np.sqrt(win_size)
    return (jnp.asarray(np.cos(angle) * factor, jnp.bfloat16), jnp.asarray(np.sin(angle) * factor, jnp.bfloat16))

def matmul(left, right):
    return jnp.dot(left, right, preferred_element_type=jnp.float32)

def position_terms(window, measured, probe_modes, cos_table, sin_table):
    win_size = window.shape[1]
    mode_count = probe_modes.shape[2]
    wide_shape = (win_size, mode_count * win_size)
    tall_shape = (win_size * mode_count, win_size)
    cube_shape = (win_size, mode_count, win_size)
    object_re = window[0].astype(jnp.float32)[:, None, :]
    object_im = window[1].astype(jnp.float32)[:, None, :]
    probe_re = probe_modes[0].astype(jnp.float32)
    probe_im = probe_modes[1].astype(jnp.float32)
    exit_re = (probe_re * object_re - probe_im * object_im).astype(jnp.bfloat16).reshape(wide_shape)
    exit_im = (probe_re * object_im + probe_im * object_re).astype(jnp.bfloat16).reshape(wide_shape)
    half_re = (matmul(cos_table, exit_re) + matmul(sin_table, exit_im)).astype(jnp.bfloat16).reshape(tall_shape)
    half_im = (matmul(cos_table, exit_im) - matmul(sin_table, exit_re)).astype(jnp.bfloat16).reshape(tall_shape)
    wave_re = (matmul(half_re, cos_table) + matmul(half_im, sin_table)).reshape(cube_shape)
    wave_im = (matmul(half_im, cos_table) - matmul(half_re, sin_table)).reshape(cube_shape)
    model_amp = jnp.sqrt(lax.optimization_barrier(jnp.sum(wave_re * wave_re + wave_im * wave_im, axis=1)))
    amp_ratio = (1.0 - measured / jnp.maximum(model_amp, 1.0))[:, None, :]
    resid_re = (wave_re * amp_ratio).astype(jnp.bfloat16).reshape(wide_shape)
    resid_im = (wave_im * amp_ratio).astype(jnp.bfloat16).reshape(wide_shape)
    back_re = (matmul(cos_table, resid_re) - matmul(sin_table, resid_im)).astype(jnp.bfloat16).reshape(tall_shape)
    back_im = (matmul(cos_table, resid_im) + matmul(sin_table, resid_re)).astype(jnp.bfloat16).reshape(tall_shape)
    diff_re = (matmul(back_re, cos_table) - matmul(back_im, sin_table)).reshape(cube_shape)
    diff_im = (matmul(back_im, cos_table) + matmul(back_re, sin_table)).reshape(cube_shape)
    grad_re = lax.optimization_barrier(jnp.sum(probe_re * diff_re + probe_im * diff_im, axis=1))
    grad_im = lax.optimization_barrier(jnp.sum(probe_re * diff_im - probe_im * diff_re, axis=1))
    term_re = object_re * diff_re + object_im * diff_im
    term_im = object_re * diff_im - object_im * diff_re
    norm_term = jnp.mean(object_re * object_re + object_im * object_im)
    return (jnp.stack([grad_re, grad_im]), jnp.stack([term_re, term_im]), norm_term)

def reference(object_field, probe_modes, positions, counts, intensities):
    cos_table, sin_table = dft_tables(WIN)
    slot_ids = jnp.arange(SLOTS, dtype=jnp.int32)
    live_mask = (slot_ids[None, None, :] < counts[:, :, None]).reshape(-1)
    live_order = jnp.argsort(1 - live_mask.astype(jnp.int32), stable=True)[:SLOTS * N_ROW * N_COL // 2]
    live_starts = positions.reshape(-1, 2)[live_order].astype(jnp.int32)
    live_intens = intensities.reshape(-1, WIN, WIN)[live_order]

    def advance(running, slot_item):
        start_pair, intensity = slot_item
        anchor = jnp.zeros((), jnp.int32)
        corner = (anchor, start_pair[0], start_pair[1])
        window = lax.dynamic_slice(object_field, corner, (2, WIN, WIN))
        measured = jnp.sqrt(intensity.astype(jnp.float32))
        grad_window, probe_term, norm_term = position_terms(window, measured, probe_modes, cos_table, sin_table)
        gradient, probe_sum, weight = running
        current = lax.dynamic_slice(gradient, corner, (2, WIN, WIN))
        gradient = lax.dynamic_update_slice(gradient, current + grad_window, corner)
        return ((gradient, probe_sum + probe_term, weight + norm_term), None)
    initial = (jnp.zeros((2, NR, NC), jnp.float32), jnp.zeros((2, WIN, MODES, WIN), jnp.float32), jnp.zeros((), jnp.float32))
    (gradient, probe_sum, weight), ignored = lax.scan(advance, initial, (live_starts, live_intens))
    probe_float = probe_modes.astype(jnp.float32)
    power = jnp.max(lax.optimization_barrier(jnp.sum(probe_float[0] * probe_float[0] + probe_float[1] * probe_float[1], axis=1)))
    new_object = object_field.astype(jnp.float32) - gradient / power
    new_probe = probe_float - 4.0 * probe_sum / weight
    return (new_object, new_probe)
```

```python
import functools

import jax
import jax.numpy as jnp
import ml_dtypes
import numpy as np
from jax import lax
from jax.experimental import pallas as pl
from jax.experimental.pallas import tpu as pltpu
from jax.sharding import PartitionSpec as P

LANES = 128
CHUNK = 32


def from_behind(block, axis, distance):
    devices = range(lax.axis_size(axis))
    route = [(i - distance, i) for i in devices if i - distance in devices]
    return lax.ppermute(block, axis, route)


def dft_blocks(win):
    grid = np.arange(win)
    angle = 2.0 * np.pi * (grid[:, None] * grid[None, :] % win) / win
    factor = 1.0 / np.sqrt(win)
    cos_table = (np.cos(angle) * factor).astype(ml_dtypes.bfloat16)
    sin_table = (np.sin(angle) * factor).astype(ml_dtypes.bfloat16)
    forward = np.block([[cos_table, sin_table], [-sin_table, cos_table]])
    return forward, np.ascontiguousarray(forward.T)


def dot(left, right):
    return jnp.dot(left, right, preferred_element_type=jnp.float32)


def gradient_kernel(
    modes,
    starts,
    count,
    own,
    below,
    right,
    corner,
    probe,
    intens,
    forward,
    inverse,
    own_grad,
    low_grad,
    right_grad,
    probe_out,
    norm_out,
    field,
    grad,
    window,
    wide,
    tall,
    wave,
    probe_sum,
):
    win = probe.shape[1]
    rows, cols = own.shape[1], own.shape[2]
    chunks = range(0, win, CHUNK)
    spread = win // LANES + 1

    def put_blocks(part, row, first, values):
        for b in range(values.shape[1] // LANES):
            piece = values[:, b * LANES : (b + 1) * LANES].astype(jnp.float32)
            field[part, first + b, row : row + CHUNK, :] = piece

    def take_blocks(part, at, first, number):
        return jnp.concatenate([grad[part, first + b, at, :] for b in range(number)], axis=1)

    for part in range(2):
        for r in range(0, rows, CHUNK):
            at = pl.ds(r, CHUNK)
            put_blocks(part, r, 0, own[part, at, :])
            put_blocks(part, r, cols // LANES, right[part, at, :])
        for r in range(0, win, CHUNK):
            at = pl.ds(r, CHUNK)
            put_blocks(part, rows + r, 0, below[part, at, :])
            put_blocks(part, rows + r, cols // LANES, corner[part, at, :])
    grad[...] = jnp.zeros_like(grad)
    probe_sum[...] = jnp.zeros_like(probe_sum)
    norm_out[...] = jnp.zeros_like(norm_out)
    lane = lax.broadcasted_iota(jnp.int32, (CHUNK, LANES), 1)

    def one_position(slot, carry):
        y, x = starts[2 * slot], starts[2 * slot + 1]
        base = x // LANES
        shift = x - base * LANES
        back_shift = (LANES - shift) % LANES
        keep = lane < LANES - shift
        for r in chunks:
            at = pl.ds(r, CHUNK)
            obj = []
            for part in range(2):
                turned = [
                    pltpu.roll(field[part, base + b, pl.ds(y + r, CHUNK), :], back_shift, 1)
                    for b in range(spread)
                ]
                piece = jnp.concatenate(
                    [jnp.where(keep, a, b) for a, b in zip(turned[:-1], turned[1:])], axis=1
                )
                window[part, at, :] = piece
                obj.append(piece)
            squares = obj[0] * obj[0] + obj[1] * obj[1]
            norm_out[...] += jnp.sum(squares.reshape(CHUNK // 8, 8, win), axis=0)
            for k in range(modes):
                cs = pl.ds(k * win, win)
                p_re = probe[0, at, cs].astype(jnp.float32)
                p_im = probe[1, at, cs].astype(jnp.float32)
                wide[at, cs] = (p_re * obj[0] - p_im * obj[1]).astype(jnp.bfloat16)
                wide[pl.ds(win + r, CHUNK), cs] = (p_re * obj[1] + p_im * obj[0]).astype(
                    jnp.bfloat16
                )

        def to_tall(table):
            for k in range(modes):
                half = dot(table[...], wide[:, k * win : (k + 1) * win]).astype(jnp.bfloat16)
                tall[k * win : (k + 1) * win, :win] = half[:win]
                tall[k * win : (k + 1) * win, win:] = half[win:]

        to_tall(forward)
        for k in range(modes):
            ks = slice(k * win, (k + 1) * win)
            wave[ks, :] = dot(tall[ks, :], inverse[...])
        for r in chunks:
            at = pl.ds(r, CHUNK)
            power = jnp.zeros((CHUNK, win), jnp.float32)
            for k in range(modes):
                w = wave[pl.ds(k * win + r, CHUNK), :]
                power = power + w[:, :win] * w[:, :win] + w[:, win:] * w[:, win:]
            measured = jnp.sqrt(intens[slot, at, :].astype(jnp.float32))
            ratio = 1.0 - measured / jnp.maximum(jnp.sqrt(power), 1.0)
            for k in range(modes):
                w = wave[pl.ds(k * win + r, CHUNK), :]
                cs = pl.ds(k * win, win)
                wide[at, cs] = (w[:, :win] * ratio).astype(jnp.bfloat16)
                wide[pl.ds(win + r, CHUNK), cs] = (w[:, win:] * ratio).astype(jnp.bfloat16)
        to_tall(inverse)
        for k in range(modes):
            ks = slice(k * win, (k + 1) * win)
            wave[ks, :] = dot(tall[ks, :], forward[...])
        for r in chunks:
            at = pl.ds(r, CHUNK)
            obj = (window[0, at, :], window[1, at, :])
            sums = [jnp.zeros((CHUNK, win), jnp.float32) for _ in range(2)]
            for k in range(modes):
                cs = pl.ds(k * win, win)
                d = wave[pl.ds(k * win + r, CHUNK), :]
                d_re, d_im = d[:, :win], d[:, win:]
                p_re = probe[0, at, cs].astype(jnp.float32)
                p_im = probe[1, at, cs].astype(jnp.float32)
                sums[0] = sums[0] + (p_re * d_re + p_im * d_im)
                sums[1] = sums[1] + (p_re * d_im - p_im * d_re)
                probe_sum[0, at, cs] += obj[0] * d_re + obj[1] * d_im
                probe_sum[1, at, cs] += obj[0] * d_im - obj[1] * d_re
            for part in range(2):
                turned = [
                    pltpu.roll(sums[part][:, c : c + LANES], shift, 1)
                    for c in range(0, win, LANES)
                ]
                turned = [jnp.zeros_like(turned[0])] + turned + [jnp.zeros_like(turned[0])]
                keep_high = lane >= shift
                for b in range(spread):
                    grad[part, base + b, pl.ds(y + r, CHUNK), :] += jnp.where(
                        keep_high, turned[b + 1], turned[b]
                    )
        return carry

    lax.fori_loop(0, count[0], one_position, 0)
    for part in range(2):
        for r in range(0, rows, CHUNK):
            at = pl.ds(r, CHUNK)
            own_grad[part, at, :] = take_blocks(part, at, 0, cols // LANES)
        for r in range(0, win, CHUNK):
            at, of = pl.ds(r, CHUNK), pl.ds(rows + r, CHUNK)
            low_grad[part, at, :] = take_blocks(part, of, 0, cols // LANES)
        for r in range(0, rows + win, CHUNK):
            at = pl.ds(r, CHUNK)
            piece = take_blocks(part, at, cols // LANES, win // LANES)
            right_grad[part, at, :] = piece.astype(jnp.bfloat16)
        for r in chunks:
            at = pl.ds(r, CHUNK)
            probe_out[part, at, :] = probe_sum[part, at, :].astype(jnp.bfloat16)


def position_gradients(starts, count, own, below, right, corner, probe, intens):
    win, modes = intens.shape[1], probe.shape[2] // intens.shape[1]
    rows, cols = own.shape[1:]
    forward, inverse = dft_blocks(win)
    f32, bf16 = jnp.float32, jnp.bfloat16
    smem = pl.BlockSpec(memory_space=pltpu.SMEM)
    vmem = pl.BlockSpec(memory_space=pltpu.VMEM)
    slots = intens.shape[0]
    flops = 32 * slots * modes * win**3
    return pl.pallas_call(
        functools.partial(gradient_kernel, modes),
        out_shape=(
            jax.ShapeDtypeStruct((2, rows, cols), f32),
            jax.ShapeDtypeStruct((2, win, cols), f32),
            jax.ShapeDtypeStruct((2, rows + win, win), bf16),
            jax.ShapeDtypeStruct((2, win, modes * win), bf16),
            jax.ShapeDtypeStruct((8, win), f32),
        ),
        in_specs=[smem] * 2 + [vmem] * 8,
        out_specs=(vmem,) * 5,
        scratch_shapes=[
            pltpu.VMEM((2, (cols + win) // LANES, rows + win, LANES), f32),
            pltpu.VMEM((2, (cols + win) // LANES, rows + win, LANES), f32),
            pltpu.VMEM((2, win, win), f32),
            pltpu.VMEM((2 * win, modes * win), bf16),
            pltpu.VMEM((modes * win, 2 * win), bf16),
            pltpu.VMEM((modes * win, 2 * win), f32),
            pltpu.VMEM((2, win, modes * win), f32),
        ],
        compiler_params=pltpu.CompilerParams(vmem_limit_bytes=40 * 1024 * 1024),
        cost_estimate=pl.CostEstimate(flops=flops, bytes_accessed=12 << 20, transcendentals=0),
    )(starts, count, own, below, right, corner, probe, intens, forward, inverse)


def body(object_field, probe_modes, positions, counts, intensities):
    win = probe_modes.shape[1]
    modes = probe_modes.shape[2]
    tile_rows, tile_cols = object_field.shape[1:]
    row_index = lax.axis_index("row")
    col_index = lax.axis_index("col")
    anchor = jnp.stack([row_index * tile_rows, col_index * tile_cols]).astype(jnp.int32)
    starts = (positions[0, 0] - anchor[None, :]).reshape(-1)
    below = from_behind(object_field[:, :win, :], "row", -1)
    right = from_behind(object_field[:, :, :win], "col", -1)
    corner = from_behind(below[:, :, :win], "col", -1)
    probe_flat = probe_modes.reshape(2, win, modes * win)
    probe_float = probe_modes.astype(jnp.float32)
    power = jnp.max(
        jnp.sum(probe_float[0] * probe_float[0] + probe_float[1] * probe_float[1], axis=1)
    )
    own_grad, low_grad, right_grad, probe_part, norm_part = position_gradients(
        starts, counts[0], object_field, below, right, corner, probe_flat, intensities[0, 0]
    )
    probe_total = lax.psum(probe_part, ("row", "col")).astype(jnp.float32)
    weight = lax.psum(jnp.sum(norm_part) / (win * win), ("row", "col"))
    from_left = from_behind(right_grad, "col", 1).astype(jnp.float32)
    low_sum = jnp.concatenate(
        [low_grad[:, :, :win] + from_left[:, tile_rows:, :], low_grad[:, :, win:]], axis=2
    )
    from_above = from_behind(low_sum.astype(jnp.bfloat16), "row", 1).astype(jnp.float32)
    gradient = jnp.concatenate(
        [own_grad[:, :, :win] + from_left[:, :tile_rows, :], own_grad[:, :, win:]], axis=2
    )
    gradient = jnp.concatenate(
        [gradient[:, :win, :] + from_above, gradient[:, win:, :]], axis=1
    )
    new_object = object_field.astype(jnp.float32) - gradient / power
    probe_total = probe_total.reshape(2, win, modes, win)
    new_probe = probe_float - 4.0 * probe_total / weight
    return (new_object, new_probe)


def solution(mesh):
    placed = (
        P(None, ("grp", "row"), "col"),
        P(None, None, "grp", None),
        P(("grp", "row"), "col", None, None),
        P(("grp", "row"), "col"),
        P(("grp", "row"), "col", None, None, None),
    )
    return jax.shard_map(
        body,
        mesh=mesh,
        in_specs=placed,
        out_specs=(P(None, ("grp", "row"), "col"), P(None, None, "grp", None)),
        check_vma=False,
    )
```

```python
import functools

import jax
import jax.numpy as jnp
import ml_dtypes
import numpy as np
from jax import lax
from jax.experimental import pallas as pl
from jax.experimental.pallas import tpu as pltpu
from jax.sharding import PartitionSpec as P

LANES = 128
CHUNK = 32
TAIL = 16
MIB = 1 << 20


def from_behind(block, axis, distance):
    devices = range(lax.axis_size(axis))
    route = [(i - distance, i) for i in devices if i - distance in devices]
    return lax.ppermute(block, axis, route)


def dft_blocks(win):
    grid = np.arange(win)
    angle = 2.0 * np.pi * (grid[:, None] * grid[None, :] % win) / win
    factor = 1.0 / np.sqrt(win)
    cos_table = (np.cos(angle) * factor).astype(ml_dtypes.bfloat16)
    sin_table = (np.sin(angle) * factor).astype(ml_dtypes.bfloat16)
    forward = np.block([[cos_table, sin_table], [-sin_table, cos_table]])
    return forward, np.ascontiguousarray(forward.T)


def dot(left, right):
    return jnp.dot(left, right, preferred_element_type=jnp.float32)


def gradient_kernel(
    modes,
    starts,
    count,
    power,
    own,
    below,
    right,
    corner,
    probe,
    intens_hbm,
    forward_hbm,
    inverse_hbm,
    own_grad,
    low_grad,
    right_grad,
    keep_out,
    send_out,
    norm_out,
    intens,
    forward,
    inverse,
    sems,
    field,
    grad,
    window,
    wide,
    tall,
    wave,
    total,
    grad_sum,
    probe_sum,
):
    sources = (forward_hbm, inverse_hbm, intens_hbm)
    copies = [
        pltpu.make_async_copy(source, target, sems.at[i])
        for i, (source, target) in enumerate(zip(sources, (forward, inverse, intens)))
    ]
    for copy in copies:
        copy.start()
    win = probe.shape[1]
    rows, cols = own.shape[1], own.shape[2]
    chunks = range(0, win, CHUNK)
    spread = win // LANES + 1
    col_index = lax.axis_index("col")
    row_anchor = lax.axis_index("row") * rows
    col_anchor = col_index * cols

    def put_blocks(part, row, first, values):
        for b in range(values.shape[1] // LANES):
            piece = values[:, b * LANES : (b + 1) * LANES].astype(jnp.float32)
            field[part, first + b, row : row + CHUNK, :] = piece

    grad[...] = jnp.zeros_like(grad)
    probe_sum[...] = jnp.zeros_like(probe_sum)
    norm_out[...] = jnp.zeros_like(norm_out)
    for source, row_at, col_at in (
        (own, 0, 0),
        (right, 0, cols),
        (below, rows, 0),
        (corner, rows, cols),
    ):
        for part in range(2):
            for r in range(0, source.shape[1], CHUNK):
                put_blocks(part, row_at + r, col_at // LANES, source[part, r : r + CHUNK, :])
    for copy in copies:
        copy.wait()
    lane = lax.broadcasted_iota(jnp.int32, (CHUNK, LANES), 1)

    def one_position(slot, carry):
        y, x = starts[2 * slot] - row_anchor, starts[2 * slot + 1] - col_anchor
        base = x // LANES
        shift = x - base * LANES
        back_shift = (LANES - shift) % LANES
        keep = lane < LANES - shift
        for r in chunks:
            at = pl.ds(r, CHUNK)
            obj = []
            for part in range(2):
                turned = [
                    pltpu.roll(field[part, base + b, pl.ds(y + r, CHUNK), :], back_shift, 1)
                    for b in range(spread)
                ]
                piece = jnp.concatenate(
                    [jnp.where(keep, a, b) for a, b in zip(turned[:-1], turned[1:])], axis=1
                )
                window[part, at, :] = piece
                obj.append(piece)
            squares = obj[0] * obj[0] + obj[1] * obj[1]
            norm_out[...] += jnp.sum(squares.reshape(CHUNK // 8, 8, win), axis=0)

        def exit_wave(k):
            cs = pl.ds(k * win, win)
            for r in chunks:
                at = pl.ds(r, CHUNK)
                o_re, o_im = window[0, at, :], window[1, at, :]
                p_re = probe[0, at, cs].astype(jnp.float32)
                p_im = probe[1, at, cs].astype(jnp.float32)
                wide[k, at, :] = (p_re * o_re - p_im * o_im).astype(jnp.bfloat16)
                wide[k, pl.ds(win + r, CHUNK), :] = (p_re * o_im + p_im * o_re).astype(
                    jnp.bfloat16
                )

        def rows_transform(table, k):
            half = dot(table[...], wide[k]).astype(jnp.bfloat16)
            tall[k, :, :win] = half[:win]
            tall[k, :, win:] = half[win:]

        def cols_transform(table, k):
            wave[k] = dot(tall[k], table[...])

        def add_power(k):
            for r in chunks:
                at = pl.ds(r, CHUNK)
                w_re, w_im = wave[k, at, :win], wave[k, at, win:]
                term = w_re * w_re + w_im * w_im
                if k == 0:
                    total[at, :] = term
                elif k < modes - 1:
                    total[at, :] += term
                else:
                    amp = jnp.sqrt(total[at, :] + term)
                    measured = jnp.sqrt(intens[slot, at, :].astype(jnp.float32))
                    total[at, :] = 1.0 - measured / jnp.maximum(amp, 1.0)

        def residual(k):
            for r in chunks:
                at = pl.ds(r, CHUNK)
                ratio = total[at, :]
                wide[k, at, :] = (wave[k, at, :win] * ratio).astype(jnp.bfloat16)
                wide[k, pl.ds(win + r, CHUNK), :] = (wave[k, at, win:] * ratio).astype(
                    jnp.bfloat16
                )

        def gradients(k):
            cs = pl.ds(k * win, win)
            for r in chunks:
                at = pl.ds(r, CHUNK)
                o_re, o_im = window[0, at, :], window[1, at, :]
                d_re, d_im = wave[k, at, :win], wave[k, at, win:]
                p_re = probe[0, at, cs].astype(jnp.float32)
                p_im = probe[1, at, cs].astype(jnp.float32)
                sums = (p_re * d_re + p_im * d_im, p_re * d_im - p_im * d_re)
                terms = (o_re * d_re + o_im * d_im, o_re * d_im - o_im * d_re)
                for part in range(2):
                    if k == 0:
                        grad_sum[part, at, :] = sums[part]
                    else:
                        grad_sum[part, at, :] += sums[part]
                    for b in range(win // LANES):
                        probe_sum[k, part, b, at, :] += terms[part][:, b * LANES : (b + 1) * LANES]

        def skewed(*stages):
            for step in range(modes + len(stages) - 1):
                for i, stage in enumerate(stages):
                    if 0 <= step - i < modes:
                        stage(step - i)

        skewed(
            exit_wave,
            functools.partial(rows_transform, forward),
            functools.partial(cols_transform, inverse),
            add_power,
        )
        skewed(
            residual,
            functools.partial(rows_transform, inverse),
            functools.partial(cols_transform, forward),
            gradients,
        )
        keep_high = lane >= shift
        for r in chunks:
            at = pl.ds(r, CHUNK)
            for part in range(2):
                turned = [
                    pltpu.roll(grad_sum[part, at, c : c + LANES], shift, 1)
                    for c in range(0, win, LANES)
                ]
                turned = [jnp.zeros_like(turned[0])] + turned + [jnp.zeros_like(turned[0])]
                for b in range(spread):
                    grad[part, base + b, pl.ds(y + r, CHUNK), :] += jnp.where(
                        keep_high, turned[b + 1], turned[b]
                    )
        return carry

    lax.fori_loop(0, count[0], one_position, 0)
    half = modes // 2
    for m in range(half):
        keep_mode = col_index * half + m
        send_mode = (1 - col_index) * half + m
        keep_out[m] = probe_sum[keep_mode]
        send_out[m] = probe_sum[send_mode].astype(jnp.bfloat16)
    scale = 1.0 / jnp.full((8, LANES), power[0], jnp.float32)
    scale = jnp.concatenate([scale] * (CHUNK // 8), axis=0)

    def take_blocks(part, at, first, number):
        return jnp.concatenate(
            [grad[part, first + b, at, :] * scale for b in range(number)], axis=1
        )

    for part in range(2):
        for r in range(0, rows + win, CHUNK):
            at = pl.ds(r, CHUNK)
            piece = take_blocks(part, at, cols // LANES, win // LANES)
            right_grad[part, at, :] = piece.astype(jnp.bfloat16)
        for r in range(0, rows, CHUNK):
            at = pl.ds(r, CHUNK)
            own_grad[part, at, :] = take_blocks(part, at, 0, cols // LANES)
        for r in range(0, win, CHUNK):
            at, of = pl.ds(r, CHUNK), pl.ds(rows + r, CHUNK)
            low_grad[part, at, :] = take_blocks(part, of, 0, cols // LANES)


def position_gradients(starts, count, power, own, below, right, corner, probe, intens):
    win, modes = intens.shape[1], probe.shape[2] // intens.shape[1]
    rows, cols = own.shape[1:]
    forward, inverse = dft_blocks(win)
    f32, bf16 = jnp.float32, jnp.bfloat16
    smem = pl.BlockSpec(memory_space=pltpu.SMEM)
    vmem = pl.BlockSpec(memory_space=pltpu.VMEM)
    slots = intens.shape[0]
    flops = 32 * slots * modes * win**3
    half_blocks = (modes // 2, 2, win // LANES, win, LANES)
    copied = (intens, forward, inverse)
    return pl.pallas_call(
        functools.partial(gradient_kernel, modes),
        out_shape=(
            jax.ShapeDtypeStruct((2, rows, cols), f32),
            jax.ShapeDtypeStruct((2, win, cols), f32),
            jax.ShapeDtypeStruct((2, rows + win, win), bf16),
            jax.ShapeDtypeStruct(half_blocks, f32),
            jax.ShapeDtypeStruct(half_blocks, bf16),
            jax.ShapeDtypeStruct((8, win), f32),
        ),
        in_specs=[smem] * 3 + [vmem] * 5 + [pl.BlockSpec(memory_space=pl.ANY)] * 3,
        out_specs=(vmem,) * 6,
        scratch_shapes=[pltpu.VMEM(array.shape, bf16) for array in copied]
        + [
            pltpu.SemaphoreType.DMA((len(copied),)),
            pltpu.VMEM((2, (cols + win) // LANES, rows + win, LANES), f32),
            pltpu.VMEM((2, (cols + win) // LANES, rows + win, LANES), f32),
            pltpu.VMEM((2, win, win), f32),
            pltpu.VMEM((modes, 2 * win, win), bf16),
            pltpu.VMEM((modes, win, 2 * win), bf16),
            pltpu.VMEM((modes, win, 2 * win), f32),
            pltpu.VMEM((win, win), f32),
            pltpu.VMEM((2, win, win), f32),
            pltpu.VMEM((modes, 2, win // LANES, win, LANES), f32),
        ],
        compiler_params=pltpu.CompilerParams(vmem_limit_bytes=28 * MIB),
        cost_estimate=pl.CostEstimate(flops=flops, bytes_accessed=12 << 20, transcendentals=0),
    )(starts, count, power, own, below, right, corner, probe, intens, forward, inverse)


def in_three(value):
    full = jnp.full((TAIL, LANES), value, jnp.float32)
    high = full.astype(jnp.bfloat16).astype(jnp.float32)
    mid = (full - high).astype(jnp.bfloat16).astype(jnp.float32)
    low = full - high - mid
    row = lax.broadcasted_iota(jnp.int32, (TAIL, LANES), 0)
    lane = lax.broadcasted_iota(jnp.int32, (TAIL, LANES), 1)
    tile = jnp.where(row == 0, high, jnp.where(row == 1, mid, jnp.where(row == 2, low, 0.0)))
    return jnp.where(lane == 0, tile, 0.0).astype(jnp.bfloat16)


def small_call(kernel, shapes, *operands, limit=4):
    return pl.pallas_call(
        kernel,
        out_shape=shapes,
        compiler_params=pltpu.CompilerParams(vmem_limit_bytes=limit * MIB),
    )(*operands)


def token_shape():
    return jax.ShapeDtypeStruct((8, LANES), jnp.float32)


def prepare_kernel(own, probe, right_part, power):
    win = right_part.shape[2]
    modes = probe.shape[2] // win
    largest = jnp.zeros((8, win), jnp.float32)
    for r in range(0, probe.shape[1], CHUNK):
        at = slice(r, r + CHUNK)
        total = jnp.zeros((CHUNK, win), jnp.float32)
        for k in range(modes):
            for part in range(2):
                p = probe[part, at, k * win : (k + 1) * win].astype(jnp.float32)
                total = total + p * p
        largest = jnp.maximum(largest, jnp.max(total.reshape(CHUNK // 8, 8, win), axis=0))
    power[0, 0] = jnp.max(largest)
    right_part[...] = own[:, :, :win]


def prepare(own, probe):
    win = probe.shape[1]
    return pl.pallas_call(
        prepare_kernel,
        out_shape=(
            jax.ShapeDtypeStruct(own.shape[:2] + (win,), own.dtype),
            jax.ShapeDtypeStruct((1, 1), jnp.float32),
        ),
        out_specs=(
            pl.BlockSpec(memory_space=pltpu.VMEM),
            pl.BlockSpec(memory_space=pltpu.SMEM),
        ),
        compiler_params=pltpu.CompilerParams(vmem_limit_bytes=4 * MIB),
    )(own, probe)


def chip_sum_kernel(pixels, keep, received, norm, token, payload):
    number, size = payload.shape[0], payload.shape[1] - TAIL
    tail = in_three(jnp.sum(norm[...]) / pixels)
    for i in range(number):
        at = slice(i * size, (i + 1) * size)
        payload[i, :size, :] = (keep[at, :] + received[at, :].astype(jnp.float32)).astype(
            jnp.bfloat16
        )
        payload[i, size:, :] = tail


def chip_sum(keep, received, norm, token, pixels, number):
    size = keep.shape[0] // number
    return small_call(
        functools.partial(chip_sum_kernel, pixels),
        jax.ShapeDtypeStruct((number, size + TAIL, LANES), jnp.bfloat16),
        keep,
        received,
        norm,
        token,
    )


def chunk_sum_kernel(parts, token, payload):
    number, size = parts.shape[0], parts.shape[1] - TAIL
    tail = jnp.zeros((TAIL, LANES), jnp.float32)
    for i in range(number):
        tail = tail + parts[i, size:, :].astype(jnp.float32)
    tail = in_three(jnp.sum(tail))
    piece = min(size, 2 * CHUNK)
    for r in range(0, size, piece):
        at = slice(r, r + piece)
        total = jnp.zeros((piece, LANES), jnp.float32)
        for i in range(number):
            total = total + parts[i, at, :].astype(jnp.float32)
        total = total.astype(jnp.bfloat16)
        for i in range(number):
            payload[i, at, :] = total
    for i in range(number):
        payload[i, size:, :] = tail


def chunk_sum(parts, token):
    return small_call(
        chunk_sum_kernel, jax.ShapeDtypeStruct(parts.shape, jnp.bfloat16), parts, token
    )


def probe_update_kernel(mine, other, probe, new_probe):
    win, modes = new_probe.shape[1], new_probe.shape[2]
    size = mine.shape[1] - TAIL
    piece = min(size, CHUNK)
    on_left = lax.axis_index("col") == 0
    tails = mine[0, size:, :].astype(jnp.float32) + other[0, size:, :].astype(jnp.float32)
    factor = 4.0 / jnp.full((piece, LANES), jnp.sum(tails), jnp.float32)
    half = modes // 2
    for m in range(half):
        for part in range(2):
            for b in range(win // LANES):
                block = ((m * 2 + part) * (win // LANES) + b) * win
                for r in range(0, win, piece):
                    chunk, offset = divmod(block + r, size)
                    here = mine[chunk, offset : offset + piece, :].astype(jnp.float32)
                    there = other[chunk, offset : offset + piece, :].astype(jnp.float32)
                    low = jnp.where(on_left, here, there)
                    high = jnp.where(on_left, there, here)
                    for k, total in ((m, low), (half + m, high)):
                        col = k * win + b * LANES
                        old = probe[part, r : r + piece, col : col + LANES].astype(jnp.float32)
                        new_probe[part, r : r + piece, k, b * LANES : (b + 1) * LANES] = (
                            old - factor * total
                        )


def probe_update(mine, other, probe, shape):
    return small_call(
        probe_update_kernel, jax.ShapeDtypeStruct(shape, jnp.float32), mine, other, probe
    )


def low_sum_kernel(low_grad, from_left, low_sum, token):
    win = from_left.shape[2]
    rows = from_left.shape[1] - low_grad.shape[1]
    token[...] = jnp.zeros_like(token)
    for part in range(2):
        for r in range(0, low_grad.shape[1], CHUNK):
            at = slice(r, r + CHUNK)
            arrived = from_left[part, rows + r : rows + r + CHUNK, :].astype(jnp.float32)
            low_sum[part, at, :win] = (low_grad[part, at, :win] + arrived).astype(jnp.bfloat16)
            low_sum[part, at, win:] = low_grad[part, at, win:].astype(jnp.bfloat16)


def low_sum_of(low_grad, from_left):
    return small_call(
        low_sum_kernel,
        (jax.ShapeDtypeStruct(low_grad.shape, jnp.bfloat16), token_shape()),
        low_grad,
        from_left,
    )


def object_update_kernel(old, own_grad, from_left, from_above, new_object, token):
    token[...] = jnp.zeros_like(token)
    win, depth = from_left.shape[2], from_above.shape[1]
    for part in range(2):
        for r in range(0, old.shape[1], CHUNK):
            at = slice(r, r + CHUNK)
            total = own_grad[part, at, :]
            if r < depth:
                total = total + from_above[part, at, :].astype(jnp.float32)
            updated = old[part, at, :].astype(jnp.float32) - total
            arrived = from_left[part, at, :].astype(jnp.float32)
            new_object[part, at, :win] = updated[:, :win] - arrived
            new_object[part, at, win:] = updated[:, win:]


def object_update(old, own_grad, from_left, from_above):
    return small_call(
        object_update_kernel,
        (jax.ShapeDtypeStruct(old.shape, jnp.float32), token_shape()),
        old,
        own_grad,
        from_left,
        from_above,
    )


def swap_cores(block):
    return lax.ppermute(block, "col", [(0, 1), (1, 0)])


def body(object_field, probe_modes, positions, counts, intensities):
    win = probe_modes.shape[1]
    modes = probe_modes.shape[2]
    number = lax.axis_size("row")
    below = from_behind(object_field[:, :win, :], "row", -1)
    probe_flat = probe_modes.reshape(2, win, modes * win)
    right_part, power = prepare(object_field, probe_flat)
    right = from_behind(right_part, "col", -1)
    corner_part = below[:, :, :win] + right[:, :win, :] * jnp.zeros((), jnp.bfloat16)
    corner = from_behind(corner_part, "col", -1)
    own_grad, low_grad, right_grad, keep, send, norm = position_gradients(
        positions.reshape(-1),
        counts.reshape(-1),
        power.reshape(1),
        object_field,
        below,
        right,
        corner,
        probe_flat,
        intensities[0, 0],
    )
    half_rows = keep.size // LANES
    received = swap_cores(send.reshape(half_rows, LANES))
    from_left = from_behind(right_grad, "col", 1)
    low_sum, token = low_sum_of(low_grad, from_left)
    from_above = from_behind(low_sum, "row", 1)
    payload = chip_sum(keep.reshape(half_rows, LANES), received, norm, token, win * win, number)
    parts = lax.all_to_all(payload, "row", 0, 0, tiled=True)
    new_object, token = object_update(object_field, own_grad, from_left, from_above)
    mine = lax.all_to_all(chunk_sum(parts, token), "row", 0, 0, tiled=True)
    other = swap_cores(mine)
    new_probe = probe_update(mine, other, probe_flat, probe_modes.shape)
    return (new_object, new_probe)


def solution(mesh):
    placed = (
        P(None, ("grp", "row"), "col"),
        P(None, None, "grp", None),
        P(("grp", "row"), "col", None, None),
        P(("grp", "row"), "col"),
        P(("grp", "row"), "col", None, None, None),
    )
    return jax.shard_map(
        body,
        mesh=mesh,
        in_specs=placed,
        out_specs=(P(None, ("grp", "row"), "col"), P(None, None, "grp", None)),
        check_vma=False,
    )
```

```python
import functools

import jax
import jax.numpy as jnp
import ml_dtypes
import numpy as np
from jax import lax
from jax.experimental import pallas as pl
from jax.experimental.pallas import tpu as pltpu
from jax.sharding import PartitionSpec as P

LANES = 128
CHUNK = 32
FINE = 16
TAIL = 16
MIB = 1 << 20
LOW_WEIGHT = 8


def from_behind(block, axis, distance):
    devices = range(lax.axis_size(axis))
    route = [(i - distance, i) for i in devices if i - distance in devices]
    return lax.ppermute(block, axis, route)


def dft_blocks(win):
    grid = np.arange(win)
    angle = 2.0 * np.pi * (grid[:, None] * grid[None, :] % win) / win
    factor = 1.0 / np.sqrt(win)
    cos_table = (np.cos(angle) * factor).astype(ml_dtypes.bfloat16)
    sin_table = (np.sin(angle) * factor).astype(ml_dtypes.bfloat16)
    blocks = []
    for parity in range(2):
        cos_part, sin_part = cos_table[parity::2, : win // 2], sin_table[parity::2, : win // 2]
        blocks.append(np.block([[cos_part, sin_part], [-sin_part, cos_part]]))
    return np.stack(blocks + [block.T for block in blocks])


def dot(left, right):
    return jnp.dot(left, right, preferred_element_type=jnp.float32)


def gradient_kernel(
    modes,
    starts,
    count,
    power,
    own,
    below,
    right,
    corner,
    probe,
    measured,
    tables,
    own_grad,
    low_grad,
    right_grad,
    keep_out,
    send_out,
    norm_out,
    field,
    grad,
    window,
    wide,
    tall,
    wave,
    probe_sum,
):
    win = probe.shape[1]
    rows, cols = own.shape[1], own.shape[2]
    half = win // 2
    fine = range(0, win, FINE)
    spread = win // LANES + 1
    col_index = lax.axis_index("col")
    row_anchor = lax.axis_index("row") * rows
    col_anchor = col_index * cols

    def put_blocks(part, row, first, values):
        for b in range(values.shape[1] // LANES):
            piece = values[:, b * LANES : (b + 1) * LANES].astype(jnp.float32)
            field[part, first + b, row : row + CHUNK, :] = piece

    grad[...] = jnp.zeros_like(grad)
    probe_sum[...] = jnp.zeros_like(probe_sum)
    norm_out[...] = jnp.zeros_like(norm_out)
    for source, row_at, col_at in (
        (own, 0, 0),
        (right, 0, cols),
        (below, rows, 0),
        (corner, rows, cols),
    ):
        for part in range(2):
            for r in range(0, source.shape[1], CHUNK):
                put_blocks(part, row_at + r, col_at // LANES, source[part, r : r + CHUNK, :])
    lane = lax.broadcasted_iota(jnp.int32, (FINE, LANES), 1)

    def one_position(slot, carry):
        y, x = starts[0, slot] - row_anchor, starts[1, slot] - col_anchor
        base = x // LANES
        shift = x - base * LANES
        back_shift = (LANES - shift) % LANES
        keep = lane < LANES - shift
        for r in range(0, half, FINE):
            objs = []
            for start in (r, r + half):
                at = pl.ds(start, FINE)
                obj = []
                for part in range(2):
                    turned = [
                        pltpu.roll(field[part, base + b, pl.ds(y + start, FINE), :], back_shift, 1)
                        for b in range(spread)
                    ]
                    piece = jnp.concatenate(
                        [jnp.where(keep, a, b) for a, b in zip(turned[:-1], turned[1:])], axis=1
                    )
                    window[part, at, :] = piece
                    obj.append(piece)
                squares = obj[0] * obj[0] + obj[1] * obj[1]
                norm_out[...] += jnp.sum(squares.reshape(FINE // 8, 8, win), axis=0)
                objs.append(obj)
            for k in range(modes):
                cs = pl.ds(k * win, win)
                exits = []
                for start, (o_re, o_im) in zip((r, r + half), objs):
                    p_re = probe[0, pl.ds(start, FINE), cs].astype(jnp.float32)
                    p_im = probe[1, pl.ds(start, FINE), cs].astype(jnp.float32)
                    exits.append((p_re * o_re - p_im * o_im, p_re * o_im + p_im * o_re))
                for part in range(2):
                    low, high = exits[0][part], exits[1][part]
                    at = pl.ds(part * half + r, FINE)
                    wide[k, 0, at, :] = (low + high).astype(jnp.bfloat16)
                    wide[k, 1, at, :] = (low - high).astype(jnp.bfloat16)

        for k in range(modes):
            for parity in range(2):
                out = dot(tables[parity], wide[k, parity])
                at = pl.ds(k * win + parity * half, half)
                for part in range(2):
                    low = out[part * half : (part + 1) * half, :half]
                    high = out[part * half : (part + 1) * half, half:]
                    to = pl.ds(part * half, half)
                    tall[0, at, to] = (low + high).astype(jnp.bfloat16)
                    tall[1, at, to] = (low - high).astype(jnp.bfloat16)
        for parity in range(2):
            wave[parity] = dot(tall[parity], tables[2 + parity])

        for r in fine:
            for parity in range(2):
                waves = []
                total = jnp.zeros((FINE, half), jnp.float32)
                for k in range(modes):
                    ka = pl.ds(k * win + r, FINE)
                    waves.append((wave[parity, ka, :half], wave[parity, ka, half:]))
                    total = total + (waves[k][0] * waves[k][0] + waves[k][1] * waves[k][1])
                gs = pl.ds(parity * half, half)
                amp = measured[slot, pl.ds(r, FINE), gs]
                ratio = 1.0 - amp / jnp.maximum(jnp.sqrt(total), 1.0)
                for k in range(modes):
                    for part in range(2):
                        at = pl.ds(part * half + r % half, FINE)
                        wide[k, r // half, at, gs] = (waves[k][part] * ratio).astype(jnp.bfloat16)

        for k in range(modes):
            even = dot(tables[2], wide[k, 0])
            odd = dot(tables[3], wide[k, 1])
            for place, out in enumerate((even + odd, even - odd)):
                at = pl.ds(k * win + place * half, half)
                for part in range(2):
                    for parity in range(2):
                        tall[parity, at, part * half : (part + 1) * half] = out[
                            part * half : (part + 1) * half, parity * half : (parity + 1) * half
                        ].astype(jnp.bfloat16)
        for parity in range(2):
            wave[parity] = dot(tall[parity], tables[parity])

        keep_high = lane >= shift
        for r in fine:
            at = pl.ds(r, FINE)
            sums = [[jnp.zeros((FINE, LANES), jnp.float32) for _ in range(2)] for _ in range(2)]
            for b in range(2):
                bs = pl.ds(b * half, half)
                o_re, o_im = window[0, at, bs], window[1, at, bs]
                for k in range(modes):
                    cs = pl.ds(k * win + b * half, half)
                    ka = pl.ds(k * win + r, FINE)
                    even, odd = wave[0, ka, :], wave[1, ka, :]
                    d = even + odd if b == 0 else even - odd
                    d_re, d_im = d[:, :half], d[:, half:]
                    p_re = probe[0, at, cs].astype(jnp.float32)
                    p_im = probe[1, at, cs].astype(jnp.float32)
                    sums[0][b] = sums[0][b] + (p_re * d_re + p_im * d_im)
                    sums[1][b] = sums[1][b] + (p_re * d_im - p_im * d_re)
                    probe_sum[k, 0, b, at, :] += o_re * d_re + o_im * d_im
                    probe_sum[k, 1, b, at, :] += o_re * d_im - o_im * d_re
            for part in range(2):
                turned = [pltpu.roll(piece, shift, 1) for piece in sums[part]]
                turned = [jnp.zeros_like(turned[0])] + turned + [jnp.zeros_like(turned[0])]
                for b in range(spread):
                    grad[part, base + b, pl.ds(y + r, FINE), :] += jnp.where(
                        keep_high, turned[b + 1], turned[b]
                    )
        return carry

    lax.fori_loop(0, count[0], one_position, 0)
    for m in range(modes // 2):
        keep_mode = col_index * (modes // 2) + m
        send_mode = (1 - col_index) * (modes // 2) + m
        keep_out[m] = probe_sum[keep_mode]
        send_out[m] = probe_sum[send_mode].astype(jnp.bfloat16)
    scale = 1.0 / jnp.full((8, LANES), power[0], jnp.float32)
    scale = jnp.concatenate([scale] * (CHUNK // 8), axis=0)

    def take_blocks(part, at, first, number):
        return jnp.concatenate(
            [grad[part, first + b, at, :] * scale for b in range(number)], axis=1
        )

    for part in range(2):
        for r in range(0, rows + win, CHUNK):
            at = pl.ds(r, CHUNK)
            piece = take_blocks(part, at, cols // LANES, win // LANES)
            right_grad[part, at, :] = piece.astype(jnp.bfloat16)
        for r in range(0, rows, CHUNK):
            at = pl.ds(r, CHUNK)
            own_grad[part, at, :] = take_blocks(part, at, 0, cols // LANES)
        for r in range(0, win, CHUNK):
            at, of = pl.ds(r, CHUNK), pl.ds(rows + r, CHUNK)
            low_grad[part, at, :] = take_blocks(part, of, 0, cols // LANES)


def position_gradients(starts, count, power, own, below, right, corner, probe, measured, tables):
    win, modes = probe.shape[1], probe.shape[2] // probe.shape[1]
    rows, cols = own.shape[1:]
    f32, bf16 = jnp.float32, jnp.bfloat16
    smem = pl.BlockSpec(memory_space=pltpu.SMEM)
    vmem = pl.BlockSpec(memory_space=pltpu.VMEM)
    if win != 2 * LANES:
        raise ValueError("window size")
    slots = measured.shape[0]
    flops = 16 * slots * modes * win**3
    half_blocks = (modes // 2, 2, win // LANES, win, LANES)
    return pl.pallas_call(
        functools.partial(gradient_kernel, modes),
        out_shape=(
            jax.ShapeDtypeStruct((2, rows, cols), f32),
            jax.ShapeDtypeStruct((2, win, cols), f32),
            jax.ShapeDtypeStruct((2, rows + win, win), bf16),
            jax.ShapeDtypeStruct(half_blocks, f32),
            jax.ShapeDtypeStruct(half_blocks, bf16),
            jax.ShapeDtypeStruct((8, win), f32),
        ),
        in_specs=[smem] * 3 + [vmem] * 7,
        out_specs=(vmem,) * 6,
        scratch_shapes=[
            pltpu.VMEM((2, (cols + win) // LANES, rows + win, LANES), f32),
            pltpu.VMEM((2, (cols + win) // LANES, rows + win, LANES), f32),
            pltpu.VMEM((2, win, win), f32),
            pltpu.VMEM((modes, 2, win, win), bf16),
            pltpu.VMEM((2, modes * win, win), bf16),
            pltpu.VMEM((2, modes * win, win), f32),
            pltpu.VMEM((modes, 2, win // LANES, win, LANES), f32),
        ],
        compiler_params=pltpu.CompilerParams(vmem_limit_bytes=26 * MIB),
        cost_estimate=pl.CostEstimate(flops=flops, bytes_accessed=12 << 20, transcendentals=0),
    )(starts, count, power, own, below, right, corner, probe, measured, tables)


def in_three(value):
    full = jnp.full((TAIL, LANES), value, jnp.float32)
    high = full.astype(jnp.bfloat16).astype(jnp.float32)
    mid = (full - high).astype(jnp.bfloat16).astype(jnp.float32)
    low = full - high - mid
    row = lax.broadcasted_iota(jnp.int32, (TAIL, LANES), 0)
    lane = lax.broadcasted_iota(jnp.int32, (TAIL, LANES), 1)
    tile = jnp.where(row == 0, high, jnp.where(row == 1, mid, jnp.where(row == 2, low, 0.0)))
    return jnp.where(lane == 0, tile, 0.0).astype(jnp.bfloat16)


def small_call(kernel, shapes, *operands, weight=1):
    return pl.pallas_call(
        kernel,
        out_shape=shapes,
        compiler_params=pltpu.CompilerParams(vmem_limit_bytes=4 * MIB),
        cost_estimate=pl.CostEstimate(flops=0, bytes_accessed=weight * MIB, transcendentals=0),
    )(*operands)


def first_columns_kernel(block, token, first):
    first[...] = block[:, :, : first.shape[2]]


def first_columns(block, token):
    return small_call(
        first_columns_kernel, jax.ShapeDtypeStruct(token.shape, block.dtype), block, token
    )


def token_shape():
    return jax.ShapeDtypeStruct((8, LANES), jnp.float32)


def prepare_kernel(own, probe, intens, blocks, right_part, tables, measured, power):
    right_part[...] = own[:, :, : right_part.shape[2]]
    tables[...] = blocks[...]
    count, size, _ = intens.shape
    row = lax.broadcasted_iota(jnp.int32, (size, size), 0)
    col = lax.broadcasted_iota(jnp.int32, (size, size), 1)
    to_even_first = (col == jnp.where(row < size // 2, 2 * row, 2 * row - size + 1)).astype(
        jnp.float32
    )
    from_left = to_even_first.astype(jnp.bfloat16)
    from_right = (row == jnp.where(col < size // 2, 2 * col, 2 * col - size + 1)).astype(
        jnp.float32
    )
    from_right = from_right.astype(jnp.bfloat16)
    for slot in range(count):
        turned = dot(from_left, intens[slot]).astype(jnp.bfloat16)
        measured[slot] = jnp.sqrt(dot(turned, from_right))
    win = right_part.shape[2]
    modes = probe.shape[2] // win
    largest = jnp.zeros((8, win), jnp.float32)
    for r in range(0, probe.shape[1], CHUNK):
        at = slice(r, r + CHUNK)
        total = jnp.zeros((CHUNK, win), jnp.float32)
        for k in range(modes):
            for part in range(2):
                p = probe[part, at, k * win : (k + 1) * win].astype(jnp.float32)
                total = total + p * p
        largest = jnp.maximum(largest, jnp.max(total.reshape(CHUNK // 8, 8, win), axis=0))
    power[0, 0] = jnp.max(largest)


def prepare(own, probe, intens):
    win = probe.shape[1]
    blocks = dft_blocks(win)
    vmem = pl.BlockSpec(memory_space=pltpu.VMEM)
    return pl.pallas_call(
        prepare_kernel,
        out_shape=(
            jax.ShapeDtypeStruct(own.shape[:2] + (win,), own.dtype),
            jax.ShapeDtypeStruct(blocks.shape, jnp.bfloat16),
            jax.ShapeDtypeStruct(intens.shape, jnp.float32),
            jax.ShapeDtypeStruct((1, 1), jnp.float32),
        ),
        out_specs=(vmem, vmem, vmem, pl.BlockSpec(memory_space=pltpu.SMEM)),
        compiler_params=pltpu.CompilerParams(vmem_limit_bytes=8 * MIB),
    )(own, probe, intens, blocks)


def block_shapes(kept, size, ways):
    sends = jax.ShapeDtypeStruct((kept * size + TAIL, LANES), jnp.bfloat16)
    return (jax.ShapeDtypeStruct((kept, size, LANES), jnp.float32),) + (sends,) * (ways - 1)


def put_block(j, total, kept, sends):
    ways = len(sends) + 1
    if j % ways == 0:
        kept[j // ways] = total
    else:
        size = total.shape[0]
        sends[j % ways - 1][pl.ds(j // ways * size, size), :] = total.astype(jnp.bfloat16)


def put_weight(weight, sends):
    tile = in_three(weight)
    for sent in sends:
        sent[pl.ds(sent.shape[0] - TAIL, TAIL), :] = tile


def weight_of(block):
    return jnp.sum(block[pl.ds(block.shape[0] - TAIL, TAIL), :].astype(jnp.float32))


def chip_sum_kernel(pixels, keep, received, norm, kept, *sends):
    me = lax.axis_index("row")
    size = kept.shape[1]
    for j in range(keep.shape[0] // size):
        at = pl.ds(pl.multiple_of((j ^ me) * size, size), size)
        put_block(j, keep[at, :] + received[at, :].astype(jnp.float32), kept, sends)
    put_weight(jnp.sum(norm[...]) / pixels, sends)


def chip_sum(keep, received, norm, pixels, number, ways):
    return small_call(
        functools.partial(chip_sum_kernel, pixels),
        block_shapes(number // ways, keep.shape[0] // number, ways),
        keep,
        received,
        norm,
    )


def scatter_sum_kernel(number, mine, sent, *refs):
    received, kept, sends = refs[:number], refs[number], refs[number + 1 :]
    size = mine.shape[1]
    for j in range(mine.shape[0]):
        total = mine[j]
        for block in received:
            total = total + block[pl.ds(j * size, size), :].astype(jnp.float32)
        put_block(j, total, kept, sends)
    put_weight(sum([weight_of(block) for block in received], weight_of(sent)), sends)


def scatter_sum(mine, sent, received, ways):
    number, size, _ = mine.shape
    return small_call(
        functools.partial(scatter_sum_kernel, len(received)),
        block_shapes(number // ways, size, ways),
        mine,
        sent,
        *received,
    )


def last_sum_kernel(mine, sent, *refs):
    received, chunk, tail = refs[:-2], refs[-2], refs[-1]
    total = mine[0]
    for block in received:
        total = total + block[pl.ds(0, mine.shape[1]), :].astype(jnp.float32)
    chunk[...] = total.astype(jnp.bfloat16)
    tail[...] = in_three(sum([weight_of(block) for block in received], weight_of(sent)))


def last_sum(mine, sent, received):
    return small_call(
        last_sum_kernel,
        (
            jax.ShapeDtypeStruct(mine.shape[1:], jnp.bfloat16),
            jax.ShapeDtypeStruct((TAIL, LANES), jnp.bfloat16),
        ),
        mine,
        sent,
        *received,
    )


def join_kernel(*refs):
    joined = refs[-1]
    at = 0
    for block in refs[1:-1]:
        joined[pl.ds(at, block.shape[0]), :] = block[...]
        at += block.shape[0]


def join(token, blocks):
    rows = sum(block.shape[0] for block in blocks)
    return small_call(
        join_kernel, jax.ShapeDtypeStruct((rows, LANES), blocks[0].dtype), token, *blocks
    )


def swap_rows(block, step):
    number = lax.axis_size("row")
    return lax.ppermute(block, "row", [(i, i ^ step) for i in range(number)])


def row_digits():
    number = lax.axis_size("row")
    if number & (number - 1) or number < 2:
        raise ValueError("row size")
    bits = number.bit_length() - 1
    return [(shift, 1 << min(2, bits - shift)) for shift in range(0, bits, 2)]


def probe_update_kernel(size, digits, mine, other, probe, new_probe, updated, sems):
    _, win, modes, _ = updated.shape
    number = mine.shape[0] // size
    me = lax.axis_index("row")
    piece = min(size, CHUNK)
    on_left = lax.axis_index("col") == 0
    tail = pl.ds(number * size, TAIL)
    tails = mine[tail, :].astype(jnp.float32) + other[tail, :].astype(jnp.float32)
    factor = 4.0 / jnp.full((piece, LANES), jnp.sum(tails), jnp.float32)
    half = modes // 2

    def place(chunk):
        j = chunk ^ me
        at, span = 0, 1
        for shift, ways in reversed(digits):
            at = at + ((j >> shift) & (ways - 1)) * span
            span *= ways
        return at * size

    def update(part, b, m, r):
        block = ((m * 2 + part) * (win // LANES) + b) * win
        chunk, offset = divmod(block + r, size)
        at = pl.ds(pl.multiple_of(place(chunk) + offset, piece), piece)
        here = mine[at, :].astype(jnp.float32)
        there = other[at, :].astype(jnp.float32)
        low = jnp.where(on_left, here, there)
        high = jnp.where(on_left, there, here)
        for k, total in ((m, low), (half + m, high)):
            col = k * win + b * LANES
            old = probe[part, r : r + piece, col : col + LANES].astype(jnp.float32)
            updated[part, r : r + piece, k, b * LANES : (b + 1) * LANES] = old - factor * total

    stretch = win // 4
    copies = []
    for part in range(2):
        for start in range(0, win, stretch):
            for r in range(start, start + stretch, piece):
                for m in range(half):
                    for b in range(win // LANES):
                        update(part, b, m, r)
            at = (part, pl.ds(start, stretch))
            copies.append(
                pltpu.make_async_copy(updated.at[at], new_probe.at[at], sems.at[len(copies)])
            )
            copies[-1].start()
    for copy in copies:
        copy.wait()


def probe_update(mine, other, probe, shape, size, digits):
    vmem = pl.BlockSpec(memory_space=pltpu.VMEM)
    return pl.pallas_call(
        functools.partial(probe_update_kernel, size, digits),
        out_shape=jax.ShapeDtypeStruct(shape, jnp.float32),
        in_specs=[vmem] * 3,
        out_specs=pl.BlockSpec(memory_space=pl.ANY),
        scratch_shapes=[pltpu.VMEM(shape, jnp.float32), pltpu.SemaphoreType.DMA((8,))],
        compiler_params=pltpu.CompilerParams(vmem_limit_bytes=6 * MIB),
    )(mine, other, probe)


def low_sum_kernel(part, low_grad, from_left, token, low_sum):
    win = from_left.shape[2]
    rows = from_left.shape[1] - low_grad.shape[1]
    for r in range(0, low_grad.shape[1], CHUNK):
        at = slice(r, r + CHUNK)
        arrived = from_left[part, rows + r : rows + r + CHUNK, :].astype(jnp.float32)
        low_sum[at, :win] = (low_grad[part, at, :win] + arrived).astype(jnp.bfloat16)
        low_sum[at, win:] = low_grad[part, at, win:].astype(jnp.bfloat16)


def low_sum_of(part, low_grad, from_left, token):
    return small_call(
        functools.partial(low_sum_kernel, part),
        jax.ShapeDtypeStruct(low_grad.shape[1:], jnp.bfloat16),
        low_grad,
        from_left,
        token,
        weight=LOW_WEIGHT,
    )


def object_update_kernel(old, own_grad, from_left, above_re, above_im, new_object, token):
    token[...] = jnp.zeros_like(token)
    win, depth = from_left.shape[2], above_re.shape[0]
    from_above = (above_re, above_im)
    for part in range(2):
        for r in range(0, old.shape[1], CHUNK):
            at = slice(r, r + CHUNK)
            total = own_grad[part, at, :]
            if r < depth:
                total = total + from_above[part][at, :].astype(jnp.float32)
            updated = old[part, at, :].astype(jnp.float32) - total
            arrived = from_left[part, at, :].astype(jnp.float32)
            new_object[part, at, :win] = updated[:, :win] - arrived
            new_object[part, at, win:] = updated[:, win:]


def object_update(old, own_grad, from_left, above_re, above_im):
    return small_call(
        object_update_kernel,
        (jax.ShapeDtypeStruct(old.shape, jnp.float32), token_shape()),
        old,
        own_grad,
        from_left,
        above_re,
        above_im,
    )


def swap_cores(block):
    return lax.ppermute(block, "col", [(0, 1), (1, 0)])


def body(object_field, probe_modes, positions, counts, intensities):
    win = probe_modes.shape[1]
    modes = probe_modes.shape[2]
    number = lax.axis_size("row")
    below = from_behind(object_field[:, :win, :], "row", -1)
    probe_flat = probe_modes.reshape(2, win, modes * win)
    right_part, tables, measured, power = prepare(
        object_field, probe_flat, intensities[0, 0]
    )
    right = from_behind(right_part, "col", -1)
    corner = from_behind(first_columns(below, right), "col", -1)
    own_grad, low_grad, right_grad, keep, send, norm = position_gradients(
        positions[0, 0].T,
        counts.reshape(-1),
        power.reshape(1),
        object_field,
        below,
        right,
        corner,
        probe_flat,
        measured,
        tables,
    )
    half_rows = keep.size // LANES
    received = swap_cores(send.reshape(half_rows, LANES))
    from_left = from_behind(right_grad, "col", 1)
    digits = row_digits()
    first = digits[0]
    mine, *sends = chip_sum(
        keep.reshape(half_rows, LANES), received, norm, win * win, number, first[1]
    )
    for place, (shift, ways) in enumerate(digits):
        received = [swap_rows(block, (i + 1) << shift) for i, block in enumerate(sends)]
        if place + 1 < len(digits):
            mine, *sends = scatter_sum(mine, sends[0], received, digits[place + 1][1])
            if place == 0:
                low_re = low_sum_of(0, low_grad, from_left, sends[0])
        else:
            gathered, tail = last_sum(mine, sends[0], received)
            low_im = low_sum_of(1, low_grad, from_left, tail)
    above_re = from_behind(low_re, "row", 1)
    above_im = from_behind(low_im, "row", 1)
    new_object, token = object_update(object_field, own_grad, from_left, above_re, above_im)
    for shift, ways in digits[:0:-1]:
        pieces = [swap_rows(gathered, i << shift) for i in range(1, ways)]
        gathered = join(tail, [gathered] + pieces)
    pieces = [swap_rows(gathered, i << first[0]) for i in range(1, first[1])]
    gathered = join(token, [gathered] + pieces + [tail])
    other = swap_cores(gathered)
    size = half_rows // number
    new_probe = probe_update(gathered, other, probe_flat, probe_modes.shape, size, digits)
    return (new_object, new_probe)


def solution(mesh):
    placed = (
        P(None, ("grp", "row"), "col"),
        P(None, None, "grp", None),
        P(("grp", "row"), "col", None, None),
        P(("grp", "row"), "col"),
        P(("grp", "row"), "col", None, None, None),
    )
    return jax.shard_map(
        body,
        mesh=mesh,
        in_specs=placed,
        out_specs=(P(None, ("grp", "row"), "col"), P(None, None, "grp", None)),
        check_vma=False,
    )
```

```python
import functools

import jax
import jax.numpy as jnp
import ml_dtypes
import numpy as np
from jax import lax
from jax.experimental import pallas as pl
from jax.experimental.pallas import tpu as pltpu
from jax.sharding import PartitionSpec as P

LANES = 128
CHUNK = 32
FINE = 16
TAIL = 16
MIB = 1 << 20
LOW_WEIGHT = 8


def from_behind(block, axis, distance):
    devices = range(lax.axis_size(axis))
    route = [(i - distance, i) for i in devices if i - distance in devices]
    return lax.ppermute(block, axis, route)


def dft_blocks(win):
    grid = np.arange(win)
    angle = 2.0 * np.pi * (grid[:, None] * grid[None, :] % win) / win
    factor = 1.0 / np.sqrt(win)
    cos_table = (np.cos(angle) * factor).astype(ml_dtypes.bfloat16)
    sin_table = (np.sin(angle) * factor).astype(ml_dtypes.bfloat16)
    blocks = []
    for parity in range(2):
        cos_part, sin_part = cos_table[parity::2, : win // 2], sin_table[parity::2, : win // 2]
        blocks.append(np.block([[cos_part, sin_part], [-sin_part, cos_part]]))
    return np.stack(blocks + [block.T for block in blocks])


def dot(left, right):
    return jnp.dot(left, right, preferred_element_type=jnp.float32)


def gradient_kernel(
    modes,
    starts,
    count,
    power,
    own,
    below,
    right,
    corner,
    probe,
    measured,
    tables,
    own_grad,
    low_grad,
    right_grad,
    keep_out,
    send_out,
    norm_out,
    field,
    grad,
    window,
    wide,
    tall,
    wave,
    probe_sum,
):
    win = probe.shape[1]
    rows, cols = own.shape[1], own.shape[2]
    half = win // 2
    fine = range(0, win, FINE)
    spread = win // LANES + 1
    col_index = lax.axis_index("col")
    row_anchor = lax.axis_index("row") * rows
    col_anchor = col_index * cols

    def put_blocks(part, row, first, values):
        for b in range(values.shape[1] // LANES):
            piece = values[:, b * LANES : (b + 1) * LANES].astype(jnp.float32)
            field[part, first + b, row : row + CHUNK, :] = piece

    grad[...] = jnp.zeros_like(grad)
    probe_sum[...] = jnp.zeros_like(probe_sum)
    norm_out[...] = jnp.zeros_like(norm_out)
    for source, row_at, col_at in (
        (own, 0, 0),
        (right, 0, cols),
        (below, rows, 0),
        (corner, rows, cols),
    ):
        for part in range(2):
            for r in range(0, source.shape[1], CHUNK):
                put_blocks(part, row_at + r, col_at // LANES, source[part, r : r + CHUNK, :])
    lane = lax.broadcasted_iota(jnp.int32, (FINE, LANES), 1)

    def one_position(slot, carry):
        y, x = starts[0, slot] - row_anchor, starts[1, slot] - col_anchor
        base = x // LANES
        shift = x - base * LANES
        back_shift = (LANES - shift) % LANES
        keep = lane < LANES - shift
        for r in range(0, half, FINE):
            objs = []
            for start in (r, r + half):
                at = pl.ds(start, FINE)
                obj = []
                for part in range(2):
                    turned = [
                        pltpu.roll(field[part, base + b, pl.ds(y + start, FINE), :], back_shift, 1)
                        for b in range(spread)
                    ]
                    piece = jnp.concatenate(
                        [jnp.where(keep, a, b) for a, b in zip(turned[:-1], turned[1:])], axis=1
                    )
                    window[part, at, :] = piece
                    obj.append(piece)
                squares = obj[0] * obj[0] + obj[1] * obj[1]
                norm_out[...] += jnp.sum(squares.reshape(FINE // 8, 8, win), axis=0)
                objs.append(obj)
            for k in range(modes):
                cs = pl.ds(k * win, win)
                exits = []
                for start, (o_re, o_im) in zip((r, r + half), objs):
                    p_re, p_im = probe[0, pl.ds(start, FINE), cs], probe[1, pl.ds(start, FINE), cs]
                    exits.append((p_re * o_re - p_im * o_im, p_re * o_im + p_im * o_re))
                for part in range(2):
                    low, high = exits[0][part], exits[1][part]
                    at = pl.ds(part * half + r, FINE)
                    wide[k, 0, at, :] = (low + high).astype(jnp.bfloat16)
                    wide[k, 1, at, :] = (low - high).astype(jnp.bfloat16)

        for k in range(modes):
            for parity in range(2):
                out = dot(tables[parity], wide[k, parity])
                at = pl.ds(k * win + parity * half, half)
                for part in range(2):
                    low = out[part * half : (part + 1) * half, :half]
                    high = out[part * half : (part + 1) * half, half:]
                    to = pl.ds(part * half, half)
                    tall[0, at, to] = (low + high).astype(jnp.bfloat16)
                    tall[1, at, to] = (low - high).astype(jnp.bfloat16)
        for parity in range(2):
            wave[parity] = dot(tall[parity], tables[2 + parity])

        for r in fine:
            for parity in range(2):
                waves = []
                total = jnp.zeros((FINE, half), jnp.float32)
                for k in range(modes):
                    ka = pl.ds(k * win + r, FINE)
                    waves.append((wave[parity, ka, :half], wave[parity, ka, half:]))
                    total = total + (waves[k][0] * waves[k][0] + waves[k][1] * waves[k][1])
                gs = pl.ds(parity * half, half)
                amp = measured[slot, pl.ds(r, FINE), gs]
                ratio = 1.0 - amp * lax.rsqrt(jnp.maximum(total, 1.0))
                for k in range(modes):
                    for part in range(2):
                        at = pl.ds(part * half + r % half, FINE)
                        wide[k, r // half, at, gs] = (waves[k][part] * ratio).astype(jnp.bfloat16)

        for k in range(modes):
            even = dot(tables[2], wide[k, 0])
            odd = dot(tables[3], wide[k, 1])
            for place, out in enumerate((even + odd, even - odd)):
                at = pl.ds(k * win + place * half, half)
                for part in range(2):
                    for parity in range(2):
                        tall[parity, at, part * half : (part + 1) * half] = out[
                            part * half : (part + 1) * half, parity * half : (parity + 1) * half
                        ].astype(jnp.bfloat16)
        for parity in range(2):
            wave[parity] = dot(tall[parity], tables[parity])

        keep_high = lane >= shift
        for r in fine:
            at = pl.ds(r, FINE)
            sums = [[jnp.zeros((FINE, LANES), jnp.float32) for _ in range(2)] for _ in range(2)]
            for b in range(2):
                bs = pl.ds(b * half, half)
                o_re, o_im = window[0, at, bs], window[1, at, bs]
                for k in range(modes):
                    cs = pl.ds(k * win + b * half, half)
                    ka = pl.ds(k * win + r, FINE)
                    even, odd = wave[0, ka, :], wave[1, ka, :]
                    d = even + odd if b == 0 else even - odd
                    d_re, d_im = d[:, :half], d[:, half:]
                    p_re, p_im = probe[0, at, cs], probe[1, at, cs]
                    sums[0][b] = sums[0][b] + (p_re * d_re + p_im * d_im)
                    sums[1][b] = sums[1][b] + (p_re * d_im - p_im * d_re)
                    probe_sum[k, 0, b, at, :] += o_re * d_re + o_im * d_im
                    probe_sum[k, 1, b, at, :] += o_re * d_im - o_im * d_re
            for part in range(2):
                turned = [pltpu.roll(piece, shift, 1) for piece in sums[part]]
                turned = [jnp.zeros_like(turned[0])] + turned + [jnp.zeros_like(turned[0])]
                for b in range(spread):
                    grad[part, base + b, pl.ds(y + r, FINE), :] += jnp.where(
                        keep_high, turned[b + 1], turned[b]
                    )
        return carry

    lax.fori_loop(0, count[0], one_position, 0)
    for m in range(modes // 2):
        keep_mode = col_index * (modes // 2) + m
        send_mode = (1 - col_index) * (modes // 2) + m
        keep_out[m] = probe_sum[keep_mode]
        send_out[m] = probe_sum[send_mode].astype(jnp.bfloat16)
    scale = 1.0 / jnp.full((8, LANES), power[0], jnp.float32)
    scale = jnp.concatenate([scale] * (CHUNK // 8), axis=0)

    def take_blocks(part, at, first, number):
        return jnp.concatenate(
            [grad[part, first + b, at, :] * scale for b in range(number)], axis=1
        )

    for part in range(2):
        for r in range(0, rows + win, CHUNK):
            at = pl.ds(r, CHUNK)
            piece = take_blocks(part, at, cols // LANES, win // LANES)
            right_grad[part, at, :] = piece.astype(jnp.bfloat16)
        for r in range(0, rows, CHUNK):
            at = pl.ds(r, CHUNK)
            own_grad[part, at, :] = take_blocks(part, at, 0, cols // LANES)
        for r in range(0, win, CHUNK):
            at, of = pl.ds(r, CHUNK), pl.ds(rows + r, CHUNK)
            low_grad[part, at, :] = take_blocks(part, of, 0, cols // LANES)


def position_gradients(starts, count, power, own, below, right, corner, probe, measured, tables):
    win, modes = probe.shape[1], probe.shape[2] // probe.shape[1]
    rows, cols = own.shape[1:]
    f32, bf16 = jnp.float32, jnp.bfloat16
    smem = pl.BlockSpec(memory_space=pltpu.SMEM)
    vmem = pl.BlockSpec(memory_space=pltpu.VMEM)
    if win != 2 * LANES:
        raise ValueError("window size")
    slots = measured.shape[0]
    flops = 16 * slots * modes * win**3
    half_blocks = (modes // 2, 2, win // LANES, win, LANES)
    return pl.pallas_call(
        functools.partial(gradient_kernel, modes),
        out_shape=(
            jax.ShapeDtypeStruct((2, rows, cols), f32),
            jax.ShapeDtypeStruct((2, win, cols), f32),
            jax.ShapeDtypeStruct((2, rows + win, win), bf16),
            jax.ShapeDtypeStruct(half_blocks, f32),
            jax.ShapeDtypeStruct(half_blocks, bf16),
            jax.ShapeDtypeStruct((8, win), f32),
        ),
        in_specs=[smem] * 3 + [vmem] * 7,
        out_specs=(vmem,) * 6,
        scratch_shapes=[
            pltpu.VMEM((2, (cols + win) // LANES, rows + win, LANES), f32),
            pltpu.VMEM((2, (cols + win) // LANES, rows + win, LANES), f32),
            pltpu.VMEM((2, win, win), f32),
            pltpu.VMEM((modes, 2, win, win), bf16),
            pltpu.VMEM((2, modes * win, win), bf16),
            pltpu.VMEM((2, modes * win, win), f32),
            pltpu.VMEM((modes, 2, win // LANES, win, LANES), f32),
        ],
        compiler_params=pltpu.CompilerParams(vmem_limit_bytes=26 * MIB),
        cost_estimate=pl.CostEstimate(flops=flops, bytes_accessed=12 << 20, transcendentals=0),
    )(starts, count, power, own, below, right, corner, probe, measured, tables)


def in_three(value):
    full = jnp.full((TAIL, LANES), value, jnp.float32)
    high = full.astype(jnp.bfloat16).astype(jnp.float32)
    mid = (full - high).astype(jnp.bfloat16).astype(jnp.float32)
    low = full - high - mid
    row = lax.broadcasted_iota(jnp.int32, (TAIL, LANES), 0)
    lane = lax.broadcasted_iota(jnp.int32, (TAIL, LANES), 1)
    tile = jnp.where(row == 0, high, jnp.where(row == 1, mid, jnp.where(row == 2, low, 0.0)))
    return jnp.where(lane == 0, tile, 0.0).astype(jnp.bfloat16)


def small_call(kernel, shapes, *operands, weight=1):
    return pl.pallas_call(
        kernel,
        out_shape=shapes,
        compiler_params=pltpu.CompilerParams(vmem_limit_bytes=4 * MIB),
        cost_estimate=pl.CostEstimate(flops=0, bytes_accessed=weight * MIB, transcendentals=0),
    )(*operands)


def first_columns_kernel(block, token, first):
    first[...] = block[:, :, : first.shape[2]]


def first_columns(block, token):
    return small_call(
        first_columns_kernel, jax.ShapeDtypeStruct(token.shape, block.dtype), block, token
    )


def token_shape():
    return jax.ShapeDtypeStruct((8, LANES), jnp.float32)


def prepare_kernel(own, probe, intens, blocks, right_part, tables, measured, wide_probe, power):
    right_part[...] = own[:, :, : right_part.shape[2]]
    tables[...] = blocks[...]
    count, size, _ = intens.shape
    row = lax.broadcasted_iota(jnp.int32, (size, size), 0)
    col = lax.broadcasted_iota(jnp.int32, (size, size), 1)
    to_even_first = (col == jnp.where(row < size // 2, 2 * row, 2 * row - size + 1)).astype(
        jnp.float32
    )
    from_left = to_even_first.astype(jnp.bfloat16)
    from_right = (row == jnp.where(col < size // 2, 2 * col, 2 * col - size + 1)).astype(
        jnp.float32
    )
    from_right = from_right.astype(jnp.bfloat16)
    for slot in range(count):
        turned = dot(from_left, intens[slot]).astype(jnp.bfloat16)
        measured[slot] = jnp.sqrt(dot(turned, from_right))
    win = right_part.shape[2]
    modes = probe.shape[2] // win
    largest = jnp.zeros((8, win), jnp.float32)
    for r in range(0, probe.shape[1], CHUNK):
        at = slice(r, r + CHUNK)
        total = jnp.zeros((CHUNK, win), jnp.float32)
        for k in range(modes):
            for part in range(2):
                p = probe[part, at, k * win : (k + 1) * win].astype(jnp.float32)
                wide_probe[part, at, k * win : (k + 1) * win] = p
                total = total + p * p
        largest = jnp.maximum(largest, jnp.max(total.reshape(CHUNK // 8, 8, win), axis=0))
    power[0, 0] = jnp.max(largest)


def prepare(own, probe, intens):
    win = probe.shape[1]
    blocks = dft_blocks(win)
    vmem = pl.BlockSpec(memory_space=pltpu.VMEM)
    return pl.pallas_call(
        prepare_kernel,
        out_shape=(
            jax.ShapeDtypeStruct(own.shape[:2] + (win,), own.dtype),
            jax.ShapeDtypeStruct(blocks.shape, jnp.bfloat16),
            jax.ShapeDtypeStruct(intens.shape, jnp.float32),
            jax.ShapeDtypeStruct(probe.shape, jnp.float32),
            jax.ShapeDtypeStruct((1, 1), jnp.float32),
        ),
        out_specs=(vmem, vmem, vmem, vmem, pl.BlockSpec(memory_space=pltpu.SMEM)),
        compiler_params=pltpu.CompilerParams(vmem_limit_bytes=8 * MIB),
    )(own, probe, intens, blocks)


def block_shapes(number, size, ways):
    if not ways:
        return (jax.ShapeDtypeStruct((number * size + TAIL, LANES), jnp.bfloat16),)
    sends = jax.ShapeDtypeStruct((number // ways * size + TAIL, LANES), jnp.bfloat16)
    return (jax.ShapeDtypeStruct((number // ways, size, LANES), jnp.float32),) + (sends,) * (ways - 1)


def put_block(j, total, outs):
    size = total.shape[0]
    if len(outs) == 1:
        outs[0][pl.ds(j * size, size), :] = total.astype(jnp.bfloat16)
    elif j % len(outs) == 0:
        outs[0][j // len(outs)] = total
    else:
        at = pl.ds(j // len(outs) * size, size)
        outs[j % len(outs)][at, :] = total.astype(jnp.bfloat16)


def put_weight(weight, outs):
    tile = in_three(weight)
    for sent in outs if len(outs) == 1 else outs[1:]:
        sent[pl.ds(sent.shape[0] - TAIL, TAIL), :] = tile


def weight_of(block):
    return jnp.sum(block[pl.ds(block.shape[0] - TAIL, TAIL), :].astype(jnp.float32))


def chip_sum_kernel(pixels, size, keep, received, norm, *outs):
    me = lax.axis_index("row")
    for j in range(keep.shape[0] // size):
        at = pl.ds(pl.multiple_of((j ^ me) * size, size), size)
        put_block(j, keep[at, :] + received[at, :].astype(jnp.float32), outs)
    put_weight(jnp.sum(norm[...]) / pixels, outs)


def chip_sum(keep, received, norm, pixels, number, ways):
    size = keep.shape[0] // number
    return small_call(
        functools.partial(chip_sum_kernel, pixels, size),
        block_shapes(number, size, ways),
        keep,
        received,
        norm,
    )


def scatter_sum_kernel(number, mine, sent, *refs):
    received, outs = refs[:number], refs[number:]
    size = mine.shape[1]
    for j in range(mine.shape[0]):
        total = mine[j]
        for block in received:
            total = total + block[pl.ds(j * size, size), :].astype(jnp.float32)
        put_block(j, total, outs)
    put_weight(sum([weight_of(block) for block in received], weight_of(sent)), outs)


def scatter_sum(mine, sent, received, ways):
    number, size, _ = mine.shape
    return small_call(
        functools.partial(scatter_sum_kernel, len(received)),
        block_shapes(number, size, ways),
        mine,
        sent,
        *received,
    )


def pair_up(terms):
    while len(terms) > 1:
        terms = [a + b for a, b in zip(terms[::2], terms[1::2])]
    return terms[0]


def exchange_sum_kernel(size, *refs):
    blocks, chunks, tail = refs[:-2], refs[-2], refs[-1]
    for j in range(chunks.shape[0] // size):
        terms = [
            block[pl.ds((j ^ i) * size, size), :].astype(jnp.float32)
            for i, block in enumerate(blocks)
        ]
        chunks[pl.ds(j * size, size), :] = pair_up(terms).astype(jnp.bfloat16)
    tail[...] = in_three(pair_up([weight_of(block) for block in blocks]))


def exchange_sum(blocks, size):
    rows = blocks[0].shape[0] - TAIL
    return small_call(
        functools.partial(exchange_sum_kernel, size),
        (
            jax.ShapeDtypeStruct((rows, LANES), jnp.bfloat16),
            jax.ShapeDtypeStruct((TAIL, LANES), jnp.bfloat16),
        ),
        *blocks,
    )


def join_kernel(*refs):
    joined = refs[-1]
    at = 0
    for block in refs[1:-1]:
        joined[pl.ds(at, block.shape[0]), :] = block[...]
        at += block.shape[0]


def join(token, blocks):
    rows = sum(block.shape[0] for block in blocks)
    return small_call(
        join_kernel, jax.ShapeDtypeStruct((rows, LANES), blocks[0].dtype), token, *blocks
    )


def swap_rows(block, step):
    number = lax.axis_size("row")
    return lax.ppermute(block, "row", [(i, i ^ step) for i in range(number)])


def row_digits():
    number = lax.axis_size("row")
    if number & (number - 1) or number < 2:
        raise ValueError("row size")
    bits = number.bit_length() - 1
    return [(shift, 1 << min(2, bits - shift)) for shift in range(0, bits, 2)]


def probe_update_kernel(size, digits, mine, other, probe, new_probe, updated, sems):
    _, win, modes, _ = updated.shape
    number = mine.shape[0] // size
    me = lax.axis_index("row")
    piece = min(size, CHUNK)
    on_left = lax.axis_index("col") == 0
    tail = pl.ds(number * size, TAIL)
    tails = mine[tail, :].astype(jnp.float32) + other[tail, :].astype(jnp.float32)
    factor = 4.0 / jnp.full((piece, LANES), jnp.sum(tails), jnp.float32)
    half = modes // 2

    def place(chunk):
        j = chunk ^ me
        at, span = 0, 1
        for shift, ways in reversed(digits):
            at = at + ((j >> shift) & (ways - 1)) * span
            span *= ways
        return at * size

    def update(part, b, m, r):
        block = ((m * 2 + part) * (win // LANES) + b) * win
        chunk, offset = divmod(block + r, size)
        at = pl.ds(pl.multiple_of(place(chunk) + offset, piece), piece)
        here = mine[at, :].astype(jnp.float32)
        there = other[at, :].astype(jnp.float32)
        low = jnp.where(on_left, here, there)
        high = jnp.where(on_left, there, here)
        for k, total in ((m, low), (half + m, high)):
            col = k * win + b * LANES
            old = probe[part, r : r + piece, col : col + LANES]
            updated[part, r : r + piece, k, b * LANES : (b + 1) * LANES] = old - factor * total

    stretch = win // 4
    copies = []
    for part in range(2):
        for start in range(0, win, stretch):
            for r in range(start, start + stretch, piece):
                for m in range(half):
                    for b in range(win // LANES):
                        update(part, b, m, r)
            at = (part, pl.ds(start, stretch))
            copies.append(
                pltpu.make_async_copy(updated.at[at], new_probe.at[at], sems.at[len(copies)])
            )
            copies[-1].start()
    for copy in copies:
        copy.wait()


def probe_update(mine, other, probe, shape, size, digits):
    vmem = pl.BlockSpec(memory_space=pltpu.VMEM)
    return pl.pallas_call(
        functools.partial(probe_update_kernel, size, digits),
        out_shape=jax.ShapeDtypeStruct(shape, jnp.float32),
        in_specs=[vmem] * 3,
        out_specs=pl.BlockSpec(memory_space=pl.ANY),
        scratch_shapes=[pltpu.VMEM(shape, jnp.float32), pltpu.SemaphoreType.DMA((8,))],
        compiler_params=pltpu.CompilerParams(vmem_limit_bytes=6 * MIB),
    )(mine, other, probe)


def low_sum_kernel(part, low_grad, from_left, token, low_sum):
    win = from_left.shape[2]
    rows = from_left.shape[1] - low_grad.shape[1]
    for r in range(0, low_grad.shape[1], CHUNK):
        at = slice(r, r + CHUNK)
        arrived = from_left[part, rows + r : rows + r + CHUNK, :].astype(jnp.float32)
        low_sum[at, :win] = (low_grad[part, at, :win] + arrived).astype(jnp.bfloat16)
        low_sum[at, win:] = low_grad[part, at, win:].astype(jnp.bfloat16)


def low_sum_of(part, low_grad, from_left, token):
    return small_call(
        functools.partial(low_sum_kernel, part),
        jax.ShapeDtypeStruct(low_grad.shape[1:], jnp.bfloat16),
        low_grad,
        from_left,
        token,
        weight=LOW_WEIGHT,
    )


def object_update_kernel(old, own_grad, from_left, above_re, above_im, new_object, token):
    token[...] = jnp.zeros_like(token)
    win, depth = from_left.shape[2], above_re.shape[0]
    from_above = (above_re, above_im)
    for part in range(2):
        for r in range(0, old.shape[1], CHUNK):
            at = slice(r, r + CHUNK)
            total = own_grad[part, at, :]
            if r < depth:
                total = total + from_above[part][at, :].astype(jnp.float32)
            updated = old[part, at, :].astype(jnp.float32) - total
            arrived = from_left[part, at, :].astype(jnp.float32)
            new_object[part, at, :win] = updated[:, :win] - arrived
            new_object[part, at, win:] = updated[:, win:]


def object_update(old, own_grad, from_left, above_re, above_im):
    return small_call(
        object_update_kernel,
        (jax.ShapeDtypeStruct(old.shape, jnp.float32), token_shape()),
        old,
        own_grad,
        from_left,
        above_re,
        above_im,
    )


def swap_cores(block):
    return lax.ppermute(block, "col", [(0, 1), (1, 0)])


def body(object_field, probe_modes, positions, counts, intensities):
    win = probe_modes.shape[1]
    modes = probe_modes.shape[2]
    number = lax.axis_size("row")
    below = from_behind(object_field[:, :win, :], "row", -1)
    right_part, tables, measured, probe, power = prepare(
        object_field, probe_modes.reshape(2, win, modes * win), intensities[0, 0]
    )
    right = from_behind(right_part, "col", -1)
    corner = from_behind(first_columns(below, right), "col", -1)
    own_grad, low_grad, right_grad, keep, send, norm = position_gradients(
        positions[0, 0].T,
        counts.reshape(-1),
        power.reshape(1),
        object_field,
        below,
        right,
        corner,
        probe,
        measured,
        tables,
    )
    half_rows = keep.size // LANES
    received = swap_cores(send.reshape(half_rows, LANES))
    from_left = from_behind(right_grad, "col", 1)
    digits = row_digits()
    size = half_rows // number
    ways = [digit[1] for digit in digits[:-1]] + [0]
    outs = chip_sum(keep.reshape(half_rows, LANES), received, norm, win * win, number, ways[0])
    for place, (shift, _) in enumerate(digits[:-1]):
        mine, *sends = outs
        received = [swap_rows(block, (i + 1) << shift) for i, block in enumerate(sends)]
        outs = scatter_sum(mine, sends[0], received, ways[place + 1])
    low_re = low_sum_of(0, low_grad, from_left, outs[0])
    low_im = low_sum_of(1, low_grad, from_left, outs[0])
    above_re = from_behind(low_re, "row", 1)
    above_im = from_behind(low_im, "row", 1)
    new_object, token = object_update(object_field, own_grad, from_left, above_re, above_im)
    shift, count = digits[-1]
    partners = [swap_rows(outs[0], i << shift) for i in range(1, count)]
    gathered, tail = exchange_sum(list(outs) + partners, size)
    for place, (shift, count) in reversed(list(enumerate(digits[:-1]))):
        pieces = [gathered] + [swap_rows(gathered, i << shift) for i in range(1, count)]
        gathered = join(token, pieces + [tail]) if place == 0 else join(tail, pieces)
    if len(digits) == 1:
        gathered = join(token, [gathered, tail])
    other = swap_cores(gathered)
    new_probe = probe_update(gathered, other, probe, probe_modes.shape, size, digits)
    return (new_object, new_probe)


def solution(mesh):
    placed = (
        P(None, ("grp", "row"), "col"),
        P(None, None, "grp", None),
        P(("grp", "row"), "col", None, None),
        P(("grp", "row"), "col"),
        P(("grp", "row"), "col", None, None, None),
    )
    return jax.shard_map(
        body,
        mesh=mesh,
        in_specs=placed,
        out_specs=(P(None, ("grp", "row"), "col"), P(None, None, "grp", None)),
        check_vma=False,
    )
```

```python
import functools

import jax
import jax.numpy as jnp
import ml_dtypes
import numpy as np
from jax import lax
from jax.experimental import pallas as pl
from jax.experimental.pallas import tpu as pltpu
from jax.sharding import PartitionSpec as P

LANES = 128
CHUNK = 32
FINE = 16
TAIL = 16
MIB = 1 << 20
LOW_WEIGHT = 8
SPLIT = 4


def from_behind(block, axis, distance):
    devices = range(lax.axis_size(axis))
    route = [(i - distance, i) for i in devices if i - distance in devices]
    return lax.ppermute(block, axis, route)


def dft_blocks(win):
    grid = np.arange(win)
    angle = 2.0 * np.pi * (grid[:, None] * grid[None, :] % win) / win
    factor = 1.0 / np.sqrt(win)
    cos_table = (np.cos(angle) * factor).astype(ml_dtypes.bfloat16)
    sin_table = (np.sin(angle) * factor).astype(ml_dtypes.bfloat16)
    blocks = []
    for parity in range(2):
        cos_part, sin_part = cos_table[parity::2, : win // 2], sin_table[parity::2, : win // 2]
        blocks.append(np.block([[cos_part, sin_part], [-sin_part, cos_part]]))
    return np.stack(blocks + [block.T for block in blocks])


def dot(left, right):
    return jnp.dot(left, right, preferred_element_type=jnp.float32)


def gradient_kernel(
    modes,
    starts,
    count,
    power,
    own,
    below,
    right,
    corner,
    probe,
    measured,
    tables,
    own_grad,
    low_grad,
    right_grad,
    keep_out,
    send_out,
    norm_out,
    field,
    grad,
    window,
    wide,
    tall,
    wave,
    probe_sum,
):
    win = probe.shape[1]
    rows, cols = own.shape[1], own.shape[2]
    half = win // 2
    fine = range(0, win, FINE)
    spread = win // LANES + 1
    col_index = lax.axis_index("col")
    row_anchor = lax.axis_index("row") * rows
    col_anchor = col_index * cols

    def put_blocks(part, row, first, values):
        for b in range(values.shape[1] // LANES):
            piece = values[:, b * LANES : (b + 1) * LANES].astype(jnp.float32)
            field[part, first + b, row : row + CHUNK, :] = piece

    grad[...] = jnp.zeros_like(grad)
    probe_sum[...] = jnp.zeros_like(probe_sum)
    norm_out[...] = jnp.zeros_like(norm_out)
    for source, row_at, col_at in (
        (own, 0, 0),
        (right, 0, cols),
        (below, rows, 0),
        (corner, rows, cols),
    ):
        for part in range(2):
            for r in range(0, source.shape[1], CHUNK):
                put_blocks(part, row_at + r, col_at // LANES, source[part, r : r + CHUNK, :])
    lane = lax.broadcasted_iota(jnp.int32, (FINE, LANES), 1)

    def one_position(slot, carry):
        y, x = starts[0, slot] - row_anchor, starts[1, slot] - col_anchor
        base = x // LANES
        shift = x - base * LANES
        back_shift = (LANES - shift) % LANES
        keep = lane < LANES - shift
        for r in range(0, half, FINE):
            objs = []
            for start in (r, r + half):
                at = pl.ds(start, FINE)
                obj = []
                for part in range(2):
                    turned = [
                        pltpu.roll(field[part, base + b, pl.ds(y + start, FINE), :], back_shift, 1)
                        for b in range(spread)
                    ]
                    piece = jnp.concatenate(
                        [jnp.where(keep, a, b) for a, b in zip(turned[:-1], turned[1:])], axis=1
                    )
                    window[part, at, :] = piece
                    obj.append(piece)
                squares = obj[0] * obj[0] + obj[1] * obj[1]
                norm_out[...] += jnp.sum(squares.reshape(FINE // 8, 8, win), axis=0)
                objs.append(obj)
            for k in range(modes):
                cs = pl.ds(k * win, win)
                exits = []
                for start, (o_re, o_im) in zip((r, r + half), objs):
                    p_re, p_im = probe[0, pl.ds(start, FINE), cs], probe[1, pl.ds(start, FINE), cs]
                    exits.append((p_re * o_re - p_im * o_im, p_re * o_im + p_im * o_re))
                for part in range(2):
                    low, high = exits[0][part], exits[1][part]
                    at = pl.ds(part * half + r, FINE)
                    wide[k, 0, at, :] = (low + high).astype(jnp.bfloat16)
                    wide[k, 1, at, :] = (low - high).astype(jnp.bfloat16)

        for k in range(modes):
            for parity in range(2):
                out = dot(tables[parity], wide[k, parity])
                at = pl.ds(k * win + parity * half, half)
                for part in range(2):
                    low = out[part * half : (part + 1) * half, :half]
                    high = out[part * half : (part + 1) * half, half:]
                    to = pl.ds(part * half, half)
                    tall[0, at, to] = (low + high).astype(jnp.bfloat16)
                    tall[1, at, to] = (low - high).astype(jnp.bfloat16)
        for parity in range(2):
            wave[parity] = dot(tall[parity], tables[2 + parity])

        for r in fine:
            for parity in range(2):
                waves = []
                total = jnp.zeros((FINE, half), jnp.float32)
                for k in range(modes):
                    ka = pl.ds(k * win + r, FINE)
                    waves.append((wave[parity, ka, :half], wave[parity, ka, half:]))
                    total = total + (waves[k][0] * waves[k][0] + waves[k][1] * waves[k][1])
                gs = pl.ds(parity * half, half)
                amp = measured[slot, pl.ds(r, FINE), gs]
                ratio = 1.0 - amp * lax.rsqrt(jnp.maximum(total, 1.0))
                for k in range(modes):
                    for part in range(2):
                        at = pl.ds(part * half + r % half, FINE)
                        wide[k, r // half, at, gs] = (waves[k][part] * ratio).astype(jnp.bfloat16)

        for k in range(modes):
            even = dot(tables[2], wide[k, 0])
            odd = dot(tables[3], wide[k, 1])
            for place, out in enumerate((even + odd, even - odd)):
                at = pl.ds(k * win + place * half, half)
                for part in range(2):
                    for parity in range(2):
                        tall[parity, at, part * half : (part + 1) * half] = out[
                            part * half : (part + 1) * half, parity * half : (parity + 1) * half
                        ].astype(jnp.bfloat16)
        for parity in range(2):
            wave[parity] = dot(tall[parity], tables[parity])

        keep_high = lane >= shift
        for r in fine:
            at = pl.ds(r, FINE)
            sums = [[jnp.zeros((FINE, LANES), jnp.float32) for _ in range(2)] for _ in range(2)]
            for b in range(2):
                bs = pl.ds(b * half, half)
                o_re, o_im = window[0, at, bs], window[1, at, bs]
                for k in range(modes):
                    cs = pl.ds(k * win + b * half, half)
                    ka = pl.ds(k * win + r, FINE)
                    even, odd = wave[0, ka, :], wave[1, ka, :]
                    d = even + odd if b == 0 else even - odd
                    d_re, d_im = d[:, :half], d[:, half:]
                    p_re, p_im = probe[0, at, cs], probe[1, at, cs]
                    sums[0][b] = sums[0][b] + (p_re * d_re + p_im * d_im)
                    sums[1][b] = sums[1][b] + (p_re * d_im - p_im * d_re)
                    probe_sum[k, 0, b, at, :] += o_re * d_re + o_im * d_im
                    probe_sum[k, 1, b, at, :] += o_re * d_im - o_im * d_re
            for part in range(2):
                turned = [pltpu.roll(piece, shift, 1) for piece in sums[part]]
                turned = [jnp.zeros_like(turned[0])] + turned + [jnp.zeros_like(turned[0])]
                for b in range(spread):
                    grad[part, base + b, pl.ds(y + r, FINE), :] += jnp.where(
                        keep_high, turned[b + 1], turned[b]
                    )
        return carry

    lax.fori_loop(0, count[0], one_position, 0)
    for m in range(modes // 2):
        keep_mode = col_index * (modes // 2) + m
        send_mode = (1 - col_index) * (modes // 2) + m
        keep_out[m] = probe_sum[keep_mode]
        send_out[m] = probe_sum[send_mode].astype(jnp.bfloat16)
    scale = 1.0 / jnp.full((8, LANES), power[0], jnp.float32)
    scale = jnp.concatenate([scale] * (CHUNK // 8), axis=0)

    def take_blocks(part, at, first, number):
        return jnp.concatenate(
            [grad[part, first + b, at, :] * scale for b in range(number)], axis=1
        )

    for part in range(2):
        for r in range(0, rows + win, CHUNK):
            at = pl.ds(r, CHUNK)
            piece = take_blocks(part, at, cols // LANES, win // LANES)
            right_grad[part, at, :] = piece.astype(jnp.bfloat16)
        for r in range(0, rows, CHUNK):
            at = pl.ds(r, CHUNK)
            own_grad[part, at, :] = take_blocks(part, at, 0, cols // LANES)
        for r in range(0, win, CHUNK):
            at, of = pl.ds(r, CHUNK), pl.ds(rows + r, CHUNK)
            low_grad[part, at, :] = take_blocks(part, of, 0, cols // LANES)


def position_gradients(starts, count, power, own, below, right, corner, probe, measured, tables):
    win, modes = probe.shape[1], probe.shape[2] // probe.shape[1]
    rows, cols = own.shape[1:]
    f32, bf16 = jnp.float32, jnp.bfloat16
    smem = pl.BlockSpec(memory_space=pltpu.SMEM)
    vmem = pl.BlockSpec(memory_space=pltpu.VMEM)
    if win != 2 * LANES:
        raise ValueError("window size")
    slots = measured.shape[0]
    flops = 16 * slots * modes * win**3
    half_blocks = (modes // 2, 2, win // LANES, win, LANES)
    return pl.pallas_call(
        functools.partial(gradient_kernel, modes),
        out_shape=(
            jax.ShapeDtypeStruct((2, rows, cols), f32),
            jax.ShapeDtypeStruct((2, win, cols), f32),
            jax.ShapeDtypeStruct((2, rows + win, win), bf16),
            jax.ShapeDtypeStruct(half_blocks, f32),
            jax.ShapeDtypeStruct(half_blocks, bf16),
            jax.ShapeDtypeStruct((8, win), f32),
        ),
        in_specs=[smem] * 3 + [vmem] * 7,
        out_specs=(vmem,) * 6,
        scratch_shapes=[
            pltpu.VMEM((2, (cols + win) // LANES, rows + win, LANES), f32),
            pltpu.VMEM((2, (cols + win) // LANES, rows + win, LANES), f32),
            pltpu.VMEM((2, win, win), f32),
            pltpu.VMEM((modes, 2, win, win), bf16),
            pltpu.VMEM((2, modes * win, win), bf16),
            pltpu.VMEM((2, modes * win, win), f32),
            pltpu.VMEM((modes, 2, win // LANES, win, LANES), f32),
        ],
        compiler_params=pltpu.CompilerParams(vmem_limit_bytes=26 * MIB),
        cost_estimate=pl.CostEstimate(flops=flops, bytes_accessed=12 << 20, transcendentals=0),
    )(starts, count, power, own, below, right, corner, probe, measured, tables)


def in_three(value):
    full = jnp.full((TAIL, LANES), value, jnp.float32)
    high = full.astype(jnp.bfloat16).astype(jnp.float32)
    mid = (full - high).astype(jnp.bfloat16).astype(jnp.float32)
    low = full - high - mid
    row = lax.broadcasted_iota(jnp.int32, (TAIL, LANES), 0)
    lane = lax.broadcasted_iota(jnp.int32, (TAIL, LANES), 1)
    tile = jnp.where(row == 0, high, jnp.where(row == 1, mid, jnp.where(row == 2, low, 0.0)))
    return jnp.where(lane == 0, tile, 0.0).astype(jnp.bfloat16)


def small_call(kernel, shapes, *operands, weight=1):
    return pl.pallas_call(
        kernel,
        out_shape=shapes,
        compiler_params=pltpu.CompilerParams(vmem_limit_bytes=4 * MIB),
        cost_estimate=pl.CostEstimate(flops=0, bytes_accessed=weight * MIB, transcendentals=0),
    )(*operands)


def first_columns_kernel(block, token, first):
    first[...] = block[:, :, : first.shape[2]]


def first_columns(block, token):
    return small_call(
        first_columns_kernel, jax.ShapeDtypeStruct(token.shape, block.dtype), block, token
    )


def prepare_kernel(own, probe, intens, blocks, right_part, tables, measured, wide_probe, power):
    right_part[...] = own[:, :, : right_part.shape[2]]
    tables[...] = blocks[...]
    count, size, _ = intens.shape
    row = lax.broadcasted_iota(jnp.int32, (size, size), 0)
    col = lax.broadcasted_iota(jnp.int32, (size, size), 1)
    to_even_first = (col == jnp.where(row < size // 2, 2 * row, 2 * row - size + 1)).astype(
        jnp.float32
    )
    from_left = to_even_first.astype(jnp.bfloat16)
    from_right = (row == jnp.where(col < size // 2, 2 * col, 2 * col - size + 1)).astype(
        jnp.float32
    )
    from_right = from_right.astype(jnp.bfloat16)
    for slot in range(count):
        turned = dot(from_left, intens[slot]).astype(jnp.bfloat16)
        measured[slot] = jnp.sqrt(dot(turned, from_right))
    win = right_part.shape[2]
    modes = probe.shape[2] // win
    largest = jnp.zeros((8, win), jnp.float32)
    for r in range(0, probe.shape[1], CHUNK):
        at = slice(r, r + CHUNK)
        total = jnp.zeros((CHUNK, win), jnp.float32)
        for k in range(modes):
            for part in range(2):
                p = probe[part, at, k * win : (k + 1) * win].astype(jnp.float32)
                wide_probe[part, at, k * win : (k + 1) * win] = p
                total = total + p * p
        largest = jnp.maximum(largest, jnp.max(total.reshape(CHUNK // 8, 8, win), axis=0))
    power[0, 0] = jnp.max(largest)


def prepare(own, probe, intens):
    win = probe.shape[1]
    blocks = dft_blocks(win)
    vmem = pl.BlockSpec(memory_space=pltpu.VMEM)
    return pl.pallas_call(
        prepare_kernel,
        out_shape=(
            jax.ShapeDtypeStruct(own.shape[:2] + (win,), own.dtype),
            jax.ShapeDtypeStruct(blocks.shape, jnp.bfloat16),
            jax.ShapeDtypeStruct(intens.shape, jnp.float32),
            jax.ShapeDtypeStruct(probe.shape, jnp.float32),
            jax.ShapeDtypeStruct((1, 1), jnp.float32),
        ),
        out_specs=(vmem, vmem, vmem, vmem, pl.BlockSpec(memory_space=pltpu.SMEM)),
        compiler_params=pltpu.CompilerParams(vmem_limit_bytes=8 * MIB),
    )(own, probe, intens, blocks)


def block_shapes(number, size, ways):
    if not ways:
        return (jax.ShapeDtypeStruct((number * size + TAIL, LANES), jnp.bfloat16),)
    sends = jax.ShapeDtypeStruct((number // ways * size + TAIL, LANES), jnp.bfloat16)
    return (jax.ShapeDtypeStruct((number // ways, size, LANES), jnp.float32),) + (sends,) * (ways - 1)


def put_block(j, total, outs):
    size = total.shape[0]
    if len(outs) == 1:
        outs[0][pl.ds(j * size, size), :] = total.astype(jnp.bfloat16)
    elif j % len(outs) == 0:
        outs[0][j // len(outs)] = total
    else:
        at = pl.ds(j // len(outs) * size, size)
        outs[j % len(outs)][at, :] = total.astype(jnp.bfloat16)


def put_weight(weight, outs):
    tile = in_three(weight)
    for sent in outs if len(outs) == 1 else outs[1:]:
        sent[pl.ds(sent.shape[0] - TAIL, TAIL), :] = tile


def weight_of(block):
    return jnp.sum(block[pl.ds(block.shape[0] - TAIL, TAIL), :].astype(jnp.float32))


def chip_sum_kernel(pixels, size, keep, received, norm, *outs):
    me = lax.axis_index("row")
    for j in range(keep.shape[0] // size):
        at = pl.ds(pl.multiple_of((j ^ me) * size, size), size)
        put_block(j, keep[at, :] + received[at, :].astype(jnp.float32), outs)
    put_weight(jnp.sum(norm[...]) / pixels, outs)


def chip_sum(keep, received, norm, pixels, number, ways):
    size = keep.shape[0] // number
    return small_call(
        functools.partial(chip_sum_kernel, pixels, size),
        block_shapes(number, size, ways),
        keep,
        received,
        norm,
    )


def scatter_sum_kernel(number, mine, sent, *refs):
    received, outs = refs[:number], refs[number:]
    size = mine.shape[1]
    for j in range(mine.shape[0]):
        total = mine[j]
        for block in received:
            total = total + block[pl.ds(j * size, size), :].astype(jnp.float32)
        put_block(j, total, outs)
    put_weight(sum([weight_of(block) for block in received], weight_of(sent)), outs)


def scatter_sum(mine, sent, received, ways):
    number, size, _ = mine.shape
    return small_call(
        functools.partial(scatter_sum_kernel, len(received)),
        block_shapes(number, size, ways),
        mine,
        sent,
        *received,
    )


def pair_up(terms):
    while len(terms) > 1:
        terms = [a + b for a, b in zip(terms[::2], terms[1::2])]
    return terms[0]


def exchange_sum_kernel(size, *refs):
    blocks, chunks = refs[:-1], refs[-1]
    for j in range((chunks.shape[0] - TAIL) // size):
        terms = [
            block[pl.ds((j ^ i) * size, size), :].astype(jnp.float32)
            for i, block in enumerate(blocks)
        ]
        chunks[pl.ds(j * size, size), :] = pair_up(terms).astype(jnp.bfloat16)
    put_weight(pair_up([weight_of(block) for block in blocks]), (chunks,))


def exchange_sum(blocks, size):
    return small_call(
        functools.partial(exchange_sum_kernel, size),
        jax.ShapeDtypeStruct(blocks[0].shape, jnp.bfloat16),
        *blocks,
    )


def copy_chunks(blocks, joined):
    at = 0
    for block in blocks:
        rows = block.shape[0] - TAIL
        joined[pl.ds(at, rows), :] = block[pl.ds(0, rows), :]
        at += rows
    joined[pl.ds(at, TAIL), :] = blocks[0][pl.ds(blocks[0].shape[0] - TAIL, TAIL), :]


def join_kernel(*refs):
    copy_chunks(refs[:-1], refs[-1])


def join(blocks):
    rows = sum(block.shape[0] - TAIL for block in blocks) + TAIL
    return small_call(join_kernel, jax.ShapeDtypeStruct((rows, LANES), blocks[0].dtype), *blocks)


def swap_rows(block, step):
    number = lax.axis_size("row")
    return lax.ppermute(block, "row", [(i, i ^ step) for i in range(number)])


def row_digits():
    number = lax.axis_size("row")
    if number & (number - 1) or number < 2:
        raise ValueError("row size")
    bits = number.bit_length() - 1
    return [(shift, 1 << min(2, bits - shift)) for shift in range(0, bits, 2)]


def probe_update_kernel(size, digits, *refs):
    *blocks, probe, token, new_probe, mine, other, updated, sems = refs
    copy_chunks(blocks[: len(blocks) // 2], mine)
    copy_chunks(blocks[len(blocks) // 2 :], other)
    _, win, modes, _ = updated.shape
    number = mine.shape[0] // size
    me = lax.axis_index("row")
    piece = min(size, CHUNK)
    on_left = lax.axis_index("col") == 0
    tail = pl.ds(number * size, TAIL)
    tails = mine[tail, :].astype(jnp.float32) + other[tail, :].astype(jnp.float32)
    factor = 4.0 / jnp.full((piece, LANES), jnp.sum(tails), jnp.float32)
    half = modes // 2

    def place(chunk):
        j = chunk ^ me
        at, span = 0, 1
        for shift, ways in reversed(digits):
            at = at + ((j >> shift) & (ways - 1)) * span
            span *= ways
        return at * size

    def update(part, b, m, r):
        block = ((m * 2 + part) * (win // LANES) + b) * win
        chunk, offset = divmod(block + r, size)
        at = pl.ds(pl.multiple_of(place(chunk) + offset, piece), piece)
        here = mine[at, :].astype(jnp.float32)
        there = other[at, :].astype(jnp.float32)
        low = jnp.where(on_left, here, there)
        high = jnp.where(on_left, there, here)
        for k, total in ((m, low), (half + m, high)):
            col = k * win + b * LANES
            old = probe[part, r : r + piece, col : col + LANES]
            updated[part, r : r + piece, k, b * LANES : (b + 1) * LANES] = old - factor * total

    stretch = win // 4
    copies = []
    for part in range(2):
        for start in range(0, win, stretch):
            for r in range(start, start + stretch, piece):
                for m in range(half):
                    for b in range(win // LANES):
                        update(part, b, m, r)
            at = (part, pl.ds(start, stretch))
            copies.append(
                pltpu.make_async_copy(updated.at[at], new_probe.at[at], sems.at[len(copies)])
            )
            copies[-1].start()
    for copy in copies:
        copy.wait()


def probe_update(mine, other, probe, token, shape, size, digits):
    vmem = pl.BlockSpec(memory_space=pltpu.VMEM)
    rows = sum(block.shape[0] - TAIL for block in mine) + TAIL
    operands = (*mine, *other, probe, token)
    return pl.pallas_call(
        functools.partial(probe_update_kernel, size, digits),
        out_shape=jax.ShapeDtypeStruct(shape, jnp.float32),
        in_specs=[vmem] * len(operands),
        out_specs=pl.BlockSpec(memory_space=pl.ANY),
        scratch_shapes=[
            pltpu.VMEM((rows, LANES), jnp.bfloat16),
            pltpu.VMEM((rows, LANES), jnp.bfloat16),
            pltpu.VMEM(shape, jnp.float32),
            pltpu.SemaphoreType.DMA((8,)),
        ],
        compiler_params=pltpu.CompilerParams(vmem_limit_bytes=8 * MIB),
    )(*operands)


def low_sum_kernel(first, low_grad, from_left, token, low_sum):
    win = from_left.shape[2]
    rows = from_left.shape[1] - low_grad.shape[1]
    for part in range(2):
        for r in range(0, low_sum.shape[1], CHUNK):
            at, of = slice(r, r + CHUNK), slice(first + r, first + r + CHUNK)
            arrived = from_left[part, rows + first + r : rows + first + r + CHUNK, :]
            total = low_grad[part, of, :win] + arrived.astype(jnp.float32)
            low_sum[part, at, :win] = total.astype(jnp.bfloat16)
            low_sum[part, at, win:] = low_grad[part, of, win:].astype(jnp.bfloat16)


def low_sum_of(first, count, low_grad, from_left, token):
    return small_call(
        functools.partial(low_sum_kernel, first),
        jax.ShapeDtypeStruct((2, count, low_grad.shape[2]), jnp.bfloat16),
        low_grad,
        from_left,
        token,
        weight=LOW_WEIGHT,
    )


def object_update_kernel(old, own_grad, from_left, above_first, above_last, new_object, token):
    token[...] = jnp.zeros_like(token)
    win, split = from_left.shape[2], above_first.shape[1]
    depth = split + above_last.shape[1]
    for part in range(2):
        for r in range(0, old.shape[1], CHUNK):
            at = slice(r, r + CHUNK)
            total = own_grad[part, at, :]
            if r < split:
                total = total + above_first[part, at, :].astype(jnp.float32)
            elif r < depth:
                total = total + above_last[part, r - split : r - split + CHUNK, :].astype(jnp.float32)
            updated = old[part, at, :].astype(jnp.float32) - total
            arrived = from_left[part, at, :].astype(jnp.float32)
            new_object[part, at, :win] = updated[:, :win] - arrived
            new_object[part, at, win:] = updated[:, win:]


def object_update(old, own_grad, from_left, above_first, above_last):
    return small_call(
        object_update_kernel,
        (
            jax.ShapeDtypeStruct(old.shape, jnp.float32),
            jax.ShapeDtypeStruct((8, LANES), jnp.float32),
        ),
        old,
        own_grad,
        from_left,
        above_first,
        above_last,
    )


def swap_cores(block):
    return lax.ppermute(block, "col", [(0, 1), (1, 0)])


def body(object_field, probe_modes, positions, counts, intensities):
    win = probe_modes.shape[1]
    modes = probe_modes.shape[2]
    number = lax.axis_size("row")
    below = from_behind(object_field[:, :win, :], "row", -1)
    right_part, tables, measured, probe, power = prepare(
        object_field, probe_modes.reshape(2, win, modes * win), intensities[0, 0]
    )
    right = from_behind(right_part, "col", -1)
    corner = from_behind(first_columns(below, right), "col", -1)
    own_grad, low_grad, right_grad, keep, send, norm = position_gradients(
        positions[0, 0].T,
        counts.reshape(-1),
        power.reshape(1),
        object_field,
        below,
        right,
        corner,
        probe,
        measured,
        tables,
    )
    half_rows = keep.size // LANES
    received = swap_cores(send.reshape(half_rows, LANES))
    from_left = from_behind(right_grad, "col", 1)
    digits = row_digits()
    size = half_rows // number
    ways = [digit[1] for digit in digits[:-1]] + [0]
    outs = chip_sum(keep.reshape(half_rows, LANES), received, norm, win * win, number, ways[0])
    for place, (shift, _) in enumerate(digits[:-1]):
        mine, *sends = outs
        received = [swap_rows(block, (i + 1) << shift) for i, block in enumerate(sends)]
        outs = scatter_sum(mine, sends[0], received, ways[place + 1])
    split = SPLIT * win // 8
    low_first = low_sum_of(0, split, low_grad, from_left, outs[0])
    above_first = from_behind(low_first, "row", 1)
    shift, count = digits[-1]
    partners = [swap_rows(outs[0], i << shift) for i in range(1, count)]
    gathered = exchange_sum(list(outs) + partners, size)
    low_last = low_sum_of(split, win - split, low_grad, from_left, gathered)
    above_last = from_behind(low_last, "row", 1)
    mine = [gathered]
    for shift, count in digits[-2::-1]:
        gathered = mine[0] if len(mine) == 1 else join(mine)
        mine = [gathered] + [swap_rows(gathered, i << shift) for i in range(1, count)]
    other = [swap_cores(block) for block in mine]
    new_object, token = object_update(
        object_field, own_grad, from_left, above_first, above_last
    )
    new_probe = probe_update(mine, other, probe, token, probe_modes.shape, size, digits)
    return (new_object, new_probe)


def solution(mesh):
    placed = (
        P(None, ("grp", "row"), "col"),
        P(None, None, "grp", None),
        P(("grp", "row"), "col", None, None),
        P(("grp", "row"), "col"),
        P(("grp", "row"), "col", None, None, None),
    )
    return jax.shard_map(
        body,
        mesh=mesh,
        in_specs=placed,
        out_specs=(P(None, ("grp", "row"), "col"), P(None, None, "grp", None)),
        check_vma=False,
    )
```

```python
import functools

import jax
import jax.numpy as jnp
import ml_dtypes
import numpy as np
from jax import lax
from jax.experimental import pallas as pl
from jax.experimental.pallas import tpu as pltpu
from jax.sharding import PartitionSpec as P

LANES = 128
CHUNK = 32
FINE = 16
TAIL = 16
MIB = 1 << 20
LOW_WEIGHT = 8
PIECES = (4, 4)


def from_behind(block, axis, distance):
    devices = range(lax.axis_size(axis))
    route = [(i - distance, i) for i in devices if i - distance in devices]
    return lax.ppermute(block, axis, route)


def dft_blocks(win):
    grid = np.arange(win)
    angle = 2.0 * np.pi * (grid[:, None] * grid[None, :] % win) / win
    factor = 1.0 / np.sqrt(win)
    cos_table = (np.cos(angle) * factor).astype(ml_dtypes.bfloat16)
    sin_table = (np.sin(angle) * factor).astype(ml_dtypes.bfloat16)
    blocks = []
    for parity in range(2):
        cos_part, sin_part = cos_table[parity::2, : win // 2], sin_table[parity::2, : win // 2]
        blocks.append(np.block([[cos_part, sin_part], [-sin_part, cos_part]]))
    return np.stack(blocks + [block.T for block in blocks])


def dot(left, right):
    return jnp.dot(left, right, preferred_element_type=jnp.float32)


def gradient_kernel(
    modes,
    starts,
    count,
    power,
    own,
    below,
    right,
    corner,
    probe,
    measured,
    tables,
    own_grad,
    low_grad,
    right_grad,
    keep_out,
    send_out,
    norm_out,
    field,
    grad,
    window,
    wide,
    tall,
    wave,
    probe_sum,
):
    win = probe.shape[1]
    rows, cols = own.shape[1], own.shape[2]
    half = win // 2
    fine = range(0, win, FINE)
    spread = win // LANES + 1
    col_index = lax.axis_index("col")
    row_anchor = lax.axis_index("row") * rows
    col_anchor = col_index * cols

    def put_blocks(part, row, first, values):
        for b in range(values.shape[1] // LANES):
            piece = values[:, b * LANES : (b + 1) * LANES].astype(jnp.float32)
            field[part, first + b, row : row + CHUNK, :] = piece

    grad[...] = jnp.zeros_like(grad)
    probe_sum[...] = jnp.zeros_like(probe_sum)
    norm_out[...] = jnp.zeros_like(norm_out)
    for source, row_at, col_at in (
        (own, 0, 0),
        (right, 0, cols),
        (below, rows, 0),
        (corner, rows, cols),
    ):
        for part in range(2):
            for r in range(0, source.shape[1], CHUNK):
                put_blocks(part, row_at + r, col_at // LANES, source[part, r : r + CHUNK, :])
    lane = lax.broadcasted_iota(jnp.int32, (FINE, LANES), 1)

    def one_position(slot, carry):
        y, x = starts[0, slot] - row_anchor, starts[1, slot] - col_anchor
        base = x // LANES
        shift = x - base * LANES
        back_shift = (LANES - shift) % LANES
        keep = lane < LANES - shift
        for r in range(0, half, FINE):
            objs = []
            for start in (r, r + half):
                at = pl.ds(start, FINE)
                obj = []
                for part in range(2):
                    turned = [
                        pltpu.roll(field[part, base + b, pl.ds(y + start, FINE), :], back_shift, 1)
                        for b in range(spread)
                    ]
                    piece = jnp.concatenate(
                        [jnp.where(keep, a, b) for a, b in zip(turned[:-1], turned[1:])], axis=1
                    )
                    window[part, at, :] = piece
                    obj.append(piece)
                squares = obj[0] * obj[0] + obj[1] * obj[1]
                norm_out[...] += jnp.sum(squares.reshape(FINE // 8, 8, win), axis=0)
                objs.append(obj)
            for k in range(modes):
                cs = pl.ds(k * win, win)
                exits = []
                for start, (o_re, o_im) in zip((r, r + half), objs):
                    p_re, p_im = probe[0, pl.ds(start, FINE), cs], probe[1, pl.ds(start, FINE), cs]
                    exits.append((p_re * o_re - p_im * o_im, p_re * o_im + p_im * o_re))
                for part in range(2):
                    low, high = exits[0][part], exits[1][part]
                    at = pl.ds(part * half + r, FINE)
                    wide[k, 0, at, :] = (low + high).astype(jnp.bfloat16)
                    wide[k, 1, at, :] = (low - high).astype(jnp.bfloat16)

        for k in range(modes):
            for parity in range(2):
                out = dot(tables[parity], wide[k, parity])
                at = pl.ds(k * win + parity * half, half)
                for part in range(2):
                    low = out[part * half : (part + 1) * half, :half]
                    high = out[part * half : (part + 1) * half, half:]
                    to = pl.ds(part * half, half)
                    tall[0, at, to] = (low + high).astype(jnp.bfloat16)
                    tall[1, at, to] = (low - high).astype(jnp.bfloat16)
        for parity in range(2):
            wave[parity] = dot(tall[parity], tables[2 + parity])

        for r in fine:
            for parity in range(2):
                waves = []
                total = jnp.zeros((FINE, half), jnp.float32)
                for k in range(modes):
                    ka = pl.ds(k * win + r, FINE)
                    waves.append((wave[parity, ka, :half], wave[parity, ka, half:]))
                    total = total + (waves[k][0] * waves[k][0] + waves[k][1] * waves[k][1])
                gs = pl.ds(parity * half, half)
                amp = measured[slot, pl.ds(r, FINE), gs]
                ratio = 1.0 - amp * lax.rsqrt(jnp.maximum(total, 1.0))
                for k in range(modes):
                    for part in range(2):
                        at = pl.ds(part * half + r % half, FINE)
                        wide[k, r // half, at, gs] = (waves[k][part] * ratio).astype(jnp.bfloat16)

        for k in range(modes):
            even = dot(tables[2], wide[k, 0])
            odd = dot(tables[3], wide[k, 1])
            for place, out in enumerate((even + odd, even - odd)):
                at = pl.ds(k * win + place * half, half)
                for part in range(2):
                    for parity in range(2):
                        tall[parity, at, part * half : (part + 1) * half] = out[
                            part * half : (part + 1) * half, parity * half : (parity + 1) * half
                        ].astype(jnp.bfloat16)
        for parity in range(2):
            wave[parity] = dot(tall[parity], tables[parity])

        keep_high = lane >= shift
        for r in fine:
            at = pl.ds(r, FINE)
            sums = [[jnp.zeros((FINE, LANES), jnp.float32) for _ in range(2)] for _ in range(2)]
            for b in range(2):
                bs = pl.ds(b * half, half)
                o_re, o_im = window[0, at, bs], window[1, at, bs]
                for k in range(modes):
                    cs = pl.ds(k * win + b * half, half)
                    ka = pl.ds(k * win + r, FINE)
                    even, odd = wave[0, ka, :], wave[1, ka, :]
                    d = even + odd if b == 0 else even - odd
                    d_re, d_im = d[:, :half], d[:, half:]
                    p_re, p_im = probe[0, at, cs], probe[1, at, cs]
                    sums[0][b] = sums[0][b] + (p_re * d_re + p_im * d_im)
                    sums[1][b] = sums[1][b] + (p_re * d_im - p_im * d_re)
                    probe_sum[k, 0, b, at, :] += o_re * d_re + o_im * d_im
                    probe_sum[k, 1, b, at, :] += o_re * d_im - o_im * d_re
            for part in range(2):
                turned = [pltpu.roll(piece, shift, 1) for piece in sums[part]]
                turned = [jnp.zeros_like(turned[0])] + turned + [jnp.zeros_like(turned[0])]
                for b in range(spread):
                    grad[part, base + b, pl.ds(y + r, FINE), :] += jnp.where(
                        keep_high, turned[b + 1], turned[b]
                    )
        return carry

    lax.fori_loop(0, count[0], one_position, 0)
    for m in range(modes // 2):
        keep_mode = col_index * (modes // 2) + m
        send_mode = (1 - col_index) * (modes // 2) + m
        keep_out[m] = probe_sum[keep_mode]
        send_out[m] = probe_sum[send_mode].astype(jnp.bfloat16)
    scale = 1.0 / jnp.full((8, LANES), power[0], jnp.float32)
    scale = jnp.concatenate([scale] * (CHUNK // 8), axis=0)

    def take_blocks(part, at, first, number):
        return jnp.concatenate(
            [grad[part, first + b, at, :] * scale for b in range(number)], axis=1
        )

    for part in range(2):
        for r in range(0, rows + win, CHUNK):
            at = pl.ds(r, CHUNK)
            piece = take_blocks(part, at, cols // LANES, win // LANES)
            right_grad[part, at, :] = piece.astype(jnp.bfloat16)
        for r in range(0, rows, CHUNK):
            at = pl.ds(r, CHUNK)
            own_grad[part, at, :] = take_blocks(part, at, 0, cols // LANES)
        for r in range(0, win, CHUNK):
            at, of = pl.ds(r, CHUNK), pl.ds(rows + r, CHUNK)
            low_grad[part, at, :] = take_blocks(part, of, 0, cols // LANES)


def position_gradients(starts, count, power, own, below, right, corner, probe, measured, tables):
    win, modes = probe.shape[1], probe.shape[2] // probe.shape[1]
    rows, cols = own.shape[1:]
    f32, bf16 = jnp.float32, jnp.bfloat16
    smem = pl.BlockSpec(memory_space=pltpu.SMEM)
    vmem = pl.BlockSpec(memory_space=pltpu.VMEM)
    if win != 2 * LANES:
        raise ValueError("window size")
    slots = measured.shape[0]
    flops = 16 * slots * modes * win**3
    half_blocks = (modes // 2, 2, win // LANES, win, LANES)
    return pl.pallas_call(
        functools.partial(gradient_kernel, modes),
        out_shape=(
            jax.ShapeDtypeStruct((2, rows, cols), f32),
            jax.ShapeDtypeStruct((2, win, cols), f32),
            jax.ShapeDtypeStruct((2, rows + win, win), bf16),
            jax.ShapeDtypeStruct(half_blocks, f32),
            jax.ShapeDtypeStruct(half_blocks, bf16),
            jax.ShapeDtypeStruct((8, win), f32),
        ),
        in_specs=[smem] * 3 + [vmem] * 7,
        out_specs=(vmem,) * 6,
        scratch_shapes=[
            pltpu.VMEM((2, (cols + win) // LANES, rows + win, LANES), f32),
            pltpu.VMEM((2, (cols + win) // LANES, rows + win, LANES), f32),
            pltpu.VMEM((2, win, win), f32),
            pltpu.VMEM((modes, 2, win, win), bf16),
            pltpu.VMEM((2, modes * win, win), bf16),
            pltpu.VMEM((2, modes * win, win), f32),
            pltpu.VMEM((modes, 2, win // LANES, win, LANES), f32),
        ],
        compiler_params=pltpu.CompilerParams(vmem_limit_bytes=26 * MIB),
        cost_estimate=pl.CostEstimate(flops=flops, bytes_accessed=12 << 20, transcendentals=0),
    )(starts, count, power, own, below, right, corner, probe, measured, tables)


def in_three(value):
    full = jnp.full((TAIL, LANES), value, jnp.float32)
    high = full.astype(jnp.bfloat16).astype(jnp.float32)
    mid = (full - high).astype(jnp.bfloat16).astype(jnp.float32)
    low = full - high - mid
    row = lax.broadcasted_iota(jnp.int32, (TAIL, LANES), 0)
    lane = lax.broadcasted_iota(jnp.int32, (TAIL, LANES), 1)
    tile = jnp.where(row == 0, high, jnp.where(row == 1, mid, jnp.where(row == 2, low, 0.0)))
    return jnp.where(lane == 0, tile, 0.0).astype(jnp.bfloat16)


def small_call(kernel, shapes, *operands, weight=1):
    return pl.pallas_call(
        kernel,
        out_shape=shapes,
        compiler_params=pltpu.CompilerParams(vmem_limit_bytes=4 * MIB),
        cost_estimate=pl.CostEstimate(flops=0, bytes_accessed=weight * MIB, transcendentals=0),
    )(*operands)


def first_columns_kernel(block, token, first):
    first[...] = block[:, :, : first.shape[2]]


def first_columns(block, token):
    return small_call(
        first_columns_kernel, jax.ShapeDtypeStruct(token.shape, block.dtype), block, token
    )


def prepare_kernel(own, probe, intens, blocks, right_part, tables, measured, wide_probe, power):
    right_part[...] = own[:, :, : right_part.shape[2]]
    tables[...] = blocks[...]
    count, size, _ = intens.shape
    row = lax.broadcasted_iota(jnp.int32, (size, size), 0)
    col = lax.broadcasted_iota(jnp.int32, (size, size), 1)
    to_even_first = (col == jnp.where(row < size // 2, 2 * row, 2 * row - size + 1)).astype(
        jnp.float32
    )
    from_left = to_even_first.astype(jnp.bfloat16)
    from_right = (row == jnp.where(col < size // 2, 2 * col, 2 * col - size + 1)).astype(
        jnp.float32
    )
    from_right = from_right.astype(jnp.bfloat16)
    for slot in range(count):
        turned = dot(from_left, intens[slot]).astype(jnp.bfloat16)
        measured[slot] = jnp.sqrt(dot(turned, from_right))
    win = right_part.shape[2]
    modes = probe.shape[2] // win
    largest = jnp.zeros((8, win), jnp.float32)
    for r in range(0, probe.shape[1], CHUNK):
        at = slice(r, r + CHUNK)
        total = jnp.zeros((CHUNK, win), jnp.float32)
        for k in range(modes):
            for part in range(2):
                p = probe[part, at, k * win : (k + 1) * win].astype(jnp.float32)
                wide_probe[part, at, k * win : (k + 1) * win] = p
                total = total + p * p
        largest = jnp.maximum(largest, jnp.max(total.reshape(CHUNK // 8, 8, win), axis=0))
    power[0, 0] = jnp.max(largest)


def prepare(own, probe, intens):
    win = probe.shape[1]
    blocks = dft_blocks(win)
    vmem = pl.BlockSpec(memory_space=pltpu.VMEM)
    return pl.pallas_call(
        prepare_kernel,
        out_shape=(
            jax.ShapeDtypeStruct(own.shape[:2] + (win,), own.dtype),
            jax.ShapeDtypeStruct(blocks.shape, jnp.bfloat16),
            jax.ShapeDtypeStruct(intens.shape, jnp.float32),
            jax.ShapeDtypeStruct(probe.shape, jnp.float32),
            jax.ShapeDtypeStruct((1, 1), jnp.float32),
        ),
        out_specs=(vmem, vmem, vmem, vmem, pl.BlockSpec(memory_space=pltpu.SMEM)),
        compiler_params=pltpu.CompilerParams(vmem_limit_bytes=8 * MIB),
    )(own, probe, intens, blocks)


def block_shapes(number, size, ways):
    if not ways:
        return (jax.ShapeDtypeStruct((number * size + TAIL, LANES), jnp.bfloat16),)
    sends = jax.ShapeDtypeStruct((number // ways * size + TAIL, LANES), jnp.bfloat16)
    return (jax.ShapeDtypeStruct((number // ways, size, LANES), jnp.float32),) + (sends,) * (ways - 1)


def put_block(j, total, outs):
    size = total.shape[0]
    if len(outs) == 1:
        outs[0][pl.ds(j * size, size), :] = total.astype(jnp.bfloat16)
    elif j % len(outs) == 0:
        outs[0][j // len(outs)] = total
    else:
        at = pl.ds(j // len(outs) * size, size)
        outs[j % len(outs)][at, :] = total.astype(jnp.bfloat16)


def put_weight(weight, outs):
    tile = in_three(weight)
    for sent in outs if len(outs) == 1 else outs[1:]:
        sent[pl.ds(sent.shape[0] - TAIL, TAIL), :] = tile


def weight_of(block):
    return jnp.sum(block[pl.ds(block.shape[0] - TAIL, TAIL), :].astype(jnp.float32))


def chip_sum_kernel(pixels, size, keep, received, norm, *outs):
    me = lax.axis_index("row")
    for j in range(keep.shape[0] // size):
        at = pl.ds(pl.multiple_of((j ^ me) * size, size), size)
        put_block(j, keep[at, :] + received[at, :].astype(jnp.float32), outs)
    put_weight(jnp.sum(norm[...]) / pixels, outs)


def chip_sum(keep, received, norm, pixels, number, ways):
    size = keep.shape[0] // number
    return small_call(
        functools.partial(chip_sum_kernel, pixels, size),
        block_shapes(number, size, ways),
        keep,
        received,
        norm,
    )


def scatter_sum_kernel(number, mine, sent, *refs):
    received, outs = refs[:number], refs[number:]
    size = mine.shape[1]
    for j in range(mine.shape[0]):
        total = mine[j]
        for block in received:
            total = total + block[pl.ds(j * size, size), :].astype(jnp.float32)
        put_block(j, total, outs)
    put_weight(sum([weight_of(block) for block in received], weight_of(sent)), outs)


def scatter_sum(mine, sent, received, ways):
    number, size, _ = mine.shape
    return small_call(
        functools.partial(scatter_sum_kernel, len(received)),
        block_shapes(number, size, ways),
        mine,
        sent,
        *received,
    )


def pair_up(terms):
    while len(terms) > 1:
        terms = [a + b for a, b in zip(terms[::2], terms[1::2])]
    return terms[0]


def exchange_sum_kernel(size, *refs):
    *blocks, _, chunks = refs
    for j in range((chunks.shape[0] - TAIL) // size):
        terms = [
            block[pl.ds((j ^ i) * size, size), :].astype(jnp.float32)
            for i, block in enumerate(blocks)
        ]
        chunks[pl.ds(j * size, size), :] = pair_up(terms).astype(jnp.bfloat16)
    put_weight(pair_up([weight_of(block) for block in blocks]), (chunks,))


def exchange_sum(blocks, token, size):
    return small_call(
        functools.partial(exchange_sum_kernel, size),
        jax.ShapeDtypeStruct(blocks[0].shape, jnp.bfloat16),
        *blocks,
        token,
    )


def copy_chunks(blocks, joined):
    at = 0
    for block in blocks:
        rows = block.shape[0] - TAIL
        joined[pl.ds(at, rows), :] = block[pl.ds(0, rows), :]
        at += rows
    joined[pl.ds(at, TAIL), :] = blocks[0][pl.ds(blocks[0].shape[0] - TAIL, TAIL), :]


def join_kernel(*refs):
    copy_chunks(refs[:-1], refs[-1])


def join(blocks):
    rows = sum(block.shape[0] - TAIL for block in blocks) + TAIL
    return small_call(join_kernel, jax.ShapeDtypeStruct((rows, LANES), blocks[0].dtype), *blocks)


def swap_rows(block, step):
    number = lax.axis_size("row")
    return lax.ppermute(block, "row", [(i, i ^ step) for i in range(number)])


def row_digits():
    number = lax.axis_size("row")
    if number & (number - 1) or number < 2:
        raise ValueError("row size")
    bits = number.bit_length() - 1
    return [(shift, 1 << min(2, bits - shift)) for shift in range(0, bits, 2)]


def probe_update_kernel(size, digits, *refs):
    *blocks, probe, token, new_probe, mine, other, updated, sems = refs
    copy_chunks(blocks[: len(blocks) // 2], mine)
    copy_chunks(blocks[len(blocks) // 2 :], other)
    _, win, modes, _ = updated.shape
    number = mine.shape[0] // size
    me = lax.axis_index("row")
    piece = min(size, CHUNK)
    on_left = lax.axis_index("col") == 0
    tail = pl.ds(number * size, TAIL)
    tails = mine[tail, :].astype(jnp.float32) + other[tail, :].astype(jnp.float32)
    factor = 4.0 / jnp.full((piece, LANES), jnp.sum(tails), jnp.float32)
    half = modes // 2

    def place(chunk):
        j = chunk ^ me
        at, span = 0, 1
        for shift, ways in reversed(digits):
            at = at + ((j >> shift) & (ways - 1)) * span
            span *= ways
        return at * size

    def update(part, b, m, r):
        block = ((m * 2 + part) * (win // LANES) + b) * win
        chunk, offset = divmod(block + r, size)
        at = pl.ds(pl.multiple_of(place(chunk) + offset, piece), piece)
        here = mine[at, :].astype(jnp.float32)
        there = other[at, :].astype(jnp.float32)
        low = jnp.where(on_left, here, there)
        high = jnp.where(on_left, there, here)
        for k, total in ((m, low), (half + m, high)):
            col = k * win + b * LANES
            old = probe[part, r : r + piece, col : col + LANES]
            updated[part, r : r + piece, k, b * LANES : (b + 1) * LANES] = old - factor * total

    stretch = win // 4
    copies = []
    for part in range(2):
        for start in range(0, win, stretch):
            for r in range(start, start + stretch, piece):
                for m in range(half):
                    for b in range(win // LANES):
                        update(part, b, m, r)
            at = (part, pl.ds(start, stretch))
            copies.append(
                pltpu.make_async_copy(updated.at[at], new_probe.at[at], sems.at[len(copies)])
            )
            copies[-1].start()
    for copy in copies:
        copy.wait()


def probe_update(mine, other, probe, token, shape, size, digits):
    vmem = pl.BlockSpec(memory_space=pltpu.VMEM)
    rows = sum(block.shape[0] - TAIL for block in mine) + TAIL
    operands = (*mine, *other, probe, token)
    return pl.pallas_call(
        functools.partial(probe_update_kernel, size, digits),
        out_shape=jax.ShapeDtypeStruct(shape, jnp.float32),
        in_specs=[vmem] * len(operands),
        out_specs=pl.BlockSpec(memory_space=pl.ANY),
        scratch_shapes=[
            pltpu.VMEM((rows, LANES), jnp.bfloat16),
            pltpu.VMEM((rows, LANES), jnp.bfloat16),
            pltpu.VMEM(shape, jnp.float32),
            pltpu.SemaphoreType.DMA((8,)),
        ],
        compiler_params=pltpu.CompilerParams(vmem_limit_bytes=8 * MIB),
    )(*operands)


def low_sum_kernel(first, low_grad, from_left, token, low_sum):
    win = from_left.shape[2]
    rows = from_left.shape[1] - low_grad.shape[1]
    for part in range(2):
        for r in range(0, low_sum.shape[1], CHUNK):
            at, of = slice(r, r + CHUNK), slice(first + r, first + r + CHUNK)
            arrived = from_left[part, rows + first + r : rows + first + r + CHUNK, :]
            total = low_grad[part, of, :win] + arrived.astype(jnp.float32)
            low_sum[part, at, :win] = total.astype(jnp.bfloat16)
            low_sum[part, at, win:] = low_grad[part, of, win:].astype(jnp.bfloat16)


def low_sum_of(first, count, low_grad, from_left, token):
    return small_call(
        functools.partial(low_sum_kernel, first),
        jax.ShapeDtypeStruct((2, count, low_grad.shape[2]), jnp.bfloat16),
        low_grad,
        from_left,
        token,
        weight=LOW_WEIGHT,
    )


def arrival_kernel(block, token):
    token[...] = jnp.zeros_like(token)


def arrival(block):
    return small_call(arrival_kernel, jax.ShapeDtypeStruct((8, LANES), jnp.float32), block)


def object_update_kernel(old, own_grad, from_left, *refs):
    *above, new_object, token = refs
    token[...] = jnp.zeros_like(token)
    win = from_left.shape[2]
    starts = [sum(piece.shape[1] for piece in above[:i]) for i in range(len(above))]
    for part in range(2):
        for r in range(0, old.shape[1], CHUNK):
            at = slice(r, r + CHUNK)
            total = own_grad[part, at, :]
            for start, piece in zip(starts, above):
                if start <= r < start + piece.shape[1]:
                    arrived = piece[part, r - start : r - start + CHUNK, :]
                    total = total + arrived.astype(jnp.float32)
            updated = old[part, at, :].astype(jnp.float32) - total
            arrived = from_left[part, at, :].astype(jnp.float32)
            new_object[part, at, :win] = updated[:, :win] - arrived
            new_object[part, at, win:] = updated[:, win:]


def object_update(old, own_grad, from_left, above):
    return small_call(
        object_update_kernel,
        (
            jax.ShapeDtypeStruct(old.shape, jnp.float32),
            jax.ShapeDtypeStruct((8, LANES), jnp.float32),
        ),
        old,
        own_grad,
        from_left,
        *above,
    )


def swap_cores(block):
    return lax.ppermute(block, "col", [(0, 1), (1, 0)])


def body(object_field, probe_modes, positions, counts, intensities):
    win = probe_modes.shape[1]
    modes = probe_modes.shape[2]
    number = lax.axis_size("row")
    below = from_behind(object_field[:, :win, :], "row", -1)
    right_part, tables, measured, probe, power = prepare(
        object_field, probe_modes.reshape(2, win, modes * win), intensities[0, 0]
    )
    right = from_behind(right_part, "col", -1)
    corner = from_behind(first_columns(below, right), "col", -1)
    own_grad, low_grad, right_grad, keep, send, norm = position_gradients(
        positions[0, 0].T,
        counts.reshape(-1),
        power.reshape(1),
        object_field,
        below,
        right,
        corner,
        probe,
        measured,
        tables,
    )
    half_rows = keep.size // LANES
    received = swap_cores(send.reshape(half_rows, LANES))
    from_left = from_behind(right_grad, "col", 1)
    digits = row_digits()
    size = half_rows // number
    ways = [digit[1] for digit in digits[:-1]] + [0]
    outs = chip_sum(keep.reshape(half_rows, LANES), received, norm, win * win, number, ways[0])
    above = []

    def send_halo(token):
        first = sum(piece.shape[1] for piece in above)
        count = PIECES[len(above)] * win // sum(PIECES)
        above.append(from_behind(low_sum_of(first, count, low_grad, from_left, token), "row", 1))

    send_halo(outs[0])
    for place, (shift, _) in enumerate(digits[:-1]):
        mine, *sends = outs
        received = [swap_rows(block, (i + 1) << shift) for i, block in enumerate(sends)]
        outs = scatter_sum(mine, sends[0], received, ways[place + 1])
    shift, count = digits[-1]
    partners = [swap_rows(outs[0], i << shift) for i in range(1, count)]
    gathered = exchange_sum(list(outs) + partners, arrival(above[0]), size)
    send_halo(gathered)
    mine = [gathered]
    for shift, count in digits[-2::-1]:
        gathered = mine[0] if len(mine) == 1 else join(mine)
        mine = [gathered] + [swap_rows(gathered, i << shift) for i in range(1, count)]
    other = [swap_cores(block) for block in mine]
    new_object, token = object_update(object_field, own_grad, from_left, above)
    new_probe = probe_update(mine, other, probe, token, probe_modes.shape, size, digits)
    return (new_object, new_probe)


def solution(mesh):
    placed = (
        P(None, ("grp", "row"), "col"),
        P(None, None, "grp", None),
        P(("grp", "row"), "col", None, None),
        P(("grp", "row"), "col"),
        P(("grp", "row"), "col", None, None, None),
    )
    return jax.shard_map(
        body,
        mesh=mesh,
        in_specs=placed,
        out_specs=(P(None, ("grp", "row"), "col"), P(None, None, "grp", None)),
        check_vma=False,
    )
```

```python
import functools

import jax
import jax.numpy as jnp
import ml_dtypes
import numpy as np
from jax import lax
from jax.experimental import pallas as pl
from jax.experimental.pallas import tpu as pltpu
from jax.sharding import PartitionSpec as P

LANES = 128
CHUNK = 32
FINE = 16
TAIL = 16
MIB = 1 << 20
LOW_WEIGHT = 8
SPLIT = 4


def from_behind(block, axis, distance):
    devices = range(lax.axis_size(axis))
    route = [(i - distance, i) for i in devices if i - distance in devices]
    return lax.ppermute(block, axis, route)


def from_next_row(block, col):
    rows, cols = lax.axis_size("row"), lax.axis_size("col")
    route = [((r + 1) * cols + col, r * cols + col) for r in range(rows - 1)]
    return lax.ppermute(block, ("row", "col"), route)


def dft_blocks(win):
    grid = np.arange(win)
    angle = 2.0 * np.pi * (grid[:, None] * grid[None, :] % win) / win
    factor = 1.0 / np.sqrt(win)
    cos_table = (np.cos(angle) * factor).astype(ml_dtypes.bfloat16)
    sin_table = (np.sin(angle) * factor).astype(ml_dtypes.bfloat16)
    blocks = []
    for parity in range(2):
        cos_part, sin_part = cos_table[parity::2, : win // 2], sin_table[parity::2, : win // 2]
        blocks.append(np.block([[cos_part, sin_part], [-sin_part, cos_part]]))
    return np.stack(blocks + [block.T for block in blocks])


def dot(left, right):
    return jnp.dot(left, right, preferred_element_type=jnp.float32)


def gradient_kernel(
    modes,
    starts,
    count,
    power,
    own,
    below_left,
    below_right,
    right,
    corner,
    probe,
    measured,
    tables,
    own_grad,
    low_grad,
    right_grad,
    keep_out,
    send_out,
    norm_out,
    field,
    grad,
    window,
    wide,
    tall,
    wave,
    probe_sum,
):
    win = probe.shape[1]
    rows, cols = own.shape[1], own.shape[2]
    half = win // 2
    fine = range(0, win, FINE)
    spread = win // LANES + 1
    col_index = lax.axis_index("col")
    row_anchor = lax.axis_index("row") * rows
    col_anchor = col_index * cols

    def put_blocks(part, row, first, values):
        for b in range(values.shape[1] // LANES):
            field[part, first + b, row : row + CHUNK, :] = values[:, b * LANES : (b + 1) * LANES]

    grad[...] = jnp.zeros_like(grad)
    probe_sum[...] = jnp.zeros_like(probe_sum)
    norm_out[...] = jnp.zeros_like(norm_out)
    for row_at, col_at, *sources in (
        (0, 0, own),
        (0, cols, right),
        (rows, 0, below_left, below_right),
        (rows, cols, corner),
    ):
        for part in range(2):
            for r in range(0, sources[0].shape[1], CHUNK):
                pieces = [source[part, r : r + CHUNK, :].astype(jnp.float32) for source in sources]
                put_blocks(part, row_at + r, col_at // LANES, sum(pieces[1:], pieces[0]))
    lane = lax.broadcasted_iota(jnp.int32, (FINE, LANES), 1)

    def one_position(slot, carry):
        y, x = starts[0, slot] - row_anchor, starts[1, slot] - col_anchor
        base = x // LANES
        shift = x - base * LANES
        back_shift = (LANES - shift) % LANES
        keep = lane < LANES - shift
        for r in range(0, half, FINE):
            objs = []
            for start in (r, r + half):
                at = pl.ds(start, FINE)
                obj = []
                for part in range(2):
                    turned = [
                        pltpu.roll(field[part, base + b, pl.ds(y + start, FINE), :], back_shift, 1)
                        for b in range(spread)
                    ]
                    piece = jnp.concatenate(
                        [jnp.where(keep, a, b) for a, b in zip(turned[:-1], turned[1:])], axis=1
                    )
                    window[part, at, :] = piece
                    obj.append(piece)
                squares = obj[0] * obj[0] + obj[1] * obj[1]
                norm_out[...] += jnp.sum(squares.reshape(FINE // 8, 8, win), axis=0)
                objs.append(obj)
            for k in range(modes):
                cs = pl.ds(k * win, win)
                exits = []
                for start, (o_re, o_im) in zip((r, r + half), objs):
                    p_re, p_im = probe[0, pl.ds(start, FINE), cs], probe[1, pl.ds(start, FINE), cs]
                    exits.append((p_re * o_re - p_im * o_im, p_re * o_im + p_im * o_re))
                for part in range(2):
                    low, high = exits[0][part], exits[1][part]
                    at = pl.ds(part * half + r, FINE)
                    wide[k, 0, at, :] = (low + high).astype(jnp.bfloat16)
                    wide[k, 1, at, :] = (low - high).astype(jnp.bfloat16)

        for k in range(modes):
            for parity in range(2):
                out = dot(tables[parity], wide[k, parity])
                at = pl.ds(k * win + parity * half, half)
                for part in range(2):
                    low = out[part * half : (part + 1) * half, :half]
                    high = out[part * half : (part + 1) * half, half:]
                    to = pl.ds(part * half, half)
                    tall[0, at, to] = (low + high).astype(jnp.bfloat16)
                    tall[1, at, to] = (low - high).astype(jnp.bfloat16)
        for parity in range(2):
            wave[parity] = dot(tall[parity], tables[2 + parity])

        for r in fine:
            for parity in range(2):
                waves = []
                total = jnp.zeros((FINE, half), jnp.float32)
                for k in range(modes):
                    ka = pl.ds(k * win + r, FINE)
                    waves.append((wave[parity, ka, :half], wave[parity, ka, half:]))
                    total = total + (waves[k][0] * waves[k][0] + waves[k][1] * waves[k][1])
                gs = pl.ds(parity * half, half)
                amp = measured[slot, pl.ds(r, FINE), gs]
                ratio = 1.0 - amp * lax.rsqrt(jnp.maximum(total, 1.0))
                for k in range(modes):
                    for part in range(2):
                        at = pl.ds(part * half + r % half, FINE)
                        wide[k, r // half, at, gs] = (waves[k][part] * ratio).astype(jnp.bfloat16)

        for k in range(modes):
            even = dot(tables[2], wide[k, 0])
            odd = dot(tables[3], wide[k, 1])
            for place, out in enumerate((even + odd, even - odd)):
                at = pl.ds(k * win + place * half, half)
                for part in range(2):
                    for parity in range(2):
                        tall[parity, at, part * half : (part + 1) * half] = out[
                            part * half : (part + 1) * half, parity * half : (parity + 1) * half
                        ].astype(jnp.bfloat16)
        for parity in range(2):
            wave[parity] = dot(tall[parity], tables[parity])

        keep_high = lane >= shift
        for r in fine:
            at = pl.ds(r, FINE)
            sums = [[jnp.zeros((FINE, LANES), jnp.float32) for _ in range(2)] for _ in range(2)]
            for b in range(2):
                bs = pl.ds(b * half, half)
                o_re, o_im = window[0, at, bs], window[1, at, bs]
                for k in range(modes):
                    cs = pl.ds(k * win + b * half, half)
                    ka = pl.ds(k * win + r, FINE)
                    even, odd = wave[0, ka, :], wave[1, ka, :]
                    d = even + odd if b == 0 else even - odd
                    d_re, d_im = d[:, :half], d[:, half:]
                    p_re, p_im = probe[0, at, cs], probe[1, at, cs]
                    sums[0][b] = sums[0][b] + (p_re * d_re + p_im * d_im)
                    sums[1][b] = sums[1][b] + (p_re * d_im - p_im * d_re)
                    probe_sum[k, 0, b, at, :] += o_re * d_re + o_im * d_im
                    probe_sum[k, 1, b, at, :] += o_re * d_im - o_im * d_re
            for part in range(2):
                turned = [pltpu.roll(piece, shift, 1) for piece in sums[part]]
                turned = [jnp.zeros_like(turned[0])] + turned + [jnp.zeros_like(turned[0])]
                for b in range(spread):
                    grad[part, base + b, pl.ds(y + r, FINE), :] += jnp.where(
                        keep_high, turned[b + 1], turned[b]
                    )
        return carry

    lax.fori_loop(0, count[0], one_position, 0)
    for m in range(modes // 2):
        keep_mode = col_index * (modes // 2) + m
        send_mode = (1 - col_index) * (modes // 2) + m
        keep_out[m] = probe_sum[keep_mode]
        send_out[m] = probe_sum[send_mode].astype(jnp.bfloat16)
    scale = 1.0 / jnp.full((8, LANES), power[0], jnp.float32)
    scale = jnp.concatenate([scale] * (CHUNK // 8), axis=0)

    def take_blocks(part, at, first, number):
        return jnp.concatenate(
            [grad[part, first + b, at, :] * scale for b in range(number)], axis=1
        )

    for part in range(2):
        for r in range(0, rows + win, CHUNK):
            at = pl.ds(r, CHUNK)
            piece = take_blocks(part, at, cols // LANES, win // LANES)
            right_grad[part, at, :] = piece.astype(jnp.bfloat16)
        for r in range(0, rows, CHUNK):
            at = pl.ds(r, CHUNK)
            own_grad[part, at, :] = take_blocks(part, at, 0, cols // LANES)
        for r in range(0, win, CHUNK):
            at, of = pl.ds(r, CHUNK), pl.ds(rows + r, CHUNK)
            low_grad[part, at, :] = take_blocks(part, of, 0, cols // LANES)


def position_gradients(starts, count, power, own, below, right, corner, probe, measured, tables):
    win, modes = probe.shape[1], probe.shape[2] // probe.shape[1]
    rows, cols = own.shape[1:]
    f32, bf16 = jnp.float32, jnp.bfloat16
    smem = pl.BlockSpec(memory_space=pltpu.SMEM)
    vmem = pl.BlockSpec(memory_space=pltpu.VMEM)
    if win != 2 * LANES:
        raise ValueError("window size")
    slots = measured.shape[0]
    flops = 16 * slots * modes * win**3
    half_blocks = (modes // 2, 2, win // LANES, win, LANES)
    return pl.pallas_call(
        functools.partial(gradient_kernel, modes),
        out_shape=(
            jax.ShapeDtypeStruct((2, rows, cols), f32),
            jax.ShapeDtypeStruct((2, win, cols), f32),
            jax.ShapeDtypeStruct((2, rows + win, win), bf16),
            jax.ShapeDtypeStruct(half_blocks, f32),
            jax.ShapeDtypeStruct(half_blocks, bf16),
            jax.ShapeDtypeStruct((8, win), f32),
        ),
        in_specs=[smem] * 3 + [vmem] * 8,
        out_specs=(vmem,) * 6,
        scratch_shapes=[
            pltpu.VMEM((2, (cols + win) // LANES, rows + win, LANES), f32),
            pltpu.VMEM((2, (cols + win) // LANES, rows + win, LANES), f32),
            pltpu.VMEM((2, win, win), f32),
            pltpu.VMEM((modes, 2, win, win), bf16),
            pltpu.VMEM((2, modes * win, win), bf16),
            pltpu.VMEM((2, modes * win, win), f32),
            pltpu.VMEM((modes, 2, win // LANES, win, LANES), f32),
        ],
        compiler_params=pltpu.CompilerParams(vmem_limit_bytes=26 * MIB),
        cost_estimate=pl.CostEstimate(flops=flops, bytes_accessed=12 << 20, transcendentals=0),
    )(starts, count, power, own, *below, right, corner, probe, measured, tables)


def in_three(value):
    full = jnp.full((TAIL, LANES), value, jnp.float32)
    high = full.astype(jnp.bfloat16).astype(jnp.float32)
    mid = (full - high).astype(jnp.bfloat16).astype(jnp.float32)
    low = full - high - mid
    row = lax.broadcasted_iota(jnp.int32, (TAIL, LANES), 0)
    lane = lax.broadcasted_iota(jnp.int32, (TAIL, LANES), 1)
    tile = jnp.where(row == 0, high, jnp.where(row == 1, mid, jnp.where(row == 2, low, 0.0)))
    return jnp.where(lane == 0, tile, 0.0).astype(jnp.bfloat16)


def small_call(kernel, shapes, *operands, weight=1):
    return pl.pallas_call(
        kernel,
        out_shape=shapes,
        compiler_params=pltpu.CompilerParams(vmem_limit_bytes=4 * MIB),
        cost_estimate=pl.CostEstimate(flops=0, bytes_accessed=weight * MIB, transcendentals=0),
    )(*operands)


def first_columns_kernel(block, token, first):
    first[...] = block[:, :, : first.shape[2]]


def first_columns(block, token):
    return small_call(
        first_columns_kernel, jax.ShapeDtypeStruct(token.shape, block.dtype), block, token
    )


def prepare_kernel(own, probe, intens, blocks, first_rows, right_part, tables, measured, wide_probe, power):
    first_rows[...] = own[:, : first_rows.shape[1], :]
    right_part[...] = own[:, :, : right_part.shape[2]]
    tables[...] = blocks[...]
    count, size, _ = intens.shape
    row = lax.broadcasted_iota(jnp.int32, (size, size), 0)
    col = lax.broadcasted_iota(jnp.int32, (size, size), 1)
    to_even_first = (col == jnp.where(row < size // 2, 2 * row, 2 * row - size + 1)).astype(
        jnp.float32
    )
    from_left = to_even_first.astype(jnp.bfloat16)
    from_right = (row == jnp.where(col < size // 2, 2 * col, 2 * col - size + 1)).astype(
        jnp.float32
    )
    from_right = from_right.astype(jnp.bfloat16)
    for slot in range(count):
        turned = dot(from_left, intens[slot]).astype(jnp.bfloat16)
        measured[slot] = jnp.sqrt(dot(turned, from_right))
    win = right_part.shape[2]
    modes = probe.shape[2] // win
    largest = jnp.zeros((8, win), jnp.float32)
    for r in range(0, probe.shape[1], CHUNK):
        at = slice(r, r + CHUNK)
        total = jnp.zeros((CHUNK, win), jnp.float32)
        for k in range(modes):
            for part in range(2):
                p = probe[part, at, k * win : (k + 1) * win].astype(jnp.float32)
                wide_probe[part, at, k * win : (k + 1) * win] = p
                total = total + p * p
        largest = jnp.maximum(largest, jnp.max(total.reshape(CHUNK // 8, 8, win), axis=0))
    power[0, 0] = jnp.max(largest)


def prepare(own, probe, intens):
    win = probe.shape[1]
    blocks = dft_blocks(win)
    vmem = pl.BlockSpec(memory_space=pltpu.VMEM)
    return pl.pallas_call(
        prepare_kernel,
        out_shape=(
            jax.ShapeDtypeStruct((2, win, own.shape[2]), own.dtype),
            jax.ShapeDtypeStruct(own.shape[:2] + (win,), own.dtype),
            jax.ShapeDtypeStruct(blocks.shape, jnp.bfloat16),
            jax.ShapeDtypeStruct(intens.shape, jnp.float32),
            jax.ShapeDtypeStruct(probe.shape, jnp.float32),
            jax.ShapeDtypeStruct((1, 1), jnp.float32),
        ),
        out_specs=(vmem, vmem, vmem, vmem, vmem, pl.BlockSpec(memory_space=pltpu.SMEM)),
        compiler_params=pltpu.CompilerParams(vmem_limit_bytes=8 * MIB),
    )(own, probe, intens, blocks)


def block_shapes(number, size, ways):
    if not ways:
        return (jax.ShapeDtypeStruct((number * size + TAIL, LANES), jnp.bfloat16),)
    sends = jax.ShapeDtypeStruct((number // ways * size + TAIL, LANES), jnp.bfloat16)
    return (jax.ShapeDtypeStruct((number // ways, size, LANES), jnp.float32),) + (sends,) * (ways - 1)


def put_block(j, total, outs):
    size = total.shape[0]
    if len(outs) == 1:
        outs[0][pl.ds(j * size, size), :] = total.astype(jnp.bfloat16)
    elif j % len(outs) == 0:
        outs[0][j // len(outs)] = total
    else:
        at = pl.ds(j // len(outs) * size, size)
        outs[j % len(outs)][at, :] = total.astype(jnp.bfloat16)


def put_weight(weight, outs):
    tile = in_three(weight)
    for sent in outs if len(outs) == 1 else outs[1:]:
        sent[pl.ds(sent.shape[0] - TAIL, TAIL), :] = tile


def weight_of(block):
    return jnp.sum(block[pl.ds(block.shape[0] - TAIL, TAIL), :].astype(jnp.float32))


def chip_sum_kernel(pixels, size, keep, received, norm, *outs):
    me = lax.axis_index("row")
    for j in range(keep.shape[0] // size):
        at = pl.ds(pl.multiple_of((j ^ me) * size, size), size)
        put_block(j, keep[at, :] + received[at, :].astype(jnp.float32), outs)
    put_weight(jnp.sum(norm[...]) / pixels, outs)


def chip_sum(keep, received, norm, pixels, number, ways):
    size = keep.shape[0] // number
    return small_call(
        functools.partial(chip_sum_kernel, pixels, size),
        block_shapes(number, size, ways),
        keep,
        received,
        norm,
    )


def scatter_sum_kernel(number, mine, sent, *refs):
    received, outs = refs[:number], refs[number:]
    size = mine.shape[1]
    for j in range(mine.shape[0]):
        total = mine[j]
        for block in received:
            total = total + block[pl.ds(j * size, size), :].astype(jnp.float32)
        put_block(j, total, outs)
    put_weight(sum([weight_of(block) for block in received], weight_of(sent)), outs)


def scatter_sum(mine, sent, received, ways):
    number, size, _ = mine.shape
    return small_call(
        functools.partial(scatter_sum_kernel, len(received)),
        block_shapes(number, size, ways),
        mine,
        sent,
        *received,
    )


def pair_up(terms):
    while len(terms) > 1:
        terms = [a + b for a, b in zip(terms[::2], terms[1::2])]
    return terms[0]


def exchange_sum_kernel(size, *refs):
    blocks, chunks = refs[:-1], refs[-1]
    for j in range((chunks.shape[0] - TAIL) // size):
        terms = [
            block[pl.ds((j ^ i) * size, size), :].astype(jnp.float32)
            for i, block in enumerate(blocks)
        ]
        chunks[pl.ds(j * size, size), :] = pair_up(terms).astype(jnp.bfloat16)
    put_weight(pair_up([weight_of(block) for block in blocks]), (chunks,))


def exchange_sum(blocks, size):
    return small_call(
        functools.partial(exchange_sum_kernel, size),
        jax.ShapeDtypeStruct(blocks[0].shape, jnp.bfloat16),
        *blocks,
    )


def copy_chunks(blocks, joined):
    at = 0
    for block in blocks:
        rows = block.shape[0] - TAIL
        joined[pl.ds(at, rows), :] = block[pl.ds(0, rows), :]
        at += rows
    joined[pl.ds(at, TAIL), :] = blocks[0][pl.ds(blocks[0].shape[0] - TAIL, TAIL), :]


def join_kernel(*refs):
    copy_chunks(refs[:-1], refs[-1])


def join(blocks):
    rows = sum(block.shape[0] - TAIL for block in blocks) + TAIL
    return small_call(join_kernel, jax.ShapeDtypeStruct((rows, LANES), blocks[0].dtype), *blocks)


def swap_rows(block, step):
    number = lax.axis_size("row")
    return lax.ppermute(block, "row", [(i, i ^ step) for i in range(number)])


def row_digits():
    number = lax.axis_size("row")
    if number & (number - 1) or number < 2:
        raise ValueError("row size")
    bits = number.bit_length() - 1
    return [(shift, 1 << min(2, bits - shift)) for shift in range(0, bits, 2)]


def probe_update_kernel(size, digits, *refs):
    *blocks, probe, token, new_probe, mine, other, updated, sems = refs
    copy_chunks(blocks[: len(blocks) // 2], mine)
    copy_chunks(blocks[len(blocks) // 2 :], other)
    _, win, modes, _ = updated.shape
    number = mine.shape[0] // size
    me = lax.axis_index("row")
    piece = min(size, CHUNK)
    on_left = lax.axis_index("col") == 0
    tail = pl.ds(number * size, TAIL)
    tails = mine[tail, :].astype(jnp.float32) + other[tail, :].astype(jnp.float32)
    factor = 4.0 / jnp.full((piece, LANES), jnp.sum(tails), jnp.float32)
    half = modes // 2

    def place(chunk):
        j = chunk ^ me
        at, span = 0, 1
        for shift, ways in reversed(digits):
            at = at + ((j >> shift) & (ways - 1)) * span
            span *= ways
        return at * size

    def update(part, b, m, r):
        block = ((m * 2 + part) * (win // LANES) + b) * win
        chunk, offset = divmod(block + r, size)
        at = pl.ds(pl.multiple_of(place(chunk) + offset, piece), piece)
        here = mine[at, :].astype(jnp.float32)
        there = other[at, :].astype(jnp.float32)
        low = jnp.where(on_left, here, there)
        high = jnp.where(on_left, there, here)
        for k, total in ((m, low), (half + m, high)):
            col = k * win + b * LANES
            old = probe[part, r : r + piece, col : col + LANES]
            updated[part, r : r + piece, k, b * LANES : (b + 1) * LANES] = old - factor * total

    stretch = win // 4
    copies = []
    for part in range(2):
        for start in range(0, win, stretch):
            for r in range(start, start + stretch, piece):
                for m in range(half):
                    for b in range(win // LANES):
                        update(part, b, m, r)
            at = (part, pl.ds(start, stretch))
            copies.append(
                pltpu.make_async_copy(updated.at[at], new_probe.at[at], sems.at[len(copies)])
            )
            copies[-1].start()
    for copy in copies:
        copy.wait()


def probe_update(mine, other, probe, token, shape, size, digits):
    vmem = pl.BlockSpec(memory_space=pltpu.VMEM)
    rows = sum(block.shape[0] - TAIL for block in mine) + TAIL
    operands = (*mine, *other, probe, token)
    return pl.pallas_call(
        functools.partial(probe_update_kernel, size, digits),
        out_shape=jax.ShapeDtypeStruct(shape, jnp.float32),
        in_specs=[vmem] * len(operands),
        out_specs=pl.BlockSpec(memory_space=pl.ANY),
        scratch_shapes=[
            pltpu.VMEM((rows, LANES), jnp.bfloat16),
            pltpu.VMEM((rows, LANES), jnp.bfloat16),
            pltpu.VMEM(shape, jnp.float32),
            pltpu.SemaphoreType.DMA((8,)),
        ],
        compiler_params=pltpu.CompilerParams(vmem_limit_bytes=8 * MIB),
    )(*operands)


def low_sum_kernel(first, low_grad, from_left, token, low_sum):
    win = from_left.shape[2]
    rows = from_left.shape[1] - low_grad.shape[1]
    for part in range(2):
        for r in range(0, low_sum.shape[1], CHUNK):
            at, of = slice(r, r + CHUNK), slice(first + r, first + r + CHUNK)
            arrived = from_left[part, rows + first + r : rows + first + r + CHUNK, :]
            total = low_grad[part, of, :win] + arrived.astype(jnp.float32)
            low_sum[part, at, :win] = total.astype(jnp.bfloat16)
            low_sum[part, at, win:] = low_grad[part, of, win:].astype(jnp.bfloat16)


def low_sum_of(first, count, low_grad, from_left, token):
    return small_call(
        functools.partial(low_sum_kernel, first),
        jax.ShapeDtypeStruct((2, count, low_grad.shape[2]), jnp.bfloat16),
        low_grad,
        from_left,
        token,
        weight=LOW_WEIGHT,
    )


def object_update_kernel(old, own_grad, from_left, above_first, above_last, new_object, token):
    token[...] = jnp.zeros_like(token)
    win, split = from_left.shape[2], above_first.shape[1]
    depth = split + above_last.shape[1]
    for part in range(2):
        for r in range(0, old.shape[1], CHUNK):
            at = slice(r, r + CHUNK)
            total = own_grad[part, at, :]
            if r < split:
                total = total + above_first[part, at, :].astype(jnp.float32)
            elif r < depth:
                total = total + above_last[part, r - split : r - split + CHUNK, :].astype(jnp.float32)
            updated = old[part, at, :].astype(jnp.float32) - total
            arrived = from_left[part, at, :].astype(jnp.float32)
            new_object[part, at, :win] = updated[:, :win] - arrived
            new_object[part, at, win:] = updated[:, win:]


def object_update(old, own_grad, from_left, above_first, above_last):
    return small_call(
        object_update_kernel,
        (
            jax.ShapeDtypeStruct(old.shape, jnp.float32),
            jax.ShapeDtypeStruct((8, LANES), jnp.float32),
        ),
        old,
        own_grad,
        from_left,
        above_first,
        above_last,
    )


def swap_cores(block):
    return lax.ppermute(block, "col", [(0, 1), (1, 0)])


def body(object_field, probe_modes, positions, counts, intensities):
    win = probe_modes.shape[1]
    modes = probe_modes.shape[2]
    number = lax.axis_size("row")
    below_right = from_next_row(object_field[:, :win, :], 1)
    first_rows, right_part, tables, measured, probe, power = prepare(
        object_field, probe_modes.reshape(2, win, modes * win), intensities[0, 0]
    )
    right = from_behind(right_part, "col", -1)
    below_left = from_next_row(first_rows, 0)
    corner = from_behind(first_columns(below_right, right), "col", -1)
    own_grad, low_grad, right_grad, keep, send, norm = position_gradients(
        positions[0, 0].T,
        counts.reshape(-1),
        power.reshape(1),
        object_field,
        (below_left, below_right),
        right,
        corner,
        probe,
        measured,
        tables,
    )
    half_rows = keep.size // LANES
    received = swap_cores(send.reshape(half_rows, LANES))
    from_left = from_behind(right_grad, "col", 1)
    digits = row_digits()
    size = half_rows // number
    ways = [digit[1] for digit in digits[:-1]] + [0]
    outs = chip_sum(keep.reshape(half_rows, LANES), received, norm, win * win, number, ways[0])
    for place, (shift, _) in enumerate(digits[:-1]):
        mine, *sends = outs
        received = [swap_rows(block, (i + 1) << shift) for i, block in enumerate(sends)]
        outs = scatter_sum(mine, sends[0], received, ways[place + 1])
    split = SPLIT * win // 8
    low_first = low_sum_of(0, split, low_grad, from_left, outs[0])
    above_first = from_behind(low_first, "row", 1)
    shift, count = digits[-1]
    partners = [swap_rows(outs[0], i << shift) for i in range(1, count)]
    gathered = exchange_sum(list(outs) + partners, size)
    low_last = low_sum_of(split, win - split, low_grad, from_left, gathered)
    above_last = from_behind(low_last, "row", 1)
    mine = [gathered]
    for shift, count in digits[-2::-1]:
        gathered = mine[0] if len(mine) == 1 else join(mine)
        mine = [gathered] + [swap_rows(gathered, i << shift) for i in range(1, count)]
    other = [swap_cores(block) for block in mine]
    new_object, token = object_update(
        object_field, own_grad, from_left, above_first, above_last
    )
    new_probe = probe_update(mine, other, probe, token, probe_modes.shape, size, digits)
    return (new_object, new_probe)


def solution(mesh):
    placed = (
        P(None, ("grp", "row"), "col"),
        P(None, None, "grp", None),
        P(("grp", "row"), "col", None, None),
        P(("grp", "row"), "col"),
        P(("grp", "row"), "col", None, None, None),
    )
    return jax.shard_map(
        body,
        mesh=mesh,
        in_specs=placed,
        out_specs=(P(None, ("grp", "row"), "col"), P(None, None, "grp", None)),
        check_vma=False,
    )
```

```python
import functools

import jax
import jax.numpy as jnp
import ml_dtypes
import numpy as np
from jax import lax
from jax.experimental import pallas as pl
from jax.experimental.pallas import tpu as pltpu
from jax.sharding import PartitionSpec as P

LANES = 128
CHUNK = 32
FINE = 16
TAIL = 16
MIB = 1 << 20
LOW_WEIGHT = 8
SPLIT = 4


def from_behind(block, axis, distance):
    devices = range(lax.axis_size(axis))
    route = [(i - distance, i) for i in devices if i - distance in devices]
    return lax.ppermute(block, axis, route)


def from_next_row(block, col):
    rows, cols = lax.axis_size("row"), lax.axis_size("col")
    route = [((r + 1) * cols + col, r * cols + col) for r in range(rows - 1)]
    return lax.ppermute(block, ("row", "col"), route)


def dft_blocks(win):
    grid = np.arange(win)
    angle = 2.0 * np.pi * (grid[:, None] * grid[None, :] % win) / win
    factor = 1.0 / np.sqrt(win)
    cos_table = (np.cos(angle) * factor).astype(ml_dtypes.bfloat16)
    sin_table = (np.sin(angle) * factor).astype(ml_dtypes.bfloat16)
    blocks = []
    for parity in range(2):
        cos_part, sin_part = cos_table[parity::2, : win // 2], sin_table[parity::2, : win // 2]
        blocks.append(np.block([[cos_part, sin_part], [-sin_part, cos_part]]))
    return np.stack(blocks + [block.T for block in blocks])


def dot(left, right):
    return jnp.dot(left, right, preferred_element_type=jnp.float32)


def gradient_kernel(
    modes,
    starts,
    count,
    power,
    own,
    below_left,
    below_right,
    right,
    corner,
    probe,
    measured,
    tables,
    own_grad,
    low_grad,
    right_grad,
    keep_out,
    send_out,
    norm_out,
    field,
    grad,
    window,
    wide,
    tall,
    wave,
    probe_sum,
):
    win = probe.shape[1]
    rows, cols = own.shape[1], own.shape[2]
    half = win // 2
    fine = range(0, win, FINE)
    spread = win // LANES + 1
    col_index = lax.axis_index("col")
    row_anchor = lax.axis_index("row") * rows
    col_anchor = col_index * cols

    def put_blocks(part, row, first, values):
        for b in range(values.shape[1] // LANES):
            field[part, first + b, row : row + CHUNK, :] = values[:, b * LANES : (b + 1) * LANES]

    grad[...] = jnp.zeros_like(grad)
    probe_sum[...] = jnp.zeros_like(probe_sum)
    norm_out[...] = jnp.zeros_like(norm_out)
    for row_at, col_at, *sources in (
        (0, 0, own),
        (0, cols, right),
        (rows, 0, below_left, below_right),
        (rows, cols, corner),
    ):
        for part in range(2):
            for r in range(0, sources[0].shape[1], CHUNK):
                pieces = [source[part, r : r + CHUNK, :].astype(jnp.float32) for source in sources]
                put_blocks(part, row_at + r, col_at // LANES, sum(pieces[1:], pieces[0]))
    lane = lax.broadcasted_iota(jnp.int32, (FINE, LANES), 1)

    def one_position(slot, carry):
        y, x = starts[0, slot] - row_anchor, starts[1, slot] - col_anchor
        base = x // LANES
        shift = x - base * LANES
        back_shift = (LANES - shift) % LANES
        keep = lane < LANES - shift
        for r in range(0, half, FINE):
            objs = []
            for start in (r, r + half):
                at = pl.ds(start, FINE)
                obj = []
                for part in range(2):
                    turned = [
                        pltpu.roll(field[part, base + b, pl.ds(y + start, FINE), :], back_shift, 1)
                        for b in range(spread)
                    ]
                    piece = jnp.concatenate(
                        [jnp.where(keep, a, b) for a, b in zip(turned[:-1], turned[1:])], axis=1
                    )
                    window[part, at, :] = piece
                    obj.append(piece)
                squares = obj[0] * obj[0] + obj[1] * obj[1]
                norm_out[...] += jnp.sum(squares.reshape(FINE // 8, 8, win), axis=0)
                objs.append(obj)
            for k in range(modes):
                cs = pl.ds(k * win, win)
                exits = []
                for start, (o_re, o_im) in zip((r, r + half), objs):
                    p_re, p_im = probe[0, pl.ds(start, FINE), cs], probe[1, pl.ds(start, FINE), cs]
                    exits.append((p_re * o_re - p_im * o_im, p_re * o_im + p_im * o_re))
                for part in range(2):
                    low, high = exits[0][part], exits[1][part]
                    at = pl.ds(part * half + r, FINE)
                    wide[k, 0, at, :] = (low + high).astype(jnp.bfloat16)
                    wide[k, 1, at, :] = (low - high).astype(jnp.bfloat16)

        for k in range(modes):
            for parity in range(2):
                out = dot(tables[parity], wide[k, parity])
                at = pl.ds(k * win + parity * half, half)
                for part in range(2):
                    low = out[part * half : (part + 1) * half, :half]
                    high = out[part * half : (part + 1) * half, half:]
                    to = pl.ds(part * half, half)
                    tall[0, at, to] = (low + high).astype(jnp.bfloat16)
                    tall[1, at, to] = (low - high).astype(jnp.bfloat16)
        for parity in range(2):
            wave[parity] = dot(tall[parity], tables[2 + parity])

        for r in fine:
            for parity in range(2):
                waves = []
                total = jnp.zeros((FINE, half), jnp.float32)
                for k in range(modes):
                    ka = pl.ds(k * win + r, FINE)
                    waves.append((wave[parity, ka, :half], wave[parity, ka, half:]))
                    total = total + (waves[k][0] * waves[k][0] + waves[k][1] * waves[k][1])
                gs = pl.ds(parity * half, half)
                amp = measured[slot, pl.ds(r, FINE), gs]
                ratio = 1.0 - amp * lax.rsqrt(jnp.maximum(total, 1.0))
                for k in range(modes):
                    for part in range(2):
                        at = pl.ds(part * half + r % half, FINE)
                        wide[k, r // half, at, gs] = (waves[k][part] * ratio).astype(jnp.bfloat16)

        for k in range(modes):
            even = dot(tables[2], wide[k, 0])
            odd = dot(tables[3], wide[k, 1])
            for place, out in enumerate((even + odd, even - odd)):
                at = pl.ds(k * win + place * half, half)
                for part in range(2):
                    for parity in range(2):
                        tall[parity, at, part * half : (part + 1) * half] = out[
                            part * half : (part + 1) * half, parity * half : (parity + 1) * half
                        ].astype(jnp.bfloat16)
        for parity in range(2):
            wave[parity] = dot(tall[parity], tables[parity])

        keep_high = lane >= shift
        for r in fine:
            at = pl.ds(r, FINE)
            sums = [[jnp.zeros((FINE, LANES), jnp.float32) for _ in range(2)] for _ in range(2)]
            for b in range(2):
                bs = pl.ds(b * half, half)
                o_re, o_im = window[0, at, bs], window[1, at, bs]
                for k in range(modes):
                    cs = pl.ds(k * win + b * half, half)
                    ka = pl.ds(k * win + r, FINE)
                    even, odd = wave[0, ka, :], wave[1, ka, :]
                    d = even + odd if b == 0 else even - odd
                    d_re, d_im = d[:, :half], d[:, half:]
                    p_re, p_im = probe[0, at, cs], probe[1, at, cs]
                    sums[0][b] = sums[0][b] + (p_re * d_re + p_im * d_im)
                    sums[1][b] = sums[1][b] + (p_re * d_im - p_im * d_re)
                    probe_sum[k, 0, b, at, :] += o_re * d_re + o_im * d_im
                    probe_sum[k, 1, b, at, :] += o_re * d_im - o_im * d_re
            for part in range(2):
                turned = [pltpu.roll(piece, shift, 1) for piece in sums[part]]
                turned = [jnp.zeros_like(turned[0])] + turned + [jnp.zeros_like(turned[0])]
                for b in range(spread):
                    grad[part, base + b, pl.ds(y + r, FINE), :] += jnp.where(
                        keep_high, turned[b + 1], turned[b]
                    )
        return carry

    lax.fori_loop(0, count[0], one_position, 0)
    for m in range(modes // 2):
        keep_mode = col_index * (modes // 2) + m
        send_mode = (1 - col_index) * (modes // 2) + m
        keep_out[m] = probe_sum[keep_mode]
        send_out[m] = probe_sum[send_mode].astype(jnp.bfloat16)
    scale = 1.0 / jnp.full((8, LANES), power[0], jnp.float32)
    scale = jnp.concatenate([scale] * (CHUNK // 8), axis=0)

    def take_blocks(part, at, first, number):
        return jnp.concatenate(
            [grad[part, first + b, at, :] * scale for b in range(number)], axis=1
        )

    for part in range(2):
        for r in range(0, rows + win, CHUNK):
            at = pl.ds(r, CHUNK)
            piece = take_blocks(part, at, cols // LANES, win // LANES)
            right_grad[part, at, :] = piece.astype(jnp.bfloat16)
        for r in range(0, rows, CHUNK):
            at = pl.ds(r, CHUNK)
            own_grad[part, at, :] = take_blocks(part, at, 0, cols // LANES)
        for r in range(0, win, CHUNK):
            at, of = pl.ds(r, CHUNK), pl.ds(rows + r, CHUNK)
            low_grad[part, at, :] = take_blocks(part, of, 0, cols // LANES)


def position_gradients(starts, count, power, own, below, right, corner, probe, measured, tables):
    win, modes = probe.shape[1], probe.shape[2] // probe.shape[1]
    rows, cols = own.shape[1:]
    f32, bf16 = jnp.float32, jnp.bfloat16
    smem = pl.BlockSpec(memory_space=pltpu.SMEM)
    vmem = pl.BlockSpec(memory_space=pltpu.VMEM)
    if win != 2 * LANES:
        raise ValueError("window size")
    slots = measured.shape[0]
    flops = 16 * slots * modes * win**3
    half_blocks = (modes // 2, 2, win // LANES, win, LANES)
    return pl.pallas_call(
        functools.partial(gradient_kernel, modes),
        out_shape=(
            jax.ShapeDtypeStruct((2, rows, cols), f32),
            jax.ShapeDtypeStruct((2, win, cols), f32),
            jax.ShapeDtypeStruct((2, rows + win, win), bf16),
            jax.ShapeDtypeStruct(half_blocks, f32),
            jax.ShapeDtypeStruct(half_blocks, bf16),
            jax.ShapeDtypeStruct((8, win), f32),
        ),
        in_specs=[smem] * 3 + [vmem] * 8,
        out_specs=(vmem,) * 6,
        scratch_shapes=[
            pltpu.VMEM((2, (cols + win) // LANES, rows + win, LANES), f32),
            pltpu.VMEM((2, (cols + win) // LANES, rows + win, LANES), f32),
            pltpu.VMEM((2, win, win), f32),
            pltpu.VMEM((modes, 2, win, win), bf16),
            pltpu.VMEM((2, modes * win, win), bf16),
            pltpu.VMEM((2, modes * win, win), f32),
            pltpu.VMEM((modes, 2, win // LANES, win, LANES), f32),
        ],
        compiler_params=pltpu.CompilerParams(vmem_limit_bytes=26 * MIB),
        cost_estimate=pl.CostEstimate(flops=flops, bytes_accessed=12 << 20, transcendentals=0),
    )(starts, count, power, own, *below, right, corner, probe, measured, tables)


def in_three(value):
    full = jnp.full((TAIL, LANES), value, jnp.float32)
    high = full.astype(jnp.bfloat16).astype(jnp.float32)
    mid = (full - high).astype(jnp.bfloat16).astype(jnp.float32)
    low = full - high - mid
    row = lax.broadcasted_iota(jnp.int32, (TAIL, LANES), 0)
    lane = lax.broadcasted_iota(jnp.int32, (TAIL, LANES), 1)
    tile = jnp.where(row == 0, high, jnp.where(row == 1, mid, jnp.where(row == 2, low, 0.0)))
    return jnp.where(lane == 0, tile, 0.0).astype(jnp.bfloat16)


def small_call(kernel, shapes, *operands, weight=1):
    return pl.pallas_call(
        kernel,
        out_shape=shapes,
        compiler_params=pltpu.CompilerParams(vmem_limit_bytes=4 * MIB),
        cost_estimate=pl.CostEstimate(flops=0, bytes_accessed=weight * MIB, transcendentals=0),
    )(*operands)


def first_columns_kernel(block, token, first):
    first[...] = block[:, :, : first.shape[2]]


def first_columns(block, size, token):
    shape = block.shape[:2] + (size,)
    return small_call(
        first_columns_kernel, jax.ShapeDtypeStruct(shape, block.dtype), block, token
    )


def copies_kernel(block, token, first_rows, first_cols):
    first_rows[...] = block[:, : first_rows.shape[1], :]
    first_cols[...] = block[:, :, : first_cols.shape[2]]


def copies(block, size, token):
    parts, rows, cols = block.shape
    shapes = ((parts, size, cols), (parts, rows, size))
    return small_call(
        copies_kernel,
        tuple(jax.ShapeDtypeStruct(shape, block.dtype) for shape in shapes),
        block,
        token,
    )


def prepare_kernel(probe, intens, blocks, token, tables, measured, wide_probe, power):
    tables[...] = blocks[...]
    count, size, _ = intens.shape
    row = lax.broadcasted_iota(jnp.int32, (size, size), 0)
    col = lax.broadcasted_iota(jnp.int32, (size, size), 1)
    to_even_first = (col == jnp.where(row < size // 2, 2 * row, 2 * row - size + 1)).astype(
        jnp.float32
    )
    from_left = to_even_first.astype(jnp.bfloat16)
    from_right = (row == jnp.where(col < size // 2, 2 * col, 2 * col - size + 1)).astype(
        jnp.float32
    )
    from_right = from_right.astype(jnp.bfloat16)
    for slot in range(count):
        turned = dot(from_left, intens[slot]).astype(jnp.bfloat16)
        measured[slot] = jnp.sqrt(dot(turned, from_right))
    win = probe.shape[1]
    modes = probe.shape[2] // win
    largest = jnp.zeros((8, win), jnp.float32)
    for r in range(0, probe.shape[1], CHUNK):
        at = slice(r, r + CHUNK)
        total = jnp.zeros((CHUNK, win), jnp.float32)
        for k in range(modes):
            for part in range(2):
                p = probe[part, at, k * win : (k + 1) * win].astype(jnp.float32)
                wide_probe[part, at, k * win : (k + 1) * win] = p
                total = total + p * p
        largest = jnp.maximum(largest, jnp.max(total.reshape(CHUNK // 8, 8, win), axis=0))
    power[0, 0] = jnp.max(largest)


def prepare(probe, intens, token):
    win = probe.shape[1]
    blocks = dft_blocks(win)
    vmem = pl.BlockSpec(memory_space=pltpu.VMEM)
    return pl.pallas_call(
        prepare_kernel,
        out_shape=(
            jax.ShapeDtypeStruct(blocks.shape, jnp.bfloat16),
            jax.ShapeDtypeStruct(intens.shape, jnp.float32),
            jax.ShapeDtypeStruct(probe.shape, jnp.float32),
            jax.ShapeDtypeStruct((1, 1), jnp.float32),
        ),
        out_specs=(vmem, vmem, vmem, pl.BlockSpec(memory_space=pltpu.SMEM)),
        compiler_params=pltpu.CompilerParams(vmem_limit_bytes=8 * MIB),
    )(probe, intens, blocks, token)


def block_shapes(number, size, ways):
    if not ways:
        return (jax.ShapeDtypeStruct((number * size + TAIL, LANES), jnp.bfloat16),)
    sends = jax.ShapeDtypeStruct((number // ways * size + TAIL, LANES), jnp.bfloat16)
    return (jax.ShapeDtypeStruct((number // ways, size, LANES), jnp.float32),) + (sends,) * (ways - 1)


def put_block(j, total, outs):
    size = total.shape[0]
    if len(outs) == 1:
        outs[0][pl.ds(j * size, size), :] = total.astype(jnp.bfloat16)
    elif j % len(outs) == 0:
        outs[0][j // len(outs)] = total
    else:
        at = pl.ds(j // len(outs) * size, size)
        outs[j % len(outs)][at, :] = total.astype(jnp.bfloat16)


def put_weight(weight, outs):
    tile = in_three(weight)
    for sent in outs if len(outs) == 1 else outs[1:]:
        sent[pl.ds(sent.shape[0] - TAIL, TAIL), :] = tile


def weight_of(block):
    return jnp.sum(block[pl.ds(block.shape[0] - TAIL, TAIL), :].astype(jnp.float32))


def chip_sum_kernel(pixels, size, keep, received, norm, *outs):
    me = lax.axis_index("row")
    for j in range(keep.shape[0] // size):
        at = pl.ds(pl.multiple_of((j ^ me) * size, size), size)
        put_block(j, keep[at, :] + received[at, :].astype(jnp.float32), outs)
    put_weight(jnp.sum(norm[...]) / pixels, outs)


def chip_sum(keep, received, norm, pixels, number, ways):
    size = keep.shape[0] // number
    return small_call(
        functools.partial(chip_sum_kernel, pixels, size),
        block_shapes(number, size, ways),
        keep,
        received,
        norm,
    )


def scatter_sum_kernel(number, mine, sent, *refs):
    received, outs = refs[:number], refs[number:]
    size = mine.shape[1]
    for j in range(mine.shape[0]):
        total = mine[j]
        for block in received:
            total = total + block[pl.ds(j * size, size), :].astype(jnp.float32)
        put_block(j, total, outs)
    put_weight(sum([weight_of(block) for block in received], weight_of(sent)), outs)


def scatter_sum(mine, sent, received, ways):
    number, size, _ = mine.shape
    return small_call(
        functools.partial(scatter_sum_kernel, len(received)),
        block_shapes(number, size, ways),
        mine,
        sent,
        *received,
    )


def pair_up(terms):
    while len(terms) > 1:
        terms = [a + b for a, b in zip(terms[::2], terms[1::2])]
    return terms[0]


def exchange_sum_kernel(size, *refs):
    blocks, chunks = refs[:-1], refs[-1]
    for j in range((chunks.shape[0] - TAIL) // size):
        terms = [
            block[pl.ds((j ^ i) * size, size), :].astype(jnp.float32)
            for i, block in enumerate(blocks)
        ]
        chunks[pl.ds(j * size, size), :] = pair_up(terms).astype(jnp.bfloat16)
    put_weight(pair_up([weight_of(block) for block in blocks]), (chunks,))


def exchange_sum(blocks, size):
    return small_call(
        functools.partial(exchange_sum_kernel, size),
        jax.ShapeDtypeStruct(blocks[0].shape, jnp.bfloat16),
        *blocks,
    )


def copy_chunks(blocks, joined):
    at = 0
    for block in blocks:
        rows = block.shape[0] - TAIL
        joined[pl.ds(at, rows), :] = block[pl.ds(0, rows), :]
        at += rows
    joined[pl.ds(at, TAIL), :] = blocks[0][pl.ds(blocks[0].shape[0] - TAIL, TAIL), :]


def join_kernel(*refs):
    copy_chunks(refs[:-1], refs[-1])


def join(blocks):
    rows = sum(block.shape[0] - TAIL for block in blocks) + TAIL
    return small_call(join_kernel, jax.ShapeDtypeStruct((rows, LANES), blocks[0].dtype), *blocks)


def swap_rows(block, step):
    number = lax.axis_size("row")
    return lax.ppermute(block, "row", [(i, i ^ step) for i in range(number)])


def row_digits():
    number = lax.axis_size("row")
    if number & (number - 1) or number < 2:
        raise ValueError("row size")
    bits = number.bit_length() - 1
    return [(shift, 1 << min(2, bits - shift)) for shift in range(0, bits, 2)]


def probe_update_kernel(size, digits, *refs):
    *blocks, probe, token, new_probe, mine, other, updated, sems = refs
    copy_chunks(blocks[: len(blocks) // 2], mine)
    copy_chunks(blocks[len(blocks) // 2 :], other)
    _, win, modes, _ = updated.shape
    number = mine.shape[0] // size
    me = lax.axis_index("row")
    piece = min(size, CHUNK)
    on_left = lax.axis_index("col") == 0
    tail = pl.ds(number * size, TAIL)
    tails = mine[tail, :].astype(jnp.float32) + other[tail, :].astype(jnp.float32)
    factor = 4.0 / jnp.full((piece, LANES), jnp.sum(tails), jnp.float32)
    half = modes // 2

    def place(chunk):
        j = chunk ^ me
        at, span = 0, 1
        for shift, ways in reversed(digits):
            at = at + ((j >> shift) & (ways - 1)) * span
            span *= ways
        return at * size

    def update(part, b, m, r):
        block = ((m * 2 + part) * (win // LANES) + b) * win
        chunk, offset = divmod(block + r, size)
        at = pl.ds(pl.multiple_of(place(chunk) + offset, piece), piece)
        here = mine[at, :].astype(jnp.float32)
        there = other[at, :].astype(jnp.float32)
        low = jnp.where(on_left, here, there)
        high = jnp.where(on_left, there, here)
        for k, total in ((m, low), (half + m, high)):
            col = k * win + b * LANES
            old = probe[part, r : r + piece, col : col + LANES]
            updated[part, r : r + piece, k, b * LANES : (b + 1) * LANES] = old - factor * total

    stretch = win // 4
    copies = []
    for part in range(2):
        for start in range(0, win, stretch):
            for r in range(start, start + stretch, piece):
                for m in range(half):
                    for b in range(win // LANES):
                        update(part, b, m, r)
            at = (part, pl.ds(start, stretch))
            copies.append(
                pltpu.make_async_copy(updated.at[at], new_probe.at[at], sems.at[len(copies)])
            )
            copies[-1].start()
    for copy in copies:
        copy.wait()


def probe_update(mine, other, probe, token, shape, size, digits):
    vmem = pl.BlockSpec(memory_space=pltpu.VMEM)
    rows = sum(block.shape[0] - TAIL for block in mine) + TAIL
    operands = (*mine, *other, probe, token)
    return pl.pallas_call(
        functools.partial(probe_update_kernel, size, digits),
        out_shape=jax.ShapeDtypeStruct(shape, jnp.float32),
        in_specs=[vmem] * len(operands),
        out_specs=pl.BlockSpec(memory_space=pl.ANY),
        scratch_shapes=[
            pltpu.VMEM((rows, LANES), jnp.bfloat16),
            pltpu.VMEM((rows, LANES), jnp.bfloat16),
            pltpu.VMEM(shape, jnp.float32),
            pltpu.SemaphoreType.DMA((8,)),
        ],
        compiler_params=pltpu.CompilerParams(vmem_limit_bytes=8 * MIB),
    )(*operands)


def low_sum_kernel(first, low_grad, from_left, token, low_sum):
    win = from_left.shape[2]
    rows = from_left.shape[1] - low_grad.shape[1]
    for part in range(2):
        for r in range(0, low_sum.shape[1], CHUNK):
            at, of = slice(r, r + CHUNK), slice(first + r, first + r + CHUNK)
            arrived = from_left[part, rows + first + r : rows + first + r + CHUNK, :]
            total = low_grad[part, of, :win] + arrived.astype(jnp.float32)
            low_sum[part, at, :win] = total.astype(jnp.bfloat16)
            low_sum[part, at, win:] = low_grad[part, of, win:].astype(jnp.bfloat16)


def low_sum_of(first, count, low_grad, from_left, token):
    return small_call(
        functools.partial(low_sum_kernel, first),
        jax.ShapeDtypeStruct((2, count, low_grad.shape[2]), jnp.bfloat16),
        low_grad,
        from_left,
        token,
        weight=LOW_WEIGHT,
    )


def object_update_kernel(old, own_grad, from_left, above_first, above_last, new_object, token):
    token[...] = jnp.zeros_like(token)
    win, split = from_left.shape[2], above_first.shape[1]
    depth = split + above_last.shape[1]
    for part in range(2):
        for r in range(0, old.shape[1], CHUNK):
            at = slice(r, r + CHUNK)
            total = own_grad[part, at, :]
            if r < split:
                total = total + above_first[part, at, :].astype(jnp.float32)
            elif r < depth:
                total = total + above_last[part, r - split : r - split + CHUNK, :].astype(jnp.float32)
            updated = old[part, at, :].astype(jnp.float32) - total
            arrived = from_left[part, at, :].astype(jnp.float32)
            new_object[part, at, :win] = updated[:, :win] - arrived
            new_object[part, at, win:] = updated[:, win:]


def object_update(old, own_grad, from_left, above_first, above_last):
    return small_call(
        object_update_kernel,
        (
            jax.ShapeDtypeStruct(old.shape, jnp.float32),
            jax.ShapeDtypeStruct((8, LANES), jnp.float32),
        ),
        old,
        own_grad,
        from_left,
        above_first,
        above_last,
    )


def swap_cores(block):
    return lax.ppermute(block, "col", [(0, 1), (1, 0)])


def body(object_field, probe_modes, positions, counts, intensities):
    win = probe_modes.shape[1]
    modes = probe_modes.shape[2]
    number = lax.axis_size("row")
    below_right = from_next_row(object_field[:, :win, :], 1)
    probe_flat = probe_modes.reshape(2, win, modes * win)
    first_rows, first_cols = copies(object_field, win, probe_flat)
    below_left = from_next_row(first_rows, 0)
    right = from_behind(first_cols, "col", -1)
    tables, measured, probe, power = prepare(probe_flat, intensities[0, 0], right)
    corner = from_behind(first_columns(below_right, win, tables), "col", -1)
    own_grad, low_grad, right_grad, keep, send, norm = position_gradients(
        positions[0, 0].T,
        counts.reshape(-1),
        power.reshape(1),
        object_field,
        (below_left, below_right),
        right,
        corner,
        probe,
        measured,
        tables,
    )
    half_rows = keep.size // LANES
    received = swap_cores(send.reshape(half_rows, LANES))
    from_left = from_behind(right_grad, "col", 1)
    digits = row_digits()
    size = half_rows // number
    ways = [digit[1] for digit in digits[:-1]] + [0]
    outs = chip_sum(keep.reshape(half_rows, LANES), received, norm, win * win, number, ways[0])
    for place, (shift, _) in enumerate(digits[:-1]):
        mine, *sends = outs
        received = [swap_rows(block, (i + 1) << shift) for i, block in enumerate(sends)]
        outs = scatter_sum(mine, sends[0], received, ways[place + 1])
    split = SPLIT * win // 8
    low_first = low_sum_of(0, split, low_grad, from_left, outs[0])
    above_first = from_behind(low_first, "row", 1)
    shift, count = digits[-1]
    partners = [swap_rows(outs[0], i << shift) for i in range(1, count)]
    gathered = exchange_sum(list(outs) + partners, size)
    low_last = low_sum_of(split, win - split, low_grad, from_left, gathered)
    above_last = from_behind(low_last, "row", 1)
    mine = [gathered]
    for shift, count in digits[-2::-1]:
        gathered = mine[0] if len(mine) == 1 else join(mine)
        mine = [gathered] + [swap_rows(gathered, i << shift) for i in range(1, count)]
    other = [swap_cores(block) for block in mine]
    new_object, token = object_update(
        object_field, own_grad, from_left, above_first, above_last
    )
    new_probe = probe_update(mine, other, probe, token, probe_modes.shape, size, digits)
    return (new_object, new_probe)


def solution(mesh):
    placed = (
        P(None, ("grp", "row"), "col"),
        P(None, None, "grp", None),
        P(("grp", "row"), "col", None, None),
        P(("grp", "row"), "col"),
        P(("grp", "row"), "col", None, None, None),
    )
    return jax.shard_map(
        body,
        mesh=mesh,
        in_specs=placed,
        out_specs=(P(None, ("grp", "row"), "col"), P(None, None, "grp", None)),
        check_vma=False,
    )
```

```python
import functools

import jax
import jax.numpy as jnp
import ml_dtypes
import numpy as np
from jax import lax
from jax.experimental import pallas as pl
from jax.experimental.pallas import tpu as pltpu
from jax.sharding import PartitionSpec as P

LANES = 128
CHUNK = 32
FINE = 16
TAIL = 16
MIB = 1 << 20
LOW_WEIGHT = 8
SPLIT = 4


def from_behind(block, axis, distance):
    devices = range(lax.axis_size(axis))
    route = [(i - distance, i) for i in devices if i - distance in devices]
    return lax.ppermute(block, axis, route)


def from_next_row(block, col):
    rows, cols = lax.axis_size("row"), lax.axis_size("col")
    route = [((r + 1) * cols + col, r * cols + col) for r in range(rows - 1)]
    return lax.ppermute(block, ("row", "col"), route)


def dft_blocks(win):
    grid = np.arange(win)
    angle = 2.0 * np.pi * (grid[:, None] * grid[None, :] % win) / win
    factor = 1.0 / np.sqrt(win)
    cos_table = (np.cos(angle) * factor).astype(ml_dtypes.bfloat16)
    sin_table = (np.sin(angle) * factor).astype(ml_dtypes.bfloat16)
    blocks = []
    for parity in range(2):
        cos_part, sin_part = cos_table[parity::2, : win // 2], sin_table[parity::2, : win // 2]
        blocks.append(np.block([[cos_part, sin_part], [-sin_part, cos_part]]))
    return np.stack(blocks + [block.T for block in blocks])


def dot(left, right):
    return jnp.dot(left, right, preferred_element_type=jnp.float32)


def gradient_kernel(
    modes,
    starts,
    count,
    power,
    own,
    below_left,
    below_right,
    right,
    corner,
    probe,
    measured,
    tables,
    own_grad,
    low_grad,
    right_grad,
    keep_out,
    send_out,
    norm_out,
    field,
    grad,
    window,
    wide,
    tall,
    wave,
    total,
    grad_sum,
    probe_sum,
):
    win = probe.shape[1]
    rows, cols = own.shape[1], own.shape[2]
    half = win // 2
    fine = range(0, win, FINE)
    spread = win // LANES + 1
    col_index = lax.axis_index("col")
    row_anchor = lax.axis_index("row") * rows
    col_anchor = col_index * cols

    def put_blocks(part, row, first, values):
        for b in range(values.shape[1] // LANES):
            field[part, first + b, row : row + CHUNK, :] = values[:, b * LANES : (b + 1) * LANES]

    grad[...] = jnp.zeros_like(grad)
    probe_sum[...] = jnp.zeros_like(probe_sum)
    norm_out[...] = jnp.zeros_like(norm_out)
    for row_at, col_at, *sources in (
        (0, 0, own),
        (0, cols, right),
        (rows, 0, below_left, below_right),
        (rows, cols, corner),
    ):
        for part in range(2):
            for r in range(0, sources[0].shape[1], CHUNK):
                pieces = [source[part, r : r + CHUNK, :].astype(jnp.float32) for source in sources]
                put_blocks(part, row_at + r, col_at // LANES, sum(pieces[1:], pieces[0]))
    lane = lax.broadcasted_iota(jnp.int32, (FINE, LANES), 1)

    def one_position(slot, carry):
        y, x = starts[0, slot] - row_anchor, starts[1, slot] - col_anchor
        base = x // LANES
        shift = x - base * LANES
        back_shift = (LANES - shift) % LANES
        keep = lane < LANES - shift
        for r in fine:
            at = pl.ds(r, FINE)
            obj = []
            for part in range(2):
                turned = [
                    pltpu.roll(field[part, base + b, pl.ds(y + r, FINE), :], back_shift, 1)
                    for b in range(spread)
                ]
                piece = jnp.concatenate(
                    [jnp.where(keep, a, b) for a, b in zip(turned[:-1], turned[1:])], axis=1
                )
                window[part, at, :] = piece
                obj.append(piece)
            squares = obj[0] * obj[0] + obj[1] * obj[1]
            norm_out[...] += jnp.sum(squares.reshape(FINE // 8, 8, win), axis=0)

        def exits(k):
            cs = pl.ds(k * win, win)
            for r in range(0, half, FINE):
                pair = []
                for start in (r, r + half):
                    at = pl.ds(start, FINE)
                    o_re, o_im = window[0, at, :], window[1, at, :]
                    p_re, p_im = probe[0, at, cs], probe[1, at, cs]
                    pair.append((p_re * o_re - p_im * o_im, p_re * o_im + p_im * o_re))
                for part in range(2):
                    low, high = pair[0][part], pair[1][part]
                    at = pl.ds(part * half + r, FINE)
                    wide[k, 0, at, :] = (low + high).astype(jnp.bfloat16)
                    wide[k, 1, at, :] = (low - high).astype(jnp.bfloat16)

        def rows_forward(k):
            for parity in range(2):
                out = dot(tables[parity], wide[k, parity])
                at = pl.ds(k * win + parity * half, half)
                for part in range(2):
                    low = out[part * half : (part + 1) * half, :half]
                    high = out[part * half : (part + 1) * half, half:]
                    to = pl.ds(part * half, half)
                    tall[0, at, to] = (low + high).astype(jnp.bfloat16)
                    tall[1, at, to] = (low - high).astype(jnp.bfloat16)

        def cols(first, k):
            at = pl.ds(k * win, win)
            for parity in range(2):
                wave[parity, at, :] = dot(tall[parity, at, :], tables[first + parity])

        def powers(k):
            for r in fine:
                for parity in range(2):
                    ka, gs = pl.ds(k * win + r, FINE), pl.ds(parity * half, half)
                    w_re, w_im = wave[parity, ka, :half], wave[parity, ka, half:]
                    term = w_re * w_re + w_im * w_im
                    if k == 0:
                        total[pl.ds(r, FINE), gs] = term
                    elif k < modes - 1:
                        total[pl.ds(r, FINE), gs] += term
                    else:
                        largest = jnp.maximum(total[pl.ds(r, FINE), gs] + term, 1.0)
                        amp = measured[slot, pl.ds(r, FINE), gs]
                        total[pl.ds(r, FINE), gs] = 1.0 - amp * lax.rsqrt(largest)

        def residuals(k):
            for r in fine:
                for parity in range(2):
                    ka, gs = pl.ds(k * win + r, FINE), pl.ds(parity * half, half)
                    ratio = total[pl.ds(r, FINE), gs]
                    for part in range(2):
                        at = pl.ds(part * half + r % half, FINE)
                        w = wave[parity, ka, part * half : (part + 1) * half]
                        wide[k, r // half, at, gs] = (w * ratio).astype(jnp.bfloat16)

        def rows_back(k):
            even = dot(tables[2], wide[k, 0])
            odd = dot(tables[3], wide[k, 1])
            for place, out in enumerate((even + odd, even - odd)):
                at = pl.ds(k * win + place * half, half)
                for part in range(2):
                    for parity in range(2):
                        tall[parity, at, part * half : (part + 1) * half] = out[
                            part * half : (part + 1) * half, parity * half : (parity + 1) * half
                        ].astype(jnp.bfloat16)

        def gradients(k):
            for r in fine:
                at, ka = pl.ds(r, FINE), pl.ds(k * win + r, FINE)
                even, odd = wave[0, ka, :], wave[1, ka, :]
                for b, d in enumerate((even + odd, even - odd)):
                    bs, cs = pl.ds(b * half, half), pl.ds(k * win + b * half, half)
                    o_re, o_im = window[0, at, bs], window[1, at, bs]
                    d_re, d_im = d[:, :half], d[:, half:]
                    p_re, p_im = probe[0, at, cs], probe[1, at, cs]
                    probe_sum[k, 0, b, at, :] += o_re * d_re + o_im * d_im
                    probe_sum[k, 1, b, at, :] += o_re * d_im - o_im * d_re
                    terms = (p_re * d_re + p_im * d_im, p_re * d_im - p_im * d_re)
                    for part in range(2):
                        if k == 0:
                            grad_sum[part, at, bs] = terms[part]
                        else:
                            grad_sum[part, at, bs] += terms[part]

        def skewed(*stages):
            for step in range(modes + len(stages) - 1):
                for i, stage in enumerate(stages):
                    if 0 <= step - i < modes:
                        stage(step - i)

        skewed(exits, rows_forward, functools.partial(cols, 2), powers)
        skewed(residuals, rows_back, functools.partial(cols, 0), gradients)
        keep_high = lane >= shift
        for r in fine:
            at = pl.ds(r, FINE)
            for part in range(2):
                turned = [
                    pltpu.roll(grad_sum[part, at, b * LANES : (b + 1) * LANES], shift, 1)
                    for b in range(2)
                ]
                turned = [jnp.zeros_like(turned[0])] + turned + [jnp.zeros_like(turned[0])]
                for b in range(spread):
                    grad[part, base + b, pl.ds(y + r, FINE), :] += jnp.where(
                        keep_high, turned[b + 1], turned[b]
                    )
        return carry

    lax.fori_loop(0, count[0], one_position, 0)
    for m in range(modes // 2):
        keep_mode = col_index * (modes // 2) + m
        send_mode = (1 - col_index) * (modes // 2) + m
        keep_out[m] = probe_sum[keep_mode]
        send_out[m] = probe_sum[send_mode].astype(jnp.bfloat16)
    scale = 1.0 / jnp.full((8, LANES), power[0], jnp.float32)
    scale = jnp.concatenate([scale] * (CHUNK // 8), axis=0)

    def take_blocks(part, at, first, number):
        return jnp.concatenate(
            [grad[part, first + b, at, :] * scale for b in range(number)], axis=1
        )

    for part in range(2):
        for r in range(0, rows + win, CHUNK):
            at = pl.ds(r, CHUNK)
            piece = take_blocks(part, at, cols // LANES, win // LANES)
            right_grad[part, at, :] = piece.astype(jnp.bfloat16)
        for r in range(0, rows, CHUNK):
            at = pl.ds(r, CHUNK)
            own_grad[part, at, :] = take_blocks(part, at, 0, cols // LANES)
        for r in range(0, win, CHUNK):
            at, of = pl.ds(r, CHUNK), pl.ds(rows + r, CHUNK)
            low_grad[part, at, :] = take_blocks(part, of, 0, cols // LANES)


def position_gradients(starts, count, power, own, below, right, corner, probe, measured, tables):
    win, modes = probe.shape[1], probe.shape[2] // probe.shape[1]
    rows, cols = own.shape[1:]
    f32, bf16 = jnp.float32, jnp.bfloat16
    smem = pl.BlockSpec(memory_space=pltpu.SMEM)
    vmem = pl.BlockSpec(memory_space=pltpu.VMEM)
    if win != 2 * LANES:
        raise ValueError("window size")
    slots = measured.shape[0]
    flops = 16 * slots * modes * win**3
    half_blocks = (modes // 2, 2, win // LANES, win, LANES)
    return pl.pallas_call(
        functools.partial(gradient_kernel, modes),
        out_shape=(
            jax.ShapeDtypeStruct((2, rows, cols), f32),
            jax.ShapeDtypeStruct((2, win, cols), f32),
            jax.ShapeDtypeStruct((2, rows + win, win), bf16),
            jax.ShapeDtypeStruct(half_blocks, f32),
            jax.ShapeDtypeStruct(half_blocks, bf16),
            jax.ShapeDtypeStruct((8, win), f32),
        ),
        in_specs=[smem] * 3 + [vmem] * 8,
        out_specs=(vmem,) * 6,
        scratch_shapes=[
            pltpu.VMEM((2, (cols + win) // LANES, rows + win, LANES), f32),
            pltpu.VMEM((2, (cols + win) // LANES, rows + win, LANES), f32),
            pltpu.VMEM((2, win, win), f32),
            pltpu.VMEM((modes, 2, win, win), bf16),
            pltpu.VMEM((2, modes * win, win), bf16),
            pltpu.VMEM((2, modes * win, win), f32),
            pltpu.VMEM((win, win), f32),
            pltpu.VMEM((2, win, win), f32),
            pltpu.VMEM((modes, 2, win // LANES, win, LANES), f32),
        ],
        compiler_params=pltpu.CompilerParams(vmem_limit_bytes=26 * MIB),
        cost_estimate=pl.CostEstimate(flops=flops, bytes_accessed=12 << 20, transcendentals=0),
    )(starts, count, power, own, *below, right, corner, probe, measured, tables)


def in_three(value):
    full = jnp.full((TAIL, LANES), value, jnp.float32)
    high = full.astype(jnp.bfloat16).astype(jnp.float32)
    mid = (full - high).astype(jnp.bfloat16).astype(jnp.float32)
    low = full - high - mid
    row = lax.broadcasted_iota(jnp.int32, (TAIL, LANES), 0)
    lane = lax.broadcasted_iota(jnp.int32, (TAIL, LANES), 1)
    tile = jnp.where(row == 0, high, jnp.where(row == 1, mid, jnp.where(row == 2, low, 0.0)))
    return jnp.where(lane == 0, tile, 0.0).astype(jnp.bfloat16)


def small_call(kernel, shapes, *operands, weight=1):
    return pl.pallas_call(
        kernel,
        out_shape=shapes,
        compiler_params=pltpu.CompilerParams(vmem_limit_bytes=4 * MIB),
        cost_estimate=pl.CostEstimate(flops=0, bytes_accessed=weight * MIB, transcendentals=0),
    )(*operands)


def first_columns_kernel(block, token, first):
    first[...] = block[:, :, : first.shape[2]]


def first_columns(block, size, token):
    shape = block.shape[:2] + (size,)
    return small_call(
        first_columns_kernel, jax.ShapeDtypeStruct(shape, block.dtype), block, token
    )


def copies_kernel(block, token, first_rows, first_cols):
    first_rows[...] = block[:, : first_rows.shape[1], :]
    first_cols[...] = block[:, :, : first_cols.shape[2]]


def copies(block, size, token):
    parts, rows, cols = block.shape
    shapes = ((parts, size, cols), (parts, rows, size))
    return small_call(
        copies_kernel,
        tuple(jax.ShapeDtypeStruct(shape, block.dtype) for shape in shapes),
        block,
        token,
    )


def prepare_kernel(probe, intens, blocks, token, tables, measured, wide_probe, power):
    tables[...] = blocks[...]
    count, size, _ = intens.shape
    row = lax.broadcasted_iota(jnp.int32, (size, size), 0)
    col = lax.broadcasted_iota(jnp.int32, (size, size), 1)
    to_even_first = (col == jnp.where(row < size // 2, 2 * row, 2 * row - size + 1)).astype(
        jnp.float32
    )
    from_left = to_even_first.astype(jnp.bfloat16)
    from_right = (row == jnp.where(col < size // 2, 2 * col, 2 * col - size + 1)).astype(
        jnp.float32
    )
    from_right = from_right.astype(jnp.bfloat16)
    for slot in range(count):
        turned = dot(from_left, intens[slot]).astype(jnp.bfloat16)
        measured[slot] = jnp.sqrt(dot(turned, from_right))
    win = probe.shape[1]
    modes = probe.shape[2] // win
    largest = jnp.zeros((8, win), jnp.float32)
    for r in range(0, probe.shape[1], CHUNK):
        at = slice(r, r + CHUNK)
        total = jnp.zeros((CHUNK, win), jnp.float32)
        for k in range(modes):
            for part in range(2):
                p = probe[part, at, k * win : (k + 1) * win].astype(jnp.float32)
                wide_probe[part, at, k * win : (k + 1) * win] = p
                total = total + p * p
        largest = jnp.maximum(largest, jnp.max(total.reshape(CHUNK // 8, 8, win), axis=0))
    power[0, 0] = jnp.max(largest)


def prepare(probe, intens, token):
    win = probe.shape[1]
    blocks = dft_blocks(win)
    vmem = pl.BlockSpec(memory_space=pltpu.VMEM)
    return pl.pallas_call(
        prepare_kernel,
        out_shape=(
            jax.ShapeDtypeStruct(blocks.shape, jnp.bfloat16),
            jax.ShapeDtypeStruct(intens.shape, jnp.float32),
            jax.ShapeDtypeStruct(probe.shape, jnp.float32),
            jax.ShapeDtypeStruct((1, 1), jnp.float32),
        ),
        out_specs=(vmem, vmem, vmem, pl.BlockSpec(memory_space=pltpu.SMEM)),
        compiler_params=pltpu.CompilerParams(vmem_limit_bytes=8 * MIB),
    )(probe, intens, blocks, token)


def block_shapes(number, size, ways):
    if not ways:
        return (jax.ShapeDtypeStruct((number * size + TAIL, LANES), jnp.bfloat16),)
    sends = jax.ShapeDtypeStruct((number // ways * size + TAIL, LANES), jnp.bfloat16)
    return (jax.ShapeDtypeStruct((number // ways, size, LANES), jnp.float32),) + (sends,) * (ways - 1)


def put_block(j, total, outs):
    size = total.shape[0]
    if len(outs) == 1:
        outs[0][pl.ds(j * size, size), :] = total.astype(jnp.bfloat16)
    elif j % len(outs) == 0:
        outs[0][j // len(outs)] = total
    else:
        at = pl.ds(j // len(outs) * size, size)
        outs[j % len(outs)][at, :] = total.astype(jnp.bfloat16)


def put_weight(weight, outs):
    tile = in_three(weight)
    for sent in outs if len(outs) == 1 else outs[1:]:
        sent[pl.ds(sent.shape[0] - TAIL, TAIL), :] = tile


def weight_of(block):
    return jnp.sum(block[pl.ds(block.shape[0] - TAIL, TAIL), :].astype(jnp.float32))


def chip_sum_kernel(pixels, size, keep, received, norm, *outs):
    me = lax.axis_index("row")
    for j in range(keep.shape[0] // size):
        at = pl.ds(pl.multiple_of((j ^ me) * size, size), size)
        put_block(j, keep[at, :] + received[at, :].astype(jnp.float32), outs)
    put_weight(jnp.sum(norm[...]) / pixels, outs)


def chip_sum(keep, received, norm, pixels, number, ways):
    size = keep.shape[0] // number
    return small_call(
        functools.partial(chip_sum_kernel, pixels, size),
        block_shapes(number, size, ways),
        keep,
        received,
        norm,
    )


def scatter_sum_kernel(number, mine, sent, *refs):
    received, outs = refs[:number], refs[number:]
    size = mine.shape[1]
    for j in range(mine.shape[0]):
        total = mine[j]
        for block in received:
            total = total + block[pl.ds(j * size, size), :].astype(jnp.float32)
        put_block(j, total, outs)
    put_weight(sum([weight_of(block) for block in received], weight_of(sent)), outs)


def scatter_sum(mine, sent, received, ways):
    number, size, _ = mine.shape
    return small_call(
        functools.partial(scatter_sum_kernel, len(received)),
        block_shapes(number, size, ways),
        mine,
        sent,
        *received,
    )


def pair_up(terms):
    while len(terms) > 1:
        terms = [a + b for a, b in zip(terms[::2], terms[1::2])]
    return terms[0]


def exchange_sum_kernel(size, *refs):
    blocks, chunks = refs[:-1], refs[-1]
    for j in range((chunks.shape[0] - TAIL) // size):
        terms = [
            block[pl.ds((j ^ i) * size, size), :].astype(jnp.float32)
            for i, block in enumerate(blocks)
        ]
        chunks[pl.ds(j * size, size), :] = pair_up(terms).astype(jnp.bfloat16)
    put_weight(pair_up([weight_of(block) for block in blocks]), (chunks,))


def exchange_sum(blocks, size):
    return small_call(
        functools.partial(exchange_sum_kernel, size),
        jax.ShapeDtypeStruct(blocks[0].shape, jnp.bfloat16),
        *blocks,
    )


def copy_chunks(blocks, joined):
    at = 0
    for block in blocks:
        rows = block.shape[0] - TAIL
        joined[pl.ds(at, rows), :] = block[pl.ds(0, rows), :]
        at += rows
    joined[pl.ds(at, TAIL), :] = blocks[0][pl.ds(blocks[0].shape[0] - TAIL, TAIL), :]


def join_kernel(*refs):
    copy_chunks(refs[:-1], refs[-1])


def join(blocks):
    rows = sum(block.shape[0] - TAIL for block in blocks) + TAIL
    return small_call(join_kernel, jax.ShapeDtypeStruct((rows, LANES), blocks[0].dtype), *blocks)


def swap_rows(block, step):
    number = lax.axis_size("row")
    return lax.ppermute(block, "row", [(i, i ^ step) for i in range(number)])


def row_digits():
    number = lax.axis_size("row")
    if number & (number - 1) or number < 2:
        raise ValueError("row size")
    bits = number.bit_length() - 1
    return [(shift, 1 << min(2, bits - shift)) for shift in range(0, bits, 2)]


def probe_update_kernel(size, digits, *refs):
    *blocks, probe, token, new_probe, mine, other, updated, sems = refs
    copy_chunks(blocks[: len(blocks) // 2], mine)
    copy_chunks(blocks[len(blocks) // 2 :], other)
    _, win, modes, _ = updated.shape
    number = mine.shape[0] // size
    me = lax.axis_index("row")
    piece = min(size, CHUNK)
    on_left = lax.axis_index("col") == 0
    tail = pl.ds(number * size, TAIL)
    tails = mine[tail, :].astype(jnp.float32) + other[tail, :].astype(jnp.float32)
    factor = 4.0 / jnp.full((piece, LANES), jnp.sum(tails), jnp.float32)
    half = modes // 2

    def place(chunk):
        j = chunk ^ me
        at, span = 0, 1
        for shift, ways in reversed(digits):
            at = at + ((j >> shift) & (ways - 1)) * span
            span *= ways
        return at * size

    def update(part, b, m, r):
        block = ((m * 2 + part) * (win // LANES) + b) * win
        chunk, offset = divmod(block + r, size)
        at = pl.ds(pl.multiple_of(place(chunk) + offset, piece), piece)
        here = mine[at, :].astype(jnp.float32)
        there = other[at, :].astype(jnp.float32)
        low = jnp.where(on_left, here, there)
        high = jnp.where(on_left, there, here)
        for k, total in ((m, low), (half + m, high)):
            col = k * win + b * LANES
            old = probe[part, r : r + piece, col : col + LANES]
            updated[part, r : r + piece, k, b * LANES : (b + 1) * LANES] = old - factor * total

    stretch = win // 4
    copies = []
    for part in range(2):
        for start in range(0, win, stretch):
            for r in range(start, start + stretch, piece):
                for m in range(half):
                    for b in range(win // LANES):
                        update(part, b, m, r)
            at = (part, pl.ds(start, stretch))
            copies.append(
                pltpu.make_async_copy(updated.at[at], new_probe.at[at], sems.at[len(copies)])
            )
            copies[-1].start()
    for copy in copies:
        copy.wait()


def probe_update(mine, other, probe, token, shape, size, digits):
    vmem = pl.BlockSpec(memory_space=pltpu.VMEM)
    rows = sum(block.shape[0] - TAIL for block in mine) + TAIL
    operands = (*mine, *other, probe, token)
    return pl.pallas_call(
        functools.partial(probe_update_kernel, size, digits),
        out_shape=jax.ShapeDtypeStruct(shape, jnp.float32),
        in_specs=[vmem] * len(operands),
        out_specs=pl.BlockSpec(memory_space=pl.ANY),
        scratch_shapes=[
            pltpu.VMEM((rows, LANES), jnp.bfloat16),
            pltpu.VMEM((rows, LANES), jnp.bfloat16),
            pltpu.VMEM(shape, jnp.float32),
            pltpu.SemaphoreType.DMA((8,)),
        ],
        compiler_params=pltpu.CompilerParams(vmem_limit_bytes=8 * MIB),
    )(*operands)


def low_sum_kernel(first, low_grad, from_left, token, low_sum):
    win = from_left.shape[2]
    rows = from_left.shape[1] - low_grad.shape[1]
    for part in range(2):
        for r in range(0, low_sum.shape[1], CHUNK):
            at, of = slice(r, r + CHUNK), slice(first + r, first + r + CHUNK)
            arrived = from_left[part, rows + first + r : rows + first + r + CHUNK, :]
            total = low_grad[part, of, :win] + arrived.astype(jnp.float32)
            low_sum[part, at, :win] = total.astype(jnp.bfloat16)
            low_sum[part, at, win:] = low_grad[part, of, win:].astype(jnp.bfloat16)


def low_sum_of(first, count, low_grad, from_left, token):
    return small_call(
        functools.partial(low_sum_kernel, first),
        jax.ShapeDtypeStruct((2, count, low_grad.shape[2]), jnp.bfloat16),
        low_grad,
        from_left,
        token,
        weight=LOW_WEIGHT,
    )


def object_update_kernel(
    old, own_grad, from_left, above_first, above_last, new_object, token, updated, sems
):
    token[...] = jnp.zeros_like(token)
    win, split = from_left.shape[2], above_first.shape[1]
    depth = split + above_last.shape[1]
    rows = old.shape[1]
    stretch = rows // 2
    copies = []
    for part in range(2):
        for start in range(0, rows, stretch):
            for r in range(start, start + stretch, CHUNK):
                at = slice(r, r + CHUNK)
                total = own_grad[part, at, :]
                if r < split:
                    total = total + above_first[part, at, :].astype(jnp.float32)
                elif r < depth:
                    arrived = above_last[part, r - split : r - split + CHUNK, :]
                    total = total + arrived.astype(jnp.float32)
                new = old[part, at, :].astype(jnp.float32) - total
                arrived = from_left[part, at, :].astype(jnp.float32)
                updated[part, at, :win] = new[:, :win] - arrived
                updated[part, at, win:] = new[:, win:]
            at = (part, pl.ds(start, stretch))
            copies.append(
                pltpu.make_async_copy(updated.at[at], new_object.at[at], sems.at[len(copies)])
            )
            copies[-1].start()
    for copy in copies:
        copy.wait()


def object_update(old, own_grad, from_left, above_first, above_last):
    vmem = pl.BlockSpec(memory_space=pltpu.VMEM)
    return pl.pallas_call(
        object_update_kernel,
        out_shape=(
            jax.ShapeDtypeStruct(old.shape, jnp.float32),
            jax.ShapeDtypeStruct((8, LANES), jnp.float32),
        ),
        in_specs=[vmem] * 5,
        out_specs=(pl.BlockSpec(memory_space=pl.ANY), vmem),
        scratch_shapes=[pltpu.VMEM(old.shape, jnp.float32), pltpu.SemaphoreType.DMA((4,))],
        compiler_params=pltpu.CompilerParams(vmem_limit_bytes=4 * MIB),
    )(old, own_grad, from_left, above_first, above_last)


def swap_cores(block):
    return lax.ppermute(block, "col", [(0, 1), (1, 0)])


def body(object_field, probe_modes, positions, counts, intensities):
    win = probe_modes.shape[1]
    modes = probe_modes.shape[2]
    number = lax.axis_size("row")
    below_right = from_next_row(object_field[:, :win, :], 1)
    probe_flat = probe_modes.reshape(2, win, modes * win)
    first_rows, first_cols = copies(object_field, win, probe_flat)
    below_left = from_next_row(first_rows, 0)
    right = from_behind(first_cols, "col", -1)
    tables, measured, probe, power = prepare(probe_flat, intensities[0, 0], right)
    corner = from_behind(first_columns(below_right, win, tables), "col", -1)
    own_grad, low_grad, right_grad, keep, send, norm = position_gradients(
        positions[0, 0].T,
        counts.reshape(-1),
        power.reshape(1),
        object_field,
        (below_left, below_right),
        right,
        corner,
        probe,
        measured,
        tables,
    )
    half_rows = keep.size // LANES
    received = swap_cores(send.reshape(half_rows, LANES))
    from_left = from_behind(right_grad, "col", 1)
    digits = row_digits()
    size = half_rows // number
    ways = [digit[1] for digit in digits[:-1]] + [0]
    outs = chip_sum(keep.reshape(half_rows, LANES), received, norm, win * win, number, ways[0])
    for place, (shift, _) in enumerate(digits[:-1]):
        mine, *sends = outs
        received = [swap_rows(block, (i + 1) << shift) for i, block in enumerate(sends)]
        outs = scatter_sum(mine, sends[0], received, ways[place + 1])
    split = SPLIT * win // 8
    low_first = low_sum_of(0, split, low_grad, from_left, outs[0])
    above_first = from_behind(low_first, "row", 1)
    shift, count = digits[-1]
    partners = [swap_rows(outs[0], i << shift) for i in range(1, count)]
    gathered = exchange_sum(list(outs) + partners, size)
    low_last = low_sum_of(split, win - split, low_grad, from_left, gathered)
    above_last = from_behind(low_last, "row", 1)
    mine = [gathered]
    for shift, count in digits[-2::-1]:
        gathered = mine[0] if len(mine) == 1 else join(mine)
        mine = [gathered] + [swap_rows(gathered, i << shift) for i in range(1, count)]
    other = [swap_cores(block) for block in mine]
    new_object, token = object_update(
        object_field, own_grad, from_left, above_first, above_last
    )
    new_probe = probe_update(mine, other, probe, token, probe_modes.shape, size, digits)
    return (new_object, new_probe)


def solution(mesh):
    placed = (
        P(None, ("grp", "row"), "col"),
        P(None, None, "grp", None),
        P(("grp", "row"), "col", None, None),
        P(("grp", "row"), "col"),
        P(("grp", "row"), "col", None, None, None),
    )
    return jax.shard_map(
        body,
        mesh=mesh,
        in_specs=placed,
        out_specs=(P(None, ("grp", "row"), "col"), P(None, None, "grp", None)),
        check_vma=False,
    )
```

```python
import functools

import jax
import jax.numpy as jnp
import ml_dtypes
import numpy as np
from jax import lax
from jax.experimental import pallas as pl
from jax.experimental.pallas import tpu as pltpu
from jax.sharding import PartitionSpec as P

LANES = 128
CHUNK = 32
FINE = 16
TAIL = 16
MIB = 1 << 20
LOW_WEIGHT = 8
SPLIT = 4


def from_behind(block, axis, distance):
    devices = range(lax.axis_size(axis))
    route = [(i - distance, i) for i in devices if i - distance in devices]
    return lax.ppermute(block, axis, route)


def from_next_row(block, col):
    rows, cols = lax.axis_size("row"), lax.axis_size("col")
    route = [((r + 1) * cols + col, r * cols + col) for r in range(rows - 1)]
    return lax.ppermute(block, ("row", "col"), route)


def dft_blocks(win):
    grid = np.arange(win)
    angle = 2.0 * np.pi * (grid[:, None] * grid[None, :] % win) / win
    factor = 1.0 / np.sqrt(win)
    cos_table = (np.cos(angle) * factor).astype(ml_dtypes.bfloat16)
    sin_table = (np.sin(angle) * factor).astype(ml_dtypes.bfloat16)
    blocks = []
    for parity in range(2):
        cos_part, sin_part = cos_table[parity::2, : win // 2], sin_table[parity::2, : win // 2]
        blocks.append(np.block([[cos_part, sin_part], [-sin_part, cos_part]]))
    return np.stack(blocks + [block.T for block in blocks])


def dot(left, right):
    return jnp.dot(left, right, preferred_element_type=jnp.float32)


def gradient_kernel(
    modes,
    starts,
    count,
    power,
    own,
    below_left,
    below_right,
    right,
    corner,
    probe,
    measured,
    tables,
    own_grad,
    low_grad,
    right_grad,
    keep_out,
    send_out,
    norm_out,
    field,
    grad,
    window,
    wide,
    tall,
    wave,
    probe_sum,
):
    win = probe.shape[1]
    rows, cols = own.shape[1], own.shape[2]
    half = win // 2
    fine = range(0, win, FINE)
    spread = win // LANES + 1
    col_index = lax.axis_index("col")
    row_anchor = lax.axis_index("row") * rows
    col_anchor = col_index * cols

    def put_blocks(part, row, first, values):
        for b in range(values.shape[1] // LANES):
            field[part, first + b, row : row + CHUNK, :] = values[:, b * LANES : (b + 1) * LANES]

    grad[...] = jnp.zeros_like(grad)
    probe_sum[...] = jnp.zeros_like(probe_sum)
    norm_out[...] = jnp.zeros_like(norm_out)
    for row_at, col_at, *sources in (
        (0, 0, own),
        (0, cols, right),
        (rows, 0, below_left, below_right),
        (rows, cols, corner),
    ):
        for part in range(2):
            for r in range(0, sources[0].shape[1], CHUNK):
                pieces = [source[part, r : r + CHUNK, :].astype(jnp.float32) for source in sources]
                put_blocks(part, row_at + r, col_at // LANES, sum(pieces[1:], pieces[0]))
    lane = lax.broadcasted_iota(jnp.int32, (FINE, LANES), 1)

    def one_position(slot, carry):
        y, x = starts[0, slot] - row_anchor, starts[1, slot] - col_anchor
        base = x // LANES
        shift = x - base * LANES
        back_shift = (LANES - shift) % LANES
        keep = lane < LANES - shift
        for r in range(0, half, FINE):
            objs = []
            for start in (r, r + half):
                at = pl.ds(start, FINE)
                obj = []
                for part in range(2):
                    turned = [
                        pltpu.roll(field[part, base + b, pl.ds(y + start, FINE), :], back_shift, 1)
                        for b in range(spread)
                    ]
                    piece = jnp.concatenate(
                        [jnp.where(keep, a, b) for a, b in zip(turned[:-1], turned[1:])], axis=1
                    )
                    window[part, at, :] = piece
                    obj.append(piece)
                squares = obj[0] * obj[0] + obj[1] * obj[1]
                norm_out[...] += jnp.sum(squares.reshape(FINE // 8, 8, win), axis=0)
                objs.append(obj)
            for k in range(modes):
                cs = pl.ds(k * win, win)
                exits = []
                for start, (o_re, o_im) in zip((r, r + half), objs):
                    p_re, p_im = probe[0, pl.ds(start, FINE), cs], probe[1, pl.ds(start, FINE), cs]
                    exits.append((p_re * o_re - p_im * o_im, p_re * o_im + p_im * o_re))
                for part in range(2):
                    low, high = exits[0][part], exits[1][part]
                    at = pl.ds(part * half + r, FINE)
                    wide[k, 0, at, :] = (low + high).astype(jnp.bfloat16)
                    wide[k, 1, at, :] = (low - high).astype(jnp.bfloat16)

        for k in range(modes):
            for parity in range(2):
                out = dot(tables[parity], wide[k, parity])
                at = pl.ds(k * win + parity * half, half)
                for part in range(2):
                    low = out[part * half : (part + 1) * half, :half]
                    high = out[part * half : (part + 1) * half, half:]
                    to = pl.ds(part * half, half)
                    tall[0, at, to] = (low + high).astype(jnp.bfloat16)
                    tall[1, at, to] = (low - high).astype(jnp.bfloat16)
        for parity in range(2):
            wave[parity] = dot(tall[parity], tables[2 + parity])

        for r in fine:
            for parity in range(2):
                waves = []
                total = jnp.zeros((FINE, half), jnp.float32)
                for k in range(modes):
                    ka = pl.ds(k * win + r, FINE)
                    waves.append((wave[parity, ka, :half], wave[parity, ka, half:]))
                    total = total + (waves[k][0] * waves[k][0] + waves[k][1] * waves[k][1])
                gs = pl.ds(parity * half, half)
                amp = measured[slot, pl.ds(r, FINE), gs]
                ratio = 1.0 - amp * lax.rsqrt(jnp.maximum(total, 1.0))
                for k in range(modes):
                    for part in range(2):
                        at = pl.ds(part * half + r % half, FINE)
                        wide[k, r // half, at, gs] = (waves[k][part] * ratio).astype(jnp.bfloat16)

        for k in range(modes):
            even = dot(tables[2], wide[k, 0])
            odd = dot(tables[3], wide[k, 1])
            for place, out in enumerate((even + odd, even - odd)):
                at = pl.ds(k * win + place * half, half)
                for part in range(2):
                    for parity in range(2):
                        tall[parity, at, part * half : (part + 1) * half] = out[
                            part * half : (part + 1) * half, parity * half : (parity + 1) * half
                        ].astype(jnp.bfloat16)
        for parity in range(2):
            wave[parity] = dot(tall[parity], tables[parity])

        keep_high = lane >= shift
        for r in fine:
            at = pl.ds(r, FINE)
            sums = [[jnp.zeros((FINE, LANES), jnp.float32) for _ in range(2)] for _ in range(2)]
            for b in range(2):
                bs = pl.ds(b * half, half)
                o_re, o_im = window[0, at, bs], window[1, at, bs]
                for k in range(modes):
                    cs = pl.ds(k * win + b * half, half)
                    ka = pl.ds(k * win + r, FINE)
                    even, odd = wave[0, ka, :], wave[1, ka, :]
                    d = even + odd if b == 0 else even - odd
                    d_re, d_im = d[:, :half], d[:, half:]
                    p_re, p_im = probe[0, at, cs], probe[1, at, cs]
                    sums[0][b] = sums[0][b] + (p_re * d_re + p_im * d_im)
                    sums[1][b] = sums[1][b] + (p_re * d_im - p_im * d_re)
                    probe_sum[k, 0, b, at, :] += o_re * d_re + o_im * d_im
                    probe_sum[k, 1, b, at, :] += o_re * d_im - o_im * d_re
            for part in range(2):
                turned = [pltpu.roll(piece, shift, 1) for piece in sums[part]]
                turned = [jnp.zeros_like(turned[0])] + turned + [jnp.zeros_like(turned[0])]
                for b in range(spread):
                    grad[part, base + b, pl.ds(y + r, FINE), :] += jnp.where(
                        keep_high, turned[b + 1], turned[b]
                    )
        return carry

    lax.fori_loop(0, count[0], one_position, 0)
    blocks = win // LANES
    for k in range(modes):
        keep_out[k] = probe_sum[k, col_index]
        for b in range(blocks):
            at = pl.ds((k * blocks + b) * win, win)
            send_out[at, :] = probe_sum[k, 1 - col_index, b].astype(jnp.bfloat16)
    put_weight(jnp.sum(norm_out[...]) / (win * win), (send_out,))
    scale = 1.0 / jnp.full((8, LANES), power[0], jnp.float32)
    scale = jnp.concatenate([scale] * (CHUNK // 8), axis=0)

    def take_blocks(part, at, first, number):
        return jnp.concatenate(
            [grad[part, first + b, at, :] * scale for b in range(number)], axis=1
        )

    for part in range(2):
        for r in range(0, rows + win, CHUNK):
            at = pl.ds(r, CHUNK)
            piece = take_blocks(part, at, cols // LANES, win // LANES)
            right_grad[part, at, :] = piece.astype(jnp.bfloat16)
        for r in range(0, rows, CHUNK):
            at = pl.ds(r, CHUNK)
            own_grad[part, at, :] = take_blocks(part, at, 0, cols // LANES)
        for r in range(0, win, CHUNK):
            at, of = pl.ds(r, CHUNK), pl.ds(rows + r, CHUNK)
            low_grad[part, at, :] = take_blocks(part, of, 0, cols // LANES)


def position_gradients(starts, count, power, own, below, right, corner, probe, measured, tables):
    win, modes = probe.shape[1], probe.shape[2] // probe.shape[1]
    rows, cols = own.shape[1:]
    f32, bf16 = jnp.float32, jnp.bfloat16
    smem = pl.BlockSpec(memory_space=pltpu.SMEM)
    vmem = pl.BlockSpec(memory_space=pltpu.VMEM)
    if win != 2 * LANES:
        raise ValueError("window size")
    slots = measured.shape[0]
    flops = 16 * slots * modes * win**3
    part_blocks = (modes, win // LANES, win, LANES)
    part_rows = modes * win // LANES * win
    return pl.pallas_call(
        functools.partial(gradient_kernel, modes),
        out_shape=(
            jax.ShapeDtypeStruct((2, rows, cols), f32),
            jax.ShapeDtypeStruct((2, win, cols), f32),
            jax.ShapeDtypeStruct((2, rows + win, win), bf16),
            jax.ShapeDtypeStruct(part_blocks, f32),
            jax.ShapeDtypeStruct((part_rows + TAIL, LANES), bf16),
            jax.ShapeDtypeStruct((8, win), f32),
        ),
        in_specs=[smem] * 3 + [vmem] * 8,
        out_specs=(vmem,) * 6,
        scratch_shapes=[
            pltpu.VMEM((2, (cols + win) // LANES, rows + win, LANES), f32),
            pltpu.VMEM((2, (cols + win) // LANES, rows + win, LANES), f32),
            pltpu.VMEM((2, win, win), f32),
            pltpu.VMEM((modes, 2, win, win), bf16),
            pltpu.VMEM((2, modes * win, win), bf16),
            pltpu.VMEM((2, modes * win, win), f32),
            pltpu.VMEM((modes, 2, win // LANES, win, LANES), f32),
        ],
        compiler_params=pltpu.CompilerParams(vmem_limit_bytes=26 * MIB),
        cost_estimate=pl.CostEstimate(flops=flops, bytes_accessed=12 << 20, transcendentals=0),
    )(starts, count, power, own, *below, right, corner, probe, measured, tables)


def in_three(value):
    full = jnp.full((TAIL, LANES), value, jnp.float32)
    high = full.astype(jnp.bfloat16).astype(jnp.float32)
    mid = (full - high).astype(jnp.bfloat16).astype(jnp.float32)
    low = full - high - mid
    row = lax.broadcasted_iota(jnp.int32, (TAIL, LANES), 0)
    lane = lax.broadcasted_iota(jnp.int32, (TAIL, LANES), 1)
    tile = jnp.where(row == 0, high, jnp.where(row == 1, mid, jnp.where(row == 2, low, 0.0)))
    return jnp.where(lane == 0, tile, 0.0).astype(jnp.bfloat16)


def small_call(kernel, shapes, *operands, weight=1):
    return pl.pallas_call(
        kernel,
        out_shape=shapes,
        compiler_params=pltpu.CompilerParams(vmem_limit_bytes=4 * MIB),
        cost_estimate=pl.CostEstimate(flops=0, bytes_accessed=weight * MIB, transcendentals=0),
    )(*operands)


def first_columns_kernel(block, token, first):
    first[...] = block[:, :, : first.shape[2]]


def first_columns(block, size, token):
    shape = block.shape[:2] + (size,)
    return small_call(
        first_columns_kernel, jax.ShapeDtypeStruct(shape, block.dtype), block, token
    )


def copies_kernel(block, token, first_rows, first_cols):
    first_rows[...] = block[:, : first_rows.shape[1], :]
    first_cols[...] = block[:, :, : first_cols.shape[2]]


def copies(block, size, token):
    parts, rows, cols = block.shape
    shapes = ((parts, size, cols), (parts, rows, size))
    return small_call(
        copies_kernel,
        tuple(jax.ShapeDtypeStruct(shape, block.dtype) for shape in shapes),
        block,
        token,
    )


def prepare_kernel(probe, intens, blocks, token, tables, measured, wide_probe, power):
    tables[...] = blocks[...]
    count, size, _ = intens.shape
    row = lax.broadcasted_iota(jnp.int32, (size, size), 0)
    col = lax.broadcasted_iota(jnp.int32, (size, size), 1)
    to_even_first = (col == jnp.where(row < size // 2, 2 * row, 2 * row - size + 1)).astype(
        jnp.float32
    )
    from_left = to_even_first.astype(jnp.bfloat16)
    from_right = (row == jnp.where(col < size // 2, 2 * col, 2 * col - size + 1)).astype(
        jnp.float32
    )
    from_right = from_right.astype(jnp.bfloat16)
    for slot in range(count):
        turned = dot(from_left, intens[slot]).astype(jnp.bfloat16)
        measured[slot] = jnp.sqrt(dot(turned, from_right))
    win = probe.shape[1]
    modes = probe.shape[2] // win
    largest = jnp.zeros((8, win), jnp.float32)
    for r in range(0, probe.shape[1], CHUNK):
        at = slice(r, r + CHUNK)
        total = jnp.zeros((CHUNK, win), jnp.float32)
        for k in range(modes):
            for part in range(2):
                p = probe[part, at, k * win : (k + 1) * win].astype(jnp.float32)
                wide_probe[part, at, k * win : (k + 1) * win] = p
                total = total + p * p
        largest = jnp.maximum(largest, jnp.max(total.reshape(CHUNK // 8, 8, win), axis=0))
    power[0, 0] = jnp.max(largest)


def prepare(probe, intens, token):
    win = probe.shape[1]
    blocks = dft_blocks(win)
    vmem = pl.BlockSpec(memory_space=pltpu.VMEM)
    return pl.pallas_call(
        prepare_kernel,
        out_shape=(
            jax.ShapeDtypeStruct(blocks.shape, jnp.bfloat16),
            jax.ShapeDtypeStruct(intens.shape, jnp.float32),
            jax.ShapeDtypeStruct(probe.shape, jnp.float32),
            jax.ShapeDtypeStruct((1, 1), jnp.float32),
        ),
        out_specs=(vmem, vmem, vmem, pl.BlockSpec(memory_space=pltpu.SMEM)),
        compiler_params=pltpu.CompilerParams(vmem_limit_bytes=8 * MIB),
    )(probe, intens, blocks, token)


def block_shapes(number, size, ways):
    if not ways:
        return (jax.ShapeDtypeStruct((number * size + TAIL, LANES), jnp.bfloat16),)
    sends = jax.ShapeDtypeStruct((number // ways * size + TAIL, LANES), jnp.bfloat16)
    return (jax.ShapeDtypeStruct((number // ways, size, LANES), jnp.float32),) + (sends,) * (ways - 1)


def put_block(j, total, outs):
    size = total.shape[0]
    if len(outs) == 1:
        outs[0][pl.ds(j * size, size), :] = total.astype(jnp.bfloat16)
    elif j % len(outs) == 0:
        outs[0][j // len(outs)] = total
    else:
        at = pl.ds(j // len(outs) * size, size)
        outs[j % len(outs)][at, :] = total.astype(jnp.bfloat16)


def put_weight(weight, outs):
    tile = in_three(weight)
    for sent in outs if len(outs) == 1 else outs[1:]:
        sent[pl.ds(sent.shape[0] - TAIL, TAIL), :] = tile


def weight_of(block):
    return jnp.sum(block[pl.ds(block.shape[0] - TAIL, TAIL), :].astype(jnp.float32))


def chip_sum_kernel(pixels, size, keep, received, norm, *outs):
    me = lax.axis_index("row")
    for j in range(keep.shape[0] // size):
        at = pl.ds(pl.multiple_of((j ^ me) * size, size), size)
        put_block(j, keep[at, :] + received[at, :].astype(jnp.float32), outs)
    put_weight(jnp.sum(norm[...]) / pixels + weight_of(received), outs)


def chip_sum(keep, received, norm, pixels, number, ways):
    size = keep.shape[0] // number
    return small_call(
        functools.partial(chip_sum_kernel, pixels, size),
        block_shapes(number, size, ways),
        keep,
        received,
        norm,
    )


def scatter_sum_kernel(number, mine, sent, *refs):
    received, outs = refs[:number], refs[number:]
    size = mine.shape[1]
    for j in range(mine.shape[0]):
        total = mine[j]
        for block in received:
            total = total + block[pl.ds(j * size, size), :].astype(jnp.float32)
        put_block(j, total, outs)
    put_weight(pair_up([weight_of(block) for block in (sent, *received)]), outs)


def scatter_sum(mine, sent, received, ways):
    number, size, _ = mine.shape
    return small_call(
        functools.partial(scatter_sum_kernel, len(received)),
        block_shapes(number, size, ways),
        mine,
        sent,
        *received,
    )


def pair_up(terms):
    while len(terms) > 1:
        terms = [a + b for a, b in zip(terms[::2], terms[1::2])]
    return terms[0]


def exchange_sum_kernel(size, *refs):
    blocks, chunks = refs[:-1], refs[-1]
    for j in range((chunks.shape[0] - TAIL) // size):
        terms = [
            block[pl.ds((j ^ i) * size, size), :].astype(jnp.float32)
            for i, block in enumerate(blocks)
        ]
        chunks[pl.ds(j * size, size), :] = pair_up(terms).astype(jnp.bfloat16)
    put_weight(pair_up([weight_of(block) for block in blocks]), (chunks,))


def exchange_sum(blocks, size):
    return small_call(
        functools.partial(exchange_sum_kernel, size),
        jax.ShapeDtypeStruct(blocks[0].shape, jnp.bfloat16),
        *blocks,
    )


def copy_chunks(blocks, joined):
    at = 0
    for block in blocks:
        rows = block.shape[0] - TAIL
        joined[pl.ds(at, rows), :] = block[pl.ds(0, rows), :]
        at += rows
    joined[pl.ds(at, TAIL), :] = blocks[0][pl.ds(blocks[0].shape[0] - TAIL, TAIL), :]


def join_kernel(*refs):
    copy_chunks(refs[:-1], refs[-1])


def join(blocks):
    rows = sum(block.shape[0] - TAIL for block in blocks) + TAIL
    return small_call(join_kernel, jax.ShapeDtypeStruct((rows, LANES), blocks[0].dtype), *blocks)


def swap_rows(block, step):
    number = lax.axis_size("row")
    return lax.ppermute(block, "row", [(i, i ^ step) for i in range(number)])


def row_digits():
    number = lax.axis_size("row")
    if number & (number - 1) or number < 2:
        raise ValueError("row size")
    bits = number.bit_length() - 1
    return [(shift, 1 << min(2, bits - shift)) for shift in range(0, bits, 2)]


def probe_update_kernel(size, digits, mine, *refs):
    *blocks, probe, new_probe, gathered, updated, sems = refs
    copy_chunks(blocks, gathered)
    win, modes, _ = updated.shape
    col_index = lax.axis_index("col")
    part = col_index if mine else 1 - col_index
    me = lax.axis_index("row")
    piece = min(size, CHUNK)
    factor = 4.0 / jnp.full((piece, LANES), weight_of(blocks[0]), jnp.float32)

    def place(chunk):
        j = chunk ^ me
        at, span = 0, 1
        for shift, ways in reversed(digits):
            at = at + ((j >> shift) & (ways - 1)) * span
            span *= ways
        return at * size

    def update(k, b, r):
        chunk, offset = divmod((k * (win // LANES) + b) * win + r, size)
        at = pl.ds(pl.multiple_of(place(chunk) + offset, piece), piece)
        total = gathered[at, :].astype(jnp.float32)
        col = k * win + b * LANES
        old = probe[part, r : r + piece, col : col + LANES]
        updated[r : r + piece, k, b * LANES : (b + 1) * LANES] = old - factor * total

    stretch = win // 4
    copies = []
    for start in range(0, win, stretch):
        for r in range(start, start + stretch, piece):
            for k in range(modes):
                for b in range(win // LANES):
                    update(k, b, r)
        at = pl.ds(start, stretch)
        copies.append(
            pltpu.make_async_copy(updated.at[at], new_probe.at[part, at], sems.at[len(copies)])
        )
        copies[-1].start()
    for copy in copies:
        copy.wait()


def probe_update(blocks, probe, shape, size, digits, first_result=None, token=None):
    vmem, anywhere = pl.BlockSpec(memory_space=pltpu.VMEM), pl.BlockSpec(memory_space=pl.ANY)
    rows = sum(block.shape[0] - TAIL for block in blocks) + TAIL
    operands = [*blocks, probe]
    mine = first_result is None
    kernel = functools.partial(probe_update_kernel, size, digits, mine)
    if not mine:
        number = len(operands)

        def kernel(*refs):
            probe_update_kernel(size, digits, mine, *refs[:number], *refs[number + 2 :])

    extra = [] if mine else [token, first_result]
    return pl.pallas_call(
        kernel,
        out_shape=jax.ShapeDtypeStruct(shape, jnp.float32),
        in_specs=[vmem] * len(operands) + [vmem, anywhere][: len(extra)],
        out_specs=anywhere,
        scratch_shapes=[
            pltpu.VMEM((rows, LANES), jnp.bfloat16),
            pltpu.VMEM(shape[1:], jnp.float32),
            pltpu.SemaphoreType.DMA((4,)),
        ],
        input_output_aliases={} if mine else {len(operands) + 1: 0},
        compiler_params=pltpu.CompilerParams(vmem_limit_bytes=4 * MIB),
    )(*operands, *extra)


def low_sum_kernel(first, low_grad, from_left, token, low_sum):
    win = from_left.shape[2]
    rows = from_left.shape[1] - low_grad.shape[1]
    for part in range(2):
        for r in range(0, low_sum.shape[1], CHUNK):
            at, of = slice(r, r + CHUNK), slice(first + r, first + r + CHUNK)
            arrived = from_left[part, rows + first + r : rows + first + r + CHUNK, :]
            total = low_grad[part, of, :win] + arrived.astype(jnp.float32)
            low_sum[part, at, :win] = total.astype(jnp.bfloat16)
            low_sum[part, at, win:] = low_grad[part, of, win:].astype(jnp.bfloat16)


def low_sum_of(first, count, low_grad, from_left, token):
    return small_call(
        functools.partial(low_sum_kernel, first),
        jax.ShapeDtypeStruct((2, count, low_grad.shape[2]), jnp.bfloat16),
        low_grad,
        from_left,
        token,
        weight=LOW_WEIGHT,
    )


def object_update_kernel(old, own_grad, from_left, above_first, above_last, new_object, token):
    token[...] = jnp.zeros_like(token)
    win, split = from_left.shape[2], above_first.shape[1]
    depth = split + above_last.shape[1]
    for part in range(2):
        for r in range(0, old.shape[1], CHUNK):
            at = slice(r, r + CHUNK)
            total = own_grad[part, at, :]
            if r < split:
                total = total + above_first[part, at, :].astype(jnp.float32)
            elif r < depth:
                total = total + above_last[part, r - split : r - split + CHUNK, :].astype(jnp.float32)
            updated = old[part, at, :].astype(jnp.float32) - total
            arrived = from_left[part, at, :].astype(jnp.float32)
            new_object[part, at, :win] = updated[:, :win] - arrived
            new_object[part, at, win:] = updated[:, win:]


def object_update(old, own_grad, from_left, above_first, above_last):
    return small_call(
        object_update_kernel,
        (
            jax.ShapeDtypeStruct(old.shape, jnp.float32),
            jax.ShapeDtypeStruct((8, LANES), jnp.float32),
        ),
        old,
        own_grad,
        from_left,
        above_first,
        above_last,
    )


def swap_cores(block):
    return lax.ppermute(block, "col", [(0, 1), (1, 0)])


def body(object_field, probe_modes, positions, counts, intensities):
    win = probe_modes.shape[1]
    modes = probe_modes.shape[2]
    number = lax.axis_size("row")
    below_right = from_next_row(object_field[:, :win, :], 1)
    probe_flat = probe_modes.reshape(2, win, modes * win)
    first_rows, first_cols = copies(object_field, win, probe_flat)
    below_left = from_next_row(first_rows, 0)
    right = from_behind(first_cols, "col", -1)
    tables, measured, probe, power = prepare(probe_flat, intensities[0, 0], right)
    corner = from_behind(first_columns(below_right, win, tables), "col", -1)
    own_grad, low_grad, right_grad, keep, send, norm = position_gradients(
        positions[0, 0].T,
        counts.reshape(-1),
        power.reshape(1),
        object_field,
        (below_left, below_right),
        right,
        corner,
        probe,
        measured,
        tables,
    )
    half_rows = keep.size // LANES
    received = swap_cores(send)
    from_left = from_behind(right_grad, "col", 1)
    digits = row_digits()
    size = half_rows // number
    ways = [digit[1] for digit in digits[:-1]] + [0]
    outs = chip_sum(keep.reshape(half_rows, LANES), received, norm, win * win, number, ways[0])
    for place, (shift, _) in enumerate(digits[:-1]):
        mine, *sends = outs
        received = [swap_rows(block, (i + 1) << shift) for i, block in enumerate(sends)]
        outs = scatter_sum(mine, sends[0], received, ways[place + 1])
    split = SPLIT * win // 8
    low_first = low_sum_of(0, split, low_grad, from_left, outs[0])
    above_first = from_behind(low_first, "row", 1)
    shift, count = digits[-1]
    partners = [swap_rows(outs[0], i << shift) for i in range(1, count)]
    gathered = exchange_sum(list(outs) + partners, size)
    low_last = low_sum_of(split, win - split, low_grad, from_left, gathered)
    above_last = from_behind(low_last, "row", 1)
    mine = [gathered]
    for shift, count in digits[-2::-1]:
        gathered = mine[0] if len(mine) == 1 else join(mine)
        arrived = [swap_rows(gathered, i << shift) for i in reversed(range(1, count))]
        mine = [gathered] + arrived[::-1]
    other = [swap_cores(block) for block in mine]
    new_object, token = object_update(
        object_field, own_grad, from_left, above_first, above_last
    )
    shape = probe_modes.shape
    first_result = probe_update(mine, probe, shape, size, digits)
    new_probe = probe_update(other, probe, shape, size, digits, first_result, token)
    return (new_object, new_probe)


def solution(mesh):
    placed = (
        P(None, ("grp", "row"), "col"),
        P(None, None, "grp", None),
        P(("grp", "row"), "col", None, None),
        P(("grp", "row"), "col"),
        P(("grp", "row"), "col", None, None, None),
    )
    return jax.shard_map(
        body,
        mesh=mesh,
        in_specs=placed,
        out_specs=(P(None, ("grp", "row"), "col"), P(None, None, "grp", None)),
        check_vma=False,
    )
```

```python
import functools

import jax
import jax.numpy as jnp
import ml_dtypes
import numpy as np
from jax import lax
from jax.experimental import pallas as pl
from jax.experimental.pallas import tpu as pltpu
from jax.sharding import PartitionSpec as P

LANES = 128
CHUNK = 32
FINE = 16
TAIL = 16
MIB = 1 << 20
LOW_WEIGHT = 8
SPLIT = 4


def from_behind(block, axis, distance):
    devices = range(lax.axis_size(axis))
    route = [(i - distance, i) for i in devices if i - distance in devices]
    return lax.ppermute(block, axis, route)


def from_next_row(block, col):
    rows, cols = lax.axis_size("row"), lax.axis_size("col")
    route = [((r + 1) * cols + col, r * cols + col) for r in range(rows - 1)]
    return lax.ppermute(block, ("row", "col"), route)


def dft_blocks(win):
    grid = np.arange(win)
    angle = 2.0 * np.pi * (grid[:, None] * grid[None, :] % win) / win
    factor = 1.0 / np.sqrt(win)
    cos_table = (np.cos(angle) * factor).astype(ml_dtypes.bfloat16)
    sin_table = (np.sin(angle) * factor).astype(ml_dtypes.bfloat16)
    blocks = []
    for parity in range(2):
        cos_part, sin_part = cos_table[parity::2, : win // 2], sin_table[parity::2, : win // 2]
        blocks.append(np.block([[cos_part, sin_part], [-sin_part, cos_part]]))
    return np.stack(blocks + [block.T for block in blocks])


def dot(left, right):
    return jnp.dot(left, right, preferred_element_type=jnp.float32)


def gradient_kernel(
    modes,
    starts,
    count,
    power,
    own,
    below_left,
    below_right,
    right,
    corner,
    probe,
    measured,
    tables,
    own_grad,
    low_grad,
    right_grad,
    keep_out,
    send_out,
    norm_out,
    field,
    grad,
    window,
    wide,
    tall,
    wave,
    probe_sum,
):
    win = probe.shape[1]
    rows, cols = own.shape[1], own.shape[2]
    half = win // 2
    fine = range(0, win, FINE)
    spread = win // LANES + 1
    col_index = lax.axis_index("col")
    row_anchor = lax.axis_index("row") * rows
    col_anchor = col_index * cols

    def put_blocks(part, row, first, values):
        for b in range(values.shape[1] // LANES):
            field[part, first + b, row : row + CHUNK, :] = values[:, b * LANES : (b + 1) * LANES]

    grad[...] = jnp.zeros_like(grad)
    probe_sum[...] = jnp.zeros_like(probe_sum)
    norm_out[...] = jnp.zeros_like(norm_out)
    for row_at, col_at, *sources in (
        (0, 0, own),
        (0, cols, right),
        (rows, 0, below_left, below_right),
        (rows, cols, corner),
    ):
        for part in range(2):
            for r in range(0, sources[0].shape[1], CHUNK):
                pieces = [source[part, r : r + CHUNK, :].astype(jnp.float32) for source in sources]
                put_blocks(part, row_at + r, col_at // LANES, sum(pieces[1:], pieces[0]))
    lane = lax.broadcasted_iota(jnp.int32, (FINE, LANES), 1)

    def one_position(slot, carry):
        y, x = starts[0, slot] - row_anchor, starts[1, slot] - col_anchor
        base = x // LANES
        shift = x - base * LANES
        back_shift = (LANES - shift) % LANES
        keep = lane < LANES - shift
        for r in range(0, half, FINE):
            objs = []
            for start in (r, r + half):
                at = pl.ds(start, FINE)
                obj = []
                for part in range(2):
                    turned = [
                        pltpu.roll(field[part, base + b, pl.ds(y + start, FINE), :], back_shift, 1)
                        for b in range(spread)
                    ]
                    piece = jnp.concatenate(
                        [jnp.where(keep, a, b) for a, b in zip(turned[:-1], turned[1:])], axis=1
                    )
                    window[part, at, :] = piece
                    obj.append(piece)
                squares = obj[0] * obj[0] + obj[1] * obj[1]
                norm_out[...] += jnp.sum(squares.reshape(FINE // 8, 8, win), axis=0)
                objs.append(obj)
            for k in range(modes):
                cs = pl.ds(k * win, win)
                exits = []
                for start, (o_re, o_im) in zip((r, r + half), objs):
                    p_re, p_im = probe[0, pl.ds(start, FINE), cs], probe[1, pl.ds(start, FINE), cs]
                    exits.append((p_re * o_re - p_im * o_im, p_re * o_im + p_im * o_re))
                for part in range(2):
                    low, high = exits[0][part], exits[1][part]
                    at = pl.ds(part * half + r, FINE)
                    wide[k, 0, at, :] = (low + high).astype(jnp.bfloat16)
                    wide[k, 1, at, :] = (low - high).astype(jnp.bfloat16)

        for k in range(modes):
            for parity in range(2):
                out = dot(tables[parity], wide[k, parity])
                at = pl.ds(k * win + parity * half, half)
                for part in range(2):
                    low = out[part * half : (part + 1) * half, :half]
                    high = out[part * half : (part + 1) * half, half:]
                    to = pl.ds(part * half, half)
                    tall[0, at, to] = (low + high).astype(jnp.bfloat16)
                    tall[1, at, to] = (low - high).astype(jnp.bfloat16)
        for parity in range(2):
            wave[parity] = dot(tall[parity], tables[2 + parity])

        for r in fine:
            for parity in range(2):
                waves = []
                total = jnp.zeros((FINE, half), jnp.float32)
                for k in range(modes):
                    ka = pl.ds(k * win + r, FINE)
                    waves.append((wave[parity, ka, :half], wave[parity, ka, half:]))
                    total = total + (waves[k][0] * waves[k][0] + waves[k][1] * waves[k][1])
                gs = pl.ds(parity * half, half)
                amp = measured[slot, pl.ds(r, FINE), gs]
                ratio = 1.0 - amp * lax.rsqrt(jnp.maximum(total, 1.0))
                for k in range(modes):
                    for part in range(2):
                        at = pl.ds(part * half + r % half, FINE)
                        wide[k, r // half, at, gs] = (waves[k][part] * ratio).astype(jnp.bfloat16)

        for k in range(modes):
            even = dot(tables[2], wide[k, 0])
            odd = dot(tables[3], wide[k, 1])
            for place, out in enumerate((even + odd, even - odd)):
                at = pl.ds(k * win + place * half, half)
                for part in range(2):
                    for parity in range(2):
                        tall[parity, at, part * half : (part + 1) * half] = out[
                            part * half : (part + 1) * half, parity * half : (parity + 1) * half
                        ].astype(jnp.bfloat16)
        for parity in range(2):
            wave[parity] = dot(tall[parity], tables[parity])

        keep_high = lane >= shift
        for r in fine:
            at = pl.ds(r, FINE)
            sums = [[jnp.zeros((FINE, LANES), jnp.float32) for _ in range(2)] for _ in range(2)]
            for b in range(2):
                bs = pl.ds(b * half, half)
                o_re, o_im = window[0, at, bs], window[1, at, bs]
                for k in range(modes):
                    cs = pl.ds(k * win + b * half, half)
                    ka = pl.ds(k * win + r, FINE)
                    even, odd = wave[0, ka, :], wave[1, ka, :]
                    d = even + odd if b == 0 else even - odd
                    d_re, d_im = d[:, :half], d[:, half:]
                    p_re, p_im = probe[0, at, cs], probe[1, at, cs]
                    sums[0][b] = sums[0][b] + (p_re * d_re + p_im * d_im)
                    sums[1][b] = sums[1][b] + (p_re * d_im - p_im * d_re)
                    probe_sum[k, 0, b, at, :] += o_re * d_re + o_im * d_im
                    probe_sum[k, 1, b, at, :] += o_re * d_im - o_im * d_re
            for part in range(2):
                turned = [pltpu.roll(piece, shift, 1) for piece in sums[part]]
                turned = [jnp.zeros_like(turned[0])] + turned + [jnp.zeros_like(turned[0])]
                for b in range(spread):
                    grad[part, base + b, pl.ds(y + r, FINE), :] += jnp.where(
                        keep_high, turned[b + 1], turned[b]
                    )
        return carry

    lax.fori_loop(0, count[0], one_position, 0)
    blocks = win // LANES
    for k in range(modes):
        keep_out[k] = probe_sum[k, col_index]
        for b in range(blocks):
            at = pl.ds((k * blocks + b) * win, win)
            send_out[at, :] = probe_sum[k, 1 - col_index, b].astype(jnp.bfloat16)
    put_weight(jnp.sum(norm_out[...]) / (win * win), (send_out,))
    scale = 1.0 / jnp.full((8, LANES), power[0], jnp.float32)
    scale = jnp.concatenate([scale] * (CHUNK // 8), axis=0)

    def take_blocks(part, at, first, number):
        return jnp.concatenate(
            [grad[part, first + b, at, :] * scale for b in range(number)], axis=1
        )

    for part in range(2):
        for r in range(0, rows + win, CHUNK):
            at = pl.ds(r, CHUNK)
            piece = take_blocks(part, at, cols // LANES, win // LANES)
            right_grad[part, at, :] = piece.astype(jnp.bfloat16)
        for r in range(0, rows, CHUNK):
            at = pl.ds(r, CHUNK)
            own_grad[part, at, :] = take_blocks(part, at, 0, cols // LANES)
        for r in range(0, win, CHUNK):
            at, of = pl.ds(r, CHUNK), pl.ds(rows + r, CHUNK)
            low_grad[part, at, :] = take_blocks(part, of, 0, cols // LANES)


def position_gradients(starts, count, power, own, below, right, corner, probe, measured, tables):
    win, modes = probe.shape[1], probe.shape[2] // probe.shape[1]
    rows, cols = own.shape[1:]
    f32, bf16 = jnp.float32, jnp.bfloat16
    smem = pl.BlockSpec(memory_space=pltpu.SMEM)
    vmem = pl.BlockSpec(memory_space=pltpu.VMEM)
    if win != 2 * LANES:
        raise ValueError("window size")
    slots = measured.shape[0]
    flops = 16 * slots * modes * win**3
    part_blocks = (modes, win // LANES, win, LANES)
    part_rows = modes * win // LANES * win
    return pl.pallas_call(
        functools.partial(gradient_kernel, modes),
        out_shape=(
            jax.ShapeDtypeStruct((2, rows, cols), f32),
            jax.ShapeDtypeStruct((2, win, cols), f32),
            jax.ShapeDtypeStruct((2, rows + win, win), bf16),
            jax.ShapeDtypeStruct(part_blocks, f32),
            jax.ShapeDtypeStruct((part_rows + TAIL, LANES), bf16),
            jax.ShapeDtypeStruct((8, win), f32),
        ),
        in_specs=[smem] * 3 + [vmem] * 8,
        out_specs=(vmem,) * 6,
        scratch_shapes=[
            pltpu.VMEM((2, (cols + win) // LANES, rows + win, LANES), f32),
            pltpu.VMEM((2, (cols + win) // LANES, rows + win, LANES), f32),
            pltpu.VMEM((2, win, win), f32),
            pltpu.VMEM((modes, 2, win, win), bf16),
            pltpu.VMEM((2, modes * win, win), bf16),
            pltpu.VMEM((2, modes * win, win), f32),
            pltpu.VMEM((modes, 2, win // LANES, win, LANES), f32),
        ],
        compiler_params=pltpu.CompilerParams(vmem_limit_bytes=26 * MIB),
        cost_estimate=pl.CostEstimate(flops=flops, bytes_accessed=12 << 20, transcendentals=0),
    )(starts, count, power, own, *below, right, corner, probe, measured, tables)


def in_three(value):
    full = jnp.full((TAIL, LANES), value, jnp.float32)
    high = full.astype(jnp.bfloat16).astype(jnp.float32)
    mid = (full - high).astype(jnp.bfloat16).astype(jnp.float32)
    low = full - high - mid
    row = lax.broadcasted_iota(jnp.int32, (TAIL, LANES), 0)
    lane = lax.broadcasted_iota(jnp.int32, (TAIL, LANES), 1)
    tile = jnp.where(row == 0, high, jnp.where(row == 1, mid, jnp.where(row == 2, low, 0.0)))
    return jnp.where(lane == 0, tile, 0.0).astype(jnp.bfloat16)


def small_call(kernel, shapes, *operands, weight=1):
    return pl.pallas_call(
        kernel,
        out_shape=shapes,
        compiler_params=pltpu.CompilerParams(vmem_limit_bytes=4 * MIB),
        cost_estimate=pl.CostEstimate(flops=0, bytes_accessed=weight * MIB, transcendentals=0),
    )(*operands)


def first_columns_kernel(block, token, first):
    first[...] = block[:, :, : first.shape[2]]


def first_columns(block, size, token):
    shape = block.shape[:2] + (size,)
    return small_call(
        first_columns_kernel, jax.ShapeDtypeStruct(shape, block.dtype), block, token
    )


def copies_kernel(block, token, first_rows, first_cols):
    first_rows[...] = block[:, : first_rows.shape[1], :]
    first_cols[...] = block[:, :, : first_cols.shape[2]]


def copies(block, size, token):
    parts, rows, cols = block.shape
    shapes = ((parts, size, cols), (parts, rows, size))
    return small_call(
        copies_kernel,
        tuple(jax.ShapeDtypeStruct(shape, block.dtype) for shape in shapes),
        block,
        token,
    )


def prepare_kernel(probe, intens, blocks, token, tables, measured, wide_probe, power):
    tables[...] = blocks[...]
    count, size, _ = intens.shape
    row = lax.broadcasted_iota(jnp.int32, (size, size), 0)
    col = lax.broadcasted_iota(jnp.int32, (size, size), 1)
    to_even_first = (col == jnp.where(row < size // 2, 2 * row, 2 * row - size + 1)).astype(
        jnp.float32
    )
    from_left = to_even_first.astype(jnp.bfloat16)
    from_right = (row == jnp.where(col < size // 2, 2 * col, 2 * col - size + 1)).astype(
        jnp.float32
    )
    from_right = from_right.astype(jnp.bfloat16)
    for slot in range(count):
        turned = dot(from_left, intens[slot]).astype(jnp.bfloat16)
        measured[slot] = jnp.sqrt(dot(turned, from_right))
    win = probe.shape[1]
    modes = probe.shape[2] // win
    largest = jnp.zeros((8, win), jnp.float32)
    for r in range(0, probe.shape[1], CHUNK):
        at = slice(r, r + CHUNK)
        total = jnp.zeros((CHUNK, win), jnp.float32)
        for k in range(modes):
            for part in range(2):
                p = probe[part, at, k * win : (k + 1) * win].astype(jnp.float32)
                wide_probe[part, at, k * win : (k + 1) * win] = p
                total = total + p * p
        largest = jnp.maximum(largest, jnp.max(total.reshape(CHUNK // 8, 8, win), axis=0))
    power[0, 0] = jnp.max(largest)


def prepare(probe, intens, token):
    win = probe.shape[1]
    blocks = dft_blocks(win)
    vmem = pl.BlockSpec(memory_space=pltpu.VMEM)
    return pl.pallas_call(
        prepare_kernel,
        out_shape=(
            jax.ShapeDtypeStruct(blocks.shape, jnp.bfloat16),
            jax.ShapeDtypeStruct(intens.shape, jnp.float32),
            jax.ShapeDtypeStruct(probe.shape, jnp.float32),
            jax.ShapeDtypeStruct((1, 1), jnp.float32),
        ),
        out_specs=(vmem, vmem, vmem, pl.BlockSpec(memory_space=pltpu.SMEM)),
        compiler_params=pltpu.CompilerParams(vmem_limit_bytes=8 * MIB),
    )(probe, intens, blocks, token)


def block_shapes(number, size, ways):
    if not ways:
        return (jax.ShapeDtypeStruct((number * size + TAIL, LANES), jnp.bfloat16),)
    sends = jax.ShapeDtypeStruct((number // ways * size + TAIL, LANES), jnp.bfloat16)
    return (jax.ShapeDtypeStruct((number // ways, size, LANES), jnp.float32),) + (sends,) * (ways - 1)


def put_block(j, total, outs):
    size = total.shape[0]
    if len(outs) == 1:
        outs[0][pl.ds(j * size, size), :] = total.astype(jnp.bfloat16)
    elif j % len(outs) == 0:
        outs[0][j // len(outs)] = total
    else:
        at = pl.ds(j // len(outs) * size, size)
        outs[j % len(outs)][at, :] = total.astype(jnp.bfloat16)


def put_weight(weight, outs):
    tile = in_three(weight)
    for sent in outs if len(outs) == 1 else outs[1:]:
        sent[pl.ds(sent.shape[0] - TAIL, TAIL), :] = tile


def weight_of(block):
    return jnp.sum(block[pl.ds(block.shape[0] - TAIL, TAIL), :].astype(jnp.float32))


def chip_sum_kernel(pixels, size, keep, received, norm, *outs):
    me = lax.axis_index("row")
    for j in range(keep.shape[0] // size):
        at = pl.ds(pl.multiple_of((j ^ me) * size, size), size)
        put_block(j, keep[at, :] + received[at, :].astype(jnp.float32), outs)
    put_weight(jnp.sum(norm[...]) / pixels + weight_of(received), outs)


def chip_sum(keep, received, norm, pixels, number, ways):
    size = keep.shape[0] // number
    return small_call(
        functools.partial(chip_sum_kernel, pixels, size),
        block_shapes(number, size, ways),
        keep,
        received,
        norm,
    )


def scatter_sum_kernel(number, mine, sent, *refs):
    received, outs = refs[:number], refs[number:]
    size = mine.shape[1]
    for j in range(mine.shape[0]):
        total = mine[j]
        for block in received:
            total = total + block[pl.ds(j * size, size), :].astype(jnp.float32)
        put_block(j, total, outs)
    put_weight(pair_up([weight_of(block) for block in (sent, *received)]), outs)


def scatter_sum(mine, sent, received, ways):
    number, size, _ = mine.shape
    return small_call(
        functools.partial(scatter_sum_kernel, len(received)),
        block_shapes(number, size, ways),
        mine,
        sent,
        *received,
    )


def pair_up(terms):
    while len(terms) > 1:
        terms = [a + b for a, b in zip(terms[::2], terms[1::2])]
    return terms[0]


def exchange_sum_kernel(size, *refs):
    blocks, chunks = refs[:-1], refs[-1]
    for j in range((chunks.shape[0] - TAIL) // size):
        terms = [
            block[pl.ds((j ^ i) * size, size), :].astype(jnp.float32)
            for i, block in enumerate(blocks)
        ]
        chunks[pl.ds(j * size, size), :] = pair_up(terms).astype(jnp.bfloat16)
    put_weight(pair_up([weight_of(block) for block in blocks]), (chunks,))


def exchange_sum(blocks, size):
    return small_call(
        functools.partial(exchange_sum_kernel, size),
        jax.ShapeDtypeStruct(blocks[0].shape, jnp.bfloat16),
        *blocks,
    )


def copy_chunks(blocks, joined):
    at = 0
    for block in blocks:
        rows = block.shape[0] - TAIL
        joined[pl.ds(at, rows), :] = block[pl.ds(0, rows), :]
        at += rows
    joined[pl.ds(at, TAIL), :] = blocks[0][pl.ds(blocks[0].shape[0] - TAIL, TAIL), :]


def join_kernel(*refs):
    copy_chunks(refs[:-1], refs[-1])


def join(blocks):
    rows = sum(block.shape[0] - TAIL for block in blocks) + TAIL
    return small_call(join_kernel, jax.ShapeDtypeStruct((rows, LANES), blocks[0].dtype), *blocks)


def swap_rows(block, step):
    number = lax.axis_size("row")
    return lax.ppermute(block, "row", [(i, i ^ step) for i in range(number)])


def row_digits():
    number = lax.axis_size("row")
    if number & (number - 1) or number < 2:
        raise ValueError("row size")
    bits = number.bit_length() - 1
    return [(shift, 1 << min(2, bits - shift)) for shift in range(0, bits, 2)]


def probe_update_kernel(size, digits, mine, *refs):
    *blocks, probe, new_probe, gathered, updated, sems = refs
    copy_chunks(blocks[::-1], gathered)
    win, modes, _ = updated.shape
    col_index = lax.axis_index("col")
    part = col_index if mine else 1 - col_index
    me = lax.axis_index("row")
    piece = min(size, CHUNK)
    factor = 4.0 / jnp.full((piece, LANES), weight_of(blocks[0]), jnp.float32)

    def place(chunk):
        j = chunk ^ me
        at, span = 0, 1
        for shift, ways in reversed(digits):
            at = at + ((j >> shift) & (ways - 1)) * span
            span *= ways
        return at * size

    def update(k, b, r):
        chunk, offset = divmod((k * (win // LANES) + b) * win + r, size)
        at = pl.ds(pl.multiple_of(place(chunk) + offset, piece), piece)
        total = gathered[at, :].astype(jnp.float32)
        col = k * win + b * LANES
        old = probe[part, r : r + piece, col : col + LANES]
        updated[r : r + piece, k, b * LANES : (b + 1) * LANES] = old - factor * total

    stretch = win // 4
    copies = []
    for start in range(0, win, stretch):
        for r in range(start, start + stretch, piece):
            for k in range(modes):
                for b in range(win // LANES):
                    update(k, b, r)
        at = pl.ds(start, stretch)
        copies.append(
            pltpu.make_async_copy(updated.at[at], new_probe.at[part, at], sems.at[len(copies)])
        )
        copies[-1].start()
    for copy in copies:
        copy.wait()


def probe_update(blocks, probe, shape, size, digits, first_result=None, token=None):
    vmem, anywhere = pl.BlockSpec(memory_space=pltpu.VMEM), pl.BlockSpec(memory_space=pl.ANY)
    rows = sum(block.shape[0] - TAIL for block in blocks) + TAIL
    operands = [*blocks[::-1], probe]
    mine = first_result is None
    kernel = functools.partial(probe_update_kernel, size, digits, mine)
    if not mine:
        number = len(operands)

        def kernel(*refs):
            probe_update_kernel(size, digits, mine, *refs[:number], *refs[number + 2 :])

    extra = [] if mine else [token, first_result]
    return pl.pallas_call(
        kernel,
        out_shape=jax.ShapeDtypeStruct(shape, jnp.float32),
        in_specs=[vmem] * len(operands) + [vmem, anywhere][: len(extra)],
        out_specs=anywhere,
        scratch_shapes=[
            pltpu.VMEM((rows, LANES), jnp.bfloat16),
            pltpu.VMEM(shape[1:], jnp.float32),
            pltpu.SemaphoreType.DMA((4,)),
        ],
        input_output_aliases={} if mine else {len(operands) + 1: 0},
        compiler_params=pltpu.CompilerParams(vmem_limit_bytes=4 * MIB),
    )(*operands, *extra)


def low_sum_kernel(first, low_grad, from_left, token, low_sum):
    win = from_left.shape[2]
    rows = from_left.shape[1] - low_grad.shape[1]
    for part in range(2):
        for r in range(0, low_sum.shape[1], CHUNK):
            at, of = slice(r, r + CHUNK), slice(first + r, first + r + CHUNK)
            arrived = from_left[part, rows + first + r : rows + first + r + CHUNK, :]
            total = low_grad[part, of, :win] + arrived.astype(jnp.float32)
            low_sum[part, at, :win] = total.astype(jnp.bfloat16)
            low_sum[part, at, win:] = low_grad[part, of, win:].astype(jnp.bfloat16)


def low_sum_of(first, count, low_grad, from_left, token):
    return small_call(
        functools.partial(low_sum_kernel, first),
        jax.ShapeDtypeStruct((2, count, low_grad.shape[2]), jnp.bfloat16),
        low_grad,
        from_left,
        token,
        weight=LOW_WEIGHT,
    )


def object_update_kernel(old, own_grad, from_left, above_first, above_last, new_object, token):
    token[...] = jnp.zeros_like(token)
    win, split = from_left.shape[2], above_first.shape[1]
    depth = split + above_last.shape[1]
    for part in range(2):
        for r in range(0, old.shape[1], CHUNK):
            at = slice(r, r + CHUNK)
            total = own_grad[part, at, :]
            if r < split:
                total = total + above_first[part, at, :].astype(jnp.float32)
            elif r < depth:
                total = total + above_last[part, r - split : r - split + CHUNK, :].astype(jnp.float32)
            updated = old[part, at, :].astype(jnp.float32) - total
            arrived = from_left[part, at, :].astype(jnp.float32)
            new_object[part, at, :win] = updated[:, :win] - arrived
            new_object[part, at, win:] = updated[:, win:]


def object_update(old, own_grad, from_left, above_first, above_last):
    return small_call(
        object_update_kernel,
        (
            jax.ShapeDtypeStruct(old.shape, jnp.float32),
            jax.ShapeDtypeStruct((8, LANES), jnp.float32),
        ),
        old,
        own_grad,
        from_left,
        above_first,
        above_last,
    )


def swap_cores(block):
    return lax.ppermute(block, "col", [(0, 1), (1, 0)])


def body(object_field, probe_modes, positions, counts, intensities):
    win = probe_modes.shape[1]
    modes = probe_modes.shape[2]
    number = lax.axis_size("row")
    below_right = from_next_row(object_field[:, :win, :], 1)
    probe_flat = probe_modes.reshape(2, win, modes * win)
    first_rows, first_cols = copies(object_field, win, probe_flat)
    below_left = from_next_row(first_rows, 0)
    right = from_behind(first_cols, "col", -1)
    tables, measured, probe, power = prepare(probe_flat, intensities[0, 0], right)
    corner = from_behind(first_columns(below_right, win, tables), "col", -1)
    own_grad, low_grad, right_grad, keep, send, norm = position_gradients(
        positions[0, 0].T,
        counts.reshape(-1),
        power.reshape(1),
        object_field,
        (below_left, below_right),
        right,
        corner,
        probe,
        measured,
        tables,
    )
    half_rows = keep.size // LANES
    received = swap_cores(send)
    from_left = from_behind(right_grad, "col", 1)
    digits = row_digits()
    size = half_rows // number
    ways = [digit[1] for digit in digits[:-1]] + [0]
    outs = chip_sum(keep.reshape(half_rows, LANES), received, norm, win * win, number, ways[0])
    for place, (shift, _) in enumerate(digits[:-1]):
        mine, *sends = outs
        received = [swap_rows(block, (i + 1) << shift) for i, block in enumerate(sends)]
        outs = scatter_sum(mine, sends[0], received, ways[place + 1])
    split = SPLIT * win // 8
    low_first = low_sum_of(0, split, low_grad, from_left, outs[0])
    above_first = from_behind(low_first, "row", 1)
    shift, count = digits[-1]
    partners = [swap_rows(outs[0], i << shift) for i in range(1, count)]
    gathered = exchange_sum(list(outs) + partners, size)
    low_last = low_sum_of(split, win - split, low_grad, from_left, gathered)
    above_last = from_behind(low_last, "row", 1)
    mine = [gathered]
    for shift, count in digits[-2::-1]:
        gathered = mine[0] if len(mine) == 1 else join(mine)
        mine = [gathered] + [swap_rows(gathered, i << shift) for i in range(1, count)]
    other = [swap_cores(block) for block in mine]
    new_object, token = object_update(
        object_field, own_grad, from_left, above_first, above_last
    )
    shape = probe_modes.shape
    first_result = probe_update(mine, probe, shape, size, digits)
    new_probe = probe_update(other, probe, shape, size, digits, first_result, token)
    return (new_object, new_probe)


def solution(mesh):
    placed = (
        P(None, ("grp", "row"), "col"),
        P(None, None, "grp", None),
        P(("grp", "row"), "col", None, None),
        P(("grp", "row"), "col"),
        P(("grp", "row"), "col", None, None, None),
    )
    return jax.shard_map(
        body,
        mesh=mesh,
        in_specs=placed,
        out_specs=(P(None, ("grp", "row"), "col"), P(None, None, "grp", None)),
        check_vma=False,
    )
```

```python
import functools

import jax
import jax.numpy as jnp
import ml_dtypes
import numpy as np
from jax import lax
from jax.experimental import pallas as pl
from jax.experimental.pallas import tpu as pltpu
from jax.sharding import PartitionSpec as P

LANES = 128
CHUNK = 32
FINE = 16
TAIL = 16
MIB = 1 << 20
LOW_WEIGHT = 8
SPLIT = 4


def from_behind(block, axis, distance):
    devices = range(lax.axis_size(axis))
    route = [(i - distance, i) for i in devices if i - distance in devices]
    return lax.ppermute(block, axis, route)


def from_next_row(block, col):
    rows, cols = lax.axis_size("row"), lax.axis_size("col")
    route = [((r + 1) * cols + col, r * cols + col) for r in range(rows - 1)]
    return lax.ppermute(block, ("row", "col"), route)


def dft_blocks(win):
    grid = np.arange(win)
    angle = 2.0 * np.pi * (grid[:, None] * grid[None, :] % win) / win
    factor = 1.0 / np.sqrt(win)
    cos_table = (np.cos(angle) * factor).astype(ml_dtypes.bfloat16)
    sin_table = (np.sin(angle) * factor).astype(ml_dtypes.bfloat16)
    blocks = []
    for parity in range(2):
        cos_part, sin_part = cos_table[parity::2, : win // 2], sin_table[parity::2, : win // 2]
        blocks.append(np.block([[cos_part, sin_part], [-sin_part, cos_part]]))
    return np.stack(blocks + [block.T for block in blocks])


def dot(left, right):
    return jnp.dot(left, right, preferred_element_type=jnp.float32)


def put_blocks(field, row, first, sources):
    parts, rows, cols = sources[0].shape
    for part in range(parts):
        for r in range(0, rows, CHUNK):
            pieces = [source[part, r : r + CHUNK, :].astype(jnp.float32) for source in sources]
            values = sum(pieces[1:], pieces[0])
            for b in range(cols // LANES):
                piece = values[:, b * LANES : (b + 1) * LANES]
                field[part, first + b, row + r : row + r + CHUNK, :] = piece


def lay_out_kernel(own, right, field, grad, probe_sum):
    put_blocks(field, 0, 0, (own,))
    put_blocks(field, 0, own.shape[2] // LANES, (right,))
    grad[...] = jnp.zeros_like(grad)
    probe_sum[...] = jnp.zeros_like(probe_sum)


def lay_out(own, right, win, modes):
    rows, cols = own.shape[1:]
    tile = (2, (cols + win) // LANES, rows + win, LANES)
    shapes = (tile, tile, (modes, 2, win // LANES, win, LANES))
    return small_call(
        lay_out_kernel,
        tuple(jax.ShapeDtypeStruct(shape, jnp.float32) for shape in shapes),
        own,
        right,
    )


def gradient_kernel(
    modes,
    starts,
    count,
    power,
    below_left,
    below_right,
    corner,
    probe,
    measured,
    tables,
    field_made,
    grad_made,
    probe_sum_made,
    own_grad,
    low_grad,
    right_grad,
    keep_out,
    send_out,
    norm_out,
    field,
    grad,
    probe_sum,
    window,
    wide,
    tall,
    wave,
):
    win = probe.shape[1]
    rows, cols = own_grad.shape[1], own_grad.shape[2]
    half = win // 2
    fine = range(0, win, FINE)
    spread = win // LANES + 1
    col_index = lax.axis_index("col")
    row_anchor = lax.axis_index("row") * rows
    col_anchor = col_index * cols

    norm_out[...] = jnp.zeros_like(norm_out)
    for first, *sources in ((0, below_left, below_right), (cols // LANES, corner)):
        put_blocks(field, rows, first, sources)
    lane = lax.broadcasted_iota(jnp.int32, (FINE, LANES), 1)

    def one_position(slot, carry):
        y, x = starts[0, slot] - row_anchor, starts[1, slot] - col_anchor
        base = x // LANES
        shift = x - base * LANES
        back_shift = (LANES - shift) % LANES
        keep = lane < LANES - shift
        for r in range(0, half, FINE):
            objs = []
            for start in (r, r + half):
                at = pl.ds(start, FINE)
                obj = []
                for part in range(2):
                    turned = [
                        pltpu.roll(field[part, base + b, pl.ds(y + start, FINE), :], back_shift, 1)
                        for b in range(spread)
                    ]
                    piece = jnp.concatenate(
                        [jnp.where(keep, a, b) for a, b in zip(turned[:-1], turned[1:])], axis=1
                    )
                    window[part, at, :] = piece
                    obj.append(piece)
                squares = obj[0] * obj[0] + obj[1] * obj[1]
                norm_out[...] += jnp.sum(squares.reshape(FINE // 8, 8, win), axis=0)
                objs.append(obj)
            for k in range(modes):
                cs = pl.ds(k * win, win)
                exits = []
                for start, (o_re, o_im) in zip((r, r + half), objs):
                    p_re, p_im = probe[0, pl.ds(start, FINE), cs], probe[1, pl.ds(start, FINE), cs]
                    exits.append((p_re * o_re - p_im * o_im, p_re * o_im + p_im * o_re))
                for part in range(2):
                    low, high = exits[0][part], exits[1][part]
                    at = pl.ds(part * half + r, FINE)
                    wide[k, 0, at, :] = (low + high).astype(jnp.bfloat16)
                    wide[k, 1, at, :] = (low - high).astype(jnp.bfloat16)

        for k in range(modes):
            for parity in range(2):
                out = dot(tables[parity], wide[k, parity])
                at = pl.ds(k * win + parity * half, half)
                for part in range(2):
                    low = out[part * half : (part + 1) * half, :half]
                    high = out[part * half : (part + 1) * half, half:]
                    to = pl.ds(part * half, half)
                    tall[0, at, to] = (low + high).astype(jnp.bfloat16)
                    tall[1, at, to] = (low - high).astype(jnp.bfloat16)
        for parity in range(2):
            wave[parity] = dot(tall[parity], tables[2 + parity])

        for r in fine:
            for parity in range(2):
                waves = []
                total = jnp.zeros((FINE, half), jnp.float32)
                for k in range(modes):
                    ka = pl.ds(k * win + r, FINE)
                    waves.append((wave[parity, ka, :half], wave[parity, ka, half:]))
                    total = total + (waves[k][0] * waves[k][0] + waves[k][1] * waves[k][1])
                gs = pl.ds(parity * half, half)
                amp = measured[slot, pl.ds(r, FINE), gs]
                ratio = 1.0 - amp * lax.rsqrt(jnp.maximum(total, 1.0))
                for k in range(modes):
                    for part in range(2):
                        at = pl.ds(part * half + r % half, FINE)
                        wide[k, r // half, at, gs] = (waves[k][part] * ratio).astype(jnp.bfloat16)

        for k in range(modes):
            even = dot(tables[2], wide[k, 0])
            odd = dot(tables[3], wide[k, 1])
            for place, out in enumerate((even + odd, even - odd)):
                at = pl.ds(k * win + place * half, half)
                for part in range(2):
                    for parity in range(2):
                        tall[parity, at, part * half : (part + 1) * half] = out[
                            part * half : (part + 1) * half, parity * half : (parity + 1) * half
                        ].astype(jnp.bfloat16)
        for parity in range(2):
            wave[parity] = dot(tall[parity], tables[parity])

        keep_high = lane >= shift
        for r in fine:
            at = pl.ds(r, FINE)
            sums = [[jnp.zeros((FINE, LANES), jnp.float32) for _ in range(2)] for _ in range(2)]
            for b in range(2):
                bs = pl.ds(b * half, half)
                o_re, o_im = window[0, at, bs], window[1, at, bs]
                for k in range(modes):
                    cs = pl.ds(k * win + b * half, half)
                    ka = pl.ds(k * win + r, FINE)
                    even, odd = wave[0, ka, :], wave[1, ka, :]
                    d = even + odd if b == 0 else even - odd
                    d_re, d_im = d[:, :half], d[:, half:]
                    p_re, p_im = probe[0, at, cs], probe[1, at, cs]
                    sums[0][b] = sums[0][b] + (p_re * d_re + p_im * d_im)
                    sums[1][b] = sums[1][b] + (p_re * d_im - p_im * d_re)
                    probe_sum[k, 0, b, at, :] += o_re * d_re + o_im * d_im
                    probe_sum[k, 1, b, at, :] += o_re * d_im - o_im * d_re
            for part in range(2):
                turned = [pltpu.roll(piece, shift, 1) for piece in sums[part]]
                turned = [jnp.zeros_like(turned[0])] + turned + [jnp.zeros_like(turned[0])]
                for b in range(spread):
                    grad[part, base + b, pl.ds(y + r, FINE), :] += jnp.where(
                        keep_high, turned[b + 1], turned[b]
                    )
        return carry

    lax.fori_loop(0, count[0], one_position, 0)
    for m in range(modes // 2):
        keep_mode = col_index * (modes // 2) + m
        send_mode = (1 - col_index) * (modes // 2) + m
        keep_out[m] = probe_sum[keep_mode]
        send_out[m] = probe_sum[send_mode].astype(jnp.bfloat16)
    scale = 1.0 / jnp.full((8, LANES), power[0], jnp.float32)
    scale = jnp.concatenate([scale] * (CHUNK // 8), axis=0)

    def take_blocks(part, at, first, number):
        return jnp.concatenate(
            [grad[part, first + b, at, :] * scale for b in range(number)], axis=1
        )

    for part in range(2):
        for r in range(0, rows + win, CHUNK):
            at = pl.ds(r, CHUNK)
            piece = take_blocks(part, at, cols // LANES, win // LANES)
            right_grad[part, at, :] = piece.astype(jnp.bfloat16)
        for r in range(0, rows, CHUNK):
            at = pl.ds(r, CHUNK)
            own_grad[part, at, :] = take_blocks(part, at, 0, cols // LANES)
        for r in range(0, win, CHUNK):
            at, of = pl.ds(r, CHUNK), pl.ds(rows + r, CHUNK)
            low_grad[part, at, :] = take_blocks(part, of, 0, cols // LANES)


def position_gradients(starts, count, power, tile, below, corner, probe, measured, tables, made):
    win, modes = probe.shape[1], probe.shape[2] // probe.shape[1]
    rows, cols = tile
    f32, bf16 = jnp.float32, jnp.bfloat16
    smem = pl.BlockSpec(memory_space=pltpu.SMEM)
    vmem = pl.BlockSpec(memory_space=pltpu.VMEM)
    if win != 2 * LANES:
        raise ValueError("window size")
    slots = measured.shape[0]
    flops = 16 * slots * modes * win**3
    half_blocks = (modes // 2, 2, win // LANES, win, LANES)
    return pl.pallas_call(
        functools.partial(gradient_kernel, modes),
        out_shape=(
            jax.ShapeDtypeStruct((2, rows, cols), f32),
            jax.ShapeDtypeStruct((2, win, cols), f32),
            jax.ShapeDtypeStruct((2, rows + win, win), bf16),
            jax.ShapeDtypeStruct(half_blocks, f32),
            jax.ShapeDtypeStruct(half_blocks, bf16),
            jax.ShapeDtypeStruct((8, win), f32),
        )
        + tuple(jax.ShapeDtypeStruct(array.shape, f32) for array in made),
        in_specs=[smem] * 3 + [vmem] * 9,
        out_specs=(vmem,) * 9,
        input_output_aliases={9: 6, 10: 7, 11: 8},
        scratch_shapes=[
            pltpu.VMEM((2, win, win), f32),
            pltpu.VMEM((modes, 2, win, win), bf16),
            pltpu.VMEM((2, modes * win, win), bf16),
            pltpu.VMEM((2, modes * win, win), f32),
        ],
        compiler_params=pltpu.CompilerParams(vmem_limit_bytes=16 * MIB),
        cost_estimate=pl.CostEstimate(flops=flops, bytes_accessed=12 << 20, transcendentals=0),
    )(starts, count, power, *below, corner, probe, measured, tables, *made)


def in_three(value):
    full = jnp.full((TAIL, LANES), value, jnp.float32)
    high = full.astype(jnp.bfloat16).astype(jnp.float32)
    mid = (full - high).astype(jnp.bfloat16).astype(jnp.float32)
    low = full - high - mid
    row = lax.broadcasted_iota(jnp.int32, (TAIL, LANES), 0)
    lane = lax.broadcasted_iota(jnp.int32, (TAIL, LANES), 1)
    tile = jnp.where(row == 0, high, jnp.where(row == 1, mid, jnp.where(row == 2, low, 0.0)))
    return jnp.where(lane == 0, tile, 0.0).astype(jnp.bfloat16)


def small_call(kernel, shapes, *operands, weight=1):
    return pl.pallas_call(
        kernel,
        out_shape=shapes,
        compiler_params=pltpu.CompilerParams(vmem_limit_bytes=4 * MIB),
        cost_estimate=pl.CostEstimate(flops=0, bytes_accessed=weight * MIB, transcendentals=0),
    )(*operands)


def first_columns_kernel(block, *refs):
    first = refs[-1]
    first[...] = block[:, :, : first.shape[2]]


def first_columns(block, size, *tokens):
    shape = block.shape[:2] + (size,)
    return small_call(
        first_columns_kernel, jax.ShapeDtypeStruct(shape, block.dtype), block, *tokens
    )


def copies_kernel(block, token, first_rows, first_cols):
    first_rows[...] = block[:, : first_rows.shape[1], :]
    first_cols[...] = block[:, :, : first_cols.shape[2]]


def copies(block, size, token):
    parts, rows, cols = block.shape
    shapes = ((parts, size, cols), (parts, rows, size))
    return small_call(
        copies_kernel,
        tuple(jax.ShapeDtypeStruct(shape, block.dtype) for shape in shapes),
        block,
        token,
    )


def prepare_kernel(probe, intens, blocks, token, tables, measured, wide_probe, power):
    tables[...] = blocks[...]
    count, size, _ = intens.shape
    row = lax.broadcasted_iota(jnp.int32, (size, size), 0)
    col = lax.broadcasted_iota(jnp.int32, (size, size), 1)
    to_even_first = (col == jnp.where(row < size // 2, 2 * row, 2 * row - size + 1)).astype(
        jnp.float32
    )
    from_left = to_even_first.astype(jnp.bfloat16)
    from_right = (row == jnp.where(col < size // 2, 2 * col, 2 * col - size + 1)).astype(
        jnp.float32
    )
    from_right = from_right.astype(jnp.bfloat16)
    for slot in range(count):
        turned = dot(from_left, intens[slot]).astype(jnp.bfloat16)
        measured[slot] = jnp.sqrt(dot(turned, from_right))
    win = probe.shape[1]
    modes = probe.shape[2] // win
    largest = jnp.zeros((8, win), jnp.float32)
    for r in range(0, probe.shape[1], CHUNK):
        at = slice(r, r + CHUNK)
        total = jnp.zeros((CHUNK, win), jnp.float32)
        for k in range(modes):
            for part in range(2):
                p = probe[part, at, k * win : (k + 1) * win].astype(jnp.float32)
                wide_probe[part, at, k * win : (k + 1) * win] = p
                total = total + p * p
        largest = jnp.maximum(largest, jnp.max(total.reshape(CHUNK // 8, 8, win), axis=0))
    power[0, 0] = jnp.max(largest)


def prepare(probe, intens, token):
    win = probe.shape[1]
    blocks = dft_blocks(win)
    vmem = pl.BlockSpec(memory_space=pltpu.VMEM)
    return pl.pallas_call(
        prepare_kernel,
        out_shape=(
            jax.ShapeDtypeStruct(blocks.shape, jnp.bfloat16),
            jax.ShapeDtypeStruct(intens.shape, jnp.float32),
            jax.ShapeDtypeStruct(probe.shape, jnp.float32),
            jax.ShapeDtypeStruct((1, 1), jnp.float32),
        ),
        out_specs=(vmem, vmem, vmem, pl.BlockSpec(memory_space=pltpu.SMEM)),
        compiler_params=pltpu.CompilerParams(vmem_limit_bytes=8 * MIB),
    )(probe, intens, blocks, token)


def block_shapes(number, size, ways):
    if not ways:
        return (jax.ShapeDtypeStruct((number * size + TAIL, LANES), jnp.bfloat16),)
    sends = jax.ShapeDtypeStruct((number // ways * size + TAIL, LANES), jnp.bfloat16)
    return (jax.ShapeDtypeStruct((number // ways, size, LANES), jnp.float32),) + (sends,) * (ways - 1)


def put_block(j, total, outs):
    size = total.shape[0]
    if len(outs) == 1:
        outs[0][pl.ds(j * size, size), :] = total.astype(jnp.bfloat16)
    elif j % len(outs) == 0:
        outs[0][j // len(outs)] = total
    else:
        at = pl.ds(j // len(outs) * size, size)
        outs[j % len(outs)][at, :] = total.astype(jnp.bfloat16)


def put_weight(weight, outs):
    tile = in_three(weight)
    for sent in outs if len(outs) == 1 else outs[1:]:
        sent[pl.ds(sent.shape[0] - TAIL, TAIL), :] = tile


def weight_of(block):
    return jnp.sum(block[pl.ds(block.shape[0] - TAIL, TAIL), :].astype(jnp.float32))


def chip_sum_kernel(pixels, size, keep, received, norm, *outs):
    me = lax.axis_index("row")
    for j in range(keep.shape[0] // size):
        at = pl.ds(pl.multiple_of((j ^ me) * size, size), size)
        put_block(j, keep[at, :] + received[at, :].astype(jnp.float32), outs)
    put_weight(jnp.sum(norm[...]) / pixels, outs)


def chip_sum(keep, received, norm, pixels, number, ways):
    size = keep.shape[0] // number
    return small_call(
        functools.partial(chip_sum_kernel, pixels, size),
        block_shapes(number, size, ways),
        keep,
        received,
        norm,
    )


def scatter_sum_kernel(number, mine, sent, *refs):
    received, outs = refs[:number], refs[number:]
    size = mine.shape[1]
    for j in range(mine.shape[0]):
        total = mine[j]
        for block in received:
            total = total + block[pl.ds(j * size, size), :].astype(jnp.float32)
        put_block(j, total, outs)
    put_weight(sum([weight_of(block) for block in received], weight_of(sent)), outs)


def scatter_sum(mine, sent, received, ways):
    number, size, _ = mine.shape
    return small_call(
        functools.partial(scatter_sum_kernel, len(received)),
        block_shapes(number, size, ways),
        mine,
        sent,
        *received,
    )


def pair_up(terms):
    while len(terms) > 1:
        terms = [a + b for a, b in zip(terms[::2], terms[1::2])]
    return terms[0]


def exchange_sum_kernel(size, *refs):
    blocks, chunks = refs[:-1], refs[-1]
    for j in range((chunks.shape[0] - TAIL) // size):
        terms = [
            block[pl.ds((j ^ i) * size, size), :].astype(jnp.float32)
            for i, block in enumerate(blocks)
        ]
        chunks[pl.ds(j * size, size), :] = pair_up(terms).astype(jnp.bfloat16)
    put_weight(pair_up([weight_of(block) for block in blocks]), (chunks,))


def exchange_sum(blocks, size):
    return small_call(
        functools.partial(exchange_sum_kernel, size),
        jax.ShapeDtypeStruct(blocks[0].shape, jnp.bfloat16),
        *blocks,
    )


def copy_chunks(blocks, joined):
    at = 0
    for block in blocks:
        rows = block.shape[0] - TAIL
        joined[pl.ds(at, rows), :] = block[pl.ds(0, rows), :]
        at += rows
    joined[pl.ds(at, TAIL), :] = blocks[0][pl.ds(blocks[0].shape[0] - TAIL, TAIL), :]


def join_kernel(*refs):
    copy_chunks(refs[:-1], refs[-1])


def join(blocks):
    rows = sum(block.shape[0] - TAIL for block in blocks) + TAIL
    return small_call(join_kernel, jax.ShapeDtypeStruct((rows, LANES), blocks[0].dtype), *blocks)


def swap_rows(block, step):
    number = lax.axis_size("row")
    return lax.ppermute(block, "row", [(i, i ^ step) for i in range(number)])


def row_digits():
    number = lax.axis_size("row")
    if number & (number - 1) or number < 2:
        raise ValueError("row size")
    bits = number.bit_length() - 1
    return [(shift, 1 << min(2, bits - shift)) for shift in range(0, bits, 2)]


def probe_update_kernel(size, digits, *refs):
    *blocks, probe, token, new_probe, mine, other, updated, sems = refs
    copy_chunks(blocks[: len(blocks) // 2], mine)
    copy_chunks(blocks[len(blocks) // 2 :], other)
    _, win, modes, _ = updated.shape
    number = mine.shape[0] // size
    me = lax.axis_index("row")
    piece = min(size, CHUNK)
    on_left = lax.axis_index("col") == 0
    tail = pl.ds(number * size, TAIL)
    tails = mine[tail, :].astype(jnp.float32) + other[tail, :].astype(jnp.float32)
    factor = 4.0 / jnp.full((piece, LANES), jnp.sum(tails), jnp.float32)
    half = modes // 2

    def place(chunk):
        j = chunk ^ me
        at, span = 0, 1
        for shift, ways in reversed(digits):
            at = at + ((j >> shift) & (ways - 1)) * span
            span *= ways
        return at * size

    def update(part, b, m, r):
        block = ((m * 2 + part) * (win // LANES) + b) * win
        chunk, offset = divmod(block + r, size)
        at = pl.ds(pl.multiple_of(place(chunk) + offset, piece), piece)
        here = mine[at, :].astype(jnp.float32)
        there = other[at, :].astype(jnp.float32)
        low = jnp.where(on_left, here, there)
        high = jnp.where(on_left, there, here)
        for k, total in ((m, low), (half + m, high)):
            col = k * win + b * LANES
            old = probe[part, r : r + piece, col : col + LANES]
            updated[part, r : r + piece, k, b * LANES : (b + 1) * LANES] = old - factor * total

    stretch = win // 4
    copies = []
    for part in range(2):
        for start in range(0, win, stretch):
            for r in range(start, start + stretch, piece):
                for m in range(half):
                    for b in range(win // LANES):
                        update(part, b, m, r)
            at = (part, pl.ds(start, stretch))
            copies.append(
                pltpu.make_async_copy(updated.at[at], new_probe.at[at], sems.at[len(copies)])
            )
            copies[-1].start()
    for copy in copies:
        copy.wait()


def probe_update(mine, other, probe, token, shape, size, digits):
    vmem = pl.BlockSpec(memory_space=pltpu.VMEM)
    rows = sum(block.shape[0] - TAIL for block in mine) + TAIL
    operands = (*mine, *other, probe, token)
    return pl.pallas_call(
        functools.partial(probe_update_kernel, size, digits),
        out_shape=jax.ShapeDtypeStruct(shape, jnp.float32),
        in_specs=[vmem] * len(operands),
        out_specs=pl.BlockSpec(memory_space=pl.ANY),
        scratch_shapes=[
            pltpu.VMEM((rows, LANES), jnp.bfloat16),
            pltpu.VMEM((rows, LANES), jnp.bfloat16),
            pltpu.VMEM(shape, jnp.float32),
            pltpu.SemaphoreType.DMA((8,)),
        ],
        compiler_params=pltpu.CompilerParams(vmem_limit_bytes=8 * MIB),
    )(*operands)


def low_sum_kernel(first, low_grad, from_left, token, low_sum):
    win = from_left.shape[2]
    rows = from_left.shape[1] - low_grad.shape[1]
    for part in range(2):
        for r in range(0, low_sum.shape[1], CHUNK):
            at, of = slice(r, r + CHUNK), slice(first + r, first + r + CHUNK)
            arrived = from_left[part, rows + first + r : rows + first + r + CHUNK, :]
            total = low_grad[part, of, :win] + arrived.astype(jnp.float32)
            low_sum[part, at, :win] = total.astype(jnp.bfloat16)
            low_sum[part, at, win:] = low_grad[part, of, win:].astype(jnp.bfloat16)


def low_sum_of(first, count, low_grad, from_left, token):
    return small_call(
        functools.partial(low_sum_kernel, first),
        jax.ShapeDtypeStruct((2, count, low_grad.shape[2]), jnp.bfloat16),
        low_grad,
        from_left,
        token,
        weight=LOW_WEIGHT,
    )


def object_update_kernel(old, own_grad, from_left, above_first, above_last, new_object, token):
    token[...] = jnp.zeros_like(token)
    win, split = from_left.shape[2], above_first.shape[1]
    depth = split + above_last.shape[1]
    for part in range(2):
        for r in range(0, old.shape[1], CHUNK):
            at = slice(r, r + CHUNK)
            total = own_grad[part, at, :]
            if r < split:
                total = total + above_first[part, at, :].astype(jnp.float32)
            elif r < depth:
                total = total + above_last[part, r - split : r - split + CHUNK, :].astype(jnp.float32)
            updated = old[part, at, :].astype(jnp.float32) - total
            arrived = from_left[part, at, :].astype(jnp.float32)
            new_object[part, at, :win] = updated[:, :win] - arrived
            new_object[part, at, win:] = updated[:, win:]


def object_update(old, own_grad, from_left, above_first, above_last):
    return small_call(
        object_update_kernel,
        (
            jax.ShapeDtypeStruct(old.shape, jnp.float32),
            jax.ShapeDtypeStruct((8, LANES), jnp.float32),
        ),
        old,
        own_grad,
        from_left,
        above_first,
        above_last,
    )


def swap_cores(block):
    return lax.ppermute(block, "col", [(0, 1), (1, 0)])


def body(object_field, probe_modes, positions, counts, intensities):
    win = probe_modes.shape[1]
    modes = probe_modes.shape[2]
    number = lax.axis_size("row")
    below_right = from_next_row(object_field[:, :win, :], 1)
    probe_flat = probe_modes.reshape(2, win, modes * win)
    first_rows, first_cols = copies(object_field, win, probe_flat)
    below_left = from_next_row(first_rows, 0)
    right = from_behind(first_cols, "col", -1)
    tables, measured, probe, power = prepare(probe_flat, intensities[0, 0], right)
    made = lay_out(object_field, right, win, modes)
    corner = from_behind(first_columns(below_right, win, tables, made[0]), "col", -1)
    own_grad, low_grad, right_grad, keep, send, norm, *_ = position_gradients(
        positions[0, 0].T,
        counts.reshape(-1),
        power.reshape(1),
        object_field.shape[1:],
        (below_left, below_right),
        corner,
        probe,
        measured,
        tables,
        made,
    )
    half_rows = keep.size // LANES
    received = swap_cores(send.reshape(half_rows, LANES))
    from_left = from_behind(right_grad, "col", 1)
    digits = row_digits()
    size = half_rows // number
    ways = [digit[1] for digit in digits[:-1]] + [0]
    outs = chip_sum(keep.reshape(half_rows, LANES), received, norm, win * win, number, ways[0])
    for place, (shift, _) in enumerate(digits[:-1]):
        mine, *sends = outs
        received = [swap_rows(block, (i + 1) << shift) for i, block in enumerate(sends)]
        outs = scatter_sum(mine, sends[0], received, ways[place + 1])
    split = SPLIT * win // 8
    low_first = low_sum_of(0, split, low_grad, from_left, outs[0])
    above_first = from_behind(low_first, "row", 1)
    shift, count = digits[-1]
    partners = [swap_rows(outs[0], i << shift) for i in range(1, count)]
    gathered = exchange_sum(list(outs) + partners, size)
    low_last = low_sum_of(split, win - split, low_grad, from_left, gathered)
    above_last = from_behind(low_last, "row", 1)
    mine = [gathered]
    for shift, count in digits[-2::-1]:
        gathered = mine[0] if len(mine) == 1 else join(mine)
        mine = [gathered] + [swap_rows(gathered, i << shift) for i in range(1, count)]
    other = [swap_cores(block) for block in mine]
    new_object, token = object_update(
        object_field, own_grad, from_left, above_first, above_last
    )
    new_probe = probe_update(mine, other, probe, token, probe_modes.shape, size, digits)
    return (new_object, new_probe)


def solution(mesh):
    placed = (
        P(None, ("grp", "row"), "col"),
        P(None, None, "grp", None),
        P(("grp", "row"), "col", None, None),
        P(("grp", "row"), "col"),
        P(("grp", "row"), "col", None, None, None),
    )
    return jax.shard_map(
        body,
        mesh=mesh,
        in_specs=placed,
        out_specs=(P(None, ("grp", "row"), "col"), P(None, None, "grp", None)),
        check_vma=False,
    )
```

```python
import functools

import jax
import jax.numpy as jnp
import ml_dtypes
import numpy as np
from jax import lax
from jax.experimental import pallas as pl
from jax.experimental.pallas import tpu as pltpu
from jax.sharding import PartitionSpec as P

LANES = 128
CHUNK = 32
FINE = 16
TAIL = 16
MIB = 1 << 20
LOW_WEIGHT = 8
SPLIT = 4


def from_behind(block, axis, distance):
    devices = range(lax.axis_size(axis))
    route = [(i - distance, i) for i in devices if i - distance in devices]
    return lax.ppermute(block, axis, route)


def from_next_row(block, col):
    rows, cols = lax.axis_size("row"), lax.axis_size("col")
    route = [((r + 1) * cols + col, r * cols + col) for r in range(rows - 1)]
    return lax.ppermute(block, ("row", "col"), route)


def dft_blocks(win):
    grid = np.arange(win)
    angle = 2.0 * np.pi * (grid[:, None] * grid[None, :] % win) / win
    factor = 1.0 / np.sqrt(win)
    cos_table = (np.cos(angle) * factor).astype(ml_dtypes.bfloat16)
    sin_table = (np.sin(angle) * factor).astype(ml_dtypes.bfloat16)
    blocks = []
    for parity in range(2):
        cos_part, sin_part = cos_table[parity::2, : win // 2], sin_table[parity::2, : win // 2]
        blocks.append(np.block([[cos_part, sin_part], [-sin_part, cos_part]]))
    return np.stack(blocks + [block.T for block in blocks])


def dot(left, right):
    return jnp.dot(left, right, preferred_element_type=jnp.float32)


def put_blocks(field, row, first, sources):
    parts, rows, cols = sources[0].shape
    for part in range(parts):
        for r in range(0, rows, CHUNK):
            pieces = [source[part, r : r + CHUNK, :].astype(jnp.float32) for source in sources]
            values = sum(pieces[1:], pieces[0])
            for b in range(cols // LANES):
                piece = values[:, b * LANES : (b + 1) * LANES]
                field[part, first + b, row + r : row + r + CHUNK, :] = piece


def lay_out_kernel(own, right, field, grad, probe_sum):
    put_blocks(field, 0, 0, (own,))
    put_blocks(field, 0, own.shape[2] // LANES, (right,))
    grad[...] = jnp.zeros_like(grad)
    probe_sum[...] = jnp.zeros_like(probe_sum)


def lay_out(own, right, win, modes):
    rows, cols = own.shape[1:]
    tile = (2, (cols + win) // LANES, rows + win, LANES)
    shapes = (tile, tile, (modes, 2, win // LANES, win, LANES))
    return small_call(
        lay_out_kernel,
        tuple(jax.ShapeDtypeStruct(shape, jnp.float32) for shape in shapes),
        own,
        right,
    )


def gradient_kernel(
    modes,
    starts,
    count,
    power,
    below_left,
    below_right,
    corner,
    probe,
    measured,
    tables,
    field_made,
    grad_made,
    probe_sum_made,
    own_grad,
    low_grad,
    right_grad,
    keep_out,
    send_out,
    norm_out,
    field,
    grad,
    probe_sum,
    window,
    wide,
    tall,
    wave,
    grad_sum,
):
    win = probe.shape[1]
    rows, cols = own_grad.shape[1], own_grad.shape[2]
    half = win // 2
    fine = range(0, win, FINE)
    spread = win // LANES + 1
    col_index = lax.axis_index("col")
    row_anchor = lax.axis_index("row") * rows
    col_anchor = col_index * cols

    norm_out[...] = jnp.zeros_like(norm_out)
    for first, *sources in ((0, below_left, below_right), (cols // LANES, corner)):
        put_blocks(field, rows, first, sources)
    lane = lax.broadcasted_iota(jnp.int32, (FINE, LANES), 1)

    def one_position(slot, carry):
        y, x = starts[0, slot] - row_anchor, starts[1, slot] - col_anchor
        base = x // LANES
        shift = x - base * LANES
        back_shift = (LANES - shift) % LANES
        keep = lane < LANES - shift
        norm = jnp.zeros((8, win), jnp.float32)
        for r in range(0, half, FINE):
            objs = []
            for start in (r, r + half):
                at = pl.ds(start, FINE)
                obj = []
                for part in range(2):
                    turned = [
                        pltpu.roll(field[part, base + b, pl.ds(y + start, FINE), :], back_shift, 1)
                        for b in range(spread)
                    ]
                    piece = jnp.concatenate(
                        [jnp.where(keep, a, b) for a, b in zip(turned[:-1], turned[1:])], axis=1
                    )
                    window[part, at, :] = piece
                    obj.append(piece)
                squares = obj[0] * obj[0] + obj[1] * obj[1]
                norm = norm + jnp.sum(squares.reshape(FINE // 8, 8, win), axis=0)
                objs.append(obj)
            for k in range(modes):
                cs = pl.ds(k * win, win)
                exits = []
                for start, (o_re, o_im) in zip((r, r + half), objs):
                    p_re, p_im = probe[0, pl.ds(start, FINE), cs], probe[1, pl.ds(start, FINE), cs]
                    exits.append((p_re * o_re - p_im * o_im, p_re * o_im + p_im * o_re))
                for part in range(2):
                    low, high = exits[0][part], exits[1][part]
                    at = pl.ds(part * half + r, FINE)
                    wide[k, 0, at, :] = (low + high).astype(jnp.bfloat16)
                    wide[k, 1, at, :] = (low - high).astype(jnp.bfloat16)

        for k in range(modes):
            for parity in range(2):
                out = dot(tables[parity], wide[k, parity])
                at = pl.ds(k * win + parity * half, half)
                for part in range(2):
                    low = out[part * half : (part + 1) * half, :half]
                    high = out[part * half : (part + 1) * half, half:]
                    to = pl.ds(part * half, half)
                    tall[0, at, to] = (low + high).astype(jnp.bfloat16)
                    tall[1, at, to] = (low - high).astype(jnp.bfloat16)
        for parity in range(2):
            wave[parity] = dot(tall[parity], tables[2 + parity])

        for r in fine:
            for parity in range(2):
                waves = []
                total = jnp.zeros((FINE, half), jnp.float32)
                for k in range(modes):
                    ka = pl.ds(k * win + r, FINE)
                    waves.append((wave[parity, ka, :half], wave[parity, ka, half:]))
                    total = total + (waves[k][0] * waves[k][0] + waves[k][1] * waves[k][1])
                gs = pl.ds(parity * half, half)
                amp = measured[slot, pl.ds(r, FINE), gs]
                ratio = 1.0 - amp * lax.rsqrt(jnp.maximum(total, 1.0))
                for k in range(modes):
                    for part in range(2):
                        at = pl.ds(part * half + r % half, FINE)
                        wide[k, r // half, at, gs] = (waves[k][part] * ratio).astype(jnp.bfloat16)

        for k in range(modes):
            even = dot(tables[2], wide[k, 0])
            odd = dot(tables[3], wide[k, 1])
            for place, out in enumerate((even + odd, even - odd)):
                at = pl.ds(k * win + place * half, half)
                for part in range(2):
                    for parity in range(2):
                        tall[parity, at, part * half : (part + 1) * half] = out[
                            part * half : (part + 1) * half, parity * half : (parity + 1) * half
                        ].astype(jnp.bfloat16)
        for parity in range(2):
            wave[parity] = dot(tall[parity], tables[parity])

        for r in fine:
            at = pl.ds(r, FINE)
            sums = [[jnp.zeros((FINE, LANES), jnp.float32) for _ in range(2)] for _ in range(2)]
            for b in range(2):
                bs = pl.ds(b * half, half)
                o_re, o_im = window[0, at, bs], window[1, at, bs]
                for k in range(modes):
                    cs = pl.ds(k * win + b * half, half)
                    ka = pl.ds(k * win + r, FINE)
                    even, odd = wave[0, ka, :], wave[1, ka, :]
                    d = even + odd if b == 0 else even - odd
                    d_re, d_im = d[:, :half], d[:, half:]
                    p_re, p_im = probe[0, at, cs], probe[1, at, cs]
                    sums[0][b] = sums[0][b] + (p_re * d_re + p_im * d_im)
                    sums[1][b] = sums[1][b] + (p_re * d_im - p_im * d_re)
                    probe_sum[k, 0, b, at, :] += o_re * d_re + o_im * d_im
                    probe_sum[k, 1, b, at, :] += o_re * d_im - o_im * d_re
            for part in range(2):
                for b in range(2):
                    grad_sum[part, b, at, :] = sums[part][b]
        norm_out[...] += norm
        high = lax.broadcasted_iota(jnp.int32, (half, LANES), 1) >= shift
        for part in range(2):
            for r in range(0, win, half):
                turned = [pltpu.roll(grad_sum[part, b, pl.ds(r, half), :], shift, 1) for b in range(2)]
                turned = [jnp.zeros_like(turned[0])] + turned + [jnp.zeros_like(turned[0])]
                for b in range(spread):
                    grad[part, base + b, pl.ds(y + r, half), :] += jnp.where(
                        high, turned[b + 1], turned[b]
                    )
        return carry

    lax.fori_loop(0, count[0], one_position, 0)
    for m in range(modes // 2):
        keep_mode = col_index * (modes // 2) + m
        send_mode = (1 - col_index) * (modes // 2) + m
        keep_out[m] = probe_sum[keep_mode]
        send_out[m] = probe_sum[send_mode].astype(jnp.bfloat16)
    scale = 1.0 / jnp.full((8, LANES), power[0], jnp.float32)
    scale = jnp.concatenate([scale] * (CHUNK // 8), axis=0)

    def take_blocks(part, at, first, number):
        return jnp.concatenate(
            [grad[part, first + b, at, :] * scale for b in range(number)], axis=1
        )

    for part in range(2):
        for r in range(0, rows + win, CHUNK):
            at = pl.ds(r, CHUNK)
            piece = take_blocks(part, at, cols // LANES, win // LANES)
            right_grad[part, at, :] = piece.astype(jnp.bfloat16)
        for r in range(0, rows, CHUNK):
            at = pl.ds(r, CHUNK)
            own_grad[part, at, :] = take_blocks(part, at, 0, cols // LANES)
        for r in range(0, win, CHUNK):
            at, of = pl.ds(r, CHUNK), pl.ds(rows + r, CHUNK)
            low_grad[part, at, :] = take_blocks(part, of, 0, cols // LANES)


def position_gradients(starts, count, power, tile, below, corner, probe, measured, tables, made):
    win, modes = probe.shape[1], probe.shape[2] // probe.shape[1]
    rows, cols = tile
    f32, bf16 = jnp.float32, jnp.bfloat16
    smem = pl.BlockSpec(memory_space=pltpu.SMEM)
    vmem = pl.BlockSpec(memory_space=pltpu.VMEM)
    if win != 2 * LANES:
        raise ValueError("window size")
    slots = measured.shape[0]
    flops = 16 * slots * modes * win**3
    half_blocks = (modes // 2, 2, win // LANES, win, LANES)
    return pl.pallas_call(
        functools.partial(gradient_kernel, modes),
        out_shape=(
            jax.ShapeDtypeStruct((2, rows, cols), f32),
            jax.ShapeDtypeStruct((2, win, cols), f32),
            jax.ShapeDtypeStruct((2, rows + win, win), bf16),
            jax.ShapeDtypeStruct(half_blocks, f32),
            jax.ShapeDtypeStruct(half_blocks, bf16),
            jax.ShapeDtypeStruct((8, win), f32),
        )
        + tuple(jax.ShapeDtypeStruct(array.shape, f32) for array in made),
        in_specs=[smem] * 3 + [vmem] * 9,
        out_specs=(vmem,) * 9,
        input_output_aliases={9: 6, 10: 7, 11: 8},
        scratch_shapes=[
            pltpu.VMEM((2, win, win), f32),
            pltpu.VMEM((modes, 2, win, win), bf16),
            pltpu.VMEM((2, modes * win, win), bf16),
            pltpu.VMEM((2, modes * win, win), f32),
            pltpu.VMEM((2, win // LANES, win, LANES), f32),
        ],
        compiler_params=pltpu.CompilerParams(vmem_limit_bytes=16 * MIB),
        cost_estimate=pl.CostEstimate(flops=flops, bytes_accessed=12 << 20, transcendentals=0),
    )(starts, count, power, *below, corner, probe, measured, tables, *made)


def in_three(value):
    full = jnp.full((TAIL, LANES), value, jnp.float32)
    high = full.astype(jnp.bfloat16).astype(jnp.float32)
    mid = (full - high).astype(jnp.bfloat16).astype(jnp.float32)
    low = full - high - mid
    row = lax.broadcasted_iota(jnp.int32, (TAIL, LANES), 0)
    lane = lax.broadcasted_iota(jnp.int32, (TAIL, LANES), 1)
    tile = jnp.where(row == 0, high, jnp.where(row == 1, mid, jnp.where(row == 2, low, 0.0)))
    return jnp.where(lane == 0, tile, 0.0).astype(jnp.bfloat16)


def small_call(kernel, shapes, *operands, weight=1):
    return pl.pallas_call(
        kernel,
        out_shape=shapes,
        compiler_params=pltpu.CompilerParams(vmem_limit_bytes=4 * MIB),
        cost_estimate=pl.CostEstimate(flops=0, bytes_accessed=weight * MIB, transcendentals=0),
    )(*operands)


def first_columns_kernel(block, *refs):
    first = refs[-1]
    first[...] = block[:, :, : first.shape[2]]


def first_columns(block, size, *tokens):
    shape = block.shape[:2] + (size,)
    return small_call(
        first_columns_kernel, jax.ShapeDtypeStruct(shape, block.dtype), block, *tokens
    )


def copies_kernel(block, token, first_rows, first_cols):
    first_rows[...] = block[:, : first_rows.shape[1], :]
    first_cols[...] = block[:, :, : first_cols.shape[2]]


def copies(block, size, token):
    parts, rows, cols = block.shape
    shapes = ((parts, size, cols), (parts, rows, size))
    return small_call(
        copies_kernel,
        tuple(jax.ShapeDtypeStruct(shape, block.dtype) for shape in shapes),
        block,
        token,
    )


def prepare_kernel(probe, intens, blocks, token, tables, measured, wide_probe, power):
    tables[...] = blocks[...]
    count, size, _ = intens.shape
    row = lax.broadcasted_iota(jnp.int32, (size, size), 0)
    col = lax.broadcasted_iota(jnp.int32, (size, size), 1)
    to_even_first = (col == jnp.where(row < size // 2, 2 * row, 2 * row - size + 1)).astype(
        jnp.float32
    )
    from_left = to_even_first.astype(jnp.bfloat16)
    from_right = (row == jnp.where(col < size // 2, 2 * col, 2 * col - size + 1)).astype(
        jnp.float32
    )
    from_right = from_right.astype(jnp.bfloat16)
    for slot in range(count):
        turned = dot(from_left, intens[slot]).astype(jnp.bfloat16)
        measured[slot] = jnp.sqrt(dot(turned, from_right))
    win = probe.shape[1]
    modes = probe.shape[2] // win
    largest = jnp.zeros((8, win), jnp.float32)
    for r in range(0, probe.shape[1], CHUNK):
        at = slice(r, r + CHUNK)
        total = jnp.zeros((CHUNK, win), jnp.float32)
        for k in range(modes):
            for part in range(2):
                p = probe[part, at, k * win : (k + 1) * win].astype(jnp.float32)
                wide_probe[part, at, k * win : (k + 1) * win] = p
                total = total + p * p
        largest = jnp.maximum(largest, jnp.max(total.reshape(CHUNK // 8, 8, win), axis=0))
    power[0, 0] = jnp.max(largest)


def prepare(probe, intens, token):
    win = probe.shape[1]
    blocks = dft_blocks(win)
    vmem = pl.BlockSpec(memory_space=pltpu.VMEM)
    return pl.pallas_call(
        prepare_kernel,
        out_shape=(
            jax.ShapeDtypeStruct(blocks.shape, jnp.bfloat16),
            jax.ShapeDtypeStruct(intens.shape, jnp.float32),
            jax.ShapeDtypeStruct(probe.shape, jnp.float32),
            jax.ShapeDtypeStruct((1, 1), jnp.float32),
        ),
        out_specs=(vmem, vmem, vmem, pl.BlockSpec(memory_space=pltpu.SMEM)),
        compiler_params=pltpu.CompilerParams(vmem_limit_bytes=8 * MIB),
    )(probe, intens, blocks, token)


def block_shapes(number, size, ways):
    if not ways:
        return (jax.ShapeDtypeStruct((number * size + TAIL, LANES), jnp.bfloat16),)
    sends = jax.ShapeDtypeStruct((number // ways * size + TAIL, LANES), jnp.bfloat16)
    return (jax.ShapeDtypeStruct((number // ways, size, LANES), jnp.float32),) + (sends,) * (ways - 1)


def put_block(j, total, outs):
    size = total.shape[0]
    if len(outs) == 1:
        outs[0][pl.ds(j * size, size), :] = total.astype(jnp.bfloat16)
    elif j % len(outs) == 0:
        outs[0][j // len(outs)] = total
    else:
        at = pl.ds(j // len(outs) * size, size)
        outs[j % len(outs)][at, :] = total.astype(jnp.bfloat16)


def put_weight(weight, outs):
    tile = in_three(weight)
    for sent in outs if len(outs) == 1 else outs[1:]:
        sent[pl.ds(sent.shape[0] - TAIL, TAIL), :] = tile


def weight_of(block):
    return jnp.sum(block[pl.ds(block.shape[0] - TAIL, TAIL), :].astype(jnp.float32))


def chip_sum_kernel(pixels, size, keep, received, norm, *outs):
    me = lax.axis_index("row")
    for j in range(keep.shape[0] // size):
        at = pl.ds(pl.multiple_of((j ^ me) * size, size), size)
        put_block(j, keep[at, :] + received[at, :].astype(jnp.float32), outs)
    put_weight(jnp.sum(norm[...]) / pixels, outs)


def chip_sum(keep, received, norm, pixels, number, ways):
    size = keep.shape[0] // number
    return small_call(
        functools.partial(chip_sum_kernel, pixels, size),
        block_shapes(number, size, ways),
        keep,
        received,
        norm,
    )


def scatter_sum_kernel(number, mine, sent, *refs):
    received, outs = refs[:number], refs[number:]
    size = mine.shape[1]
    for j in range(mine.shape[0]):
        total = mine[j]
        for block in received:
            total = total + block[pl.ds(j * size, size), :].astype(jnp.float32)
        put_block(j, total, outs)
    put_weight(sum([weight_of(block) for block in received], weight_of(sent)), outs)


def scatter_sum(mine, sent, received, ways):
    number, size, _ = mine.shape
    return small_call(
        functools.partial(scatter_sum_kernel, len(received)),
        block_shapes(number, size, ways),
        mine,
        sent,
        *received,
    )


def pair_up(terms):
    while len(terms) > 1:
        terms = [a + b for a, b in zip(terms[::2], terms[1::2])]
    return terms[0]


def exchange_sum_kernel(size, *refs):
    blocks, chunks = refs[:-1], refs[-1]
    for j in range((chunks.shape[0] - TAIL) // size):
        terms = [
            block[pl.ds((j ^ i) * size, size), :].astype(jnp.float32)
            for i, block in enumerate(blocks)
        ]
        chunks[pl.ds(j * size, size), :] = pair_up(terms).astype(jnp.bfloat16)
    put_weight(pair_up([weight_of(block) for block in blocks]), (chunks,))


def exchange_sum(blocks, size):
    return small_call(
        functools.partial(exchange_sum_kernel, size),
        jax.ShapeDtypeStruct(blocks[0].shape, jnp.bfloat16),
        *blocks,
    )


def copy_chunks(blocks, joined):
    at = 0
    for block in blocks:
        rows = block.shape[0] - TAIL
        joined[pl.ds(at, rows), :] = block[pl.ds(0, rows), :]
        at += rows
    joined[pl.ds(at, TAIL), :] = blocks[0][pl.ds(blocks[0].shape[0] - TAIL, TAIL), :]


def join_kernel(*refs):
    copy_chunks(refs[:-1], refs[-1])


def join(blocks):
    rows = sum(block.shape[0] - TAIL for block in blocks) + TAIL
    return small_call(join_kernel, jax.ShapeDtypeStruct((rows, LANES), blocks[0].dtype), *blocks)


def swap_rows(block, step):
    number = lax.axis_size("row")
    return lax.ppermute(block, "row", [(i, i ^ step) for i in range(number)])


def row_digits():
    number = lax.axis_size("row")
    if number & (number - 1) or number < 2:
        raise ValueError("row size")
    bits = number.bit_length() - 1
    return [(shift, 1 << min(2, bits - shift)) for shift in range(0, bits, 2)]


def probe_update_kernel(size, digits, *refs):
    *blocks, probe, token, new_probe, mine, other, updated, sems = refs
    copy_chunks(blocks[: len(blocks) // 2], mine)
    copy_chunks(blocks[len(blocks) // 2 :], other)
    _, win, modes, _ = updated.shape
    number = mine.shape[0] // size
    me = lax.axis_index("row")
    piece = min(size, CHUNK)
    on_left = lax.axis_index("col") == 0
    tail = pl.ds(number * size, TAIL)
    tails = mine[tail, :].astype(jnp.float32) + other[tail, :].astype(jnp.float32)
    factor = 4.0 / jnp.full((piece, LANES), jnp.sum(tails), jnp.float32)
    half = modes // 2

    def place(chunk):
        j = chunk ^ me
        at, span = 0, 1
        for shift, ways in reversed(digits):
            at = at + ((j >> shift) & (ways - 1)) * span
            span *= ways
        return at * size

    def update(part, b, m, r):
        block = ((m * 2 + part) * (win // LANES) + b) * win
        chunk, offset = divmod(block + r, size)
        at = pl.ds(pl.multiple_of(place(chunk) + offset, piece), piece)
        here = mine[at, :].astype(jnp.float32)
        there = other[at, :].astype(jnp.float32)
        low = jnp.where(on_left, here, there)
        high = jnp.where(on_left, there, here)
        for k, total in ((m, low), (half + m, high)):
            col = k * win + b * LANES
            old = probe[part, r : r + piece, col : col + LANES]
            updated[part, r : r + piece, k, b * LANES : (b + 1) * LANES] = old - factor * total

    stretch = win // 4
    copies = []
    for part in range(2):
        for start in range(0, win, stretch):
            for r in range(start, start + stretch, piece):
                for m in range(half):
                    for b in range(win // LANES):
                        update(part, b, m, r)
            at = (part, pl.ds(start, stretch))
            copies.append(
                pltpu.make_async_copy(updated.at[at], new_probe.at[at], sems.at[len(copies)])
            )
            copies[-1].start()
    for copy in copies:
        copy.wait()


def probe_update(mine, other, probe, token, shape, size, digits):
    vmem = pl.BlockSpec(memory_space=pltpu.VMEM)
    rows = sum(block.shape[0] - TAIL for block in mine) + TAIL
    operands = (*mine, *other, probe, token)
    return pl.pallas_call(
        functools.partial(probe_update_kernel, size, digits),
        out_shape=jax.ShapeDtypeStruct(shape, jnp.float32),
        in_specs=[vmem] * len(operands),
        out_specs=pl.BlockSpec(memory_space=pl.ANY),
        scratch_shapes=[
            pltpu.VMEM((rows, LANES), jnp.bfloat16),
            pltpu.VMEM((rows, LANES), jnp.bfloat16),
            pltpu.VMEM(shape, jnp.float32),
            pltpu.SemaphoreType.DMA((8,)),
        ],
        compiler_params=pltpu.CompilerParams(vmem_limit_bytes=8 * MIB),
    )(*operands)


def low_sum_kernel(first, low_grad, from_left, token, low_sum):
    win = from_left.shape[2]
    rows = from_left.shape[1] - low_grad.shape[1]
    for part in range(2):
        for r in range(0, low_sum.shape[1], CHUNK):
            at, of = slice(r, r + CHUNK), slice(first + r, first + r + CHUNK)
            arrived = from_left[part, rows + first + r : rows + first + r + CHUNK, :]
            total = low_grad[part, of, :win] + arrived.astype(jnp.float32)
            low_sum[part, at, :win] = total.astype(jnp.bfloat16)
            low_sum[part, at, win:] = low_grad[part, of, win:].astype(jnp.bfloat16)


def low_sum_of(first, count, low_grad, from_left, token):
    return small_call(
        functools.partial(low_sum_kernel, first),
        jax.ShapeDtypeStruct((2, count, low_grad.shape[2]), jnp.bfloat16),
        low_grad,
        from_left,
        token,
        weight=LOW_WEIGHT,
    )


def object_update_kernel(old, own_grad, from_left, above_first, above_last, new_object, token):
    token[...] = jnp.zeros_like(token)
    win, split = from_left.shape[2], above_first.shape[1]
    depth = split + above_last.shape[1]
    for part in range(2):
        for r in range(0, old.shape[1], CHUNK):
            at = slice(r, r + CHUNK)
            total = own_grad[part, at, :]
            if r < split:
                total = total + above_first[part, at, :].astype(jnp.float32)
            elif r < depth:
                total = total + above_last[part, r - split : r - split + CHUNK, :].astype(jnp.float32)
            updated = old[part, at, :].astype(jnp.float32) - total
            arrived = from_left[part, at, :].astype(jnp.float32)
            new_object[part, at, :win] = updated[:, :win] - arrived
            new_object[part, at, win:] = updated[:, win:]


def object_update(old, own_grad, from_left, above_first, above_last):
    return small_call(
        object_update_kernel,
        (
            jax.ShapeDtypeStruct(old.shape, jnp.float32),
            jax.ShapeDtypeStruct((8, LANES), jnp.float32),
        ),
        old,
        own_grad,
        from_left,
        above_first,
        above_last,
    )


def swap_cores(block):
    return lax.ppermute(block, "col", [(0, 1), (1, 0)])


def body(object_field, probe_modes, positions, counts, intensities):
    win = probe_modes.shape[1]
    modes = probe_modes.shape[2]
    number = lax.axis_size("row")
    below_right = from_next_row(object_field[:, :win, :], 1)
    probe_flat = probe_modes.reshape(2, win, modes * win)
    first_rows, first_cols = copies(object_field, win, probe_flat)
    below_left = from_next_row(first_rows, 0)
    right = from_behind(first_cols, "col", -1)
    tables, measured, probe, power = prepare(probe_flat, intensities[0, 0], right)
    made = lay_out(object_field, right, win, modes)
    corner = from_behind(first_columns(below_right, win, tables, made[0]), "col", -1)
    own_grad, low_grad, right_grad, keep, send, norm, *_ = position_gradients(
        positions[0, 0].T,
        counts.reshape(-1),
        power.reshape(1),
        object_field.shape[1:],
        (below_left, below_right),
        corner,
        probe,
        measured,
        tables,
        made,
    )
    half_rows = keep.size // LANES
    received = swap_cores(send.reshape(half_rows, LANES))
    from_left = from_behind(right_grad, "col", 1)
    digits = row_digits()
    size = half_rows // number
    ways = [digit[1] for digit in digits[:-1]] + [0]
    outs = chip_sum(keep.reshape(half_rows, LANES), received, norm, win * win, number, ways[0])
    for place, (shift, _) in enumerate(digits[:-1]):
        mine, *sends = outs
        received = [swap_rows(block, (i + 1) << shift) for i, block in enumerate(sends)]
        outs = scatter_sum(mine, sends[0], received, ways[place + 1])
    split = SPLIT * win // 8
    low_first = low_sum_of(0, split, low_grad, from_left, outs[0])
    above_first = from_behind(low_first, "row", 1)
    shift, count = digits[-1]
    partners = [swap_rows(outs[0], i << shift) for i in range(1, count)]
    gathered = exchange_sum(list(outs) + partners, size)
    low_last = low_sum_of(split, win - split, low_grad, from_left, gathered)
    above_last = from_behind(low_last, "row", 1)
    mine = [gathered]
    for shift, count in digits[-2::-1]:
        gathered = mine[0] if len(mine) == 1 else join(mine)
        mine = [gathered] + [swap_rows(gathered, i << shift) for i in range(1, count)]
    other = [swap_cores(block) for block in mine]
    new_object, token = object_update(
        object_field, own_grad, from_left, above_first, above_last
    )
    new_probe = probe_update(mine, other, probe, token, probe_modes.shape, size, digits)
    return (new_object, new_probe)


def solution(mesh):
    placed = (
        P(None, ("grp", "row"), "col"),
        P(None, None, "grp", None),
        P(("grp", "row"), "col", None, None),
        P(("grp", "row"), "col"),
        P(("grp", "row"), "col", None, None, None),
    )
    return jax.shard_map(
        body,
        mesh=mesh,
        in_specs=placed,
        out_specs=(P(None, ("grp", "row"), "col"), P(None, None, "grp", None)),
        check_vma=False,
    )
```

```python
import functools

import jax
import jax.numpy as jnp
import ml_dtypes
import numpy as np
from jax import lax
from jax.experimental import pallas as pl
from jax.experimental.pallas import tpu as pltpu
from jax.sharding import PartitionSpec as P

LANES = 128
CHUNK = 32
FINE = 16
TAIL = 16
MIB = 1 << 20
LOW_WEIGHT = 8
SPLIT = 4


def from_behind(block, axis, distance):
    devices = range(lax.axis_size(axis))
    route = [(i - distance, i) for i in devices if i - distance in devices]
    return lax.ppermute(block, axis, route)


def from_next_row(block, col):
    rows, cols = lax.axis_size("row"), lax.axis_size("col")
    route = [((r + 1) * cols + col, r * cols + col) for r in range(rows - 1)]
    return lax.ppermute(block, ("row", "col"), route)


def dft_blocks(win):
    grid = np.arange(win)
    angle = 2.0 * np.pi * (grid[:, None] * grid[None, :] % win) / win
    factor = 1.0 / np.sqrt(win)
    cos_table = (np.cos(angle) * factor).astype(ml_dtypes.bfloat16)
    sin_table = (np.sin(angle) * factor).astype(ml_dtypes.bfloat16)
    blocks = []
    for parity in range(2):
        cos_part, sin_part = cos_table[parity::2, : win // 2], sin_table[parity::2, : win // 2]
        blocks.append(np.block([[cos_part, sin_part], [-sin_part, cos_part]]))
    return np.stack(blocks + [block.T for block in blocks])


def dot(left, right):
    return jnp.dot(left, right, preferred_element_type=jnp.float32)


def put_blocks(field, row, first, sources):
    parts, rows, cols = sources[0].shape
    for part in range(parts):
        for r in range(0, rows, CHUNK):
            pieces = [source[part, r : r + CHUNK, :].astype(jnp.float32) for source in sources]
            values = sum(pieces[1:], pieces[0])
            for b in range(cols // LANES):
                piece = values[:, b * LANES : (b + 1) * LANES]
                field[part, first + b, row + r : row + r + CHUNK, :] = piece


def lay_out_kernel(own, right, field, grad, probe_sum):
    put_blocks(field, 0, 0, (own,))
    put_blocks(field, 0, own.shape[2] // LANES, (right,))
    grad[...] = jnp.zeros_like(grad)
    probe_sum[...] = jnp.zeros_like(probe_sum)


def lay_out(own, right, win, modes):
    rows, cols = own.shape[1:]
    tile = (2, (cols + win) // LANES, rows + win, LANES)
    shapes = (tile, tile, (modes, 2, win // LANES, win, LANES))
    return small_call(
        lay_out_kernel,
        tuple(jax.ShapeDtypeStruct(shape, jnp.float32) for shape in shapes),
        own,
        right,
    )


def gradient_kernel(
    modes,
    starts,
    count,
    power,
    below_left,
    below_right,
    corner,
    probe,
    measured,
    tables,
    field_made,
    grad_made,
    probe_sum_made,
    own_grad,
    low_grad,
    right_grad,
    keep_out,
    send_out,
    norm_out,
    field,
    grad,
    probe_sum,
    window,
    wide,
    tall,
    wave,
):
    win = probe.shape[1]
    rows, cols = own_grad.shape[1], own_grad.shape[2]
    half = win // 2
    fine = range(0, win, FINE)
    spread = win // LANES + 1
    col_index = lax.axis_index("col")
    row_anchor = lax.axis_index("row") * rows
    col_anchor = col_index * cols

    norm_out[...] = jnp.zeros_like(norm_out)
    for first, *sources in ((0, below_left, below_right), (cols // LANES, corner)):
        put_blocks(field, rows, first, sources)
    lane = lax.broadcasted_iota(jnp.int32, (FINE, LANES), 1)

    def one_position(slot, carry):
        y, x = starts[0, slot] - row_anchor, starts[1, slot] - col_anchor
        base = x // LANES
        shift = x - base * LANES
        back_shift = (LANES - shift) % LANES
        keep = lane < LANES - shift
        for r in range(0, half, FINE):
            objs = []
            for start in (r, r + half):
                at = pl.ds(start, FINE)
                obj = []
                for part in range(2):
                    turned = [
                        pltpu.roll(field[part, base + b, pl.ds(y + start, FINE), :], back_shift, 1)
                        for b in range(spread)
                    ]
                    piece = jnp.concatenate(
                        [jnp.where(keep, a, b) for a, b in zip(turned[:-1], turned[1:])], axis=1
                    )
                    window[part, at, :] = piece
                    obj.append(piece)
                squares = obj[0] * obj[0] + obj[1] * obj[1]
                norm_out[...] += jnp.sum(squares.reshape(FINE // 8, 8, win), axis=0)
                objs.append(obj)
            for k in range(modes):
                cs = pl.ds(k * win, win)
                exits = []
                for start, (o_re, o_im) in zip((r, r + half), objs):
                    p_re, p_im = probe[0, pl.ds(start, FINE), cs], probe[1, pl.ds(start, FINE), cs]
                    exits.append((p_re * o_re - p_im * o_im, p_re * o_im + p_im * o_re))
                for part in range(2):
                    low, high = exits[0][part], exits[1][part]
                    at = pl.ds(part * half + r, FINE)
                    wide[k, 0, at, :] = (low + high).astype(jnp.bfloat16)
                    wide[k, 1, at, :] = (low - high).astype(jnp.bfloat16)

        for k in range(modes):
            for parity in range(2):
                out = dot(tables[parity], wide[k, parity])
                at = pl.ds(k * win + parity * half, half)
                for part in range(2):
                    low = out[part * half : (part + 1) * half, :half]
                    high = out[part * half : (part + 1) * half, half:]
                    to = pl.ds(part * half, half)
                    tall[0, at, to] = (low + high).astype(jnp.bfloat16)
                    tall[1, at, to] = (low - high).astype(jnp.bfloat16)
        for parity in range(2):
            wave[parity] = dot(tall[parity], tables[2 + parity])

        for r in fine:
            for parity in range(2):
                waves = []
                total = jnp.zeros((FINE, half), jnp.float32)
                for k in range(modes):
                    ka = pl.ds(k * win + r, FINE)
                    waves.append((wave[parity, ka, :half], wave[parity, ka, half:]))
                    total = total + (waves[k][0] * waves[k][0] + waves[k][1] * waves[k][1])
                gs = pl.ds(parity * half, half)
                amp = measured[slot, pl.ds(r, FINE), gs]
                ratio = 1.0 - amp * lax.rsqrt(jnp.maximum(total, 1.0))
                for k in range(modes):
                    for part in range(2):
                        at = pl.ds(part * half + r % half, FINE)
                        wide[k, r // half, at, gs] = (waves[k][part] * ratio).astype(jnp.bfloat16)

        for k in range(modes):
            even = dot(tables[2], wide[k, 0])
            odd = dot(tables[3], wide[k, 1])
            for place, out in enumerate((even + odd, even - odd)):
                at = pl.ds(k * win + place * half, half)
                for part in range(2):
                    for parity in range(2):
                        tall[parity, at, part * half : (part + 1) * half] = out[
                            part * half : (part + 1) * half, parity * half : (parity + 1) * half
                        ].astype(jnp.bfloat16)
        for parity in range(2):
            wave[parity] = dot(tall[parity], tables[parity])

        keep_high = lane >= shift
        for r in fine:
            at = pl.ds(r, FINE)
            sums = [[jnp.zeros((FINE, LANES), jnp.float32) for _ in range(2)] for _ in range(2)]
            for b in range(2):
                bs = pl.ds(b * half, half)
                o_re, o_im = window[0, at, bs], window[1, at, bs]
                for k in range(modes):
                    cs = pl.ds(k * win + b * half, half)
                    ka = pl.ds(k * win + r, FINE)
                    even, odd = wave[0, ka, :], wave[1, ka, :]
                    d = even + odd if b == 0 else even - odd
                    d_re, d_im = d[:, :half], d[:, half:]
                    p_re, p_im = probe[0, at, cs], probe[1, at, cs]
                    sums[0][b] = sums[0][b] + (p_re * d_re + p_im * d_im)
                    sums[1][b] = sums[1][b] + (p_re * d_im - p_im * d_re)
                    probe_sum[k, 0, b, at, :] += o_re * d_re + o_im * d_im
                    probe_sum[k, 1, b, at, :] += o_re * d_im - o_im * d_re
            for part in range(2):
                turned = [pltpu.roll(piece, shift, 1) for piece in sums[part]]
                turned = [jnp.zeros_like(turned[0])] + turned + [jnp.zeros_like(turned[0])]
                for b in range(spread):
                    grad[part, base + b, pl.ds(y + r, FINE), :] += jnp.where(
                        keep_high, turned[b + 1], turned[b]
                    )
        return carry

    lax.fori_loop(0, count[0], one_position, 0)
    for m in range(modes // 2):
        keep_mode = col_index * (modes // 2) + m
        send_mode = (1 - col_index) * (modes // 2) + m
        keep_out[m] = probe_sum[keep_mode]
        send_out[m] = probe_sum[send_mode].astype(jnp.bfloat16)
    scale = 1.0 / jnp.full((8, LANES), power[0], jnp.float32)
    scale = jnp.concatenate([scale] * (CHUNK // 8), axis=0)

    def take_blocks(part, at, first, number):
        return jnp.concatenate(
            [grad[part, first + b, at, :] * scale for b in range(number)], axis=1
        )

    for part in range(2):
        for r in range(0, rows + win, CHUNK):
            at = pl.ds(r, CHUNK)
            piece = take_blocks(part, at, cols // LANES, win // LANES)
            right_grad[part, at, :] = piece.astype(jnp.bfloat16)
        for r in range(0, rows, CHUNK):
            at = pl.ds(r, CHUNK)
            own_grad[part, at, :] = take_blocks(part, at, 0, cols // LANES)
        for r in range(0, win, CHUNK):
            at, of = pl.ds(r, CHUNK), pl.ds(rows + r, CHUNK)
            low_grad[part, at, :] = take_blocks(part, of, 0, cols // LANES)


def position_gradients(starts, count, power, tile, below, corner, probe, measured, tables, made):
    win, modes = probe.shape[1], probe.shape[2] // probe.shape[1]
    rows, cols = tile
    f32, bf16 = jnp.float32, jnp.bfloat16
    smem = pl.BlockSpec(memory_space=pltpu.SMEM)
    vmem = pl.BlockSpec(memory_space=pltpu.VMEM)
    if win != 2 * LANES:
        raise ValueError("window size")
    slots = measured.shape[0]
    flops = 16 * slots * modes * win**3
    half_blocks = (modes // 2, 2, win // LANES, win, LANES)
    return pl.pallas_call(
        functools.partial(gradient_kernel, modes),
        out_shape=(
            jax.ShapeDtypeStruct((2, rows, cols), f32),
            jax.ShapeDtypeStruct((2, win, cols), f32),
            jax.ShapeDtypeStruct((2, rows + win, win), bf16),
            jax.ShapeDtypeStruct(half_blocks, f32),
            jax.ShapeDtypeStruct(half_blocks, bf16),
            jax.ShapeDtypeStruct((8, win), f32),
        )
        + tuple(jax.ShapeDtypeStruct(array.shape, f32) for array in made),
        in_specs=[smem] * 3 + [vmem] * 9,
        out_specs=(vmem,) * 9,
        input_output_aliases={9: 6, 10: 7, 11: 8},
        scratch_shapes=[
            pltpu.VMEM((2, win, win), f32),
            pltpu.VMEM((modes, 2, win, win), bf16),
            pltpu.VMEM((2, modes * win, win), bf16),
            pltpu.VMEM((2, modes * win, win), f32),
        ],
        compiler_params=pltpu.CompilerParams(vmem_limit_bytes=16 * MIB),
        cost_estimate=pl.CostEstimate(flops=flops, bytes_accessed=12 << 20, transcendentals=0),
    )(starts, count, power, *below, corner, probe, measured, tables, *made)


def in_three(value):
    full = jnp.full((TAIL, LANES), value, jnp.float32)
    high = full.astype(jnp.bfloat16).astype(jnp.float32)
    mid = (full - high).astype(jnp.bfloat16).astype(jnp.float32)
    low = full - high - mid
    row = lax.broadcasted_iota(jnp.int32, (TAIL, LANES), 0)
    lane = lax.broadcasted_iota(jnp.int32, (TAIL, LANES), 1)
    tile = jnp.where(row == 0, high, jnp.where(row == 1, mid, jnp.where(row == 2, low, 0.0)))
    return jnp.where(lane == 0, tile, 0.0).astype(jnp.bfloat16)


def small_call(kernel, shapes, *operands, weight=1):
    return pl.pallas_call(
        kernel,
        out_shape=shapes,
        compiler_params=pltpu.CompilerParams(vmem_limit_bytes=4 * MIB),
        cost_estimate=pl.CostEstimate(flops=0, bytes_accessed=weight * MIB, transcendentals=0),
    )(*operands)


def first_columns_kernel(block, *refs):
    first = refs[-1]
    first[...] = block[:, :, : first.shape[2]]


def first_columns(block, size, *tokens):
    shape = block.shape[:2] + (size,)
    return small_call(
        first_columns_kernel, jax.ShapeDtypeStruct(shape, block.dtype), block, *tokens
    )


def copies_kernel(block, token, same, first_cols):
    same[...] = block[...]
    first_cols[...] = block[:, :, : first_cols.shape[2]]


def copies(block, size, token):
    shapes = (block.shape, block.shape[:2] + (size,))
    return small_call(
        copies_kernel,
        tuple(jax.ShapeDtypeStruct(shape, block.dtype) for shape in shapes),
        block,
        token,
    )


def prepare_kernel(probe, intens, blocks, token, tables, measured, wide_probe, power):
    tables[...] = blocks[...]
    count, size, _ = intens.shape
    row = lax.broadcasted_iota(jnp.int32, (size, size), 0)
    col = lax.broadcasted_iota(jnp.int32, (size, size), 1)
    to_even_first = (col == jnp.where(row < size // 2, 2 * row, 2 * row - size + 1)).astype(
        jnp.float32
    )
    from_left = to_even_first.astype(jnp.bfloat16)
    from_right = (row == jnp.where(col < size // 2, 2 * col, 2 * col - size + 1)).astype(
        jnp.float32
    )
    from_right = from_right.astype(jnp.bfloat16)
    for slot in range(count):
        turned = dot(from_left, intens[slot]).astype(jnp.bfloat16)
        measured[slot] = jnp.sqrt(dot(turned, from_right))
    win = probe.shape[1]
    modes = probe.shape[2] // win
    largest = jnp.zeros((8, win), jnp.float32)
    for r in range(0, probe.shape[1], CHUNK):
        at = slice(r, r + CHUNK)
        total = jnp.zeros((CHUNK, win), jnp.float32)
        for k in range(modes):
            for part in range(2):
                p = probe[part, at, k * win : (k + 1) * win].astype(jnp.float32)
                wide_probe[part, at, k * win : (k + 1) * win] = p
                total = total + p * p
        largest = jnp.maximum(largest, jnp.max(total.reshape(CHUNK // 8, 8, win), axis=0))
    power[0, 0] = jnp.max(largest)


def prepare(probe, intens, token):
    win = probe.shape[1]
    blocks = dft_blocks(win)
    vmem = pl.BlockSpec(memory_space=pltpu.VMEM)
    return pl.pallas_call(
        prepare_kernel,
        out_shape=(
            jax.ShapeDtypeStruct(blocks.shape, jnp.bfloat16),
            jax.ShapeDtypeStruct(intens.shape, jnp.float32),
            jax.ShapeDtypeStruct(probe.shape, jnp.float32),
            jax.ShapeDtypeStruct((1, 1), jnp.float32),
        ),
        out_specs=(vmem, vmem, vmem, pl.BlockSpec(memory_space=pltpu.SMEM)),
        compiler_params=pltpu.CompilerParams(vmem_limit_bytes=8 * MIB),
    )(probe, intens, blocks, token)


def block_shapes(number, size, ways):
    if not ways:
        return (jax.ShapeDtypeStruct((number * size + TAIL, LANES), jnp.bfloat16),)
    sends = jax.ShapeDtypeStruct((number // ways * size + TAIL, LANES), jnp.bfloat16)
    return (jax.ShapeDtypeStruct((number // ways, size, LANES), jnp.float32),) + (sends,) * (ways - 1)


def put_block(j, total, outs):
    size = total.shape[0]
    if len(outs) == 1:
        outs[0][pl.ds(j * size, size), :] = total.astype(jnp.bfloat16)
    elif j % len(outs) == 0:
        outs[0][j // len(outs)] = total
    else:
        at = pl.ds(j // len(outs) * size, size)
        outs[j % len(outs)][at, :] = total.astype(jnp.bfloat16)


def put_weight(weight, outs):
    tile = in_three(weight)
    for sent in outs if len(outs) == 1 else outs[1:]:
        sent[pl.ds(sent.shape[0] - TAIL, TAIL), :] = tile


def weight_of(block):
    return jnp.sum(block[pl.ds(block.shape[0] - TAIL, TAIL), :].astype(jnp.float32))


def chip_sum_kernel(pixels, size, keep, received, norm, *outs):
    me = lax.axis_index("row")
    for j in range(keep.shape[0] // size):
        at = pl.ds(pl.multiple_of((j ^ me) * size, size), size)
        put_block(j, keep[at, :] + received[at, :].astype(jnp.float32), outs)
    put_weight(jnp.sum(norm[...]) / pixels, outs)


def chip_sum(keep, received, norm, pixels, number, ways):
    size = keep.shape[0] // number
    return small_call(
        functools.partial(chip_sum_kernel, pixels, size),
        block_shapes(number, size, ways),
        keep,
        received,
        norm,
    )


def scatter_sum_kernel(number, mine, sent, *refs):
    received, outs = refs[:number], refs[number:]
    size = mine.shape[1]
    for j in range(mine.shape[0]):
        total = mine[j]
        for block in received:
            total = total + block[pl.ds(j * size, size), :].astype(jnp.float32)
        put_block(j, total, outs)
    put_weight(sum([weight_of(block) for block in received], weight_of(sent)), outs)


def scatter_sum(mine, sent, received, ways):
    number, size, _ = mine.shape
    return small_call(
        functools.partial(scatter_sum_kernel, len(received)),
        block_shapes(number, size, ways),
        mine,
        sent,
        *received,
    )


def pair_up(terms):
    while len(terms) > 1:
        terms = [a + b for a, b in zip(terms[::2], terms[1::2])]
    return terms[0]


def exchange_sum_kernel(size, *refs):
    blocks, chunks = refs[:-1], refs[-1]
    for j in range((chunks.shape[0] - TAIL) // size):
        terms = [
            block[pl.ds((j ^ i) * size, size), :].astype(jnp.float32)
            for i, block in enumerate(blocks)
        ]
        chunks[pl.ds(j * size, size), :] = pair_up(terms).astype(jnp.bfloat16)
    put_weight(pair_up([weight_of(block) for block in blocks]), (chunks,))


def exchange_sum(blocks, size):
    return small_call(
        functools.partial(exchange_sum_kernel, size),
        jax.ShapeDtypeStruct(blocks[0].shape, jnp.bfloat16),
        *blocks,
    )


def copy_chunks(blocks, joined):
    at = 0
    for block in blocks:
        rows = block.shape[0] - TAIL
        joined[pl.ds(at, rows), :] = block[pl.ds(0, rows), :]
        at += rows
    joined[pl.ds(at, TAIL), :] = blocks[0][pl.ds(blocks[0].shape[0] - TAIL, TAIL), :]


def join_kernel(*refs):
    copy_chunks(refs[:-1], refs[-1])


def join(blocks):
    rows = sum(block.shape[0] - TAIL for block in blocks) + TAIL
    return small_call(join_kernel, jax.ShapeDtypeStruct((rows, LANES), blocks[0].dtype), *blocks)


def swap_rows(block, step):
    number = lax.axis_size("row")
    return lax.ppermute(block, "row", [(i, i ^ step) for i in range(number)])


def row_digits():
    number = lax.axis_size("row")
    if number & (number - 1) or number < 2:
        raise ValueError("row size")
    bits = number.bit_length() - 1
    return [(shift, 1 << min(2, bits - shift)) for shift in range(0, bits, 2)]


def probe_update_kernel(size, digits, *refs):
    *blocks, probe, token, new_probe, mine, other, updated, sems = refs
    copy_chunks(blocks[: len(blocks) // 2], mine)
    copy_chunks(blocks[len(blocks) // 2 :], other)
    _, win, modes, _ = updated.shape
    number = mine.shape[0] // size
    me = lax.axis_index("row")
    piece = min(size, CHUNK)
    on_left = lax.axis_index("col") == 0
    tail = pl.ds(number * size, TAIL)
    tails = mine[tail, :].astype(jnp.float32) + other[tail, :].astype(jnp.float32)
    factor = 4.0 / jnp.full((piece, LANES), jnp.sum(tails), jnp.float32)
    half = modes // 2

    def place(chunk):
        j = chunk ^ me
        at, span = 0, 1
        for shift, ways in reversed(digits):
            at = at + ((j >> shift) & (ways - 1)) * span
            span *= ways
        return at * size

    def update(part, b, m, r):
        block = ((m * 2 + part) * (win // LANES) + b) * win
        chunk, offset = divmod(block + r, size)
        at = pl.ds(pl.multiple_of(place(chunk) + offset, piece), piece)
        here = mine[at, :].astype(jnp.float32)
        there = other[at, :].astype(jnp.float32)
        low = jnp.where(on_left, here, there)
        high = jnp.where(on_left, there, here)
        for k, total in ((m, low), (half + m, high)):
            col = k * win + b * LANES
            old = probe[part, r : r + piece, col : col + LANES]
            updated[part, r : r + piece, k, b * LANES : (b + 1) * LANES] = old - factor * total

    stretch = win // 4
    copies = []
    for part in range(2):
        for start in range(0, win, stretch):
            for r in range(start, start + stretch, piece):
                for m in range(half):
                    for b in range(win // LANES):
                        update(part, b, m, r)
            at = (part, pl.ds(start, stretch))
            copies.append(
                pltpu.make_async_copy(updated.at[at], new_probe.at[at], sems.at[len(copies)])
            )
            copies[-1].start()
    for copy in copies:
        copy.wait()


def probe_update(mine, other, probe, token, shape, size, digits):
    vmem = pl.BlockSpec(memory_space=pltpu.VMEM)
    rows = sum(block.shape[0] - TAIL for block in mine) + TAIL
    operands = (*mine, *other, probe, token)
    return pl.pallas_call(
        functools.partial(probe_update_kernel, size, digits),
        out_shape=jax.ShapeDtypeStruct(shape, jnp.float32),
        in_specs=[vmem] * len(operands),
        out_specs=pl.BlockSpec(memory_space=pl.ANY),
        scratch_shapes=[
            pltpu.VMEM((rows, LANES), jnp.bfloat16),
            pltpu.VMEM((rows, LANES), jnp.bfloat16),
            pltpu.VMEM(shape, jnp.float32),
            pltpu.SemaphoreType.DMA((8,)),
        ],
        compiler_params=pltpu.CompilerParams(vmem_limit_bytes=8 * MIB),
    )(*operands)


def low_sum_kernel(first, low_grad, from_left, token, low_sum):
    win = from_left.shape[2]
    rows = from_left.shape[1] - low_grad.shape[1]
    for part in range(2):
        for r in range(0, low_sum.shape[1], CHUNK):
            at, of = slice(r, r + CHUNK), slice(first + r, first + r + CHUNK)
            arrived = from_left[part, rows + first + r : rows + first + r + CHUNK, :]
            total = low_grad[part, of, :win] + arrived.astype(jnp.float32)
            low_sum[part, at, :win] = total.astype(jnp.bfloat16)
            low_sum[part, at, win:] = low_grad[part, of, win:].astype(jnp.bfloat16)


def low_sum_of(first, count, low_grad, from_left, token):
    return small_call(
        functools.partial(low_sum_kernel, first),
        jax.ShapeDtypeStruct((2, count, low_grad.shape[2]), jnp.bfloat16),
        low_grad,
        from_left,
        token,
        weight=LOW_WEIGHT,
    )


def object_update_kernel(old, own_grad, from_left, above_first, above_last, new_object, token):
    token[...] = jnp.zeros_like(token)
    win, split = from_left.shape[2], above_first.shape[1]
    depth = split + above_last.shape[1]
    for part in range(2):
        for r in range(0, old.shape[1], CHUNK):
            at = slice(r, r + CHUNK)
            total = own_grad[part, at, :]
            if r < split:
                total = total + above_first[part, at, :].astype(jnp.float32)
            elif r < depth:
                total = total + above_last[part, r - split : r - split + CHUNK, :].astype(jnp.float32)
            updated = old[part, at, :].astype(jnp.float32) - total
            arrived = from_left[part, at, :].astype(jnp.float32)
            new_object[part, at, :win] = updated[:, :win] - arrived
            new_object[part, at, win:] = updated[:, win:]


def object_update(old, own_grad, from_left, above_first, above_last):
    return small_call(
        object_update_kernel,
        (
            jax.ShapeDtypeStruct(old.shape, jnp.float32),
            jax.ShapeDtypeStruct((8, LANES), jnp.float32),
        ),
        old,
        own_grad,
        from_left,
        above_first,
        above_last,
    )


def swap_cores(block):
    return lax.ppermute(block, "col", [(0, 1), (1, 0)])


def body(object_field, probe_modes, positions, counts, intensities):
    win = probe_modes.shape[1]
    modes = probe_modes.shape[2]
    number = lax.axis_size("row")
    below_right = from_next_row(object_field[:, :win, :], 1)
    probe_flat = probe_modes.reshape(2, win, modes * win)
    own, first_cols = copies(object_field, win, probe_flat)
    below_left = from_next_row(own[:, :win, :], 0)
    right = from_behind(first_cols, "col", -1)
    tables, measured, probe, power = prepare(probe_flat, intensities[0, 0], right)
    made = lay_out(own, right, win, modes)
    corner = from_behind(first_columns(below_right, win, tables, made[0]), "col", -1)
    own_grad, low_grad, right_grad, keep, send, norm, *_ = position_gradients(
        positions[0, 0].T,
        counts.reshape(-1),
        power.reshape(1),
        object_field.shape[1:],
        (below_left, below_right),
        corner,
        probe,
        measured,
        tables,
        made,
    )
    half_rows = keep.size // LANES
    received = swap_cores(send.reshape(half_rows, LANES))
    from_left = from_behind(right_grad, "col", 1)
    digits = row_digits()
    size = half_rows // number
    ways = [digit[1] for digit in digits[:-1]] + [0]
    outs = chip_sum(keep.reshape(half_rows, LANES), received, norm, win * win, number, ways[0])
    for place, (shift, _) in enumerate(digits[:-1]):
        mine, *sends = outs
        received = [swap_rows(block, (i + 1) << shift) for i, block in enumerate(sends)]
        outs = scatter_sum(mine, sends[0], received, ways[place + 1])
    split = SPLIT * win // 8
    low_first = low_sum_of(0, split, low_grad, from_left, outs[0])
    above_first = from_behind(low_first, "row", 1)
    shift, count = digits[-1]
    partners = [swap_rows(outs[0], i << shift) for i in range(1, count)]
    gathered = exchange_sum(list(outs) + partners, size)
    low_last = low_sum_of(split, win - split, low_grad, from_left, gathered)
    above_last = from_behind(low_last, "row", 1)
    mine = [gathered]
    for shift, count in digits[-2::-1]:
        gathered = mine[0] if len(mine) == 1 else join(mine)
        mine = [gathered] + [swap_rows(gathered, i << shift) for i in range(1, count)]
    other = [swap_cores(block) for block in mine]
    new_object, token = object_update(
        own, own_grad, from_left, above_first, above_last
    )
    new_probe = probe_update(mine, other, probe, token, probe_modes.shape, size, digits)
    return (new_object, new_probe)


def solution(mesh):
    placed = (
        P(None, ("grp", "row"), "col"),
        P(None, None, "grp", None),
        P(("grp", "row"), "col", None, None),
        P(("grp", "row"), "col"),
        P(("grp", "row"), "col", None, None, None),
    )
    return jax.shard_map(
        body,
        mesh=mesh,
        in_specs=placed,
        out_specs=(P(None, ("grp", "row"), "col"), P(None, None, "grp", None)),
        check_vma=False,
    )
```

```python
import functools

import jax
import jax.numpy as jnp
import ml_dtypes
import numpy as np
from jax import lax
from jax.experimental import pallas as pl
from jax.experimental.pallas import tpu as pltpu
from jax.sharding import PartitionSpec as P

LANES = 128
CHUNK = 32
FINE = 16
TAIL = 16
MIB = 1 << 20
LOW_WEIGHT = 8
SPLIT = 4


def from_behind(block, axis, distance):
    devices = range(lax.axis_size(axis))
    route = [(i - distance, i) for i in devices if i - distance in devices]
    return lax.ppermute(block, axis, route)


def from_next_row(block, col):
    rows, cols = lax.axis_size("row"), lax.axis_size("col")
    route = [((r + 1) * cols + col, r * cols + col) for r in range(rows - 1)]
    return lax.ppermute(block, ("row", "col"), route)


def dft_blocks(win):
    grid = np.arange(win)
    angle = 2.0 * np.pi * (grid[:, None] * grid[None, :] % win) / win
    factor = 1.0 / np.sqrt(win)
    cos_table = (np.cos(angle) * factor).astype(ml_dtypes.bfloat16)
    sin_table = (np.sin(angle) * factor).astype(ml_dtypes.bfloat16)
    blocks = []
    for parity in range(2):
        cos_part, sin_part = cos_table[parity::2, : win // 2], sin_table[parity::2, : win // 2]
        blocks.append(np.block([[cos_part, sin_part], [-sin_part, cos_part]]))
    return np.stack(blocks + [block.T for block in blocks])


def dot(left, right):
    return jnp.dot(left, right, preferred_element_type=jnp.float32)


def put_blocks(field, row, first, sources):
    parts, rows, cols = sources[0].shape
    for part in range(parts):
        for r in range(0, rows, CHUNK):
            pieces = [source[part, r : r + CHUNK, :].astype(jnp.float32) for source in sources]
            values = sum(pieces[1:], pieces[0])
            for b in range(cols // LANES):
                piece = values[:, b * LANES : (b + 1) * LANES]
                field[part, first + b, row + r : row + r + CHUNK, :] = piece


def lay_out_kernel(own, right, field, grad, probe_sum):
    put_blocks(field, 0, 0, (own,))
    put_blocks(field, 0, own.shape[2] // LANES, (right,))
    grad[...] = jnp.zeros_like(grad)
    probe_sum[...] = jnp.zeros_like(probe_sum)


def lay_out(own, right, win, modes):
    rows, cols = own.shape[1:]
    tile = (2, (cols + win) // LANES, rows + win, LANES)
    shapes = (tile, tile, (modes, 2, win // LANES, win, LANES))
    return small_call(
        lay_out_kernel,
        tuple(jax.ShapeDtypeStruct(shape, jnp.float32) for shape in shapes),
        own,
        right,
    )


def gradient_kernel(
    modes,
    starts,
    count,
    power,
    below_left,
    below_right,
    corner,
    probe,
    measured,
    tables,
    field_made,
    grad_made,
    probe_sum_made,
    own_grad,
    low_grad,
    right_grad,
    keep_out,
    send_out,
    norm_out,
    field,
    grad,
    probe_sum,
    window,
    wide,
    tall,
    wave,
):
    win = probe.shape[1]
    rows, cols = own_grad.shape[1], own_grad.shape[2]
    half = win // 2
    fine = range(0, win, FINE)
    spread = win // LANES + 1
    col_index = lax.axis_index("col")
    row_anchor = lax.axis_index("row") * rows
    col_anchor = col_index * cols

    norm_out[...] = jnp.zeros_like(norm_out)
    for first, *sources in ((0, below_left, below_right), (cols // LANES, corner)):
        put_blocks(field, rows, first, sources)
    lane = lax.broadcasted_iota(jnp.int32, (FINE, LANES), 1)

    def one_position(slot, carry):
        y, x = starts[0, slot] - row_anchor, starts[1, slot] - col_anchor
        base = x // LANES
        shift = x - base * LANES
        back_shift = (LANES - shift) % LANES
        keep = lane < LANES - shift
        for r in range(0, half, FINE):
            objs = []
            for start in (r, r + half):
                at = pl.ds(start, FINE)
                obj = []
                for part in range(2):
                    turned = [
                        pltpu.roll(field[part, base + b, pl.ds(y + start, FINE), :], back_shift, 1)
                        for b in range(spread)
                    ]
                    piece = jnp.concatenate(
                        [jnp.where(keep, a, b) for a, b in zip(turned[:-1], turned[1:])], axis=1
                    )
                    window[part, at, :] = piece
                    obj.append(piece)
                squares = obj[0] * obj[0] + obj[1] * obj[1]
                norm_out[...] += jnp.sum(squares.reshape(FINE // 8, 8, win), axis=0)
                objs.append(obj)
            for k in range(modes):
                cs = pl.ds(k * win, win)
                exits = []
                for start, (o_re, o_im) in zip((r, r + half), objs):
                    p_re, p_im = probe[0, pl.ds(start, FINE), cs], probe[1, pl.ds(start, FINE), cs]
                    exits.append((p_re * o_re - p_im * o_im, p_re * o_im + p_im * o_re))
                for part in range(2):
                    low, high = exits[0][part], exits[1][part]
                    at = pl.ds(part * half + r, FINE)
                    wide[k, 0, at, :] = (low + high).astype(jnp.bfloat16)
                    wide[k, 1, at, :] = (low - high).astype(jnp.bfloat16)

        for k in range(modes):
            for parity in range(2):
                out = dot(tables[parity], wide[k, parity])
                at = pl.ds(k * win + parity * half, half)
                for part in range(2):
                    low = out[part * half : (part + 1) * half, :half]
                    high = out[part * half : (part + 1) * half, half:]
                    to = pl.ds(part * half, half)
                    tall[0, at, to] = (low + high).astype(jnp.bfloat16)
                    tall[1, at, to] = (low - high).astype(jnp.bfloat16)
        for parity in range(2):
            wave[parity] = dot(tall[parity], tables[2 + parity])

        for r in fine:
            for parity in range(2):
                waves = []
                total = jnp.zeros((FINE, half), jnp.float32)
                for k in range(modes):
                    ka = pl.ds(k * win + r, FINE)
                    waves.append((wave[parity, ka, :half], wave[parity, ka, half:]))
                    total = total + (waves[k][0] * waves[k][0] + waves[k][1] * waves[k][1])
                gs = pl.ds(parity * half, half)
                amp = measured[slot, pl.ds(r, FINE), gs]
                ratio = 1.0 - amp * lax.rsqrt(jnp.maximum(total, 1.0))
                for k in range(modes):
                    for part in range(2):
                        at = pl.ds(part * half + r % half, FINE)
                        wide[k, r // half, at, gs] = (waves[k][part] * ratio).astype(jnp.bfloat16)

        for k in range(modes):
            even = dot(tables[2], wide[k, 0])
            odd = dot(tables[3], wide[k, 1])
            for place, out in enumerate((even + odd, even - odd)):
                at = pl.ds(k * win + place * half, half)
                for part in range(2):
                    for parity in range(2):
                        tall[parity, at, part * half : (part + 1) * half] = out[
                            part * half : (part + 1) * half, parity * half : (parity + 1) * half
                        ].astype(jnp.bfloat16)
        for parity in range(2):
            wave[parity] = dot(tall[parity], tables[parity])

        keep_high = lane >= shift
        for r in fine:
            at = pl.ds(r, FINE)
            sums = [[jnp.zeros((FINE, LANES), jnp.float32) for _ in range(2)] for _ in range(2)]
            for b in range(2):
                bs = pl.ds(b * half, half)
                o_re, o_im = window[0, at, bs], window[1, at, bs]
                for k in range(modes):
                    cs = pl.ds(k * win + b * half, half)
                    ka = pl.ds(k * win + r, FINE)
                    even, odd = wave[0, ka, :], wave[1, ka, :]
                    d = even + odd if b == 0 else even - odd
                    d_re, d_im = d[:, :half], d[:, half:]
                    p_re, p_im = probe[0, at, cs], probe[1, at, cs]
                    sums[0][b] = sums[0][b] + (p_re * d_re + p_im * d_im)
                    sums[1][b] = sums[1][b] + (p_re * d_im - p_im * d_re)
                    probe_sum[k, 0, b, at, :] += o_re * d_re + o_im * d_im
                    probe_sum[k, 1, b, at, :] += o_re * d_im - o_im * d_re
            for part in range(2):
                turned = [pltpu.roll(piece, shift, 1) for piece in sums[part]]
                turned = [jnp.zeros_like(turned[0])] + turned + [jnp.zeros_like(turned[0])]
                for b in range(spread):
                    grad[part, base + b, pl.ds(y + r, FINE), :] += jnp.where(
                        keep_high, turned[b + 1], turned[b]
                    )
        return carry

    lax.fori_loop(0, count[0], one_position, 0)
    for m in range(modes // 2):
        keep_mode = col_index * (modes // 2) + m
        send_mode = (1 - col_index) * (modes // 2) + m
        keep_out[m] = probe_sum[keep_mode]
        send_out[m] = probe_sum[send_mode].astype(jnp.bfloat16)
    scale = 1.0 / jnp.full((8, LANES), power[0], jnp.float32)
    scale = jnp.concatenate([scale] * (CHUNK // 8), axis=0)

    def take_blocks(part, at, first, number):
        return jnp.concatenate(
            [grad[part, first + b, at, :] * scale for b in range(number)], axis=1
        )

    for part in range(2):
        for r in range(0, rows + win, CHUNK):
            at = pl.ds(r, CHUNK)
            piece = take_blocks(part, at, cols // LANES, win // LANES)
            right_grad[part, at, :] = piece.astype(jnp.bfloat16)
        for r in range(0, rows, CHUNK):
            at = pl.ds(r, CHUNK)
            own_grad[part, at, :] = take_blocks(part, at, 0, cols // LANES)
        for r in range(0, win, CHUNK):
            at, of = pl.ds(r, CHUNK), pl.ds(rows + r, CHUNK)
            low_grad[part, at, :] = take_blocks(part, of, 0, cols // LANES)


def position_gradients(starts, count, power, tile, below, corner, probe, measured, tables, made):
    win, modes = probe.shape[1], probe.shape[2] // probe.shape[1]
    rows, cols = tile
    f32, bf16 = jnp.float32, jnp.bfloat16
    smem = pl.BlockSpec(memory_space=pltpu.SMEM)
    vmem = pl.BlockSpec(memory_space=pltpu.VMEM)
    if win != 2 * LANES:
        raise ValueError("window size")
    slots = measured.shape[0]
    flops = 16 * slots * modes * win**3
    half_blocks = (modes // 2, 2, win // LANES, win, LANES)
    return pl.pallas_call(
        functools.partial(gradient_kernel, modes),
        out_shape=(
            jax.ShapeDtypeStruct((2, rows, cols), f32),
            jax.ShapeDtypeStruct((2, win, cols), f32),
            jax.ShapeDtypeStruct((2, rows + win, win), bf16),
            jax.ShapeDtypeStruct(half_blocks, f32),
            jax.ShapeDtypeStruct(half_blocks, bf16),
            jax.ShapeDtypeStruct((8, win), f32),
        )
        + tuple(jax.ShapeDtypeStruct(array.shape, f32) for array in made),
        in_specs=[smem] * 3 + [vmem] * 9,
        out_specs=(vmem,) * 9,
        input_output_aliases={9: 6, 10: 7, 11: 8},
        scratch_shapes=[
            pltpu.VMEM((2, win, win), f32),
            pltpu.VMEM((modes, 2, win, win), bf16),
            pltpu.VMEM((2, modes * win, win), bf16),
            pltpu.VMEM((2, modes * win, win), f32),
        ],
        compiler_params=pltpu.CompilerParams(vmem_limit_bytes=16 * MIB),
        cost_estimate=pl.CostEstimate(flops=flops, bytes_accessed=12 << 20, transcendentals=0),
    )(starts, count, power, *below, corner, probe, measured, tables, *made)


def in_three(value):
    full = jnp.full((TAIL, LANES), value, jnp.float32)
    high = full.astype(jnp.bfloat16).astype(jnp.float32)
    mid = (full - high).astype(jnp.bfloat16).astype(jnp.float32)
    low = full - high - mid
    row = lax.broadcasted_iota(jnp.int32, (TAIL, LANES), 0)
    lane = lax.broadcasted_iota(jnp.int32, (TAIL, LANES), 1)
    tile = jnp.where(row == 0, high, jnp.where(row == 1, mid, jnp.where(row == 2, low, 0.0)))
    return jnp.where(lane == 0, tile, 0.0).astype(jnp.bfloat16)


def small_call(kernel, shapes, *operands, weight=1):
    return pl.pallas_call(
        kernel,
        out_shape=shapes,
        compiler_params=pltpu.CompilerParams(vmem_limit_bytes=4 * MIB),
        cost_estimate=pl.CostEstimate(flops=0, bytes_accessed=weight * MIB, transcendentals=0),
    )(*operands)


def first_columns_kernel(block, *refs):
    first = refs[-1]
    first[...] = block[:, :, : first.shape[2]]


def first_columns(block, size, *tokens):
    shape = block.shape[:2] + (size,)
    return small_call(
        first_columns_kernel, jax.ShapeDtypeStruct(shape, block.dtype), block, *tokens
    )


def copies_kernel(block, same, first_cols):
    same[...] = block[...]
    first_cols[...] = block[:, :, : first_cols.shape[2]]


def copies(block, size):
    shapes = (block.shape, block.shape[:2] + (size,))
    return small_call(
        copies_kernel,
        tuple(jax.ShapeDtypeStruct(shape, block.dtype) for shape in shapes),
        block,
    )


def prepare_kernel(probe, intens, blocks, token, tables, measured, wide_probe, power):
    tables[...] = blocks[...]
    count, size, _ = intens.shape
    row = lax.broadcasted_iota(jnp.int32, (size, size), 0)
    col = lax.broadcasted_iota(jnp.int32, (size, size), 1)
    to_even_first = (col == jnp.where(row < size // 2, 2 * row, 2 * row - size + 1)).astype(
        jnp.float32
    )
    from_left = to_even_first.astype(jnp.bfloat16)
    from_right = (row == jnp.where(col < size // 2, 2 * col, 2 * col - size + 1)).astype(
        jnp.float32
    )
    from_right = from_right.astype(jnp.bfloat16)
    for slot in range(count):
        turned = dot(from_left, intens[slot]).astype(jnp.bfloat16)
        measured[slot] = jnp.sqrt(dot(turned, from_right))
    win = probe.shape[1]
    modes = probe.shape[2] // win
    largest = jnp.zeros((8, win), jnp.float32)
    for r in range(0, probe.shape[1], CHUNK):
        at = slice(r, r + CHUNK)
        total = jnp.zeros((CHUNK, win), jnp.float32)
        for k in range(modes):
            for part in range(2):
                p = probe[part, at, k * win : (k + 1) * win].astype(jnp.float32)
                wide_probe[part, at, k * win : (k + 1) * win] = p
                total = total + p * p
        largest = jnp.maximum(largest, jnp.max(total.reshape(CHUNK // 8, 8, win), axis=0))
    power[0, 0] = jnp.max(largest)


def prepare(probe, intens, token):
    win = probe.shape[1]
    blocks = dft_blocks(win)
    vmem = pl.BlockSpec(memory_space=pltpu.VMEM)
    return pl.pallas_call(
        prepare_kernel,
        out_shape=(
            jax.ShapeDtypeStruct(blocks.shape, jnp.bfloat16),
            jax.ShapeDtypeStruct(intens.shape, jnp.float32),
            jax.ShapeDtypeStruct(probe.shape, jnp.float32),
            jax.ShapeDtypeStruct((1, 1), jnp.float32),
        ),
        out_specs=(vmem, vmem, vmem, pl.BlockSpec(memory_space=pltpu.SMEM)),
        compiler_params=pltpu.CompilerParams(vmem_limit_bytes=8 * MIB),
    )(probe, intens, blocks, token)


def block_shapes(number, size, ways):
    if not ways:
        return (jax.ShapeDtypeStruct((number * size + TAIL, LANES), jnp.bfloat16),)
    sends = jax.ShapeDtypeStruct((number // ways * size + TAIL, LANES), jnp.bfloat16)
    return (jax.ShapeDtypeStruct((number // ways, size, LANES), jnp.float32),) + (sends,) * (ways - 1)


def put_block(j, total, outs):
    size = total.shape[0]
    if len(outs) == 1:
        outs[0][pl.ds(j * size, size), :] = total.astype(jnp.bfloat16)
    elif j % len(outs) == 0:
        outs[0][j // len(outs)] = total
    else:
        at = pl.ds(j // len(outs) * size, size)
        outs[j % len(outs)][at, :] = total.astype(jnp.bfloat16)


def put_weight(weight, outs):
    tile = in_three(weight)
    for sent in outs if len(outs) == 1 else outs[1:]:
        sent[pl.ds(sent.shape[0] - TAIL, TAIL), :] = tile


def weight_of(block):
    return jnp.sum(block[pl.ds(block.shape[0] - TAIL, TAIL), :].astype(jnp.float32))


def chip_sum_kernel(pixels, size, keep, received, norm, *outs):
    me = lax.axis_index("row")
    for j in range(keep.shape[0] // size):
        at = pl.ds(pl.multiple_of((j ^ me) * size, size), size)
        put_block(j, keep[at, :] + received[at, :].astype(jnp.float32), outs)
    put_weight(jnp.sum(norm[...]) / pixels, outs)


def chip_sum(keep, received, norm, pixels, number, ways):
    size = keep.shape[0] // number
    return small_call(
        functools.partial(chip_sum_kernel, pixels, size),
        block_shapes(number, size, ways),
        keep,
        received,
        norm,
    )


def scatter_sum_kernel(number, mine, sent, *refs):
    received, outs = refs[:number], refs[number:]
    size = mine.shape[1]
    for j in range(mine.shape[0]):
        total = mine[j]
        for block in received:
            total = total + block[pl.ds(j * size, size), :].astype(jnp.float32)
        put_block(j, total, outs)
    put_weight(sum([weight_of(block) for block in received], weight_of(sent)), outs)


def scatter_sum(mine, sent, received, ways):
    number, size, _ = mine.shape
    return small_call(
        functools.partial(scatter_sum_kernel, len(received)),
        block_shapes(number, size, ways),
        mine,
        sent,
        *received,
    )


def pair_up(terms):
    while len(terms) > 1:
        terms = [a + b for a, b in zip(terms[::2], terms[1::2])]
    return terms[0]


def exchange_sum_kernel(size, *refs):
    blocks, chunks = refs[:-1], refs[-1]
    for j in range((chunks.shape[0] - TAIL) // size):
        terms = [
            block[pl.ds((j ^ i) * size, size), :].astype(jnp.float32)
            for i, block in enumerate(blocks)
        ]
        chunks[pl.ds(j * size, size), :] = pair_up(terms).astype(jnp.bfloat16)
    put_weight(pair_up([weight_of(block) for block in blocks]), (chunks,))


def exchange_sum(blocks, size):
    return small_call(
        functools.partial(exchange_sum_kernel, size),
        jax.ShapeDtypeStruct(blocks[0].shape, jnp.bfloat16),
        *blocks,
    )


def copy_chunks(blocks, joined):
    at = 0
    for block in blocks:
        rows = block.shape[0] - TAIL
        joined[pl.ds(at, rows), :] = block[pl.ds(0, rows), :]
        at += rows
    joined[pl.ds(at, TAIL), :] = blocks[0][pl.ds(blocks[0].shape[0] - TAIL, TAIL), :]


def join_kernel(*refs):
    copy_chunks(refs[:-1], refs[-1])


def join(blocks):
    rows = sum(block.shape[0] - TAIL for block in blocks) + TAIL
    return small_call(join_kernel, jax.ShapeDtypeStruct((rows, LANES), blocks[0].dtype), *blocks)


def swap_rows(block, step):
    number = lax.axis_size("row")
    return lax.ppermute(block, "row", [(i, i ^ step) for i in range(number)])


def row_digits():
    number = lax.axis_size("row")
    if number & (number - 1) or number < 2:
        raise ValueError("row size")
    bits = number.bit_length() - 1
    return [(shift, 1 << min(2, bits - shift)) for shift in range(0, bits, 2)]


def probe_update_kernel(size, digits, *refs):
    *blocks, probe, token, new_probe, mine, other, updated, sems = refs
    copy_chunks(blocks[: len(blocks) // 2], mine)
    copy_chunks(blocks[len(blocks) // 2 :], other)
    _, win, modes, _ = updated.shape
    number = mine.shape[0] // size
    me = lax.axis_index("row")
    piece = min(size, CHUNK)
    on_left = lax.axis_index("col") == 0
    tail = pl.ds(number * size, TAIL)
    tails = mine[tail, :].astype(jnp.float32) + other[tail, :].astype(jnp.float32)
    factor = 4.0 / jnp.full((piece, LANES), jnp.sum(tails), jnp.float32)
    half = modes // 2

    def place(chunk):
        j = chunk ^ me
        at, span = 0, 1
        for shift, ways in reversed(digits):
            at = at + ((j >> shift) & (ways - 1)) * span
            span *= ways
        return at * size

    def update(part, b, m, r):
        block = ((m * 2 + part) * (win // LANES) + b) * win
        chunk, offset = divmod(block + r, size)
        at = pl.ds(pl.multiple_of(place(chunk) + offset, piece), piece)
        here = mine[at, :].astype(jnp.float32)
        there = other[at, :].astype(jnp.float32)
        low = jnp.where(on_left, here, there)
        high = jnp.where(on_left, there, here)
        for k, total in ((m, low), (half + m, high)):
            col = k * win + b * LANES
            old = probe[part, r : r + piece, col : col + LANES]
            updated[part, r : r + piece, k, b * LANES : (b + 1) * LANES] = old - factor * total

    stretch = win // 4
    copies = []
    for part in range(2):
        for start in range(0, win, stretch):
            for r in range(start, start + stretch, piece):
                for m in range(half):
                    for b in range(win // LANES):
                        update(part, b, m, r)
            at = (part, pl.ds(start, stretch))
            copies.append(
                pltpu.make_async_copy(updated.at[at], new_probe.at[at], sems.at[len(copies)])
            )
            copies[-1].start()
    for copy in copies:
        copy.wait()


def probe_update(mine, other, probe, token, shape, size, digits):
    vmem = pl.BlockSpec(memory_space=pltpu.VMEM)
    rows = sum(block.shape[0] - TAIL for block in mine) + TAIL
    operands = (*mine, *other, probe, token)
    return pl.pallas_call(
        functools.partial(probe_update_kernel, size, digits),
        out_shape=jax.ShapeDtypeStruct(shape, jnp.float32),
        in_specs=[vmem] * len(operands),
        out_specs=pl.BlockSpec(memory_space=pl.ANY),
        scratch_shapes=[
            pltpu.VMEM((rows, LANES), jnp.bfloat16),
            pltpu.VMEM((rows, LANES), jnp.bfloat16),
            pltpu.VMEM(shape, jnp.float32),
            pltpu.SemaphoreType.DMA((8,)),
        ],
        compiler_params=pltpu.CompilerParams(vmem_limit_bytes=8 * MIB),
    )(*operands)


def low_sum_kernel(first, low_grad, from_left, token, low_sum):
    win = from_left.shape[2]
    rows = from_left.shape[1] - low_grad.shape[1]
    for part in range(2):
        for r in range(0, low_sum.shape[1], CHUNK):
            at, of = slice(r, r + CHUNK), slice(first + r, first + r + CHUNK)
            arrived = from_left[part, rows + first + r : rows + first + r + CHUNK, :]
            total = low_grad[part, of, :win] + arrived.astype(jnp.float32)
            low_sum[part, at, :win] = total.astype(jnp.bfloat16)
            low_sum[part, at, win:] = low_grad[part, of, win:].astype(jnp.bfloat16)


def low_sum_of(first, count, low_grad, from_left, token):
    return small_call(
        functools.partial(low_sum_kernel, first),
        jax.ShapeDtypeStruct((2, count, low_grad.shape[2]), jnp.bfloat16),
        low_grad,
        from_left,
        token,
        weight=LOW_WEIGHT,
    )


def object_update_kernel(old, own_grad, from_left, above_first, above_last, new_object, token):
    token[...] = jnp.zeros_like(token)
    win, split = from_left.shape[2], above_first.shape[1]
    depth = split + above_last.shape[1]
    for part in range(2):
        for r in range(0, old.shape[1], CHUNK):
            at = slice(r, r + CHUNK)
            total = own_grad[part, at, :]
            if r < split:
                total = total + above_first[part, at, :].astype(jnp.float32)
            elif r < depth:
                total = total + above_last[part, r - split : r - split + CHUNK, :].astype(jnp.float32)
            updated = old[part, at, :].astype(jnp.float32) - total
            arrived = from_left[part, at, :].astype(jnp.float32)
            new_object[part, at, :win] = updated[:, :win] - arrived
            new_object[part, at, win:] = updated[:, win:]


def object_update(old, own_grad, from_left, above_first, above_last):
    return small_call(
        object_update_kernel,
        (
            jax.ShapeDtypeStruct(old.shape, jnp.float32),
            jax.ShapeDtypeStruct((8, LANES), jnp.float32),
        ),
        old,
        own_grad,
        from_left,
        above_first,
        above_last,
    )


def swap_cores(block):
    return lax.ppermute(block, "col", [(0, 1), (1, 0)])


def body(object_field, probe_modes, positions, counts, intensities):
    win = probe_modes.shape[1]
    modes = probe_modes.shape[2]
    number = lax.axis_size("row")
    below_right = from_next_row(object_field[:, :win, :], 1)
    probe_flat = probe_modes.reshape(2, win, modes * win)
    own, first_cols = copies(object_field, win)
    below_left = from_next_row(own[:, :win, :], 0)
    right = from_behind(first_cols, "col", -1)
    tables, measured, probe, power = prepare(probe_flat, intensities[0, 0], right)
    made = lay_out(own, right, win, modes)
    corner = from_behind(first_columns(below_right, win, tables, made[0]), "col", -1)
    own_grad, low_grad, right_grad, keep, send, norm, *_ = position_gradients(
        positions[0, 0].T,
        counts.reshape(-1),
        power.reshape(1),
        object_field.shape[1:],
        (below_left, below_right),
        corner,
        probe,
        measured,
        tables,
        made,
    )
    half_rows = keep.size // LANES
    received = swap_cores(send.reshape(half_rows, LANES))
    from_left = from_behind(right_grad, "col", 1)
    digits = row_digits()
    size = half_rows // number
    ways = [digit[1] for digit in digits[:-1]] + [0]
    outs = chip_sum(keep.reshape(half_rows, LANES), received, norm, win * win, number, ways[0])
    for place, (shift, _) in enumerate(digits[:-1]):
        mine, *sends = outs
        received = [swap_rows(block, (i + 1) << shift) for i, block in enumerate(sends)]
        outs = scatter_sum(mine, sends[0], received, ways[place + 1])
    split = SPLIT * win // 8
    low_first = low_sum_of(0, split, low_grad, from_left, outs[0])
    above_first = from_behind(low_first, "row", 1)
    shift, count = digits[-1]
    partners = [swap_rows(outs[0], i << shift) for i in range(1, count)]
    gathered = exchange_sum(list(outs) + partners, size)
    low_last = low_sum_of(split, win - split, low_grad, from_left, gathered)
    above_last = from_behind(low_last, "row", 1)
    mine = [gathered]
    for shift, count in digits[-2::-1]:
        gathered = mine[0] if len(mine) == 1 else join(mine)
        mine = [gathered] + [swap_rows(gathered, i << shift) for i in range(1, count)]
    other = [swap_cores(block) for block in mine]
    new_object, token = object_update(
        own, own_grad, from_left, above_first, above_last
    )
    new_probe = probe_update(mine, other, probe, token, probe_modes.shape, size, digits)
    return (new_object, new_probe)


def solution(mesh):
    placed = (
        P(None, ("grp", "row"), "col"),
        P(None, None, "grp", None),
        P(("grp", "row"), "col", None, None),
        P(("grp", "row"), "col"),
        P(("grp", "row"), "col", None, None, None),
    )
    return jax.shard_map(
        body,
        mesh=mesh,
        in_specs=placed,
        out_specs=(P(None, ("grp", "row"), "col"), P(None, None, "grp", None)),
        check_vma=False,
    )
```

```python
import functools

import jax
import jax.numpy as jnp
import ml_dtypes
import numpy as np
from jax import lax
from jax.experimental import pallas as pl
from jax.experimental.pallas import tpu as pltpu
from jax.sharding import PartitionSpec as P

LANES = 128
CHUNK = 32
FINE = 16
TAIL = 16
MIB = 1 << 20
LOW_WEIGHT = 8
SPLIT = 4


def from_behind(block, axis, distance):
    devices = range(lax.axis_size(axis))
    route = [(i - distance, i) for i in devices if i - distance in devices]
    return lax.ppermute(block, axis, route)


def from_next_row(block, col):
    rows, cols = lax.axis_size("row"), lax.axis_size("col")
    route = [((r + 1) * cols + col, r * cols + col) for r in range(rows - 1)]
    return lax.ppermute(block, ("row", "col"), route)


def dft_blocks(win):
    grid = np.arange(win)
    angle = 2.0 * np.pi * (grid[:, None] * grid[None, :] % win) / win
    factor = 1.0 / np.sqrt(win)
    cos_table = (np.cos(angle) * factor).astype(ml_dtypes.bfloat16)
    sin_table = (np.sin(angle) * factor).astype(ml_dtypes.bfloat16)
    blocks = []
    for parity in range(2):
        cos_part, sin_part = cos_table[parity::2, : win // 2], sin_table[parity::2, : win // 2]
        blocks.append(np.block([[cos_part, sin_part], [-sin_part, cos_part]]))
    return np.stack(blocks + [block.T for block in blocks])


def dot(left, right):
    return jnp.dot(left, right, preferred_element_type=jnp.float32)


def put_blocks(field, row, first, sources):
    parts, rows, cols = sources[0].shape
    for part in range(parts):
        for r in range(0, rows, CHUNK):
            pieces = [source[part, r : r + CHUNK, :].astype(jnp.float32) for source in sources]
            values = sum(pieces[1:], pieces[0])
            for b in range(cols // LANES):
                piece = values[:, b * LANES : (b + 1) * LANES]
                field[part, first + b, row + r : row + r + CHUNK, :] = piece


def lay_out_kernel(own, right, field, grad, probe_sum):
    put_blocks(field, 0, 0, (own,))
    put_blocks(field, 0, own.shape[2] // LANES, (right,))
    grad[...] = jnp.zeros_like(grad)
    probe_sum[...] = jnp.zeros_like(probe_sum)


def lay_out(own, right, win, modes):
    rows, cols = own.shape[1:]
    tile = (2, (cols + win) // LANES, rows + win, LANES)
    shapes = (tile, tile, (modes, 2, win // LANES, win, LANES))
    return small_call(
        lay_out_kernel,
        tuple(jax.ShapeDtypeStruct(shape, jnp.float32) for shape in shapes),
        own,
        right,
    )


def gradient_kernel(
    modes,
    starts,
    count,
    power,
    below_left,
    below_right,
    corner,
    probe,
    measured,
    tables,
    field_made,
    grad_made,
    probe_sum_made,
    own_grad,
    low_grad,
    right_grad,
    keep_out,
    send_out,
    norm_out,
    field,
    grad,
    probe_sum,
    window,
    wide,
    tall,
    wave,
):
    win = probe.shape[1]
    rows, cols = own_grad.shape[1], own_grad.shape[2]
    half = win // 2
    fine = range(0, win, FINE)
    spread = win // LANES + 1
    col_index = lax.axis_index("col")
    row_anchor = lax.axis_index("row") * rows
    col_anchor = col_index * cols

    norm_out[...] = jnp.zeros_like(norm_out)
    for first, *sources in ((0, below_left, below_right), (cols // LANES, corner)):
        put_blocks(field, rows, first, sources)
    lane = lax.broadcasted_iota(jnp.int32, (FINE, LANES), 1)

    def one_position(slot, carry):
        y, x = starts[0, slot] - row_anchor, starts[1, slot] - col_anchor
        base = x // LANES
        shift = x - base * LANES
        back_shift = (LANES - shift) % LANES
        keep = lane < LANES - shift
        for r in range(0, half, FINE):
            objs = []
            for start in (r, r + half):
                at = pl.ds(start, FINE)
                obj = []
                for part in range(2):
                    turned = [
                        pltpu.roll(field[part, base + b, pl.ds(y + start, FINE), :], back_shift, 1)
                        for b in range(spread)
                    ]
                    piece = jnp.concatenate(
                        [jnp.where(keep, a, b) for a, b in zip(turned[:-1], turned[1:])], axis=1
                    )
                    window[part, at, :] = piece
                    obj.append(piece)
                squares = obj[0] * obj[0] + obj[1] * obj[1]
                norm_out[...] += jnp.sum(squares.reshape(FINE // 8, 8, win), axis=0)
                objs.append(obj)
            for k in range(modes):
                cs = pl.ds(k * win, win)
                exits = []
                for start, (o_re, o_im) in zip((r, r + half), objs):
                    p_re, p_im = probe[0, pl.ds(start, FINE), cs], probe[1, pl.ds(start, FINE), cs]
                    exits.append((p_re * o_re - p_im * o_im, p_re * o_im + p_im * o_re))
                for part in range(2):
                    low, high = exits[0][part], exits[1][part]
                    at = pl.ds(part * half + r, FINE)
                    wide[k, 0, at, :] = (low + high).astype(jnp.bfloat16)
                    wide[k, 1, at, :] = (low - high).astype(jnp.bfloat16)

        for k in range(modes):
            for parity in range(2):
                out = dot(tables[parity], wide[k, parity])
                at = pl.ds(k * win + parity * half, half)
                for part in range(2):
                    low = out[part * half : (part + 1) * half, :half]
                    high = out[part * half : (part + 1) * half, half:]
                    to = pl.ds(part * half, half)
                    tall[0, at, to] = (low + high).astype(jnp.bfloat16)
                    tall[1, at, to] = (low - high).astype(jnp.bfloat16)
        for parity in range(2):
            wave[parity] = dot(tall[parity], tables[2 + parity])

        for r in fine:
            for parity in range(2):
                waves = []
                total = jnp.zeros((FINE, half), jnp.float32)
                for k in range(modes):
                    ka = pl.ds(k * win + r, FINE)
                    waves.append((wave[parity, ka, :half], wave[parity, ka, half:]))
                    total = total + (waves[k][0] * waves[k][0] + waves[k][1] * waves[k][1])
                gs = pl.ds(parity * half, half)
                amp = measured[slot, pl.ds(r, FINE), gs]
                ratio = 1.0 - amp * lax.rsqrt(jnp.maximum(total, 1.0))
                for k in range(modes):
                    for part in range(2):
                        at = pl.ds(part * half + r % half, FINE)
                        wide[k, r // half, at, gs] = (waves[k][part] * ratio).astype(jnp.bfloat16)

        for k in range(modes):
            even = dot(tables[2], wide[k, 0])
            odd = dot(tables[3], wide[k, 1])
            for place, out in enumerate((even + odd, even - odd)):
                at = pl.ds(k * win + place * half, half)
                for part in range(2):
                    for parity in range(2):
                        tall[parity, at, part * half : (part + 1) * half] = out[
                            part * half : (part + 1) * half, parity * half : (parity + 1) * half
                        ].astype(jnp.bfloat16)
        for parity in range(2):
            wave[parity] = dot(tall[parity], tables[parity])

        keep_high = lane >= shift
        for r in fine:
            at = pl.ds(r, FINE)
            sums = [[jnp.zeros((FINE, LANES), jnp.float32) for _ in range(2)] for _ in range(2)]
            for b in range(2):
                bs = pl.ds(b * half, half)
                o_re, o_im = window[0, at, bs], window[1, at, bs]
                for k in range(modes):
                    cs = pl.ds(k * win + b * half, half)
                    ka = pl.ds(k * win + r, FINE)
                    even, odd = wave[0, ka, :], wave[1, ka, :]
                    d = even + odd if b == 0 else even - odd
                    d_re, d_im = d[:, :half], d[:, half:]
                    p_re, p_im = probe[0, at, cs], probe[1, at, cs]
                    sums[0][b] = sums[0][b] + (p_re * d_re + p_im * d_im)
                    sums[1][b] = sums[1][b] + (p_re * d_im - p_im * d_re)
                    probe_sum[k, 0, b, at, :] += o_re * d_re + o_im * d_im
                    probe_sum[k, 1, b, at, :] += o_re * d_im - o_im * d_re
            for part in range(2):
                turned = [pltpu.roll(piece, shift, 1) for piece in sums[part]]
                turned = [jnp.zeros_like(turned[0])] + turned + [jnp.zeros_like(turned[0])]
                for b in range(spread):
                    grad[part, base + b, pl.ds(y + r, FINE), :] += jnp.where(
                        keep_high, turned[b + 1], turned[b]
                    )
        return carry

    lax.fori_loop(0, count[0], one_position, 0)
    for m in range(modes // 2):
        keep_mode = col_index * (modes // 2) + m
        send_mode = (1 - col_index) * (modes // 2) + m
        keep_out[m] = probe_sum[keep_mode]
        send_out[m] = probe_sum[send_mode].astype(jnp.bfloat16)
    scale = 1.0 / jnp.full((8, LANES), power[0], jnp.float32)
    scale = jnp.concatenate([scale] * (CHUNK // 8), axis=0)

    def take_blocks(part, at, first, number):
        return jnp.concatenate(
            [grad[part, first + b, at, :] * scale for b in range(number)], axis=1
        )

    for part in range(2):
        for r in range(0, rows + win, CHUNK):
            at = pl.ds(r, CHUNK)
            piece = take_blocks(part, at, cols // LANES, win // LANES)
            right_grad[part, at, :] = piece.astype(jnp.bfloat16)
        for r in range(0, rows, CHUNK):
            at = pl.ds(r, CHUNK)
            own_grad[part, at, :] = take_blocks(part, at, 0, cols // LANES)
        for r in range(0, win, CHUNK):
            at, of = pl.ds(r, CHUNK), pl.ds(rows + r, CHUNK)
            low_grad[part, at, :] = take_blocks(part, of, 0, cols // LANES)


def position_gradients(starts, count, power, tile, below, corner, probe, measured, tables, made):
    win, modes = probe.shape[1], probe.shape[2] // probe.shape[1]
    rows, cols = tile
    f32, bf16 = jnp.float32, jnp.bfloat16
    smem = pl.BlockSpec(memory_space=pltpu.SMEM)
    vmem = pl.BlockSpec(memory_space=pltpu.VMEM)
    if win != 2 * LANES:
        raise ValueError("window size")
    slots = measured.shape[0]
    flops = 16 * slots * modes * win**3
    half_blocks = (modes // 2, 2, win // LANES, win, LANES)
    return pl.pallas_call(
        functools.partial(gradient_kernel, modes),
        out_shape=(
            jax.ShapeDtypeStruct((2, rows, cols), f32),
            jax.ShapeDtypeStruct((2, win, cols), f32),
            jax.ShapeDtypeStruct((2, rows + win, win), bf16),
            jax.ShapeDtypeStruct(half_blocks, f32),
            jax.ShapeDtypeStruct(half_blocks, bf16),
            jax.ShapeDtypeStruct((8, win), f32),
        )
        + tuple(jax.ShapeDtypeStruct(array.shape, f32) for array in made),
        in_specs=[smem] * 3 + [vmem] * 9,
        out_specs=(vmem,) * 9,
        input_output_aliases={9: 6, 10: 7, 11: 8},
        scratch_shapes=[
            pltpu.VMEM((2, win, win), f32),
            pltpu.VMEM((modes, 2, win, win), bf16),
            pltpu.VMEM((2, modes * win, win), bf16),
            pltpu.VMEM((2, modes * win, win), f32),
        ],
        compiler_params=pltpu.CompilerParams(vmem_limit_bytes=16 * MIB),
        cost_estimate=pl.CostEstimate(flops=flops, bytes_accessed=12 << 20, transcendentals=0),
    )(starts, count, power, *below, corner, probe, measured, tables, *made)


def in_three(value):
    full = jnp.full((TAIL, LANES), value, jnp.float32)
    high = full.astype(jnp.bfloat16).astype(jnp.float32)
    mid = (full - high).astype(jnp.bfloat16).astype(jnp.float32)
    low = full - high - mid
    row = lax.broadcasted_iota(jnp.int32, (TAIL, LANES), 0)
    lane = lax.broadcasted_iota(jnp.int32, (TAIL, LANES), 1)
    tile = jnp.where(row == 0, high, jnp.where(row == 1, mid, jnp.where(row == 2, low, 0.0)))
    return jnp.where(lane == 0, tile, 0.0).astype(jnp.bfloat16)


def small_call(kernel, shapes, *operands, weight=1):
    return pl.pallas_call(
        kernel,
        out_shape=shapes,
        compiler_params=pltpu.CompilerParams(vmem_limit_bytes=4 * MIB),
        cost_estimate=pl.CostEstimate(flops=0, bytes_accessed=weight * MIB, transcendentals=0),
    )(*operands)


def first_columns_kernel(block, *refs):
    first = refs[-1]
    first[...] = block[:, :, : first.shape[2]]


def first_columns(block, size, *tokens):
    shape = block.shape[:2] + (size,)
    return small_call(
        first_columns_kernel, jax.ShapeDtypeStruct(shape, block.dtype), block, *tokens
    )


def copies_kernel(block, token, first_rows, first_cols):
    first_rows[...] = block[:, : first_rows.shape[1], :]
    first_cols[...] = block[:, :, : first_cols.shape[2]]


def copies(block, size, token):
    parts, rows, cols = block.shape
    shapes = ((parts, size, cols), (parts, rows, size))
    return small_call(
        copies_kernel,
        tuple(jax.ShapeDtypeStruct(shape, block.dtype) for shape in shapes),
        block,
        token,
    )


def prepare_kernel(probe, intens, blocks, token, tables, measured, wide_probe, power):
    tables[...] = blocks[...]
    count, size, _ = intens.shape
    row = lax.broadcasted_iota(jnp.int32, (size, size), 0)
    col = lax.broadcasted_iota(jnp.int32, (size, size), 1)
    to_even_first = (col == jnp.where(row < size // 2, 2 * row, 2 * row - size + 1)).astype(
        jnp.float32
    )
    from_left = to_even_first.astype(jnp.bfloat16)
    from_right = (row == jnp.where(col < size // 2, 2 * col, 2 * col - size + 1)).astype(
        jnp.float32
    )
    from_right = from_right.astype(jnp.bfloat16)
    for slot in range(count):
        turned = dot(from_left, intens[slot]).astype(jnp.bfloat16)
        measured[slot] = jnp.sqrt(dot(turned, from_right))
    win = probe.shape[1]
    modes = probe.shape[2] // win
    largest = jnp.zeros((8, win), jnp.float32)
    for r in range(0, probe.shape[1], CHUNK):
        at = slice(r, r + CHUNK)
        total = jnp.zeros((CHUNK, win), jnp.float32)
        for k in range(modes):
            for part in range(2):
                p = probe[part, at, k * win : (k + 1) * win].astype(jnp.float32)
                wide_probe[part, at, k * win : (k + 1) * win] = p
                total = total + p * p
        largest = jnp.maximum(largest, jnp.max(total.reshape(CHUNK // 8, 8, win), axis=0))
    power[0, 0] = jnp.max(largest)


def prepare(probe, intens, token):
    win = probe.shape[1]
    blocks = dft_blocks(win)
    vmem = pl.BlockSpec(memory_space=pltpu.VMEM)
    return pl.pallas_call(
        prepare_kernel,
        out_shape=(
            jax.ShapeDtypeStruct(blocks.shape, jnp.bfloat16),
            jax.ShapeDtypeStruct(intens.shape, jnp.float32),
            jax.ShapeDtypeStruct(probe.shape, jnp.float32),
            jax.ShapeDtypeStruct((1, 1), jnp.float32),
        ),
        out_specs=(vmem, vmem, vmem, pl.BlockSpec(memory_space=pltpu.SMEM)),
        compiler_params=pltpu.CompilerParams(vmem_limit_bytes=8 * MIB),
    )(probe, intens, blocks, token)


def block_shapes(number, size, ways):
    if not ways:
        return (jax.ShapeDtypeStruct((number * size + TAIL, LANES), jnp.bfloat16),)
    sends = jax.ShapeDtypeStruct((number // ways * size + TAIL, LANES), jnp.bfloat16)
    return (jax.ShapeDtypeStruct((number // ways, size, LANES), jnp.float32),) + (sends,) * (ways - 1)


def put_block(j, total, outs):
    size = total.shape[0]
    if len(outs) == 1:
        outs[0][pl.ds(j * size, size), :] = total.astype(jnp.bfloat16)
    elif j % len(outs) == 0:
        outs[0][j // len(outs)] = total
    else:
        at = pl.ds(j // len(outs) * size, size)
        outs[j % len(outs)][at, :] = total.astype(jnp.bfloat16)


def put_weight(weight, outs):
    tile = in_three(weight)
    for sent in outs if len(outs) == 1 else outs[1:]:
        sent[pl.ds(sent.shape[0] - TAIL, TAIL), :] = tile


def weight_of(block):
    return jnp.sum(block[pl.ds(block.shape[0] - TAIL, TAIL), :].astype(jnp.float32))


def chip_sum_kernel(pixels, size, keep, received, norm, *outs):
    me = lax.axis_index("row")
    for j in range(keep.shape[0] // size):
        at = pl.ds(pl.multiple_of((j ^ me) * size, size), size)
        put_block(j, keep[at, :] + received[at, :].astype(jnp.float32), outs)
    put_weight(jnp.sum(norm[...]) / pixels, outs)


def chip_sum(keep, received, norm, pixels, number, ways):
    size = keep.shape[0] // number
    return small_call(
        functools.partial(chip_sum_kernel, pixels, size),
        block_shapes(number, size, ways),
        keep,
        received,
        norm,
    )


def scatter_sum_kernel(number, mine, sent, *refs):
    received, outs = refs[:number], refs[number:]
    size = mine.shape[1]
    for j in range(mine.shape[0]):
        total = mine[j]
        for block in received:
            total = total + block[pl.ds(j * size, size), :].astype(jnp.float32)
        put_block(j, total, outs)
    put_weight(sum([weight_of(block) for block in received], weight_of(sent)), outs)


def scatter_sum(mine, sent, received, ways):
    number, size, _ = mine.shape
    return small_call(
        functools.partial(scatter_sum_kernel, len(received)),
        block_shapes(number, size, ways),
        mine,
        sent,
        *received,
    )


def pair_up(terms):
    while len(terms) > 1:
        terms = [a + b for a, b in zip(terms[::2], terms[1::2])]
    return terms[0]


def exchange_sum_kernel(size, *refs):
    blocks, chunks = refs[:-1], refs[-1]
    for j in range((chunks.shape[0] - TAIL) // size):
        terms = [
            block[pl.ds((j ^ i) * size, size), :].astype(jnp.float32)
            for i, block in enumerate(blocks)
        ]
        chunks[pl.ds(j * size, size), :] = pair_up(terms).astype(jnp.bfloat16)
    put_weight(pair_up([weight_of(block) for block in blocks]), (chunks,))


def exchange_sum(blocks, size):
    return small_call(
        functools.partial(exchange_sum_kernel, size),
        jax.ShapeDtypeStruct(blocks[0].shape, jnp.bfloat16),
        *blocks,
    )


def copy_chunks(blocks, joined):
    at = 0
    for block in blocks:
        rows = block.shape[0] - TAIL
        joined[pl.ds(at, rows), :] = block[pl.ds(0, rows), :]
        at += rows
    joined[pl.ds(at, TAIL), :] = blocks[0][pl.ds(blocks[0].shape[0] - TAIL, TAIL), :]


def join_kernel(*refs):
    copy_chunks(refs[:-1], refs[-1])


def join(blocks):
    rows = sum(block.shape[0] - TAIL for block in blocks) + TAIL
    return small_call(join_kernel, jax.ShapeDtypeStruct((rows, LANES), blocks[0].dtype), *blocks)


def swap_rows(block, step):
    number = lax.axis_size("row")
    return lax.ppermute(block, "row", [(i, i ^ step) for i in range(number)])


def row_digits():
    number = lax.axis_size("row")
    if number & (number - 1) or number < 2:
        raise ValueError("row size")
    bits = number.bit_length() - 1
    return [(shift, 1 << min(2, bits - shift)) for shift in range(0, bits, 2)]


def probe_update_kernel(size, digits, *refs):
    *blocks, probe, token, new_probe, mine, other, updated, sems = refs
    copy_chunks(blocks[: len(blocks) // 2], mine)
    copy_chunks(blocks[len(blocks) // 2 :], other)
    _, win, modes, _ = updated.shape
    number = mine.shape[0] // size
    me = lax.axis_index("row")
    piece = min(size, CHUNK)
    on_left = lax.axis_index("col") == 0
    tail = pl.ds(number * size, TAIL)
    tails = mine[tail, :].astype(jnp.float32) + other[tail, :].astype(jnp.float32)
    factor = 4.0 / jnp.full((piece, LANES), jnp.sum(tails), jnp.float32)
    half = modes // 2

    def place(chunk):
        j = chunk ^ me
        at, span = 0, 1
        for shift, ways in reversed(digits):
            at = at + ((j >> shift) & (ways - 1)) * span
            span *= ways
        return at * size

    def update(part, b, m, r):
        block = ((m * 2 + part) * (win // LANES) + b) * win
        chunk, offset = divmod(block + r, size)
        at = pl.ds(pl.multiple_of(place(chunk) + offset, piece), piece)
        here = mine[at, :].astype(jnp.float32)
        there = other[at, :].astype(jnp.float32)
        low = jnp.where(on_left, here, there)
        high = jnp.where(on_left, there, here)
        for k, total in ((m, low), (half + m, high)):
            col = k * win + b * LANES
            old = probe[part, r : r + piece, col : col + LANES]
            updated[part, r : r + piece, k, b * LANES : (b + 1) * LANES] = old - factor * total

    stretch = win // 4
    copies = []
    for part in range(2):
        for start in range(0, win, stretch):
            for r in range(start, start + stretch, piece):
                for m in range(half):
                    for b in range(win // LANES):
                        update(part, b, m, r)
            at = (part, pl.ds(start, stretch))
            copies.append(
                pltpu.make_async_copy(updated.at[at], new_probe.at[at], sems.at[len(copies)])
            )
            copies[-1].start()
    for copy in copies:
        copy.wait()


def probe_update(mine, other, probe, token, shape, size, digits):
    vmem = pl.BlockSpec(memory_space=pltpu.VMEM)
    rows = sum(block.shape[0] - TAIL for block in mine) + TAIL
    operands = (*mine, *other, probe, token)
    return pl.pallas_call(
        functools.partial(probe_update_kernel, size, digits),
        out_shape=jax.ShapeDtypeStruct(shape, jnp.float32),
        in_specs=[vmem] * len(operands),
        out_specs=pl.BlockSpec(memory_space=pl.ANY),
        scratch_shapes=[
            pltpu.VMEM((rows, LANES), jnp.bfloat16),
            pltpu.VMEM((rows, LANES), jnp.bfloat16),
            pltpu.VMEM(shape, jnp.float32),
            pltpu.SemaphoreType.DMA((8,)),
        ],
        compiler_params=pltpu.CompilerParams(vmem_limit_bytes=8 * MIB),
    )(*operands)


def low_sum_kernel(first, low_grad, from_left, token, low_sum):
    win = from_left.shape[2]
    rows = from_left.shape[1] - low_grad.shape[1]
    for part in range(2):
        for r in range(0, low_sum.shape[1], CHUNK):
            at, of = slice(r, r + CHUNK), slice(first + r, first + r + CHUNK)
            arrived = from_left[part, rows + first + r : rows + first + r + CHUNK, :]
            total = low_grad[part, of, :win] + arrived.astype(jnp.float32)
            low_sum[part, at, :win] = total.astype(jnp.bfloat16)
            low_sum[part, at, win:] = low_grad[part, of, win:].astype(jnp.bfloat16)


def low_sum_of(first, count, low_grad, from_left, token):
    return small_call(
        functools.partial(low_sum_kernel, first),
        jax.ShapeDtypeStruct((2, count, low_grad.shape[2]), jnp.bfloat16),
        low_grad,
        from_left,
        token,
        weight=LOW_WEIGHT,
    )


def object_update_kernel(old, own_grad, from_left, above_first, swapped, forwarded, new_object, token):
    token[...] = jnp.zeros_like(token)
    win, split = from_left.shape[2], above_first.shape[1]
    depth = split + swapped.shape[1]
    odd = lax.axis_index("row") % 2 == 1
    for part in range(2):
        for r in range(0, old.shape[1], CHUNK):
            at = slice(r, r + CHUNK)
            total = own_grad[part, at, :]
            if r < split:
                total = total + above_first[part, at, :].astype(jnp.float32)
            elif r < depth:
                of = slice(r - split, r - split + CHUNK)
                arrived = jnp.where(
                    odd,
                    swapped[part, of, :].astype(jnp.float32),
                    forwarded[part, of, :].astype(jnp.float32),
                )
                total = total + arrived
            updated = old[part, at, :].astype(jnp.float32) - total
            arrived = from_left[part, at, :].astype(jnp.float32)
            new_object[part, at, :win] = updated[:, :win] - arrived
            new_object[part, at, win:] = updated[:, win:]


def object_update(old, own_grad, from_left, above_first, swapped, forwarded):
    return small_call(
        object_update_kernel,
        (
            jax.ShapeDtypeStruct(old.shape, jnp.float32),
            jax.ShapeDtypeStruct((8, LANES), jnp.float32),
        ),
        old,
        own_grad,
        from_left,
        above_first,
        swapped,
        forwarded,
    )


def swap_cores(block):
    return lax.ppermute(block, "col", [(0, 1), (1, 0)])


def body(object_field, probe_modes, positions, counts, intensities):
    win = probe_modes.shape[1]
    modes = probe_modes.shape[2]
    number = lax.axis_size("row")
    below_right = from_next_row(object_field[:, :win, :], 1)
    probe_flat = probe_modes.reshape(2, win, modes * win)
    first_rows, first_cols = copies(object_field, win, probe_flat)
    below_left = from_next_row(first_rows, 0)
    right = from_behind(first_cols, "col", -1)
    tables, measured, probe, power = prepare(probe_flat, intensities[0, 0], right)
    made = lay_out(object_field, right, win, modes)
    corner = from_behind(first_columns(below_right, win, tables, made[0]), "col", -1)
    own_grad, low_grad, right_grad, keep, send, norm, *_ = position_gradients(
        positions[0, 0].T,
        counts.reshape(-1),
        power.reshape(1),
        object_field.shape[1:],
        (below_left, below_right),
        corner,
        probe,
        measured,
        tables,
        made,
    )
    half_rows = keep.size // LANES
    received = swap_cores(send.reshape(half_rows, LANES))
    from_left = from_behind(right_grad, "col", 1)
    digits = row_digits()
    size = half_rows // number
    ways = [digit[1] for digit in digits[:-1]] + [0]
    outs = chip_sum(keep.reshape(half_rows, LANES), received, norm, win * win, number, ways[0])
    for place, (shift, _) in enumerate(digits[:-1]):
        mine, *sends = outs
        received = [swap_rows(block, (i + 1) << shift) for i, block in enumerate(sends)]
        outs = scatter_sum(mine, sends[0], received, ways[place + 1])
    split = SPLIT * win // 8
    low_first = low_sum_of(0, split, low_grad, from_left, outs[0])
    above_first = from_behind(low_first, "row", 1)
    low_last = low_sum_of(split, win - split, low_grad, from_left, outs[0])
    swapped = swap_rows(low_last, 1)
    forwarded = lax.ppermute(swapped, "row", [(i, i + 2) for i in range(0, number - 2, 2)])
    shift, count = digits[-1]
    partners = [swap_rows(outs[0], i << shift) for i in range(1, count)]
    gathered = exchange_sum(list(outs) + partners, size)
    mine = [gathered]
    for shift, count in digits[-2::-1]:
        gathered = mine[0] if len(mine) == 1 else join(mine)
        mine = [gathered] + [swap_rows(gathered, i << shift) for i in range(1, count)]
    other = [swap_cores(block) for block in mine]
    new_object, token = object_update(
        object_field, own_grad, from_left, above_first, swapped, forwarded
    )
    new_probe = probe_update(mine, other, probe, token, probe_modes.shape, size, digits)
    return (new_object, new_probe)


def solution(mesh):
    placed = (
        P(None, ("grp", "row"), "col"),
        P(None, None, "grp", None),
        P(("grp", "row"), "col", None, None),
        P(("grp", "row"), "col"),
        P(("grp", "row"), "col", None, None, None),
    )
    return jax.shard_map(
        body,
        mesh=mesh,
        in_specs=placed,
        out_specs=(P(None, ("grp", "row"), "col"), P(None, None, "grp", None)),
        check_vma=False,
    )
```

```python
import functools

import jax
import jax.numpy as jnp
import ml_dtypes
import numpy as np
from jax import lax
from jax.experimental import pallas as pl
from jax.experimental.pallas import tpu as pltpu
from jax.sharding import PartitionSpec as P

LANES = 128
CHUNK = 32
FINE = 16
TAIL = 16
MIB = 1 << 20
LOW_WEIGHT = 8
SPLIT = 4


def from_behind(block, axis, distance):
    devices = range(lax.axis_size(axis))
    route = [(i - distance, i) for i in devices if i - distance in devices]
    return lax.ppermute(block, axis, route)


def from_next_row(block, col):
    rows, cols = lax.axis_size("row"), lax.axis_size("col")
    route = [((r + 1) * cols + col, r * cols + col) for r in range(rows - 1)]
    return lax.ppermute(block, ("row", "col"), route)


def dft_blocks(win):
    grid = np.arange(win)
    angle = 2.0 * np.pi * (grid[:, None] * grid[None, :] % win) / win
    factor = 1.0 / np.sqrt(win)
    cos_table = (np.cos(angle) * factor).astype(ml_dtypes.bfloat16)
    sin_table = (np.sin(angle) * factor).astype(ml_dtypes.bfloat16)
    blocks = []
    for parity in range(2):
        cos_part, sin_part = cos_table[parity::2, : win // 2], sin_table[parity::2, : win // 2]
        blocks.append(np.block([[cos_part, sin_part], [-sin_part, cos_part]]))
    return np.stack(blocks + [block.T for block in blocks])


def dot(left, right):
    return jnp.dot(left, right, preferred_element_type=jnp.float32)


def put_blocks(field, row, first, sources):
    parts, rows, cols = sources[0].shape
    for part in range(parts):
        for r in range(0, rows, CHUNK):
            pieces = [source[part, r : r + CHUNK, :].astype(jnp.float32) for source in sources]
            values = sum(pieces[1:], pieces[0])
            for b in range(cols // LANES):
                piece = values[:, b * LANES : (b + 1) * LANES]
                field[part, first + b, row + r : row + r + CHUNK, :] = piece


def lay_out_kernel(own, right, field, grad, probe_sum):
    put_blocks(field, 0, 0, (own,))
    put_blocks(field, 0, own.shape[2] // LANES, (right,))
    grad[...] = jnp.zeros_like(grad)
    probe_sum[...] = jnp.zeros_like(probe_sum)


def lay_out(own, right, win, modes):
    rows, cols = own.shape[1:]
    tile = (2, (cols + win) // LANES, rows + win, LANES)
    shapes = (tile, tile, (modes, 2, win // LANES, win, LANES))
    return small_call(
        lay_out_kernel,
        tuple(jax.ShapeDtypeStruct(shape, jnp.float32) for shape in shapes),
        own,
        right,
    )


def gradient_kernel(
    modes,
    starts,
    count,
    power,
    below_left,
    below_right,
    corner,
    probe,
    measured,
    tables,
    field_made,
    grad_made,
    probe_sum_made,
    own_grad,
    low_grad,
    right_grad,
    keep_out,
    send_out,
    norm_out,
    field,
    grad,
    probe_sum,
    window,
    wide,
    tall,
    wave,
):
    win = probe.shape[1]
    rows, cols = own_grad.shape[1], own_grad.shape[2]
    half = win // 2
    fine = range(0, win, FINE)
    spread = win // LANES + 1
    col_index = lax.axis_index("col")
    row_anchor = lax.axis_index("row") * rows
    col_anchor = col_index * cols

    norm_out[...] = jnp.zeros_like(norm_out)
    for first, *sources in ((0, below_left, below_right), (cols // LANES, corner)):
        put_blocks(field, rows, first, sources)
    lane = lax.broadcasted_iota(jnp.int32, (FINE, LANES), 1)

    def one_position(slot, carry):
        y, x = starts[0, slot] - row_anchor, starts[1, slot] - col_anchor
        base = x // LANES
        shift = x - base * LANES
        back_shift = (LANES - shift) % LANES
        keep = lane < LANES - shift
        for r in range(0, half, FINE):
            objs = []
            for start in (r, r + half):
                at = pl.ds(start, FINE)
                obj = []
                for part in range(2):
                    turned = [
                        pltpu.roll(field[part, base + b, pl.ds(y + start, FINE), :], back_shift, 1)
                        for b in range(spread)
                    ]
                    piece = jnp.concatenate(
                        [jnp.where(keep, a, b) for a, b in zip(turned[:-1], turned[1:])], axis=1
                    )
                    window[part, at, :] = piece
                    obj.append(piece)
                squares = obj[0] * obj[0] + obj[1] * obj[1]
                norm_out[...] += jnp.sum(squares.reshape(FINE // 8, 8, win), axis=0)
                objs.append(obj)
            for k in range(modes):
                cs = pl.ds(k * win, win)
                exits = []
                for start, (o_re, o_im) in zip((r, r + half), objs):
                    p_re, p_im = probe[0, pl.ds(start, FINE), cs], probe[1, pl.ds(start, FINE), cs]
                    exits.append((p_re * o_re - p_im * o_im, p_re * o_im + p_im * o_re))
                for part in range(2):
                    low, high = exits[0][part], exits[1][part]
                    at = pl.ds(part * half + r, FINE)
                    wide[k, 0, at, :] = (low + high).astype(jnp.bfloat16)
                    wide[k, 1, at, :] = (low - high).astype(jnp.bfloat16)

        for k in range(modes):
            for parity in range(2):
                out = dot(tables[parity], wide[k, parity])
                at = pl.ds(k * win + parity * half, half)
                for part in range(2):
                    low = out[part * half : (part + 1) * half, :half]
                    high = out[part * half : (part + 1) * half, half:]
                    to = pl.ds(part * half, half)
                    tall[0, at, to] = (low + high).astype(jnp.bfloat16)
                    tall[1, at, to] = (low - high).astype(jnp.bfloat16)
        for parity in range(2):
            wave[parity] = dot(tall[parity], tables[2 + parity])

        for r in fine:
            for parity in range(2):
                waves = []
                total = jnp.zeros((FINE, half), jnp.float32)
                for k in range(modes):
                    ka = pl.ds(k * win + r, FINE)
                    waves.append((wave[parity, ka, :half], wave[parity, ka, half:]))
                    total = total + (waves[k][0] * waves[k][0] + waves[k][1] * waves[k][1])
                gs = pl.ds(parity * half, half)
                amp = measured[slot, pl.ds(r, FINE), gs]
                ratio = 1.0 - amp * lax.rsqrt(jnp.maximum(total, 1.0))
                for k in range(modes):
                    for part in range(2):
                        at = pl.ds(part * half + r % half, FINE)
                        wide[k, r // half, at, gs] = (waves[k][part] * ratio).astype(jnp.bfloat16)

        for k in range(modes):
            even = dot(tables[2], wide[k, 0])
            odd = dot(tables[3], wide[k, 1])
            for place, out in enumerate((even + odd, even - odd)):
                at = pl.ds(k * win + place * half, half)
                for part in range(2):
                    for parity in range(2):
                        tall[parity, at, part * half : (part + 1) * half] = out[
                            part * half : (part + 1) * half, parity * half : (parity + 1) * half
                        ].astype(jnp.bfloat16)
        for parity in range(2):
            wave[parity] = dot(tall[parity], tables[parity])

        keep_high = lane >= shift
        for r in fine:
            at = pl.ds(r, FINE)
            sums = [[jnp.zeros((FINE, LANES), jnp.float32) for _ in range(2)] for _ in range(2)]
            for b in range(2):
                bs = pl.ds(b * half, half)
                o_re, o_im = window[0, at, bs], window[1, at, bs]
                for k in range(modes):
                    cs = pl.ds(k * win + b * half, half)
                    ka = pl.ds(k * win + r, FINE)
                    even, odd = wave[0, ka, :], wave[1, ka, :]
                    d = even + odd if b == 0 else even - odd
                    d_re, d_im = d[:, :half], d[:, half:]
                    p_re, p_im = probe[0, at, cs], probe[1, at, cs]
                    sums[0][b] = sums[0][b] + (p_re * d_re + p_im * d_im)
                    sums[1][b] = sums[1][b] + (p_re * d_im - p_im * d_re)
                    probe_sum[k, 0, b, at, :] += o_re * d_re + o_im * d_im
                    probe_sum[k, 1, b, at, :] += o_re * d_im - o_im * d_re
            for part in range(2):
                turned = [pltpu.roll(piece, shift, 1) for piece in sums[part]]
                turned = [jnp.zeros_like(turned[0])] + turned + [jnp.zeros_like(turned[0])]
                for b in range(spread):
                    grad[part, base + b, pl.ds(y + r, FINE), :] += jnp.where(
                        keep_high, turned[b + 1], turned[b]
                    )
        return carry

    lax.fori_loop(0, count[0], one_position, 0)
    blocks = win // LANES
    for k in range(modes):
        keep_out[k] = probe_sum[k, col_index]
        for b in range(blocks):
            at = pl.ds((k * blocks + b) * win, win)
            send_out[at, :] = probe_sum[k, 1 - col_index, b].astype(jnp.bfloat16)
    put_weight(jnp.sum(norm_out[...]) / (win * win), (send_out,))
    scale = 1.0 / jnp.full((8, LANES), power[0], jnp.float32)
    scale = jnp.concatenate([scale] * (CHUNK // 8), axis=0)

    def take_blocks(part, at, first, number):
        return jnp.concatenate(
            [grad[part, first + b, at, :] * scale for b in range(number)], axis=1
        )

    for part in range(2):
        for r in range(0, rows + win, CHUNK):
            at = pl.ds(r, CHUNK)
            piece = take_blocks(part, at, cols // LANES, win // LANES)
            right_grad[part, at, :] = piece.astype(jnp.bfloat16)
        for r in range(0, rows, CHUNK):
            at = pl.ds(r, CHUNK)
            own_grad[part, at, :] = take_blocks(part, at, 0, cols // LANES)
        for r in range(0, win, CHUNK):
            at, of = pl.ds(r, CHUNK), pl.ds(rows + r, CHUNK)
            low_grad[part, at, :] = take_blocks(part, of, 0, cols // LANES)


def position_gradients(starts, count, power, tile, below, corner, probe, measured, tables, made):
    win, modes = probe.shape[1], probe.shape[2] // probe.shape[1]
    rows, cols = tile
    f32, bf16 = jnp.float32, jnp.bfloat16
    smem = pl.BlockSpec(memory_space=pltpu.SMEM)
    vmem = pl.BlockSpec(memory_space=pltpu.VMEM)
    if win != 2 * LANES:
        raise ValueError("window size")
    slots = measured.shape[0]
    flops = 16 * slots * modes * win**3
    part_blocks = (modes, win // LANES, win, LANES)
    part_rows = modes * win // LANES * win
    return pl.pallas_call(
        functools.partial(gradient_kernel, modes),
        out_shape=(
            jax.ShapeDtypeStruct((2, rows, cols), f32),
            jax.ShapeDtypeStruct((2, win, cols), f32),
            jax.ShapeDtypeStruct((2, rows + win, win), bf16),
            jax.ShapeDtypeStruct(part_blocks, f32),
            jax.ShapeDtypeStruct((part_rows + TAIL, LANES), bf16),
            jax.ShapeDtypeStruct((8, win), f32),
        )
        + tuple(jax.ShapeDtypeStruct(array.shape, f32) for array in made),
        in_specs=[smem] * 3 + [vmem] * 9,
        out_specs=(vmem,) * 9,
        input_output_aliases={9: 6, 10: 7, 11: 8},
        scratch_shapes=[
            pltpu.VMEM((2, win, win), f32),
            pltpu.VMEM((modes, 2, win, win), bf16),
            pltpu.VMEM((2, modes * win, win), bf16),
            pltpu.VMEM((2, modes * win, win), f32),
        ],
        compiler_params=pltpu.CompilerParams(vmem_limit_bytes=16 * MIB),
        cost_estimate=pl.CostEstimate(flops=flops, bytes_accessed=12 << 20, transcendentals=0),
    )(starts, count, power, *below, corner, probe, measured, tables, *made)


def in_three(value):
    full = jnp.full((TAIL, LANES), value, jnp.float32)
    high = full.astype(jnp.bfloat16).astype(jnp.float32)
    mid = (full - high).astype(jnp.bfloat16).astype(jnp.float32)
    low = full - high - mid
    row = lax.broadcasted_iota(jnp.int32, (TAIL, LANES), 0)
    lane = lax.broadcasted_iota(jnp.int32, (TAIL, LANES), 1)
    tile = jnp.where(row == 0, high, jnp.where(row == 1, mid, jnp.where(row == 2, low, 0.0)))
    return jnp.where(lane == 0, tile, 0.0).astype(jnp.bfloat16)


def small_call(kernel, shapes, *operands, weight=1):
    return pl.pallas_call(
        kernel,
        out_shape=shapes,
        compiler_params=pltpu.CompilerParams(vmem_limit_bytes=4 * MIB),
        cost_estimate=pl.CostEstimate(flops=0, bytes_accessed=weight * MIB, transcendentals=0),
    )(*operands)


def first_columns_kernel(block, *refs):
    first = refs[-1]
    first[...] = block[:, :, : first.shape[2]]


def first_columns(block, size, *tokens):
    shape = block.shape[:2] + (size,)
    return small_call(
        first_columns_kernel, jax.ShapeDtypeStruct(shape, block.dtype), block, *tokens
    )


def copies_kernel(block, token, first_rows, first_cols):
    first_rows[...] = block[:, : first_rows.shape[1], :]
    first_cols[...] = block[:, :, : first_cols.shape[2]]


def copies(block, size, token):
    parts, rows, cols = block.shape
    shapes = ((parts, size, cols), (parts, rows, size))
    return small_call(
        copies_kernel,
        tuple(jax.ShapeDtypeStruct(shape, block.dtype) for shape in shapes),
        block,
        token,
    )


def prepare_kernel(probe, intens, blocks, token, tables, measured, wide_probe, power):
    tables[...] = blocks[...]
    count, size, _ = intens.shape
    row = lax.broadcasted_iota(jnp.int32, (size, size), 0)
    col = lax.broadcasted_iota(jnp.int32, (size, size), 1)
    to_even_first = (col == jnp.where(row < size // 2, 2 * row, 2 * row - size + 1)).astype(
        jnp.float32
    )
    from_left = to_even_first.astype(jnp.bfloat16)
    from_right = (row == jnp.where(col < size // 2, 2 * col, 2 * col - size + 1)).astype(
        jnp.float32
    )
    from_right = from_right.astype(jnp.bfloat16)
    for slot in range(count):
        turned = dot(from_left, intens[slot]).astype(jnp.bfloat16)
        measured[slot] = jnp.sqrt(dot(turned, from_right))
    win = probe.shape[1]
    modes = probe.shape[2] // win
    largest = jnp.zeros((8, win), jnp.float32)
    for r in range(0, probe.shape[1], CHUNK):
        at = slice(r, r + CHUNK)
        total = jnp.zeros((CHUNK, win), jnp.float32)
        for k in range(modes):
            for part in range(2):
                p = probe[part, at, k * win : (k + 1) * win].astype(jnp.float32)
                wide_probe[part, at, k * win : (k + 1) * win] = p
                total = total + p * p
        largest = jnp.maximum(largest, jnp.max(total.reshape(CHUNK // 8, 8, win), axis=0))
    power[0, 0] = jnp.max(largest)


def prepare(probe, intens, token):
    win = probe.shape[1]
    blocks = dft_blocks(win)
    vmem = pl.BlockSpec(memory_space=pltpu.VMEM)
    return pl.pallas_call(
        prepare_kernel,
        out_shape=(
            jax.ShapeDtypeStruct(blocks.shape, jnp.bfloat16),
            jax.ShapeDtypeStruct(intens.shape, jnp.float32),
            jax.ShapeDtypeStruct(probe.shape, jnp.float32),
            jax.ShapeDtypeStruct((1, 1), jnp.float32),
        ),
        out_specs=(vmem, vmem, vmem, pl.BlockSpec(memory_space=pltpu.SMEM)),
        compiler_params=pltpu.CompilerParams(vmem_limit_bytes=8 * MIB),
    )(probe, intens, blocks, token)


def block_shapes(number, size, ways):
    if not ways:
        return (jax.ShapeDtypeStruct((number * size + TAIL, LANES), jnp.bfloat16),)
    sends = jax.ShapeDtypeStruct((number // ways * size + TAIL, LANES), jnp.bfloat16)
    return (jax.ShapeDtypeStruct((number // ways, size, LANES), jnp.float32),) + (sends,) * (ways - 1)


def put_block(j, total, outs):
    size = total.shape[0]
    if len(outs) == 1:
        outs[0][pl.ds(j * size, size), :] = total.astype(jnp.bfloat16)
    elif j % len(outs) == 0:
        outs[0][j // len(outs)] = total
    else:
        at = pl.ds(j // len(outs) * size, size)
        outs[j % len(outs)][at, :] = total.astype(jnp.bfloat16)


def put_weight(weight, outs):
    tile = in_three(weight)
    for sent in outs if len(outs) == 1 else outs[1:]:
        sent[pl.ds(sent.shape[0] - TAIL, TAIL), :] = tile


def weight_of(block):
    return jnp.sum(block[pl.ds(block.shape[0] - TAIL, TAIL), :].astype(jnp.float32))


def chip_sum_kernel(pixels, size, keep, received, norm, *outs):
    me = lax.axis_index("row")
    for j in range(keep.shape[0] // size):
        at = pl.ds(pl.multiple_of((j ^ me) * size, size), size)
        put_block(j, keep[at, :] + received[at, :].astype(jnp.float32), outs)
    put_weight(jnp.sum(norm[...]) / pixels + weight_of(received), outs)


def chip_sum(keep, received, norm, pixels, number, ways):
    size = keep.shape[0] // number
    return small_call(
        functools.partial(chip_sum_kernel, pixels, size),
        block_shapes(number, size, ways),
        keep,
        received,
        norm,
    )


def scatter_sum_kernel(number, mine, sent, *refs):
    received, outs = refs[:number], refs[number:]
    size = mine.shape[1]
    for j in range(mine.shape[0]):
        total = mine[j]
        for block in received:
            total = total + block[pl.ds(j * size, size), :].astype(jnp.float32)
        put_block(j, total, outs)
    put_weight(pair_up([weight_of(block) for block in (sent, *received)]), outs)


def scatter_sum(mine, sent, received, ways):
    number, size, _ = mine.shape
    return small_call(
        functools.partial(scatter_sum_kernel, len(received)),
        block_shapes(number, size, ways),
        mine,
        sent,
        *received,
    )


def pair_up(terms):
    while len(terms) > 1:
        terms = [a + b for a, b in zip(terms[::2], terms[1::2])]
    return terms[0]


def exchange_sum_kernel(size, *refs):
    blocks, chunks = refs[:-1], refs[-1]
    for j in range((chunks.shape[0] - TAIL) // size):
        terms = [
            block[pl.ds((j ^ i) * size, size), :].astype(jnp.float32)
            for i, block in enumerate(blocks)
        ]
        chunks[pl.ds(j * size, size), :] = pair_up(terms).astype(jnp.bfloat16)
    put_weight(pair_up([weight_of(block) for block in blocks]), (chunks,))


def exchange_sum(blocks, size):
    return small_call(
        functools.partial(exchange_sum_kernel, size),
        jax.ShapeDtypeStruct(blocks[0].shape, jnp.bfloat16),
        *blocks,
    )


def copy_chunks(blocks, joined):
    at = 0
    for block in blocks:
        rows = block.shape[0] - TAIL
        joined[pl.ds(at, rows), :] = block[pl.ds(0, rows), :]
        at += rows
    joined[pl.ds(at, TAIL), :] = blocks[0][pl.ds(blocks[0].shape[0] - TAIL, TAIL), :]


def join_kernel(*refs):
    copy_chunks(refs[:-1], refs[-1])


def join(blocks):
    rows = sum(block.shape[0] - TAIL for block in blocks) + TAIL
    return small_call(join_kernel, jax.ShapeDtypeStruct((rows, LANES), blocks[0].dtype), *blocks)


def swap_rows(block, step):
    number = lax.axis_size("row")
    return lax.ppermute(block, "row", [(i, i ^ step) for i in range(number)])


def row_digits():
    number = lax.axis_size("row")
    if number & (number - 1) or number < 2:
        raise ValueError("row size")
    bits = number.bit_length() - 1
    return [(shift, 1 << min(2, bits - shift)) for shift in range(0, bits, 2)]


def probe_update_kernel(size, digits, mine, *refs):
    *blocks, probe, new_probe, gathered, updated, sems = refs
    copy_chunks(blocks, gathered)
    win, modes, _ = updated.shape
    col_index = lax.axis_index("col")
    part = col_index if mine else 1 - col_index
    me = lax.axis_index("row")
    piece = min(size, CHUNK)
    factor = 4.0 / jnp.full((piece, LANES), weight_of(blocks[0]), jnp.float32)

    def place(chunk):
        j = chunk ^ me
        at, span = 0, 1
        for shift, ways in reversed(digits):
            at = at + ((j >> shift) & (ways - 1)) * span
            span *= ways
        return at * size

    def update(k, b, r):
        chunk, offset = divmod((k * (win // LANES) + b) * win + r, size)
        at = pl.ds(pl.multiple_of(place(chunk) + offset, piece), piece)
        total = gathered[at, :].astype(jnp.float32)
        col = k * win + b * LANES
        old = probe[part, r : r + piece, col : col + LANES]
        updated[r : r + piece, k, b * LANES : (b + 1) * LANES] = old - factor * total

    stretch = win // 4
    copies = []
    for start in range(0, win, stretch):
        for r in range(start, start + stretch, piece):
            for k in range(modes):
                for b in range(win // LANES):
                    update(k, b, r)
        at = pl.ds(start, stretch)
        copies.append(
            pltpu.make_async_copy(updated.at[at], new_probe.at[part, at], sems.at[len(copies)])
        )
        copies[-1].start()
    for copy in copies:
        copy.wait()


def probe_update(blocks, probe, shape, size, digits, first_result=None, token=None):
    vmem, anywhere = pl.BlockSpec(memory_space=pltpu.VMEM), pl.BlockSpec(memory_space=pl.ANY)
    rows = sum(block.shape[0] - TAIL for block in blocks) + TAIL
    operands = [*blocks, probe]
    mine = first_result is None
    kernel = functools.partial(probe_update_kernel, size, digits, mine)
    if not mine:
        number = len(operands)

        def kernel(*refs):
            probe_update_kernel(size, digits, mine, *refs[:number], *refs[number + 2 :])

    extra = [] if mine else [token, first_result]
    return pl.pallas_call(
        kernel,
        out_shape=jax.ShapeDtypeStruct(shape, jnp.float32),
        in_specs=[vmem] * len(operands) + [vmem, anywhere][: len(extra)],
        out_specs=anywhere,
        scratch_shapes=[
            pltpu.VMEM((rows, LANES), jnp.bfloat16),
            pltpu.VMEM(shape[1:], jnp.float32),
            pltpu.SemaphoreType.DMA((4,)),
        ],
        input_output_aliases={} if mine else {len(operands) + 1: 0},
        compiler_params=pltpu.CompilerParams(vmem_limit_bytes=4 * MIB),
    )(*operands, *extra)


def low_sum_kernel(first, low_grad, from_left, token, low_sum):
    win = from_left.shape[2]
    rows = from_left.shape[1] - low_grad.shape[1]
    for part in range(2):
        for r in range(0, low_sum.shape[1], CHUNK):
            at, of = slice(r, r + CHUNK), slice(first + r, first + r + CHUNK)
            arrived = from_left[part, rows + first + r : rows + first + r + CHUNK, :]
            total = low_grad[part, of, :win] + arrived.astype(jnp.float32)
            low_sum[part, at, :win] = total.astype(jnp.bfloat16)
            low_sum[part, at, win:] = low_grad[part, of, win:].astype(jnp.bfloat16)


def low_sum_of(first, count, low_grad, from_left, token):
    return small_call(
        functools.partial(low_sum_kernel, first),
        jax.ShapeDtypeStruct((2, count, low_grad.shape[2]), jnp.bfloat16),
        low_grad,
        from_left,
        token,
        weight=LOW_WEIGHT,
    )


def object_update_kernel(old, own_grad, from_left, above_first, swapped, forwarded, new_object, token):
    token[...] = jnp.zeros_like(token)
    win, split = from_left.shape[2], above_first.shape[1]
    depth = split + swapped.shape[1]
    odd = lax.axis_index("row") % 2 == 1
    for part in range(2):
        for r in range(0, old.shape[1], CHUNK):
            at = slice(r, r + CHUNK)
            total = own_grad[part, at, :]
            if r < split:
                total = total + above_first[part, at, :].astype(jnp.float32)
            elif r < depth:
                of = slice(r - split, r - split + CHUNK)
                arrived = jnp.where(
                    odd,
                    swapped[part, of, :].astype(jnp.float32),
                    forwarded[part, of, :].astype(jnp.float32),
                )
                total = total + arrived
            updated = old[part, at, :].astype(jnp.float32) - total
            arrived = from_left[part, at, :].astype(jnp.float32)
            new_object[part, at, :win] = updated[:, :win] - arrived
            new_object[part, at, win:] = updated[:, win:]


def object_update(old, own_grad, from_left, above_first, swapped, forwarded):
    return small_call(
        object_update_kernel,
        (
            jax.ShapeDtypeStruct(old.shape, jnp.float32),
            jax.ShapeDtypeStruct((8, LANES), jnp.float32),
        ),
        old,
        own_grad,
        from_left,
        above_first,
        swapped,
        forwarded,
    )


def swap_cores(block):
    return lax.ppermute(block, "col", [(0, 1), (1, 0)])


def body(object_field, probe_modes, positions, counts, intensities):
    win = probe_modes.shape[1]
    modes = probe_modes.shape[2]
    number = lax.axis_size("row")
    below_right = from_next_row(object_field[:, :win, :], 1)
    probe_flat = probe_modes.reshape(2, win, modes * win)
    first_rows, first_cols = copies(object_field, win, probe_flat)
    below_left = from_next_row(first_rows, 0)
    right = from_behind(first_cols, "col", -1)
    tables, measured, probe, power = prepare(probe_flat, intensities[0, 0], right)
    made = lay_out(object_field, right, win, modes)
    corner = from_behind(first_columns(below_right, win, tables, made[0]), "col", -1)
    own_grad, low_grad, right_grad, keep, send, norm, *_ = position_gradients(
        positions[0, 0].T,
        counts.reshape(-1),
        power.reshape(1),
        object_field.shape[1:],
        (below_left, below_right),
        corner,
        probe,
        measured,
        tables,
        made,
    )
    half_rows = keep.size // LANES
    received = swap_cores(send)
    from_left = from_behind(right_grad, "col", 1)
    digits = row_digits()
    size = half_rows // number
    ways = [digit[1] for digit in digits[:-1]] + [0]
    outs = chip_sum(keep.reshape(half_rows, LANES), received, norm, win * win, number, ways[0])
    for place, (shift, _) in enumerate(digits[:-1]):
        mine, *sends = outs
        received = [swap_rows(block, (i + 1) << shift) for i, block in enumerate(sends)]
        outs = scatter_sum(mine, sends[0], received, ways[place + 1])
    split = SPLIT * win // 8
    low_first = low_sum_of(0, split, low_grad, from_left, outs[0])
    above_first = from_behind(low_first, "row", 1)
    low_last = low_sum_of(split, win - split, low_grad, from_left, outs[0])
    swapped = swap_rows(low_last, 1)
    forwarded = lax.ppermute(swapped, "row", [(i, i + 2) for i in range(0, number - 2, 2)])
    shift, count = digits[-1]
    partners = [swap_rows(outs[0], i << shift) for i in range(1, count)]
    gathered = exchange_sum(list(outs) + partners, size)
    mine = [gathered]
    for shift, count in digits[-2::-1]:
        gathered = mine[0] if len(mine) == 1 else join(mine)
        mine = [gathered] + [swap_rows(gathered, i << shift) for i in range(1, count)]
    other = [swap_cores(block) for block in mine]
    new_object, token = object_update(
        object_field, own_grad, from_left, above_first, swapped, forwarded
    )
    shape = probe_modes.shape
    first_result = probe_update(mine, probe, shape, size, digits)
    new_probe = probe_update(other, probe, shape, size, digits, first_result, token)
    return (new_object, new_probe)


def solution(mesh):
    placed = (
        P(None, ("grp", "row"), "col"),
        P(None, None, "grp", None),
        P(("grp", "row"), "col", None, None),
        P(("grp", "row"), "col"),
        P(("grp", "row"), "col", None, None, None),
    )
    return jax.shard_map(
        body,
        mesh=mesh,
        in_specs=placed,
        out_specs=(P(None, ("grp", "row"), "col"), P(None, None, "grp", None)),
        check_vma=False,
    )
```
